32 devices in a mesh: fsdp: 4 (over z), ctx: 8 (over y, x, core).
Axes of the slice: x: 2, y: 2, z: 4, core: 2. Of those that a mesh axis runs over, the one named last changes fastest.
Arguments:
- tokens: bfloat16 [4, 2, 512, 1600], P('fsdp', None, 'ctx'), may hold values from -6 to 6
- first_gain: bfloat16 [1600], P('fsdp'), may hold values from 0.25 to 1.75
- first_shift: bfloat16 [1600], P('fsdp'), may hold values from -2 to 2
- mixer_weight: bfloat16 [1600, 4800], P('fsdp'), may hold values from -0.15625 to 0.15625
- query_bias: bfloat16 [1600], P('fsdp'), may hold values from -3 to 3
- value_bias: bfloat16 [1600], P('fsdp'), may hold values from -3 to 3
- merge_weight: bfloat16 [1600, 1600], P('fsdp'), may hold values from -1 to 1
- merge_bias: bfloat16 [1600], P('fsdp'), may hold values from -2 to 2
- second_gain: bfloat16 [1600], P('fsdp'), may hold values from 0.25 to 1.75
- second_shift: bfloat16 [1600], P('fsdp'), may hold values from -2 to 2
- expand_weight: bfloat16 [1600, 6400], P('fsdp'), may hold values from -0.15625 to 0.15625
- expand_bias: bfloat16 [6400], P('fsdp'), may hold values from -2 to 2
- shrink_weight: bfloat16 [6400, 1600], P('fsdp'), may hold values from -0.078125 to 0.078125
- shrink_bias: bfloat16 [1600], P('fsdp'), may hold values from -2 to 2
- cotangent: bfloat16 [4, 2, 512, 1600], P('fsdp', None, 'ctx'), may hold values from -6 to 6
Outputs:
- output: bfloat16 [4, 2, 512, 1600], P('fsdp', None, 'ctx')
- input_grad: float32 [4, 2, 512, 1600], P('fsdp', None, 'ctx')
- first_gain_grad: float32 [1600], P('fsdp')
- first_shift_grad: float32 [1600], P('fsdp')
- mixer_weight_grad: float32 [1600, 4800], P('fsdp')
- query_bias_grad: float32 [1600], P('fsdp')
- value_bias_grad: float32 [1600], P('fsdp')
- merge_weight_grad: float32 [1600, 1600], P('fsdp')
- merge_bias_grad: float32 [1600], P('fsdp')
- second_gain_grad: float32 [1600], P('fsdp')
- second_shift_grad: float32 [1600], P('fsdp')
- expand_weight_grad: float32 [1600, 6400], P('fsdp')
- expand_bias_grad: float32 [6400], P('fsdp')
- shrink_weight_grad: float32 [6400, 1600], P('fsdp')
- shrink_bias_grad: float32 [1600], P('fsdp')
The draws below stay inside these ranges and needn't reach their ends.
All inputs are finite; a program needn't handle non-finite values.
Results may differ from the reference program's by a relative error of at most 0.0095.
Values may be sent and summed in bfloat16 or wider, within the bound.
A program may use at most 384 MiB of HBM per device.

```python
import jax
import jax.numpy as jnp
from jax import lax

D = 1600
H = 25
HD = 64
FF = 6400
SEQS = 4
HALF = 512


def block_scale(stream_key, dims, pieces, smallest, top_value):
    def one(position, shards_of):
        steps = jax.random.uniform(jax.random.fold_in(jax.random.fold_in(stream_key, 6), position), (shards_of,), jnp.float32, smallest / len(pieces), top_value / len(pieces))
        return jnp.repeat(jnp.exp(steps), dims[position] // shards_of).reshape((-1,) + (1,) * (len(dims) - position - 1))

    loudness = one(*pieces[0])
    for cut in pieces[1:]:
        loudness = loudness * one(*cut)
    return loudness


def noise(stream_key, dims, width, limit, shards=(), held_as=jnp.bfloat16):
    level = block_scale(stream_key, dims, shards, -0.22, 0.18) if shards else 1.0
    values = jax.random.normal(stream_key, dims, jnp.float32) * width * level
    return jnp.minimum(jnp.maximum(values, -limit), limit).astype(held_as)


def setup_inputs(seed: int = 0) -> dict:
    key_list = jax.random.split(jax.random.key(seed), 16)
    tokens = noise(key_list[0], (SEQS, 2, HALF, D), 1.0, 6.0, ((0, 4), (2, 8)))
    first_gain = jnp.clip(1.0 + 0.15 * jax.random.normal(key_list[1], (D,), jnp.float32), 0.25, 1.75).astype(jnp.bfloat16)
    first_shift = noise(key_list[2], (D,), 0.3, 2.0, ((0, 4),))
    mixer_weight = noise(key_list[3], (D, 3 * D), D ** -0.5, 0.15625, ((0, 4),))
    query_bias = noise(key_list[4], (D,), 0.5, 3.0, ((0, 4),))
    value_bias = noise(key_list[5], (D,), 0.5, 3.0, ((0, 4),))
    merge_weight = noise(key_list[6], (D, D), 32 ** -0.5, 1.0, ((0, 4),))
    merge_bias = noise(key_list[7], (D,), 0.3, 2.0, ((0, 4),))
    second_gain = jnp.clip(1.0 + 0.15 * jax.random.normal(key_list[8], (D,), jnp.float32), 0.25, 1.75).astype(jnp.bfloat16)
    second_shift = noise(key_list[9], (D,), 0.3, 2.0, ((0, 4),))
    expand_weight = noise(key_list[10], (D, FF), D ** -0.5, 0.15625, ((0, 4),))
    expand_bias = noise(key_list[11], (FF,), 0.3, 2.0, ((0, 4),))
    shrink_weight = noise(key_list[12], (FF, D), FF ** -0.5, 0.078125, ((0, 4),))
    shrink_bias = noise(key_list[13], (D,), 0.3, 2.0, ((0, 4),))
    cotangent = noise(key_list[14], (SEQS, 2, HALF, D), 1.0, 6.0, ((0, 4), (2, 8)))
    return {"tokens": tokens, "first_gain": first_gain, "first_shift": first_shift, "mixer_weight": mixer_weight, "query_bias": query_bias, "value_bias": value_bias, "merge_weight": merge_weight, "merge_bias": merge_bias, "second_gain": second_gain, "second_shift": second_shift, "expand_weight": expand_weight, "expand_bias": expand_bias, "shrink_weight": shrink_weight, "shrink_bias": shrink_bias, "cotangent": cotangent}


EPSILON = 1e-05

@jax.custom_vjp
def low(v):
    return lax.optimization_barrier(v.astype(jnp.bfloat16)).astype(jnp.float32)

@jax.custom_vjp
def low_back(v):
    return v

def low_keep(v):
    return (low(v), None)

def low_pass(kept, grad):
    return (grad,)

def back_keep(v):
    return (v, None)

def back_low(kept, grad):
    return (low(grad),)
low.defvjp(low_keep, low_pass)
low_back.defvjp(back_keep, back_low)

def highest(left_side, right_side):
    return jnp.dot(left_side, right_side, precision=lax.Precision.HIGHEST)

def layer_norm(values, gain, shift):
    center = values - lax.optimization_barrier(jnp.mean(values, axis=-1, keepdims=True))
    spread = lax.optimization_barrier(jnp.mean(center * center, axis=-1, keepdims=True))
    return center * lax.rsqrt(spread + EPSILON) * gain + shift

def positions(length):
    half_index = jnp.arange(length // 2, dtype=jnp.int32)
    return jnp.concatenate([half_index, length - 1 - half_index])

def head_attend(query_head, key_head, value_head, allowed):
    scores = low_back(highest(query_head, key_head.T) * 0.125)
    scores = jnp.where(allowed > 0, scores, -1e+30)
    top = lax.optimization_barrier(jnp.max(scores, axis=1, keepdims=True))
    expo = jnp.exp(scores - top)
    probs = low(expo / lax.optimization_barrier(jnp.sum(expo, axis=1, keepdims=True)))
    return highest(probs, value_head)

def forward(token_rows, weights, allowed):
    first_gain, first_shift, mixer_weight, query_bias, value_bias, merge_weight, merge_bias, second_gain, second_shift, expand_weight, expand_bias, shrink_weight, shrink_bias = weights
    length = token_rows.shape[0]
    first = low(layer_norm(token_rows, first_gain, first_shift))
    mixed = highest(first, mixer_weight)
    query = low(low_back(mixed[:, :D]) + query_bias)
    keyed = low(low_back(mixed[:, D:2 * D]))
    valued = low(low_back(mixed[:, 2 * D:]) + value_bias)

    def split_heads(values):
        return values.reshape(length, H, HD).transpose(1, 0, 2)

    def one_head(triple):
        return head_attend(triple[0], triple[1], triple[2], allowed)
    outputs = lax.map(jax.checkpoint(one_head), (split_heads(query), split_heads(keyed), split_heads(valued)))
    attended = low(low_back(outputs.transpose(1, 0, 2).reshape(length, D)))
    hidden = token_rows + low_back(highest(attended, merge_weight)) + merge_bias
    second = low(layer_norm(hidden, second_gain, second_shift))
    pre = low_back(highest(second, expand_weight)) + expand_bias
    act = low(jax.nn.gelu(pre, approximate=True))
    return hidden + highest(act, shrink_weight) + shrink_bias

def reference(tokens, first_gain, first_shift, mixer_weight, query_bias, value_bias, merge_weight, merge_bias, second_gain, second_shift, expand_weight, expand_bias, shrink_weight, shrink_bias, cotangent):
    weights = tuple((member.astype(jnp.float32) for member in (first_gain, first_shift, mixer_weight, query_bias, value_bias, merge_weight, merge_bias, second_gain, second_shift, expand_weight, expand_bias, shrink_weight, shrink_bias)))
    length = 2 * HALF
    place = positions(length)
    allowed = (place[None, :] <= place[:, None]).astype(jnp.int32)

    def one_sequence(totals, paired):
        sequence, tangent = paired
        flat = sequence.astype(jnp.float32).reshape(length, D)
        result, pull = jax.vjp(lambda token_rows, params: forward(token_rows, params, allowed), flat, weights)
        row_grad, weight_grads = pull(tangent.astype(jnp.float32).reshape(length, D))
        totals = tuple((earlier + update for earlier, update in zip(totals, weight_grads)))
        return (totals, (result.astype(jnp.bfloat16).reshape(2, HALF, D), row_grad.reshape(2, HALF, D)))
    zeros = tuple((jnp.zeros_like(member) for member in weights))
    totals, (output, input_grad) = lax.scan(one_sequence, zeros, (tokens, cotangent))
    return (output, input_grad, totals[0], totals[1], totals[2], totals[3], totals[4], totals[5], totals[6], totals[7], totals[8], totals[9], totals[10], totals[11], totals[12])
```

```python
import jax
import jax.numpy as jnp
from jax import lax
from jax.sharding import PartitionSpec as P

D = 1600
H = 25
HD = 64

EPSILON = 1e-05
SCORE_SCALE = 0.125
BF = jnp.bfloat16
F32 = jnp.float32


def normalize(values):
    center = values - jnp.mean(values, axis=-1, keepdims=True)
    spread = jnp.mean(center * center, axis=-1, keepdims=True)
    inverse = lax.rsqrt(spread + EPSILON)
    return center * inverse, inverse


def norm_back(grad, gain, normal, inverse):
    scaled = grad * gain
    mean = jnp.mean(scaled, axis=-1, keepdims=True)
    along = jnp.mean(scaled * normal, axis=-1, keepdims=True)
    return inverse * (scaled - mean - normal * along)


def dot(a, b):
    return jnp.dot(a, b, preferred_element_type=F32)


def dot_t(a, b):
    return lax.dot_general(a, b, (((1,), (1,)), ((), ())), preferred_element_type=F32)


def t_dot(a, b):
    return lax.dot_general(a, b, (((0,), (0,)), ((), ())), preferred_element_type=F32)


def attend(query, key, value, allowed):
    scores = jnp.einsum("hqd,hkd->hqk", query, key, preferred_element_type=F32) * SCORE_SCALE
    scores = jnp.where(allowed[None], scores, -1e30)
    top = jnp.max(scores, axis=-1, keepdims=True)
    expo = jnp.exp(scores - top)
    total = jnp.sum(expo, axis=-1, keepdims=True)
    probs = (expo / total).astype(BF)
    return jnp.einsum("hqk,hkd->hqd", probs, value, preferred_element_type=F32), top, total


def attend_back(query, key, value, allowed, top, total, grad):
    scores = jnp.einsum("hqd,hkd->hqk", query, key, preferred_element_type=F32) * SCORE_SCALE
    scores = jnp.where(allowed[None], scores, -1e30)
    probs = jnp.exp(scores - top) / total
    probs_low = probs.astype(BF)
    prob_grad = jnp.einsum("hqd,hkd->hqk", grad, value, preferred_element_type=F32)
    offset = jnp.sum(prob_grad * probs, axis=-1, keepdims=True)
    score_grad = (probs * (prob_grad - offset)).astype(BF)
    dq = jnp.einsum("hqk,hkd->hqd", score_grad, key, preferred_element_type=F32) * SCORE_SCALE
    dk = jnp.einsum("hqk,hqd->hkd", score_grad, query, preferred_element_type=F32) * SCORE_SCALE
    dv = jnp.einsum("hqk,hqd->hkd", probs_low, grad, preferred_element_type=F32)
    return dq, dk, dv


def heads_first(values):
    rows, columns = values.shape
    return values.reshape(rows, columns // HD, HD).transpose(1, 0, 2)


def heads_last(values):
    heads, rows, _ = values.shape
    return values.transpose(1, 0, 2).reshape(rows, heads * HD)


def local(
    tokens,
    first_gain,
    first_shift,
    mixer_weight,
    query_bias,
    value_bias,
    merge_weight,
    merge_bias,
    second_gain,
    second_shift,
    expand_weight,
    expand_bias,
    shrink_weight,
    shrink_bias,
    cotangent,
):
    planes = lax.axis_size("fsdp")
    ring = lax.axis_size("ctx")
    me = lax.axis_index("ctx")
    blocks = tokens.shape[2]
    local_rows = 2 * blocks
    half = blocks * ring
    length = 2 * half
    private = H // ring
    shared = H - private * ring
    pc, sc = private * HD, shared * HD
    hc = pc + sc
    shared_at = private * ring * HD
    share = D // planes
    ff_plane = expand_bias.shape[0]
    ff_part = ff_plane // ring
    cols = D // ring

    vectors = jnp.stack(
        [first_gain, first_shift, query_bias, value_bias, merge_bias, second_gain, second_shift, shrink_bias]
    )
    vectors = lax.all_gather(vectors, "fsdp", axis=1, tiled=True).astype(F32)
    gain1, shift1, qbias, vbias, mbias, gain2, shift2, sbias = [vectors[n] for n in range(8)]

    def head_columns(weight, base):
        mine = lax.dynamic_slice_in_dim(weight, base + me * pc, pc, weight.ndim - 1)
        every = weight[..., base + shared_at : base + D]
        return [mine, every]

    mixer_part = jnp.concatenate(
        head_columns(mixer_weight, 0) + head_columns(mixer_weight, D) + head_columns(mixer_weight, 2 * D), axis=1
    )
    mixer_mine = lax.all_gather(mixer_part, "fsdp", axis=0, tiled=True)

    merge_part = lax.dynamic_slice_in_dim(merge_weight, me * cols, cols, 1)
    merge_cols = lax.all_gather(merge_part, "fsdp", axis=0, tiled=True)
    merge_full = lax.all_gather(merge_cols, "ctx", axis=1, tiled=True)

    expand_part = expand_weight.reshape(share, planes, ring, ff_part)
    expand_part = lax.dynamic_index_in_dim(expand_part, me, 2, keepdims=False)
    expand_part = lax.all_to_all(expand_part, "fsdp", 1, 0, tiled=False).reshape(D, ff_part)
    expand_mine = lax.all_gather(expand_part, "ctx", axis=1, tiled=True)

    rows = tokens.reshape(local_rows, D).astype(F32)
    normal1, inverse1 = normalize(rows)
    first = (normal1 * gain1 + shift1).astype(BF)
    first_all = lax.all_gather(first.reshape(2, blocks, D), "ctx", axis=1, tiled=True).reshape(length, D)
    tangent_low = cotangent.reshape(local_rows, D)
    tangent = tangent_low.astype(F32)
    tangent_all = lax.all_gather(tangent_low, "fsdp", axis=0, tiled=True)

    mixed = dot(first_all, mixer_mine)
    qb = jnp.concatenate(head_columns(qbias, 0), axis=0)
    vb = jnp.concatenate(head_columns(vbias, 0), axis=0)
    query = (mixed[:, :hc] + qb).astype(BF)
    key = mixed[:, hc : 2 * hc].astype(BF)
    value = (mixed[:, 2 * hc :] + vb).astype(BF)
    half_index = jnp.arange(half, dtype=jnp.int32)
    place = jnp.concatenate([half_index, length - 1 - half_index])
    early = me * blocks + jnp.arange(blocks, dtype=jnp.int32)
    own_place = jnp.concatenate([early, length - 1 - early])
    allowed = place[None, :] <= place[:, None]
    own_allowed = place[None, :] <= own_place[:, None]

    def own_rows(values):
        parts = values.reshape(2, half, values.shape[1])
        return lax.dynamic_slice_in_dim(parts, me * blocks, blocks, 1).reshape(local_rows, values.shape[1])

    qp, kp, vp = heads_first(query[:, :pc]), heads_first(key[:, :pc]), heads_first(value[:, :pc])
    qs, ks, vs = heads_first(own_rows(query[:, pc:])), heads_first(key[:, pc:]), heads_first(value[:, pc:])
    out_p, top_p, total_p = attend(qp, kp, vp, allowed)
    out_s, top_s, total_s = attend(qs, ks, vs, own_allowed)
    att_heads = heads_last(out_p).astype(BF)
    att_pieces = lax.all_to_all(att_heads.reshape(2, ring, blocks, pc), "ctx", 1, 2, tiled=False)
    attended = jnp.concatenate(
        [att_pieces.reshape(local_rows, ring * pc), heads_last(out_s).astype(BF)], axis=1
    )
    hidden = rows + dot(attended, merge_full) + mbias
    normal2, inverse2 = normalize(hidden)
    second = (normal2 * gain2 + shift2).astype(BF)
    second_all = lax.all_gather(second, "fsdp", axis=0, tiled=True)
    attended_all = lax.all_gather(attended, "ctx", axis=0, tiled=True)

    pre = dot(second_all, expand_mine) + expand_bias.astype(F32)
    act, gate_pull = jax.vjp(lambda u: jax.nn.gelu(u, approximate=True), pre)
    act_low = act.astype(BF)
    act_grad = dot_t(tangent_all, shrink_weight)
    (pre_grad,) = gate_pull(act_grad)
    pre_low = pre_grad.astype(BF)
    second_part = dot_t(pre_low, expand_mine).astype(BF)
    second_grad = lax.psum_scatter(second_part, "fsdp", scatter_dimension=0, tiled=True).astype(F32)
    out_part = dot(act_low, shrink_weight).astype(BF)
    out_sum = lax.psum_scatter(out_part, "fsdp", scatter_dimension=0, tiled=True).astype(F32)
    output = (hidden + out_sum + sbias).astype(BF).reshape(1, 2, blocks, D)
    expand_bias_grad = jnp.sum(pre_grad, axis=0)
    shrink_grad = t_dot(act_low, tangent_all).astype(BF)
    shrink_mine = lax.psum_scatter(shrink_grad, "ctx", scatter_dimension=0, tiled=True)
    shrink_owned = lax.all_gather(shrink_mine, "ctx", axis=0, tiled=True).astype(F32)
    expand_grad = t_dot(second_all, pre_low).astype(BF)
    expand_cols = lax.psum_scatter(expand_grad, "ctx", scatter_dimension=1, tiled=True)
    expand_rows = lax.all_to_all(expand_cols.reshape(planes, share, ff_part), "fsdp", 0, 1, tiled=False)
    expand_owned = (
        lax.all_gather(expand_rows, "ctx", axis=2, tiled=False).reshape(share, planes * ff_plane).astype(F32)
    )

    hidden_grad = tangent + norm_back(second_grad, gain2, normal2, inverse2)
    hidden_low = hidden_grad.astype(BF)
    att_grad = dot_t(hidden_low, merge_full).astype(BF)
    grad_pieces = lax.all_to_all(att_grad[:, :shared_at].reshape(2, blocks, ring, pc), "ctx", 2, 1, tiled=False)
    grad_p = heads_first(grad_pieces.reshape(length, pc))
    grad_s = heads_first(att_grad[:, shared_at:])
    dqp, dkp, dvp = attend_back(qp, kp, vp, allowed, top_p, total_p, grad_p)
    dqs, dks, dvs = attend_back(qs, ks, vs, own_allowed, top_s, total_s, grad_s)
    dqs_all = jnp.zeros((2, half, sc), F32)
    dqs_all = lax.dynamic_update_slice_in_dim(dqs_all, heads_last(dqs).reshape(2, blocks, sc), me * blocks, 1)
    mixed_grad = jnp.concatenate(
        [heads_last(dqp), dqs_all.reshape(length, sc)]
        + [heads_last(dkp), heads_last(dks), heads_last(dvp), heads_last(dvs)],
        axis=1,
    )
    bias_sums = jnp.sum(mixed_grad, axis=0)
    mixed_low = mixed_grad.astype(BF)
    first_part = dot_t(mixed_low, mixer_mine).astype(BF)
    first_grad = lax.psum_scatter(
        first_part.reshape(2, half, D), "ctx", scatter_dimension=1, tiled=True
    ).reshape(local_rows, D).astype(F32)
    input_grad = hidden_grad + norm_back(first_grad, gain1, normal1, inverse1)
    mixer_part_grad = t_dot(first_all, mixed_low).astype(BF)
    mixer_rows = lax.psum_scatter(mixer_part_grad, "fsdp", scatter_dimension=0, tiled=True)
    mixer_all = lax.all_gather(mixer_rows, "ctx", axis=0, tiled=False).astype(F32)

    def place_columns(values):
        mine = values[:, :, :pc].transpose(1, 0, 2).reshape(share, ring * pc)
        return [mine, jnp.sum(values[:, :, pc:], axis=0)]

    mixer_owned = jnp.concatenate(
        place_columns(mixer_all[:, :, :hc])
        + place_columns(mixer_all[:, :, hc : 2 * hc])
        + place_columns(mixer_all[:, :, 2 * hc :]),
        axis=1,
    )
    hidden_cols = lax.all_to_all(hidden_low.reshape(local_rows, ring, cols), "ctx", 1, 0, tiled=False)
    merge_grad = t_dot(attended_all, hidden_cols.reshape(length, cols)).astype(BF)
    merge_rows = lax.psum_scatter(merge_grad, "fsdp", scatter_dimension=0, tiled=True)
    merge_owned = lax.all_gather(merge_rows, "ctx", axis=1, tiled=True).astype(F32)

    def spread_bias(values):
        full = jnp.zeros((D,), F32)
        full = lax.dynamic_update_slice_in_dim(full, values[:pc], me * pc, 0)
        return full.at[shared_at:].set(values[pc:])

    sums = jnp.stack(
        [
            jnp.sum(first_grad * normal1, axis=0),
            jnp.sum(first_grad, axis=0),
            spread_bias(bias_sums[:hc]),
            spread_bias(bias_sums[2 * hc :]),
            jnp.sum(hidden_grad, axis=0),
            jnp.sum(second_grad * normal2, axis=0),
            jnp.sum(second_grad, axis=0),
            jnp.sum(tangent, axis=0),
        ]
    )
    sums = lax.psum(sums, ("fsdp", "ctx"))
    mine = lax.dynamic_slice_in_dim(sums, lax.axis_index("fsdp") * share, share, 1)
    expand_bias_owned = lax.psum(expand_bias_grad, "ctx")

    return (
        output,
        input_grad.reshape(1, 2, blocks, D),
        mine[0],
        mine[1],
        mixer_owned,
        mine[2],
        mine[3],
        merge_owned,
        mine[4],
        mine[5],
        mine[6],
        expand_owned,
        expand_bias_owned,
        shrink_owned,
        mine[7],
    )


def solution(mesh):
    token_spec = P("fsdp", None, "ctx", None)
    row = P("fsdp")
    matrix = P("fsdp", None)
    in_specs = (
        token_spec,
        row,
        row,
        matrix,
        row,
        row,
        matrix,
        row,
        row,
        row,
        matrix,
        row,
        matrix,
        row,
        token_spec,
    )
    out_specs = (
        token_spec,
        token_spec,
        row,
        row,
        matrix,
        row,
        row,
        matrix,
        row,
        row,
        row,
        matrix,
        row,
        matrix,
        row,
    )
    return jax.shard_map(local, mesh=mesh, in_specs=in_specs, out_specs=out_specs, check_vma=False)
```

```python
import functools

import jax
import jax.numpy as jnp
from jax import lax
from jax.experimental import pallas as pl
from jax.experimental.pallas import tpu as pltpu
from jax.sharding import PartitionSpec as P

D = 1600
H = 25
HD = 64

EPSILON = 1e-05
SCORE_SCALE = 0.125
BF = jnp.bfloat16
F32 = jnp.float32


def normalize(values):
    center = values - jnp.mean(values, axis=-1, keepdims=True)
    spread = jnp.mean(center * center, axis=-1, keepdims=True)
    inverse = lax.rsqrt(spread + EPSILON)
    return center * inverse, inverse


def norm_back(grad, gain, normal, inverse):
    scaled = grad * gain
    mean = jnp.mean(scaled, axis=-1, keepdims=True)
    along = jnp.mean(scaled * normal, axis=-1, keepdims=True)
    return inverse * (scaled - mean - normal * along)


def dot(a, b):
    return jnp.dot(a, b, preferred_element_type=F32)


def dot_t(a, b):
    return lax.dot_general(a, b, (((1,), (1,)), ((), ())), preferred_element_type=F32)


def t_dot(a, b):
    return lax.dot_general(a, b, (((0,), (0,)), ((), ())), preferred_element_type=F32)


def attend(query, key, value, allowed):
    scores = jnp.einsum("hqd,hkd->hqk", query, key, preferred_element_type=F32) * SCORE_SCALE
    scores = jnp.where(allowed[None], scores, -1e30)
    top = jnp.max(scores, axis=-1, keepdims=True)
    expo = jnp.exp(scores - top)
    total = jnp.sum(expo, axis=-1, keepdims=True)
    probs = (expo / total).astype(BF)
    return jnp.einsum("hqk,hkd->hqd", probs, value, preferred_element_type=F32), top, total


def attend_back(query, key, value, allowed, top, total, grad):
    scores = jnp.einsum("hqd,hkd->hqk", query, key, preferred_element_type=F32) * SCORE_SCALE
    scores = jnp.where(allowed[None], scores, -1e30)
    probs = jnp.exp(scores - top) / total
    probs_low = probs.astype(BF)
    prob_grad = jnp.einsum("hqd,hkd->hqk", grad, value, preferred_element_type=F32)
    offset = jnp.sum(prob_grad * probs, axis=-1, keepdims=True)
    score_grad = (probs * (prob_grad - offset)).astype(BF)
    dq = jnp.einsum("hqk,hkd->hqd", score_grad, key, preferred_element_type=F32) * SCORE_SCALE
    dk = jnp.einsum("hqk,hqd->hkd", score_grad, query, preferred_element_type=F32) * SCORE_SCALE
    dv = jnp.einsum("hqk,hqd->hkd", probs_low, grad, preferred_element_type=F32)
    return dq, dk, dv


def heads_first(values):
    rows, columns = values.shape
    return values.reshape(rows, columns // HD, HD).transpose(1, 0, 2)


def heads_last(values):
    heads, rows, _ = values.shape
    return values.transpose(1, 0, 2).reshape(rows, heads * HD)


MESH_ID = pl.DeviceIdType.MESH
HOPS = (2, 4, 6)


def dyn(start, size, step):
    return pl.ds(pl.multiple_of(start, step), size)


class Links:

    def __init__(self, planes):
        self.planes = planes
        self.p = lax.axis_index("fsdp")
        self.me = lax.axis_index("ctx")

    def plane(self, step):
        return (self.p + step, self.me)

    def peer(self, mask):
        return (self.p, self.me ^ mask)

    def copy(self, src, dst, send, recv, device):
        return pltpu.make_async_remote_copy(
            src_ref=src, dst_ref=dst, send_sem=send, recv_sem=recv, device_id=device, device_id_type=MESH_ID
        )

    def barrier(self, masks):
        bar = pltpu.get_barrier_semaphore()
        for mask in masks:
            pl.semaphore_signal(bar, inc=1, device_id=self.peer(mask), device_id_type=MESH_ID)
        for d in range(1, self.planes):
            to = (lax.rem(self.p + d, self.planes), self.me)
            pl.semaphore_signal(bar, inc=1, device_id=to, device_id_type=MESH_ID)
        pl.semaphore_wait(bar, len(masks) + self.planes - 1)


class LineGather:

    def __init__(self, links, src, slot, sems, local_sem):
        self.links, self.src, self.slot, self.sems, self.local_sem = links, src, slot, sems, local_sem

    def send(self, src, block, step):
        way = 1 if step > 0 else 2
        return self.links.copy(
            src, self.slot(block), self.sems.at[way, block], self.sems.at[0, block], self.links.plane(step)
        )

    def arrival(self, block):
        return self.links.copy(
            self.slot(block), self.slot(block), self.sems.at[1, block], self.sems.at[0, block], self.links.plane(0)
        )

    def start(self):
        p, last = self.links.p, self.links.planes - 1

        @pl.when(p < last)
        def _():
            self.send(self.src, p, 1).start()

        @pl.when(p > 0)
        def _():
            self.send(self.src, p, -1).start()

        pltpu.make_async_copy(self.src, self.slot(p), self.local_sem).start()

    def pump(self, d):
        p, last = self.links.p, self.links.planes - 1

        @pl.when(p >= d)
        def _():
            self.arrival(p - d).wait_recv()

            @pl.when(p < last)
            def _():
                self.send(self.slot(p - d), p - d, 1).start()

        @pl.when(p + d <= last)
        def _():
            self.arrival(p + d).wait_recv()

            @pl.when(p > 0)
            def _():
                self.send(self.slot(p + d), p + d, -1).start()

        if d == 1:
            pltpu.make_async_copy(self.src, self.slot(p), self.local_sem).wait()

    def finish(self):
        p, last = self.links.p, self.links.planes - 1
        for d in range(self.links.planes):

            @pl.when((p >= d) & (p < last))
            def _():
                self.send(self.slot(p - d), p - d, 1).wait_send()

            @pl.when((p + d <= last) & (p > 0))
            def _():
                self.send(self.slot(p + d), p + d, -1).wait_send()


class GroupGather:

    def __init__(self, links, slot, send, recv):
        self.links, self.slot, self.send_sem, self.recv_sem = links, slot, send, recv

    def copy(self, owner, mask, n):
        return self.links.copy(
            self.slot(owner), self.slot(owner), self.send_sem.at[n], self.recv_sem.at[owner], self.links.peer(mask)
        )

    def start(self):
        for n, mask in enumerate(HOPS + (1,)):
            self.copy(self.links.me, mask, n).start()

    def forward(self):
        for n, mask in enumerate(HOPS):
            owner = self.links.me ^ mask
            self.copy(owner, mask, n).wait_recv()
            self.copy(owner, 1, 4 + n).start()

    def wait(self):
        for mask in (1, 3, 5, 7):
            self.copy(self.links.me ^ mask, 1, 3).wait_recv()

    def finish(self):
        for n in range(7):
            self.copy(self.links.me, 1, n).wait_send()


class GroupSum:

    def __init__(self, links, stage, from_twin, from_far, send, twin_recv, far_recv):
        self.links, self.stage, self.from_twin, self.from_far = links, stage, from_twin, from_far
        self.send, self.twin_recv, self.far_recv = send, twin_recv, far_recv

    def to_twin(self, chip):
        return self.links.copy(
            self.stage.at[4 + chip], self.from_twin.at[chip], self.send.at[4 + chip], self.twin_recv.at[chip], self.links.peer(1)
        )

    def to_far(self, chip):
        return self.links.copy(
            self.stage.at[chip], self.from_far.at[chip - 1], self.send.at[chip], self.far_recv.at[chip - 1], self.links.peer(HOPS[chip - 1])
        )

    def run(self, block):
        me = self.links.me
        masks = (0,) + HOPS
        order = (3, 1, 2, 0)
        for chip in order:
            self.stage[4 + chip] = block(me ^ masks[chip] ^ 1).astype(BF)
            self.to_twin(chip).start()
        for chip in order[:3]:
            part = block(me ^ masks[chip])
            self.to_twin(chip).wait_recv()
            self.stage[chip] = (part + self.from_twin[chip].astype(F32)).astype(BF)
            self.to_far(chip).start()
        self.stage[0] = block(me).astype(BF)

    def total(self):
        self.to_twin(0).wait_recv()
        acc = self.stage[0].astype(F32) + self.from_twin[0].astype(F32)
        for chip in (1, 2, 3):
            self.to_far(chip).wait_recv()
            acc += self.from_far[chip - 1].astype(F32)
        return acc

    def finish(self):
        for chip in range(4):
            self.to_twin(chip).wait_send()
        for chip in (1, 2, 3):
            self.to_far(chip).wait_send()


def gelu_parts(u):
    inner = 0.7978845608 * (u + 0.044715 * (u * u * u))
    t = jnp.tanh(inner)
    value = 0.5 * u * (1.0 + t)
    slope = 0.5 * (1.0 + t) + 0.5 * u * (1.0 - t * t) * (0.7978845608 * (1.0 + 3 * 0.044715 * (u * u)))
    return value, slope


BLOCK_KEYS = (
    ((0, 256, 1),),
    ((0, 256, 0), (256, 256, 1)),
    ((0, 512, 0), (512, 256, 2), (768, 256, 0)),
    ((0, 512, 0), (768, 256, 2)),
)


def triangle(kind, shape):
    r = lax.broadcasted_iota(jnp.int32, shape, 0)
    c = lax.broadcasted_iota(jnp.int32, shape, 1)
    return c <= r if kind == 1 else c >= r


def half_mask(half):
    lane = lax.broadcasted_iota(jnp.int32, (1, 128), 1)
    return (lane // 64) == half


def softmax_pieces(q, keys, values, pieces, allowed):
    scores = []
    for start, size, kind in pieces:
        s = dot_t(q, keys[start : start + size])
        if kind:
            s = jnp.where(allowed(kind, start, s.shape), s, -1e30)
        scores.append(s)
    top = jnp.max(scores[0], axis=1, keepdims=True)
    for s in scores[1:]:
        top = jnp.maximum(top, jnp.max(s, axis=1, keepdims=True))
    total, out = 0.0, 0.0
    for s, (start, size, _) in zip(scores, pieces):
        e = jnp.exp(s - top)
        total = total + jnp.sum(e, axis=1, keepdims=True)
        out = out + dot(e.astype(BF), values[start : start + size])
    return out * (1.0 / total), top + jnp.log(total)


def forward_kernel(planes, tok, cot, vpart, m0, m1, mg, w1, w2,
                   sgrad_o, hidden_o, out_o, dw1_o, dw2_o, dgb_o, qkv_o, att_o, heads_o, vec_o, lse_o, first_o, mw_o, mfull_o,
                   vec, mw0, mw1, mgs, mfull, w1b, w2b, first_all, g_all, sec_all, qkv, att, arecv, attown,
                   act, slope, hid, lse, stage, twin, far,
                   zs, zl, gs, gr, a_s, a_r, rs_s, rs_t, rs_f, os):
    L = Links(planes)
    p, me = L.p, L.me
    share = 400
    zvec = LineGather(L, vpart, lambda b: vec.at[b], zs.at[0], zl.at[0])
    zm0 = LineGather(L, m0, lambda b: mw0.at[dyn(b * share, share, 16)], zs.at[1], zl.at[1])
    zm1 = LineGather(L, m1, lambda b: mw1.at[dyn(b * share, share, 16)], zs.at[2], zl.at[2])
    zmg = LineGather(L, mg, lambda b: mgs.at[b], zs.at[3], zl.at[3])
    zw1 = LineGather(L, w1, lambda b: w1b.at[dyn(b * share, share, 16)], zs.at[4], zl.at[4])
    zw2 = LineGather(L, w2, lambda b: w2b.at[dyn(b * 208, 208, 16)], zs.at[5], zl.at[5])
    gfirst = GroupGather(L, lambda j: first_all.at[:, j], gs.at[0], gr.at[0])
    gg = GroupGather(L, lambda j: g_all.at[j], gs.at[1], gr.at[1])
    gsec = GroupGather(L, lambda j: sec_all.at[j], gs.at[2], gr.at[2])
    gmerge = GroupGather(L, lambda j: mfull.at[:, dyn(j * 48, 48, 16)], gs.at[3], gr.at[3])

    L.barrier((1, 2, 3, 4, 5, 6, 7))
    zvec.start()
    zm0.start()
    g_all[me] = cot[...]
    rows = tok[...].astype(F32)
    normal, _ = normalize(rows)
    for d in (1, 2, 3):
        zvec.pump(d)
    vectors = (vec[0].astype(F32) + vec[1].astype(F32)) + (vec[2].astype(F32) + vec[3].astype(F32))
    first = (normal * vectors[0:1] + vectors[1:2]).astype(BF)
    first_all[:, me] = first.reshape(2, 64, D)
    gfirst.start()
    zm0.pump(1)
    zm1.start()
    zm0.pump(2)
    zm0.pump(3)
    gfirst.forward()
    gg.start()
    gfirst.wait()
    zm1.pump(1)
    zmg.start()

    def mix(weights, pair):
        bias_q = vectors[2:3, pair * 128 : pair * 128 + 128]
        bias_v = vectors[3:4, pair * 128 : pair * 128 + 128]

        def body(b, _):
            x = first_all[b // 2, pl.ds((b % 2) * 4, 4)].reshape(256, D)
            mixed = dot(x, weights[...])
            at = dyn(b * 256, 256, 256)
            qkv[pair, at] = (mixed[:, :128] + bias_q).astype(BF)
            qkv[2 + pair, at] = mixed[:, 128:256].astype(BF)
            qkv[4 + pair, at] = (mixed[:, 256:] + bias_v).astype(BF)
            return 0

        lax.fori_loop(0, 4, body, 0)

    lane = lax.broadcasted_iota(jnp.int32, (1, 128), 1)

    def note_lse(head, at, value):
        lse[at] = jnp.where(lane == head, value, lse[at] if head else 0.0)

    def attend_private(pair, half):
        mask = half_mask(half)
        for b in range(4):
            q = jnp.where(mask, qkv[pair, b * 256 : b * 256 + 256], 0) * jnp.asarray(0.125, BF)
            out, l = softmax_pieces(
                q, qkv.at[2 + pair], qkv.at[4 + pair], BLOCK_KEYS[b], lambda kind, start, shape: triangle(kind, shape)
            )
            out = jnp.where(mask, out, 0.0).astype(BF).reshape(4, 64, 128)
            at = pl.ds((b % 2) * 4, 4)
            if half == 0:
                att[pair, b // 2, at] = out
            else:
                att[pair, b // 2, at] = att[pair, b // 2, at] + out
            note_lse(2 * pair + half, slice(b * 256, b * 256 + 256), l)

    def own_allowed(kind, start, shape):
        r = lax.broadcasted_iota(jnp.int32, shape, 0)
        c = lax.broadcasted_iota(jnp.int32, shape, 1)
        rp = jnp.where(r < 64, me * 64 + r, 1023 - (me * 64 + r - 64))
        cp = jnp.where(c < 512, c, 1023 - (c - 512))
        return cp <= rp

    mix(mw0, 0)
    zm1.pump(2)
    attend_private(0, 0)
    zm1.pump(3)
    zmg.pump(1)
    zw1.start()
    attend_private(0, 1)
    zmg.pump(2)
    gg.forward()
    mix(mw1, 1)
    zmg.pump(3)
    for b in range(4):
        mfull[b, dyn(me * 48, 48, 16)] = mgs[b, 0:48]
        mfull[b, 384:400] = mgs[b, 48:64]
    gmerge.start()
    attend_private(1, 0)
    qs = jnp.concatenate([qkv[1, dyn(me * 64, 64, 64)], qkv[1, dyn(512 + me * 64, 64, 64)]], axis=0)
    mask1 = half_mask(1)
    qs = jnp.where(mask1, qs, 0) * jnp.asarray(0.125, BF)
    out_s, l_s = softmax_pieces(qs, qkv.at[3], qkv.at[5], ((0, 1024, 1),), own_allowed)
    note_lse(3, slice(0, 128), l_s)
    shared_low = jnp.where(mask1, out_s, 0.0).astype(BF)

    def exchange(mask):
        return L.copy(att.at[:, :, me ^ mask], arecv.at[me], a_s.at[mask], a_r.at[me], L.peer(mask))

    def arrived(mask):
        return L.copy(att.at[:, :, me], arecv.at[me ^ mask], a_s.at[mask], a_r.at[me ^ mask], L.peer(mask))

    for mask in range(1, 8):
        exchange(mask).start()
    zw1.pump(1)
    gmerge.forward()
    arecv[me] = att[:, :, me]
    zw2.start()
    for mask in range(1, 8):
        arrived(mask).wait_recv()
    for j in range(8):
        attown[:, 192 * j : 192 * j + 128] = arecv[j, 0].reshape(128, 128)
        attown[:, 192 * j + 128 : 192 * j + 192] = arecv[j, 1].reshape(128, 128)[:, :64]
    attown[:, 1536:1600] = shared_low[:, 64:128]
    gmerge.wait()
    hidden = rows + vectors[4:5]
    hid[...] = hidden
    for b in range(4):
        hid[...] += dot(attown[:, b * 400 : b * 400 + 400], mfull[b])
    normal2, _ = normalize(hid[...])
    sec_all[me] = (normal2 * vectors[5:6] + vectors[6:7]).astype(BF)
    gsec.start()
    gg.wait()
    zw1.pump(2)
    zw1.pump(3)
    gsec.forward()
    gsec.wait()

    def expand(b, _):
        at = dyn(b * 128, 128, 128)
        pre = dot(sec_all[b], w1b[...]) + vectors[8:9, :832]
        value, s = gelu_parts(pre)
        act[at] = value.astype(BF)
        slope[at] = s.astype(BF)
        return 0

    lax.fori_loop(0, 8, expand, 0)
    zw2.pump(1)
    g2 = g_all[...].reshape(1024, D)
    for start, size in ((0, 256), (256, 256), (512, 256), (768, 64)):
        dw2_o[start : start + size] = t_dot(act[:, start : start + size], g2).astype(BF)
    zw2.pump(2)
    zw2.pump(3)

    def contract(b, acc):
        at = dyn(b * 128, 128, 128)
        grad = dot_t(g_all[b], w2b[...]) * slope[at].astype(F32)
        slope[at] = grad.astype(BF)
        return acc + jnp.sum(grad, axis=0, keepdims=True)

    dgb_o[...] = lax.fori_loop(0, 8, contract, jnp.zeros((1, 832), F32))
    sums = GroupSum(L, stage.at[0], twin.at[0], far.at[0], rs_s.at[0], rs_t.at[0], rs_f.at[0])
    sums.run(lambda owner: dot_t(slope[dyn(owner * 128, 128, 128)], w1b[...]))
    outs = GroupSum(L, stage.at[1], twin.at[1], far.at[1], rs_s.at[1], rs_t.at[1], rs_f.at[1])
    outs.run(lambda owner: dot(act[dyn(owner * 128, 128, 128)], w2b[...]))
    for start in range(0, 1600, 256):
        size = min(256, 1600 - start)
        x = sec_all[:, :, start : start + size].reshape(1024, size)
        dw1_o[start : start + size] = t_dot(x, slope[...]).astype(BF)
    sgrad_o[...] = sums.total()
    out_o[...] = (outs.total() + hid[...] + vectors[7:8]).astype(BF)
    hidden_o[...] = hid[...]
    qkv_o[...] = qkv[...]
    att_o[...] = attown[...]
    heads_o[...] = att[...]
    vec_o[...] = vectors
    lse_o[...] = lse[...]
    copies = [
        pltpu.make_async_copy(first_all, first_o, os.at[0]),
        pltpu.make_async_copy(mw0, mw_o.at[0], os.at[1]),
        pltpu.make_async_copy(mw1, mw_o.at[1], os.at[2]),
        pltpu.make_async_copy(mfull, mfull_o, os.at[3]),
    ]
    for c in copies:
        c.start()
    for c in copies:
        c.wait()
    for z in (zvec, zm0, zm1, zmg, zw1, zw2):
        z.finish()
    for g in (gfirst, gg, gsec, gmerge):
        g.finish()
    for mask in range(1, 8):
        exchange(mask).wait_send()
    sums.finish()
    outs.finish()


def run_forward(planes, tok, cot, vpart, m0, m1, mg, w1, w2):
    any_ = pl.BlockSpec(memory_space=pl.ANY)
    vm = pl.BlockSpec(memory_space=pltpu.VMEM)
    S = jax.ShapeDtypeStruct
    V = pltpu.VMEM
    dma = pltpu.SemaphoreType.DMA
    return pl.pallas_call(
        functools.partial(forward_kernel, planes),
        out_shape=(
            S((128, D), F32), S((128, D), F32), S((128, D), BF), S((D, 832), BF), S((832, D), BF), S((1, 832), F32),
            S((6, 1024, 128), BF), S((128, D), BF), S((2, 2, 8, 64, 128), BF), S((16, D), F32), S((1024, 128), F32),
            S((2, 8, 64, D), BF), S((2, D, 384), BF), S((4, 400, D), BF),
        ),
        in_specs=[vm, vm] + [any_] * 6,
        out_specs=(vm,) * 11 + (any_,) * 3,
        scratch_shapes=[
            V((4, 16, D), BF), V((D, 384), BF), V((D, 384), BF), V((4, 64, D), BF), V((4, 400, D), BF),
            V((D, 832), BF), V((832, D), BF), V((2, 8, 64, D), BF), V((8, 128, D), BF), V((8, 128, D), BF),
            V((6, 1024, 128), BF), V((2, 2, 8, 64, 128), BF), V((8, 2, 2, 64, 128), BF), V((128, D), BF),
            V((1024, 832), BF), V((1024, 832), BF), V((128, D), F32), V((1024, 128), F32),
            V((2, 8, 128, D), BF), V((2, 4, 128, D), BF), V((2, 3, 128, D), BF),
            dma((6, 3, 4)), dma((6,)), dma((4, 7)), dma((4, 8)), dma((8,)), dma((8,)),
            dma((2, 8)), dma((2, 4)), dma((2, 3)), dma((4,)),
        ],
        compiler_params=pltpu.CompilerParams(collective_id=0, has_side_effects=True, vmem_limit_bytes=63 << 20),
        cost_estimate=pl.CostEstimate(flops=15_000_000_000, bytes_accessed=60_000_000, transcendentals=4_000_000),
    )(tok, cot, vpart, m0, m1, mg, w1, w2)


class LineSum:

    def __init__(self, links, block, slots, send, recv):
        self.links, self.block, self.slots, self.send_sem, self.recv_sem = links, block, slots, send, recv
        self.last = links.planes - 1

    def send(self, t, step):
        slot = t - 1 if step > 0 else self.last + t
        return self.links.copy(
            self.block(t), self.slots.at[slot], self.send_sem.at[t], self.recv_sem.at[slot], self.links.plane(step)
        )

    def arrival(self, slot):
        return self.links.copy(
            self.slots.at[slot], self.slots.at[slot], self.send_sem.at[0], self.recv_sem.at[slot], self.links.plane(0)
        )

    def start(self):
        @pl.when(self.links.p == 0)
        def _():
            for t in range(self.last, 0, -1):
                self.send(t, 1).start()

        @pl.when(self.links.p == self.last)
        def _():
            for t in range(self.last):
                self.send(t, -1).start()

    def add(self, t, slot):
        self.arrival(slot).wait_recv()
        ref = self.block(t)
        ref[...] = (ref[...].astype(F32) + self.slots[slot].astype(F32)).astype(BF)

    def pump(self, k):
        p, last = self.links.p, self.last
        t = last - k

        @pl.when((p > 0) & (p < t))
        def _():
            self.add(t, t - 1)
            self.send(t, 1).start()

        @pl.when((k < p) & (p < last))
        def _():
            self.add(k, last + k)
            self.send(k, -1).start()

    def total(self):
        p, last = self.links.p, self.last

        @pl.when(p > 0)
        def _():
            self.add(p, p - 1)

        @pl.when(p < last)
        def _():
            self.add(p, last + p)

    def finish(self):
        p = self.links.p
        for t in range(self.last + 1):

            @pl.when(p < t)
            def _():
                self.send(t, 1).wait_send()

            @pl.when(p > t)
            def _():
                self.send(t, -1).wait_send()


class LineExchange:

    def __init__(self, links, slots, send, recv):
        self.links, self.slots, self.send_sem, self.recv_sem = links, slots, send, recv

    def copy(self, src, d):
        planes = self.links.planes
        to = lax.rem(self.links.p + d, planes)
        return self.links.copy(src, self.slots.at[d - 1], self.send_sem.at[d - 1], self.recv_sem.at[d - 1], (to, self.links.me))

    def start(self, src):
        for d in range(1, self.links.planes):
            self.copy(src, d).start()

    def total(self, src):
        acc = src[...]
        for d in range(1, self.links.planes):
            self.copy(src, d).wait_recv()
            acc = acc + self.slots[d - 1]
        return acc

    def finish(self, src):
        for d in range(1, self.links.planes):
            self.copy(src, d).wait_send()


class OwnGather(GroupGather):

    def __init__(self, links, src, slot, send, recv, local_sem):
        super().__init__(links, slot, send, recv)
        self.src, self.local_sem = src, local_sem

    def start(self):
        for n, mask in enumerate(HOPS + (1,)):
            self.own(mask, n).start()
        pltpu.make_async_copy(self.src(), self.slot(self.links.me), self.local_sem).start()

    def own(self, mask, n):
        return self.links.copy(
            self.src(), self.slot(self.links.me), self.send_sem.at[n], self.recv_sem.at[self.links.me], self.links.peer(mask)
        )

    def finish(self):
        for n, mask in enumerate(HOPS + (1,)):
            self.own(mask, n).wait_send()
        for n, mask in enumerate(HOPS):
            self.copy(self.links.me ^ mask, 1, 4 + n).wait_send()
        pltpu.make_async_copy(self.src(), self.slot(self.links.me), self.local_sem).wait()


def backward_kernel(planes, tok, cot, sgrad, hid, vectors, attown, dgb, lse, qkv, att, mfull_h, mw_h, first_h, dw1_h, dw2_h,
                    igrad_o, va_o, vb_o, gw1_o, gw2_o, gm0_o, gm1_o, gmg_o,
                    mfull, mw, first_all, dw1, dw2, hlow, agrad, asend, gatt, att_all, hc, dkv, mgr, dmix, dmerge,
                    slot_w1, slot_w2, slot_m0, slot_m1, slot_mg, stage, twin, far, va, vb, vslot,
                    ld, ls_s, ls_r, ve_s, ve_r, gs, gr, gl, a_s, a_r, h_s, h_r, rs_s, rs_t, rs_f):
    L = Links(planes)
    p, me = L.p, L.me
    loads = [
        pltpu.make_async_copy(mfull_h, mfull, ld.at[0]),
        pltpu.make_async_copy(dw2_h, dw2, ld.at[1]),
        pltpu.make_async_copy(dw1_h, dw1, ld.at[2]),
        pltpu.make_async_copy(first_h, first_all, ld.at[3]),
        pltpu.make_async_copy(mw_h, mw, ld.at[4]),
    ]
    for c in loads:
        c.start()
    lw2 = LineSum(L, lambda t: dw2.at[dyn(t * 208, 208, 16)], slot_w2, ls_s.at[0], ls_r.at[0])
    lw1 = LineSum(L, lambda t: dw1.at[dyn(t * 400, 400, 16)], slot_w1, ls_s.at[1], ls_r.at[1])
    lm0 = LineSum(L, lambda t: dmix.at[0, dyn(t * 400, 400, 16)], slot_m0, ls_s.at[2], ls_r.at[2])
    lm1 = LineSum(L, lambda t: dmix.at[1, dyn(t * 400, 400, 16)], slot_m1, ls_s.at[3], ls_r.at[3])
    lmg = LineSum(L, lambda t: dmerge.at[dyn(t * 400, 400, 16)], slot_mg, ls_s.at[4], ls_r.at[4])
    xa = LineExchange(L, vslot.at[0], ve_s.at[0], ve_r.at[0])
    xb = LineExchange(L, vslot.at[1], ve_s.at[1], ve_r.at[1])
    gatt_all = GroupGather(L, lambda j: att_all.at[j], gs.at[0], gr.at[0])
    gw2 = OwnGather(L, lambda: lw2.block(p), lambda j: gw2_o.at[j], gs.at[1], gr.at[1], gl.at[1])
    gw1 = OwnGather(L, lambda: lw1.block(p), lambda j: gw1_o.at[j], gs.at[2], gr.at[2], gl.at[2])
    gm0 = OwnGather(L, lambda: lm0.block(p), lambda j: gm0_o.at[j], gs.at[3], gr.at[3], gl.at[3])
    gm1 = OwnGather(L, lambda: lm1.block(p), lambda j: gm1_o.at[j], gs.at[4], gr.at[4], gl.at[4])
    gmg = OwnGather(L, lambda: lmg.block(p), lambda j: gmg_o.at[j], gs.at[5], gr.at[5], gl.at[5])
    gva = OwnGather(L, lambda: va, lambda j: va_o.at[j], gs.at[6], gr.at[6], gl.at[6])
    gvb = OwnGather(L, lambda: vb, lambda j: vb_o.at[j], gs.at[7], gr.at[7], gl.at[7])
    L.barrier((1, 2, 3, 4, 5, 6, 7))

    tangent = cot[...].astype(F32)
    normal2, inverse2 = normalize(hid[...])
    grad2 = sgrad[...]
    hidden_grad = tangent + norm_back(grad2, vectors[5:6], normal2, inverse2)
    igrad_o[...] = hidden_grad
    hlow[:, 0:D] = hidden_grad.astype(BF)
    hlow[:, D:2048] = jnp.zeros((128, 2048 - D), BF)
    va[0:1] = jnp.sum(hidden_grad, axis=0, keepdims=True)
    va[1:2] = jnp.sum(grad2 * normal2, axis=0, keepdims=True)
    va[2:3] = jnp.sum(grad2, axis=0, keepdims=True)
    va[3:4] = jnp.sum(tangent, axis=0, keepdims=True)
    va[4:8] = jnp.zeros((4, D), F32)
    va[4:5, 0:832] = dgb[...]
    att_all[me] = attown[...]

    def columns(mask):
        to = me ^ mask
        return L.copy(hlow.at[:, dyn(to * 256, 256, 256)], hc.at[me], h_s.at[mask], h_r.at[me], L.peer(mask))

    def columns_in(mask):
        return L.copy(hc.at[me], hc.at[me ^ mask], h_s.at[mask], h_r.at[me ^ mask], L.peer(mask))

    loads[0].wait()
    agrad[...] = dot_t(hlow[:, 0:D], mfull[...]).astype(BF)
    for j in range(8):
        asend[j, 0] = agrad[:, 192 * j : 192 * j + 128].reshape(2, 64, 128)
        tail = agrad[:, 192 * j + 128 : 192 * j + 192]
        asend[j, 1] = jnp.concatenate([tail, jnp.zeros((128, 64), BF)], axis=1).reshape(2, 64, 128)

    def exchange(mask):
        return L.copy(asend.at[me ^ mask], gatt.at[:, :, me], a_s.at[mask], a_r.at[me], L.peer(mask))

    def arrived(mask):
        return L.copy(asend.at[me], gatt.at[:, :, me ^ mask], a_s.at[mask], a_r.at[me ^ mask], L.peer(mask))

    for mask in range(1, 8):
        exchange(mask).start()
    gatt[:, :, me] = asend[me]
    loads[1].wait()
    lw2.start()
    loads[2].wait()
    lw1.start()
    gatt_all.start()
    for mask in range(1, 8):
        columns(mask).start()
    hc[me] = hlow[:, dyn(me * 256, 256, 256)]
    dkv[...] = jnp.zeros(dkv.shape, F32)
    for mask in range(1, 8):
        arrived(mask).wait_recv()

    scale = jnp.asarray(0.125, BF)

    def head_back(pair, head, mask, q, g, o, stat, pieces, allowed):
        delta = jnp.sum(g.astype(F32) * o.astype(F32), axis=1, keepdims=True)
        dq = 0.0
        for start, size, kind in pieces:
            keys = qkv[2 + pair, start : start + size]
            s = dot_t(q, keys)
            if kind:
                s = jnp.where(allowed(kind, start, s.shape), s, -1e30)
            prob = jnp.exp(s - stat)
            ds = (prob * (dot_t(g, qkv[4 + pair, start : start + size]) - delta)).astype(BF)
            dq = dq + dot(ds, keys)
            dkv[pair, 0, start : start + size] += t_dot(ds, q)
            dkv[pair, 1, start : start + size] += t_dot(prob.astype(BF), g)
        return jnp.where(mask, dq, 0.0) * 0.125

    def private_back(pair, half):
        mask = half_mask(half)
        head = 2 * pair + half
        total = 0.0
        for b in range(4):
            at = slice(b * 256, b * 256 + 256)
            blk = (pair, b // 2, pl.ds((b % 2) * 4, 4))
            q = jnp.where(mask, qkv[pair, at], 0) * scale
            g = jnp.where(mask, gatt[blk].reshape(256, 128), 0)
            o = att[blk].reshape(256, 128)
            dq = head_back(
                pair, head, mask, q, g, o, lse[at, head : head + 1], BLOCK_KEYS[b],
                lambda kind, start, shape: triangle(kind, shape),
            )
            total = total + jnp.sum(dq, axis=0, keepdims=True)
            if half == 0:
                mgr[pair, at, 0:128] = dq.astype(BF)
            else:
                mgr[pair, at, 0:128] = mgr[pair, at, 0:128] + dq.astype(BF)
        return total

    def mixer_part(pair):
        mgr[pair, :, 128:256] = dkv[pair, 0].astype(BF)
        mgr[pair, :, 256:384] = dkv[pair, 1].astype(BF)
        va[6:7, pair * 128 : pair * 128 + 128] = jnp.sum(dkv[pair, 1], axis=0, keepdims=True)
        for start in range(0, D, 256):
            size = min(256, D - start)
            x = first_all[:, :, :, start : start + size].reshape(1024, size)
            dmix[pair, start : start + size] = t_dot(x, mgr[pair]).astype(BF)

    qb0 = private_back(0, 0)
    lw2.pump(0)
    qb0 = qb0 + private_back(0, 1)
    va[5:6, 0:128] = qb0
    loads[3].wait()
    mixer_part(0)
    lm0.start()
    gatt_all.forward()
    lw2.pump(1)
    qb1 = private_back(1, 0)
    mask1 = half_mask(1)
    own_early, own_late = dyn(me * 64, 64, 64), dyn(512 + me * 64, 64, 64)
    qs = jnp.concatenate([qkv[1, own_early], qkv[1, own_late]], axis=0)
    qs = jnp.where(mask1, qs, 0) * scale
    blank = jnp.zeros((128, 64), BF)
    g_s = jnp.concatenate([blank, agrad[:, 1536:1600]], axis=1)
    o_s = jnp.concatenate([blank, attown[:, 1536:1600]], axis=1)

    def own_allowed(kind, start, shape):
        r = lax.broadcasted_iota(jnp.int32, shape, 0)
        c = lax.broadcasted_iota(jnp.int32, shape, 1) + start
        rp = jnp.where(r < 64, me * 64 + r, 1023 - (me * 64 + r - 64))
        cp = jnp.where(c < 512, c, 1023 - (c - 512))
        return cp <= rp

    dqs = head_back(1, 3, mask1, qs, g_s, o_s, lse[0:128, 3:4], ((0, 512, 1), (512, 512, 1)), own_allowed)
    va[5:6, 128:256] = qb1 + jnp.sum(dqs, axis=0, keepdims=True)
    dqs_low = dqs.astype(BF)
    mgr[1, own_early, 0:128] = mgr[1, own_early, 0:128] + dqs_low[:64]
    mgr[1, own_late, 0:128] = mgr[1, own_late, 0:128] + dqs_low[64:]
    mixer_part(1)
    lm1.start()
    xa.start(va)
    loads[4].wait()
    sums = GroupSum(L, stage, twin, far, rs_s, rs_t, rs_f)

    def first_block(owner):
        early, late = dyn(owner * 64, 64, 64), dyn(512 + owner * 64, 64, 64)
        x0 = jnp.concatenate([mgr[0, early], mgr[0, late]], axis=0)
        x1 = jnp.concatenate([mgr[1, early], mgr[1, late]], axis=0)
        return dot_t(x0, mw[0]) + dot_t(x1, mw[1])

    sums.run(first_block)
    lw2.total()
    gw2.start()
    lw1.pump(0)
    gatt_all.wait()
    for mask in range(1, 8):
        columns_in(mask).wait_recv()
    h2 = hc[...].reshape(1024, 256)
    for start in range(0, D, 256):
        size = min(256, D - start)
        x = att_all[:, :, start : start + size].reshape(1024, size)
        dmerge[start : start + size] = t_dot(x, h2).astype(BF)
    lmg.start()
    first_grad = sums.total()
    rows = tok[...].astype(F32)
    normal1, inverse1 = normalize(rows)
    igrad_o[...] += norm_back(first_grad, vectors[0:1], normal1, inverse1)
    vb[0:1] = jnp.sum(first_grad * normal1, axis=0, keepdims=True)
    vb[1:2] = jnp.sum(first_grad, axis=0, keepdims=True)
    vb[2:8] = jnp.zeros((6, D), F32)
    xb.start(vb)
    lw1.pump(1)
    gw2.forward()
    total_a = xa.total(va)
    xa.finish(va)
    va[...] = total_a
    gva.start()
    lm0.pump(0)
    lw1.total()
    gw1.start()
    lm0.pump(1)
    lm1.pump(0)
    total_b = xb.total(vb)
    xb.finish(vb)
    vb[...] = total_b
    gvb.start()
    lm0.total()
    gm0.start()
    gva.forward()
    lm1.pump(1)
    lmg.pump(0)
    gw1.forward()
    gvb.forward()
    lm1.total()
    gm1.start()
    lmg.pump(1)
    gm0.forward()
    lmg.total()
    gmg.start()
    gm1.forward()
    gmg.forward()
    for g in (gw2, gva, gw1, gvb, gm0, gm1, gmg):
        g.wait()
    for g in (gatt_all, gw2, gw1, gm0, gm1, gmg, gva, gvb):
        g.finish()
    for s in (lw2, lw1, lm0, lm1, lmg):
        s.finish()
    for mask in range(1, 8):
        exchange(mask).wait_send()
        columns(mask).wait_send()
    sums.finish()


def run_backward(planes, *operands):
    any_ = pl.BlockSpec(memory_space=pl.ANY)
    vm = pl.BlockSpec(memory_space=pltpu.VMEM)
    S = jax.ShapeDtypeStruct
    V = pltpu.VMEM
    dma = pltpu.SemaphoreType.DMA
    return pl.pallas_call(
        functools.partial(backward_kernel, planes),
        out_shape=(
            S((128, D), F32), S((8, 8, D), F32), S((8, 8, D), F32), S((8, 400, 832), BF), S((8, 208, D), BF),
            S((8, 400, 384), BF), S((8, 400, 384), BF), S((8, 400, 256), BF),
        ),
        in_specs=[vm] * 10 + [any_] * 5,
        out_specs=(vm,) + (any_,) * 7,
        scratch_shapes=[
            V((D, D), BF), V((2, D, 384), BF), V((2, 8, 64, D), BF), V((D, 832), BF), V((832, D), BF),
            V((128, 2048), BF), V((128, D), BF), V((8, 2, 2, 64, 128), BF), V((2, 2, 8, 64, 128), BF),
            V((8, 128, D), BF), V((8, 128, 256), BF), V((2, 2, 1024, 128), F32), V((2, 1024, 384), BF),
            V((2, D, 384), BF), V((D, 256), BF),
            V((6, 400, 832), BF), V((6, 208, D), BF), V((6, 400, 384), BF), V((6, 400, 384), BF), V((6, 400, 256), BF),
            V((8, 128, D), BF), V((4, 128, D), BF), V((3, 128, D), BF), V((8, D), F32), V((8, D), F32), V((2, 3, 8, D), F32),
            dma((5,)), dma((5, 4)), dma((5, 6)), dma((2, 3)), dma((2, 3)), dma((8, 7)), dma((8, 8)), dma((8,)),
            dma((8,)), dma((8,)), dma((8,)), dma((8,)), dma((8,)), dma((4,)), dma((3,)),
        ],
        compiler_params=pltpu.CompilerParams(collective_id=1, has_side_effects=True, vmem_limit_bytes=63 << 20),
        cost_estimate=pl.CostEstimate(flops=15_000_000_000, bytes_accessed=60_000_000, transcendentals=4_000_000),
    )(*operands)


def local_plain(
    tokens,
    first_gain,
    first_shift,
    mixer_weight,
    query_bias,
    value_bias,
    merge_weight,
    merge_bias,
    second_gain,
    second_shift,
    expand_weight,
    expand_bias,
    shrink_weight,
    shrink_bias,
    cotangent,
):
    planes = lax.axis_size("fsdp")
    ring = lax.axis_size("ctx")
    me = lax.axis_index("ctx")
    blocks = tokens.shape[2]
    local_rows = 2 * blocks
    half = blocks * ring
    length = 2 * half
    private = H // ring
    shared = H - private * ring
    pc, sc = private * HD, shared * HD
    hc = pc + sc
    shared_at = private * ring * HD
    share = D // planes
    ff_plane = expand_bias.shape[0]
    ff_part = ff_plane // ring
    cols = D // ring

    vectors = jnp.stack(
        [first_gain, first_shift, query_bias, value_bias, merge_bias, second_gain, second_shift, shrink_bias]
    )
    vectors = lax.all_gather(vectors, "fsdp", axis=1, tiled=True).astype(F32)
    gain1, shift1, qbias, vbias, mbias, gain2, shift2, sbias = [vectors[n] for n in range(8)]

    def head_columns(weight, base):
        mine = lax.dynamic_slice_in_dim(weight, base + me * pc, pc, weight.ndim - 1)
        every = weight[..., base + shared_at : base + D]
        return [mine, every]

    mixer_part = jnp.concatenate(
        head_columns(mixer_weight, 0) + head_columns(mixer_weight, D) + head_columns(mixer_weight, 2 * D), axis=1
    )
    mixer_mine = lax.all_gather(mixer_part, "fsdp", axis=0, tiled=True)

    merge_part = lax.dynamic_slice_in_dim(merge_weight, me * cols, cols, 1)
    merge_cols = lax.all_gather(merge_part, "fsdp", axis=0, tiled=True)
    merge_full = lax.all_gather(merge_cols, "ctx", axis=1, tiled=True)

    expand_part = expand_weight.reshape(share, planes, ring, ff_part)
    expand_part = lax.dynamic_index_in_dim(expand_part, me, 2, keepdims=False)
    expand_part = lax.all_to_all(expand_part, "fsdp", 1, 0, tiled=False).reshape(D, ff_part)
    expand_mine = lax.all_gather(expand_part, "ctx", axis=1, tiled=True)

    rows = tokens.reshape(local_rows, D).astype(F32)
    normal1, inverse1 = normalize(rows)
    first = (normal1 * gain1 + shift1).astype(BF)
    first_all = lax.all_gather(first.reshape(2, blocks, D), "ctx", axis=1, tiled=True).reshape(length, D)
    tangent_low = cotangent.reshape(local_rows, D)
    tangent = tangent_low.astype(F32)
    tangent_all = lax.all_gather(tangent_low, "fsdp", axis=0, tiled=True)

    mixed = dot(first_all, mixer_mine)
    qb = jnp.concatenate(head_columns(qbias, 0), axis=0)
    vb = jnp.concatenate(head_columns(vbias, 0), axis=0)
    query = (mixed[:, :hc] + qb).astype(BF)
    key = mixed[:, hc : 2 * hc].astype(BF)
    value = (mixed[:, 2 * hc :] + vb).astype(BF)
    half_index = jnp.arange(half, dtype=jnp.int32)
    place = jnp.concatenate([half_index, length - 1 - half_index])
    early = me * blocks + jnp.arange(blocks, dtype=jnp.int32)
    own_place = jnp.concatenate([early, length - 1 - early])
    allowed = place[None, :] <= place[:, None]
    own_allowed = place[None, :] <= own_place[:, None]

    def own_rows(values):
        parts = values.reshape(2, half, values.shape[1])
        return lax.dynamic_slice_in_dim(parts, me * blocks, blocks, 1).reshape(local_rows, values.shape[1])

    qp, kp, vp = heads_first(query[:, :pc]), heads_first(key[:, :pc]), heads_first(value[:, :pc])
    qs, ks, vs = heads_first(own_rows(query[:, pc:])), heads_first(key[:, pc:]), heads_first(value[:, pc:])
    out_p, top_p, total_p = attend(qp, kp, vp, allowed)
    out_s, top_s, total_s = attend(qs, ks, vs, own_allowed)
    att_heads = heads_last(out_p).astype(BF)
    att_pieces = lax.all_to_all(att_heads.reshape(2, ring, blocks, pc), "ctx", 1, 2, tiled=False)
    attended = jnp.concatenate(
        [att_pieces.reshape(local_rows, ring * pc), heads_last(out_s).astype(BF)], axis=1
    )
    hidden = rows + dot(attended, merge_full) + mbias
    normal2, inverse2 = normalize(hidden)
    second = (normal2 * gain2 + shift2).astype(BF)
    second_all = lax.all_gather(second, "fsdp", axis=0, tiled=True)
    attended_all = lax.all_gather(attended, "ctx", axis=0, tiled=True)

    pre = dot(second_all, expand_mine) + expand_bias.astype(F32)
    act, gate_pull = jax.vjp(lambda u: jax.nn.gelu(u, approximate=True), pre)
    act_low = act.astype(BF)
    act_grad = dot_t(tangent_all, shrink_weight)
    (pre_grad,) = gate_pull(act_grad)
    pre_low = pre_grad.astype(BF)
    second_part = dot_t(pre_low, expand_mine).astype(BF)
    second_grad = lax.psum_scatter(second_part, "fsdp", scatter_dimension=0, tiled=True).astype(F32)
    out_part = dot(act_low, shrink_weight).astype(BF)
    out_sum = lax.psum_scatter(out_part, "fsdp", scatter_dimension=0, tiled=True).astype(F32)
    output = (hidden + out_sum + sbias).astype(BF).reshape(1, 2, blocks, D)
    expand_bias_grad = jnp.sum(pre_grad, axis=0)
    shrink_grad = t_dot(act_low, tangent_all).astype(BF)
    shrink_mine = lax.psum_scatter(shrink_grad, "ctx", scatter_dimension=0, tiled=True)
    shrink_owned = lax.all_gather(shrink_mine, "ctx", axis=0, tiled=True).astype(F32)
    expand_grad = t_dot(second_all, pre_low).astype(BF)
    expand_cols = lax.psum_scatter(expand_grad, "ctx", scatter_dimension=1, tiled=True)
    expand_rows = lax.all_to_all(expand_cols.reshape(planes, share, ff_part), "fsdp", 0, 1, tiled=False)
    expand_owned = (
        lax.all_gather(expand_rows, "ctx", axis=2, tiled=False).reshape(share, planes * ff_plane).astype(F32)
    )

    hidden_grad = tangent + norm_back(second_grad, gain2, normal2, inverse2)
    hidden_low = hidden_grad.astype(BF)
    att_grad = dot_t(hidden_low, merge_full).astype(BF)
    grad_pieces = lax.all_to_all(att_grad[:, :shared_at].reshape(2, blocks, ring, pc), "ctx", 2, 1, tiled=False)
    grad_p = heads_first(grad_pieces.reshape(length, pc))
    grad_s = heads_first(att_grad[:, shared_at:])
    dqp, dkp, dvp = attend_back(qp, kp, vp, allowed, top_p, total_p, grad_p)
    dqs, dks, dvs = attend_back(qs, ks, vs, own_allowed, top_s, total_s, grad_s)
    dqs_all = jnp.zeros((2, half, sc), F32)
    dqs_all = lax.dynamic_update_slice_in_dim(dqs_all, heads_last(dqs).reshape(2, blocks, sc), me * blocks, 1)
    mixed_grad = jnp.concatenate(
        [heads_last(dqp), dqs_all.reshape(length, sc)]
        + [heads_last(dkp), heads_last(dks), heads_last(dvp), heads_last(dvs)],
        axis=1,
    )
    bias_sums = jnp.sum(mixed_grad, axis=0)
    mixed_low = mixed_grad.astype(BF)
    first_part = dot_t(mixed_low, mixer_mine).astype(BF)
    first_grad = lax.psum_scatter(
        first_part.reshape(2, half, D), "ctx", scatter_dimension=1, tiled=True
    ).reshape(local_rows, D).astype(F32)
    input_grad = hidden_grad + norm_back(first_grad, gain1, normal1, inverse1)
    mixer_part_grad = t_dot(first_all, mixed_low).astype(BF)
    mixer_rows = lax.psum_scatter(mixer_part_grad, "fsdp", scatter_dimension=0, tiled=True)
    mixer_all = lax.all_gather(mixer_rows, "ctx", axis=0, tiled=False).astype(F32)

    def place_columns(values):
        mine = values[:, :, :pc].transpose(1, 0, 2).reshape(share, ring * pc)
        return [mine, jnp.sum(values[:, :, pc:], axis=0)]

    mixer_owned = jnp.concatenate(
        place_columns(mixer_all[:, :, :hc])
        + place_columns(mixer_all[:, :, hc : 2 * hc])
        + place_columns(mixer_all[:, :, 2 * hc :]),
        axis=1,
    )
    hidden_cols = lax.all_to_all(hidden_low.reshape(local_rows, ring, cols), "ctx", 1, 0, tiled=False)
    merge_grad = t_dot(attended_all, hidden_cols.reshape(length, cols)).astype(BF)
    merge_rows = lax.psum_scatter(merge_grad, "fsdp", scatter_dimension=0, tiled=True)
    merge_owned = lax.all_gather(merge_rows, "ctx", axis=1, tiled=True).astype(F32)

    def spread_bias(values):
        full = jnp.zeros((D,), F32)
        full = lax.dynamic_update_slice_in_dim(full, values[:pc], me * pc, 0)
        return full.at[shared_at:].set(values[pc:])

    sums = jnp.stack(
        [
            jnp.sum(first_grad * normal1, axis=0),
            jnp.sum(first_grad, axis=0),
            spread_bias(bias_sums[:hc]),
            spread_bias(bias_sums[2 * hc :]),
            jnp.sum(hidden_grad, axis=0),
            jnp.sum(second_grad * normal2, axis=0),
            jnp.sum(second_grad, axis=0),
            jnp.sum(tangent, axis=0),
        ]
    )
    sums = lax.psum(sums, ("fsdp", "ctx"))
    mine = lax.dynamic_slice_in_dim(sums, lax.axis_index("fsdp") * share, share, 1)
    expand_bias_owned = lax.psum(expand_bias_grad, "ctx")

    return (
        output,
        input_grad.reshape(1, 2, blocks, D),
        mine[0],
        mine[1],
        mixer_owned,
        mine[2],
        mine[3],
        merge_owned,
        mine[4],
        mine[5],
        mine[6],
        expand_owned,
        expand_bias_owned,
        shrink_owned,
        mine[7],
    )


def head_columns(weight, base):
    private, shared_at = 192, 1536
    mine = lax.dynamic_slice_in_dim(weight, base + lax.axis_index("ctx") * private, private, weight.ndim - 1)
    return jnp.concatenate([mine, weight[..., base + shared_at : base + D]], axis=-1)


def local_kernel(
    tokens,
    first_gain,
    first_shift,
    mixer_weight,
    query_bias,
    value_bias,
    merge_weight,
    merge_bias,
    second_gain,
    second_shift,
    expand_weight,
    expand_bias,
    shrink_weight,
    shrink_bias,
    cotangent,
):
    planes = lax.axis_size("fsdp")
    ring = lax.axis_size("ctx")
    me = lax.axis_index("ctx")
    plane = lax.axis_index("fsdp")
    blocks, half, length, local_rows = 64, 512, 1024, 128
    share = D // planes

    parts = [head_columns(mixer_weight, base) for base in (0, D, 2 * D)]
    m0 = jnp.concatenate([part[:, :128] for part in parts], axis=1)
    m1 = jnp.concatenate([part[:, 128:] for part in parts], axis=1)
    mg = jnp.concatenate([lax.dynamic_slice_in_dim(merge_weight, me * 48, 48, 0), merge_weight[384:]], axis=0)
    pieces = [lax.dynamic_slice_in_dim(expand_weight, 1600 * q + 200 * me, 200, 1) for q in range(4)]
    w1 = jnp.concatenate([jnp.pad(piece, ((0, 0), (0, 8))) for piece in pieces], axis=1)
    w2 = jnp.pad(lax.dynamic_slice_in_dim(shrink_weight, 200 * me, 200, 0), ((0, 8), (0, 0)))

    def spread(vector):
        return lax.dynamic_update_slice_in_dim(jnp.zeros((D,), BF), vector, plane * share, 0)

    def fill(vector):
        return jnp.pad(vector, (0, D - vector.shape[0]))

    bias1 = lax.dynamic_slice_in_dim(expand_bias, 200 * me, 200, 0)
    bias1 = lax.dynamic_update_slice_in_dim(jnp.zeros((D,), BF), bias1, plane * 208, 0)
    vpart = jnp.stack(
        [
            spread(first_gain),
            spread(first_shift),
            fill(head_columns(spread(query_bias), 0)),
            fill(head_columns(spread(value_bias), 0)),
            spread(merge_bias),
            spread(second_gain),
            spread(second_shift),
            spread(shrink_bias),
            bias1,
        ]
        + [jnp.zeros((D,), BF)] * 7
    )

    tok2, cot2 = tokens.reshape(local_rows, D), cotangent.reshape(local_rows, D)
    sgrad, hidden, out_own, dw1, dw2, dgb, qkv, attown, heads, vectors, lse, first_all, mws, mfull = run_forward(
        planes, tok2, cot2, vpart, m0, m1, mg, w1, w2
    )
    input_grad, va, vb, gw1, gw2, gm0, gm1, gmg = run_backward(
        planes, tok2, cot2, sgrad, hidden, vectors, attown, dgb, lse, qkv, heads, mfull.reshape(D, D), mws, first_all, dw1, dw2
    )
    shrink_owned = gw2[:, :200].reshape(1600, D).astype(F32)
    expand_owned = gw1.reshape(8, 400, 4, 208)[:, :, :, :200].transpose(1, 2, 0, 3).reshape(400, 6400).astype(F32)
    merge_owned = jnp.concatenate([gmg[j] for j in range(6)] + [gmg[6, :, :64]], axis=1).astype(F32)
    columns = []
    for n in range(3):
        at = 128 * n
        for j in range(8):
            columns += [gm0[j, :, at : at + 128].astype(F32), gm1[j, :, at : at + 64].astype(F32)]
        columns.append(jnp.sum(gm1[:, :, at + 64 : at + 128].astype(F32), axis=0))
    mixer_owned = jnp.concatenate(columns, axis=1)

    sums = jnp.sum(va, axis=0)
    lasts = jnp.sum(vb, axis=0)

    def head_vector(n):
        return jnp.concatenate([va[:, n, :192].reshape(1536), sums[n, 192:256]])

    def own(vector):
        return lax.dynamic_slice_in_dim(vector, plane * share, share, 0)

    bias1_all = va[:, 4, :832].reshape(8, 4, 208)[:, :, :200]
    expand_bias_owned = lax.dynamic_index_in_dim(bias1_all, plane, 1, keepdims=False).reshape(1600)

    return (
        out_own.reshape(1, 2, blocks, D),
        input_grad.reshape(1, 2, blocks, D),
        own(lasts[0]),
        own(lasts[1]),
        mixer_owned,
        own(head_vector(5)),
        own(head_vector(6)),
        merge_owned,
        own(sums[0]),
        own(sums[1]),
        own(sums[2]),
        expand_owned,
        expand_bias_owned,
        shrink_owned,
        own(sums[3]),
    )


def aligned(planes, ring, shape):
    return planes == 4 and ring == 8 and shape == (4, 2, 512, D)


def local(tokens, *others):
    planes, ring = lax.axis_size("fsdp"), lax.axis_size("ctx")
    whole = (tokens.shape[0] * planes, 2, tokens.shape[2] * ring, tokens.shape[3])
    if aligned(planes, ring, whole):
        return local_kernel(tokens, *others)
    return local_plain(tokens, *others)


def solution(mesh):
    token_spec = P("fsdp", None, "ctx", None)
    row = P("fsdp")
    matrix = P("fsdp", None)
    in_specs = (
        token_spec,
        row,
        row,
        matrix,
        row,
        row,
        matrix,
        row,
        row,
        row,
        matrix,
        row,
        matrix,
        row,
        token_spec,
    )
    out_specs = (
        token_spec,
        token_spec,
        row,
        row,
        matrix,
        row,
        row,
        matrix,
        row,
        row,
        row,
        matrix,
        row,
        matrix,
        row,
    )
    return jax.shard_map(local, mesh=mesh, in_specs=in_specs, out_specs=out_specs, check_vma=False)
```

```python
import functools

import jax
import jax.numpy as jnp
from jax import lax
from jax.experimental import pallas as pl
from jax.experimental.pallas import tpu as pltpu
from jax.sharding import PartitionSpec as P

D = 1600
H = 25
HD = 64

EPSILON = 1e-05
SCORE_SCALE = 0.125
BF = jnp.bfloat16
F32 = jnp.float32


def normalize(values):
    center = values - jnp.mean(values, axis=-1, keepdims=True)
    spread = jnp.mean(center * center, axis=-1, keepdims=True)
    inverse = lax.rsqrt(spread + EPSILON)
    return center * inverse, inverse


def norm_back(grad, gain, normal, inverse):
    scaled = grad * gain
    mean = jnp.mean(scaled, axis=-1, keepdims=True)
    along = jnp.mean(scaled * normal, axis=-1, keepdims=True)
    return inverse * (scaled - mean - normal * along)


def dot(a, b):
    return jnp.dot(a, b, preferred_element_type=F32)


def dot_t(a, b):
    return lax.dot_general(a, b, (((1,), (1,)), ((), ())), preferred_element_type=F32)


def t_dot(a, b):
    return lax.dot_general(a, b, (((0,), (0,)), ((), ())), preferred_element_type=F32)


def attend(query, key, value, allowed):
    scores = jnp.einsum("hqd,hkd->hqk", query, key, preferred_element_type=F32) * SCORE_SCALE
    scores = jnp.where(allowed[None], scores, -1e30)
    top = jnp.max(scores, axis=-1, keepdims=True)
    expo = jnp.exp(scores - top)
    total = jnp.sum(expo, axis=-1, keepdims=True)
    probs = (expo / total).astype(BF)
    return jnp.einsum("hqk,hkd->hqd", probs, value, preferred_element_type=F32), top, total


def attend_back(query, key, value, allowed, top, total, grad):
    scores = jnp.einsum("hqd,hkd->hqk", query, key, preferred_element_type=F32) * SCORE_SCALE
    scores = jnp.where(allowed[None], scores, -1e30)
    probs = jnp.exp(scores - top) / total
    probs_low = probs.astype(BF)
    prob_grad = jnp.einsum("hqd,hkd->hqk", grad, value, preferred_element_type=F32)
    offset = jnp.sum(prob_grad * probs, axis=-1, keepdims=True)
    score_grad = (probs * (prob_grad - offset)).astype(BF)
    dq = jnp.einsum("hqk,hkd->hqd", score_grad, key, preferred_element_type=F32) * SCORE_SCALE
    dk = jnp.einsum("hqk,hqd->hkd", score_grad, query, preferred_element_type=F32) * SCORE_SCALE
    dv = jnp.einsum("hqk,hqd->hkd", probs_low, grad, preferred_element_type=F32)
    return dq, dk, dv


def heads_first(values):
    rows, columns = values.shape
    return values.reshape(rows, columns // HD, HD).transpose(1, 0, 2)


def heads_last(values):
    heads, rows, _ = values.shape
    return values.transpose(1, 0, 2).reshape(rows, heads * HD)


MESH_ID = pl.DeviceIdType.MESH
HOPS = (2, 4, 6)


def dyn(start, size, step):
    return pl.ds(pl.multiple_of(start, step), size)


class Links:

    def __init__(self, planes):
        self.planes = planes
        self.p = lax.axis_index("fsdp")
        self.me = lax.axis_index("ctx")

    def plane(self, step):
        return (self.p + step, self.me)

    def peer(self, mask):
        return (self.p, self.me ^ mask)

    def copy(self, src, dst, send, recv, device):
        return pltpu.make_async_remote_copy(
            src_ref=src, dst_ref=dst, send_sem=send, recv_sem=recv, device_id=device, device_id_type=MESH_ID
        )

    def barrier(self, masks):
        bar = pltpu.get_barrier_semaphore()
        for mask in masks:
            pl.semaphore_signal(bar, inc=1, device_id=self.peer(mask), device_id_type=MESH_ID)
        for d in range(1, self.planes):
            to = (lax.rem(self.p + d, self.planes), self.me)
            pl.semaphore_signal(bar, inc=1, device_id=to, device_id_type=MESH_ID)
        pl.semaphore_wait(bar, len(masks) + self.planes - 1)


class LineGather:

    def __init__(self, links, src, slot, sems, local_sem):
        self.links, self.src, self.slot, self.sems, self.local_sem = links, src, slot, sems, local_sem

    def send(self, src, block, step):
        way = 1 if step > 0 else 2
        return self.links.copy(
            src, self.slot(block), self.sems.at[way, block], self.sems.at[0, block], self.links.plane(step)
        )

    def arrival(self, block):
        return self.links.copy(
            self.slot(block), self.slot(block), self.sems.at[1, block], self.sems.at[0, block], self.links.plane(0)
        )

    def start(self):
        p, last = self.links.p, self.links.planes - 1

        @pl.when(p < last)
        def _():
            self.send(self.src, p, 1).start()

        @pl.when(p > 0)
        def _():
            self.send(self.src, p, -1).start()

        pltpu.make_async_copy(self.src, self.slot(p), self.local_sem).start()

    def pump(self, d):
        p, last = self.links.p, self.links.planes - 1

        @pl.when(p >= d)
        def _():
            self.arrival(p - d).wait_recv()

            @pl.when(p < last)
            def _():
                self.send(self.slot(p - d), p - d, 1).start()

        @pl.when(p + d <= last)
        def _():
            self.arrival(p + d).wait_recv()

            @pl.when(p > 0)
            def _():
                self.send(self.slot(p + d), p + d, -1).start()

        if d == 1:
            pltpu.make_async_copy(self.src, self.slot(p), self.local_sem).wait()

    def finish(self):
        p, last = self.links.p, self.links.planes - 1
        for d in range(self.links.planes):

            @pl.when((p >= d) & (p < last))
            def _():
                self.send(self.slot(p - d), p - d, 1).wait_send()

            @pl.when((p + d <= last) & (p > 0))
            def _():
                self.send(self.slot(p + d), p + d, -1).wait_send()


class GroupGather:

    def __init__(self, links, slot, send, recv):
        self.links, self.slot, self.send_sem, self.recv_sem = links, slot, send, recv

    def copy(self, owner, mask, n):
        return self.links.copy(
            self.slot(owner), self.slot(owner), self.send_sem.at[n], self.recv_sem.at[owner], self.links.peer(mask)
        )

    def start(self):
        for n, mask in enumerate(HOPS + (1,)):
            self.copy(self.links.me, mask, n).start()

    def forward(self):
        for n, mask in enumerate(HOPS):
            owner = self.links.me ^ mask
            self.copy(owner, mask, n).wait_recv()
            self.copy(owner, 1, 4 + n).start()

    def wait(self):
        for mask in (1, 3, 5, 7):
            self.copy(self.links.me ^ mask, 1, 3).wait_recv()

    def finish(self):
        for n in range(7):
            self.copy(self.links.me, 1, n).wait_send()


class GroupSum:

    def __init__(self, links, stage, from_twin, from_far, send, twin_recv, far_recv):
        self.links, self.stage, self.from_twin, self.from_far = links, stage, from_twin, from_far
        self.send, self.twin_recv, self.far_recv = send, twin_recv, far_recv

    def to_twin(self, chip):
        return self.links.copy(
            self.stage.at[4 + chip], self.from_twin.at[chip], self.send.at[4 + chip], self.twin_recv.at[chip], self.links.peer(1)
        )

    def to_far(self, chip):
        return self.links.copy(
            self.stage.at[chip], self.from_far.at[chip - 1], self.send.at[chip], self.far_recv.at[chip - 1], self.links.peer(HOPS[chip - 1])
        )

    def run(self, block):
        me = self.links.me
        masks = (0,) + HOPS
        order = (3, 1, 2, 0)
        for chip in order:
            self.stage[4 + chip] = block(me ^ masks[chip] ^ 1).astype(BF)
            self.to_twin(chip).start()
        for chip in order[:3]:
            part = block(me ^ masks[chip])
            self.to_twin(chip).wait_recv()
            self.stage[chip] = (part + self.from_twin[chip].astype(F32)).astype(BF)
            self.to_far(chip).start()
        self.stage[0] = block(me).astype(BF)

    def total(self):
        self.to_twin(0).wait_recv()
        acc = self.stage[0].astype(F32) + self.from_twin[0].astype(F32)
        for chip in (1, 2, 3):
            self.to_far(chip).wait_recv()
            acc += self.from_far[chip - 1].astype(F32)
        return acc

    def finish(self):
        for chip in range(4):
            self.to_twin(chip).wait_send()
        for chip in (1, 2, 3):
            self.to_far(chip).wait_send()


def gelu_parts(u):
    inner = 0.7978845608 * (u + 0.044715 * (u * u * u))
    t = jnp.tanh(inner)
    value = 0.5 * u * (1.0 + t)
    slope = 0.5 * (1.0 + t) + 0.5 * u * (1.0 - t * t) * (0.7978845608 * (1.0 + 3 * 0.044715 * (u * u)))
    return value, slope


BLOCK_KEYS = (
    ((0, 256, 1),),
    ((0, 256, 0), (256, 256, 1)),
    ((0, 512, 0), (512, 256, 2), (768, 256, 0)),
    ((0, 512, 0), (768, 256, 2)),
)


def triangle(kind, shape):
    r = lax.broadcasted_iota(jnp.int32, shape, 0)
    c = lax.broadcasted_iota(jnp.int32, shape, 1)
    return c <= r if kind == 1 else c >= r


def half_mask(half):
    lane = lax.broadcasted_iota(jnp.int32, (1, 128), 1)
    return (lane // 64) == half


def softmax_pieces(q, keys, values, pieces, allowed):
    scores = []
    for start, size, kind in pieces:
        s = dot_t(q, keys[start : start + size])
        if kind:
            s = jnp.where(allowed(kind, start, s.shape), s, -1e30)
        scores.append(s)
    top = jnp.max(scores[0], axis=1, keepdims=True)
    for s in scores[1:]:
        top = jnp.maximum(top, jnp.max(s, axis=1, keepdims=True))
    total, out = 0.0, 0.0
    for s, (start, size, _) in zip(scores, pieces):
        e = jnp.exp(s - top)
        total = total + jnp.sum(e, axis=1, keepdims=True)
        out = out + dot(e.astype(BF), values[start : start + size])
    return out * (1.0 / total), top + jnp.log(total)


def forward_kernel(planes, tok, cot, vpart, m0, m1, mg, w1, w2,
                   sgrad_o, hidden_o, dw1_o, dw2_o, dgb_o, qkv_o, att_o, heads_o, vec_o, lse_o,
                   first_o, mw_o, mfull_o, act_o, w2_o, atts_o,
                   vec, mw0, mw1, mgs, mfull, w1b, w2b, first_all, g_all, sec_all, att_all, att, arecv,
                   act, slope, dw2, slot_w2, stage, twin, far,
                   zs, zl, gs, gr, a_s, a_r, rs_s, rs_t, rs_f, ls_s, ls_r, os):
    L = Links(planes)
    qkv, attown, hid, lse = qkv_o, att_o, hidden_o, lse_o
    p, me = L.p, L.me
    share = 400
    zvec = LineGather(L, vpart, lambda b: vec.at[b], zs.at[0], zl.at[0])
    zm0 = LineGather(L, m0, lambda b: mw0.at[dyn(b * share, share, 16)], zs.at[1], zl.at[1])
    zm1 = LineGather(L, m1, lambda b: mw1.at[dyn(b * share, share, 16)], zs.at[2], zl.at[2])
    zmg = LineGather(L, mg, lambda b: mgs.at[b], zs.at[3], zl.at[3])
    zw1 = LineGather(L, w1, lambda b: w1b.at[dyn(b * share, share, 16)], zs.at[4], zl.at[4])
    zw2 = LineGather(L, w2, lambda b: w2b.at[dyn(b * 208, 208, 16)], zs.at[5], zl.at[5])
    gfirst = GroupGather(L, lambda j: first_all.at[:, j], gs.at[0], gr.at[0])
    gg = GroupGather(L, lambda j: g_all.at[j], gs.at[1], gr.at[1])
    gsec = GroupGather(L, lambda j: sec_all.at[j], gs.at[2], gr.at[2])
    gatt = GroupGather(L, lambda j: att_all.at[j], gs.at[4], gr.at[4])
    lw2 = LineSum(L, lambda t: dw2.at[dyn(t * 208, 208, 16)], slot_w2, ls_s, ls_r)
    gmerge = GroupGather(L, lambda j: mfull.at[:, dyn(j * 48, 48, 16)], gs.at[3], gr.at[3])

    L.barrier((1, 2, 3, 4, 5, 6, 7))
    zvec.start()
    zm0.start()
    g_all[me] = cot[...]
    rows = tok[...].astype(F32)
    normal, _ = normalize(rows)
    for d in (1, 2, 3):
        zvec.pump(d)
    vectors = (vec[0].astype(F32) + vec[1].astype(F32)) + (vec[2].astype(F32) + vec[3].astype(F32))
    first = (normal * vectors[0:1] + vectors[1:2]).astype(BF)
    first_all[:, me] = first.reshape(2, 64, D)
    gfirst.start()
    zm0.pump(1)
    zm1.start()
    zm0.pump(2)
    zm0.pump(3)
    gfirst.forward()
    gg.start()
    gfirst.wait()
    zm1.pump(1)
    zmg.start()

    def mix(weights, pair):
        bias_q = vectors[2:3, pair * 128 : pair * 128 + 128]
        bias_v = vectors[3:4, pair * 128 : pair * 128 + 128]

        def body(b, _):
            x = first_all[b // 2, pl.ds((b % 2) * 4, 4)].reshape(256, D)
            mixed = dot(x, weights[...])
            at = dyn(b * 256, 256, 256)
            qkv[pair, at] = (mixed[:, :128] + bias_q).astype(BF)
            qkv[2 + pair, at] = mixed[:, 128:256].astype(BF)
            qkv[4 + pair, at] = (mixed[:, 256:] + bias_v).astype(BF)
            return 0

        lax.fori_loop(0, 4, body, 0)

    lane = lax.broadcasted_iota(jnp.int32, (1, 128), 1)

    def note_lse(head, at, value):
        lse[at] = jnp.where(lane == head, value, lse[at] if head else 0.0)

    def attend_private(pair, half):
        mask = half_mask(half)
        for b in range(4):
            q = jnp.where(mask, qkv[pair, b * 256 : b * 256 + 256], 0) * jnp.asarray(0.125, BF)
            out, l = softmax_pieces(
                q, qkv.at[2 + pair], qkv.at[4 + pair], BLOCK_KEYS[b], lambda kind, start, shape: triangle(kind, shape)
            )
            out = jnp.where(mask, out, 0.0).astype(BF).reshape(4, 64, 128)
            at = pl.ds((b % 2) * 4, 4)
            if half == 0:
                att[pair, b // 2, at] = out
            else:
                att[pair, b // 2, at] = att[pair, b // 2, at] + out
            note_lse(2 * pair + half, slice(b * 256, b * 256 + 256), l)

    def own_allowed(kind, start, shape):
        r = lax.broadcasted_iota(jnp.int32, shape, 0)
        c = lax.broadcasted_iota(jnp.int32, shape, 1)
        rp = jnp.where(r < 64, me * 64 + r, 1023 - (me * 64 + r - 64))
        cp = jnp.where(c < 512, c, 1023 - (c - 512))
        return cp <= rp

    mix(mw0, 0)
    zm1.pump(2)
    attend_private(0, 0)
    zm1.pump(3)
    zmg.pump(1)
    zw1.start()
    attend_private(0, 1)
    zmg.pump(2)
    gg.forward()
    mix(mw1, 1)
    outs = [
        pltpu.make_async_copy(first_all, first_o, os.at[0]),
        pltpu.make_async_copy(mw0, mw_o.at[0], os.at[1]),
        pltpu.make_async_copy(mw1, mw_o.at[1], os.at[2]),
        pltpu.make_async_copy(mfull, mfull_o, os.at[3]),
        pltpu.make_async_copy(act, act_o, os.at[4]),
        pltpu.make_async_copy(w2b, w2_o, os.at[5]),
        pltpu.make_async_copy(att_all, atts_o, os.at[6]),
    ]
    for c in outs[:3]:
        c.start()
    zmg.pump(3)
    for b in range(4):
        mfull[b, dyn(me * 48, 48, 16)] = mgs[b, 0:48]
        mfull[b, 384:400] = mgs[b, 48:64]
    gmerge.start()
    attend_private(1, 0)
    qs = jnp.concatenate([qkv[1, dyn(me * 64, 64, 64)], qkv[1, dyn(512 + me * 64, 64, 64)]], axis=0)
    mask1 = half_mask(1)
    qs = jnp.where(mask1, qs, 0) * jnp.asarray(0.125, BF)
    out_s, l_s = softmax_pieces(qs, qkv.at[3], qkv.at[5], ((0, 1024, 1),), own_allowed)
    note_lse(3, slice(0, 128), l_s)
    shared_low = jnp.where(mask1, out_s, 0.0).astype(BF)

    def exchange(mask):
        return L.copy(att.at[:, :, me ^ mask], arecv.at[me], a_s.at[mask], a_r.at[me], L.peer(mask))

    def arrived(mask):
        return L.copy(att.at[:, :, me], arecv.at[me ^ mask], a_s.at[mask], a_r.at[me ^ mask], L.peer(mask))

    for mask in range(1, 8):
        exchange(mask).start()
    zw1.pump(1)
    gmerge.forward()
    arecv[me] = att[:, :, me]
    zw2.start()
    for mask in range(1, 8):
        arrived(mask).wait_recv()
    for j in range(8):
        attown[:, 192 * j : 192 * j + 128] = arecv[j, 0].reshape(128, 128)
        attown[:, 192 * j + 128 : 192 * j + 192] = arecv[j, 1].reshape(128, 128)[:, :64]
    attown[:, 1536:1600] = shared_low[:, 64:128]
    gmerge.wait()
    hidden = rows + vectors[4:5]
    hid[...] = hidden
    for b in range(4):
        hid[...] += dot(attown[:, b * 400 : b * 400 + 400], mfull[b])
    normal2, _ = normalize(hid[...])
    sec_all[me] = (normal2 * vectors[5:6] + vectors[6:7]).astype(BF)
    gsec.start()
    outs[3].start()
    att_all[me] = attown[...]
    gg.wait()
    zw1.pump(2)
    gsec.forward()
    gatt.start()
    zw1.pump(3)
    gsec.wait()

    def expand(b, _):
        at = dyn(b * 256, 256, 256)
        pre = dot(sec_all[pl.ds(2 * b, 2)].reshape(256, D), w1b[...]) + vectors[8:9, :832]
        value, s = gelu_parts(pre)
        act[at] = value.astype(BF)
        slope[at] = s.astype(BF)
        return 0

    lax.fori_loop(0, 4, expand, 0)
    outs[4].start()
    zw2.pump(1)
    g2 = g_all[...].reshape(1024, D)
    for start, size in ((0, 256), (256, 256), (512, 256), (768, 64)):
        dw2[start : start + size] = t_dot(act[:, start : start + size], g2).astype(BF)
    lw2.start()
    gatt.forward()
    zw2.pump(2)
    lw2.pump(0)
    zw2.pump(3)
    outs[5].start()

    def contract(b, acc):
        at = dyn(b * 256, 256, 256)
        grad = dot_t(g_all[pl.ds(2 * b, 2)].reshape(256, D), w2b[...]) * slope[at].astype(F32)
        slope[at] = grad.astype(BF)
        return acc + jnp.sum(grad, axis=0, keepdims=True)

    dgb_o[...] = lax.fori_loop(0, 4, contract, jnp.zeros((1, 832), F32))
    sums = GroupSum(L, stage, twin, far, rs_s, rs_t, rs_f)
    sums.run(lambda owner: dot_t(slope[dyn(owner * 128, 128, 128)], w1b[...]))
    lw2.pump(1)
    for start in range(0, D, 256):
        size = min(256, D - start)
        x = sec_all[:, :, start : start + size].reshape(1024, size)
        dw1_o[start : start + size] = t_dot(x, slope[...]).astype(BF)
    gatt.wait()
    outs[6].start()
    sgrad_o[...] = sums.total()
    lw2.total()
    dw2_o[...] = dw2[dyn(p * 208, 208, 16)]
    heads_o[...] = att[...]
    vec_o[...] = vectors
    for c in outs:
        c.wait()
    for z in (zvec, zm0, zm1, zmg, zw1, zw2):
        z.finish()
    for g in (gfirst, gg, gsec, gmerge, gatt):
        g.finish()
    for mask in range(1, 8):
        exchange(mask).wait_send()
    sums.finish()
    lw2.finish()


def run_forward(planes, tok, cot, vpart, m0, m1, mg, w1, w2):
    any_ = pl.BlockSpec(memory_space=pl.ANY)
    vm = pl.BlockSpec(memory_space=pltpu.VMEM)
    S = jax.ShapeDtypeStruct
    V = pltpu.VMEM
    dma = pltpu.SemaphoreType.DMA
    return pl.pallas_call(
        functools.partial(forward_kernel, planes),
        out_shape=(
            S((128, D), F32), S((128, D), F32), S((D, 832), BF), S((208, D), BF), S((1, 832), F32),
            S((6, 1024, 128), BF), S((128, D), BF), S((2, 2, 8, 64, 128), BF), S((16, D), F32), S((1024, 128), F32),
            S((2, 8, 64, D), BF), S((2, D, 384), BF), S((4, 400, D), BF), S((1024, 832), BF), S((832, D), BF), S((8, 128, D), BF),
        ),
        in_specs=[vm, vm] + [any_] * 6,
        out_specs=(vm,) * 10 + (any_,) * 6,
        scratch_shapes=[
            V((4, 16, D), BF), V((D, 384), BF), V((D, 384), BF), V((4, 64, D), BF), V((4, 400, D), BF),
            V((D, 832), BF), V((832, D), BF), V((2, 8, 64, D), BF), V((8, 128, D), BF), V((8, 128, D), BF), V((8, 128, D), BF),
            V((2, 2, 8, 64, 128), BF), V((8, 2, 2, 64, 128), BF),
            V((1024, 832), BF), V((1024, 832), BF), V((832, D), BF), V((6, 208, D), BF),
            V((8, 128, D), BF), V((4, 128, D), BF), V((3, 128, D), BF),
            dma((6, 3, 4)), dma((6,)), dma((5, 7)), dma((5, 8)), dma((8,)), dma((8,)),
            dma((8,)), dma((4,)), dma((3,)), dma((4,)), dma((6,)), dma((7,)),
        ],
        compiler_params=pltpu.CompilerParams(collective_id=0, has_side_effects=True, vmem_limit_bytes=63 << 20),
        cost_estimate=pl.CostEstimate(flops=15_000_000_000, bytes_accessed=60_000_000, transcendentals=4_000_000),
    )(tok, cot, vpart, m0, m1, mg, w1, w2)


class LineSum:

    def __init__(self, links, block, slots, send, recv):
        self.links, self.block, self.slots, self.send_sem, self.recv_sem = links, block, slots, send, recv
        self.last = links.planes - 1

    def send(self, t, step):
        slot = t - 1 if step > 0 else self.last + t
        return self.links.copy(
            self.block(t), self.slots.at[slot], self.send_sem.at[t], self.recv_sem.at[slot], self.links.plane(step)
        )

    def arrival(self, slot):
        return self.links.copy(
            self.slots.at[slot], self.slots.at[slot], self.send_sem.at[0], self.recv_sem.at[slot], self.links.plane(0)
        )

    def start(self):
        @pl.when(self.links.p == 0)
        def _():
            for t in range(self.last, 0, -1):
                self.send(t, 1).start()

        @pl.when(self.links.p == self.last)
        def _():
            for t in range(self.last):
                self.send(t, -1).start()

    def add(self, t, slot):
        self.arrival(slot).wait_recv()
        ref = self.block(t)
        ref[...] = (ref[...].astype(F32) + self.slots[slot].astype(F32)).astype(BF)

    def pump(self, k):
        p, last = self.links.p, self.last
        t = last - k

        @pl.when((p > 0) & (p < t))
        def _():
            self.add(t, t - 1)
            self.send(t, 1).start()

        @pl.when((k < p) & (p < last))
        def _():
            self.add(k, last + k)
            self.send(k, -1).start()

    def total(self):
        p, last = self.links.p, self.last

        @pl.when(p > 0)
        def _():
            self.add(p, p - 1)

        @pl.when(p < last)
        def _():
            self.add(p, last + p)

    def finish(self):
        p = self.links.p
        for t in range(self.last + 1):

            @pl.when(p < t)
            def _():
                self.send(t, 1).wait_send()

            @pl.when(p > t)
            def _():
                self.send(t, -1).wait_send()


class LineExchange:

    def __init__(self, links, slots, send, recv):
        self.links, self.slots, self.send_sem, self.recv_sem = links, slots, send, recv

    def copy(self, src, d):
        planes = self.links.planes
        to = lax.rem(self.links.p + d, planes)
        return self.links.copy(src, self.slots.at[d - 1], self.send_sem.at[d - 1], self.recv_sem.at[d - 1], (to, self.links.me))

    def start(self, src):
        for d in range(1, self.links.planes):
            self.copy(src, d).start()

    def total(self, src):
        acc = src[...]
        for d in range(1, self.links.planes):
            self.copy(src, d).wait_recv()
            acc = acc + self.slots[d - 1]
        return acc

    def finish(self, src):
        for d in range(1, self.links.planes):
            self.copy(src, d).wait_send()


class OwnGather(GroupGather):

    def __init__(self, links, src, slot, send, recv, local_sem):
        super().__init__(links, slot, send, recv)
        self.src, self.local_sem = src, local_sem

    def start(self):
        for n, mask in enumerate(HOPS + (1,)):
            self.own(mask, n).start()
        pltpu.make_async_copy(self.src(), self.slot(self.links.me), self.local_sem).start()

    def own(self, mask, n):
        return self.links.copy(
            self.src(), self.slot(self.links.me), self.send_sem.at[n], self.recv_sem.at[self.links.me], self.links.peer(mask)
        )

    def finish(self):
        for n, mask in enumerate(HOPS + (1,)):
            self.own(mask, n).wait_send()
        for n, mask in enumerate(HOPS):
            self.copy(self.links.me ^ mask, 1, 4 + n).wait_send()
        pltpu.make_async_copy(self.src(), self.slot(self.links.me), self.local_sem).wait()


def backward_kernel(planes, tok, cot, sgrad, hid, vectors, attown, dgb, lse, qkv, att, dw2,
                    mfull_h, mw_h, first_h, dw1_h, act_h, w2_h, atts_h,
                    igrad_o, out_o, va_o, vb_o, gw1_o, gw2_o, gm0_o, gm1_o, gmg_o,
                    mfull, mw, first_all, dw1, act, w2b, hlow, agrad, asend, gatt, att_all, hc, dkv, mgr, dmix, dmerge,
                    slot_w1, slot_m0, slot_m1, slot_mg, stage, twin, far, va, vb, vslot,
                    ld, ls_s, ls_r, ve_s, ve_r, gs, gr, gl, a_s, a_r, h_s, h_r, rs_s, rs_t, rs_f, free):
    L = Links(planes)
    p, me = L.p, L.me
    loads = [
        pltpu.make_async_copy(mfull_h, mfull, ld.at[0]),
        pltpu.make_async_copy(dw1_h, dw1, ld.at[1]),
        pltpu.make_async_copy(act_h, act, ld.at[2]),
        pltpu.make_async_copy(w2_h, w2b, ld.at[3]),
        pltpu.make_async_copy(first_h, first_all, ld.at[4]),
        pltpu.make_async_copy(mw_h, mw, ld.at[5]),
        pltpu.make_async_copy(atts_h, att_all, ld.at[6]),
    ]
    for c in loads:
        c.start()
    lw1 = LineSum(L, lambda t: dw1.at[dyn(t * 400, 400, 16)], slot_w1, ls_s.at[1], ls_r.at[1])
    lm0 = LineSum(L, lambda t: dmix.at[0, dyn(t * 400, 400, 16)], slot_m0, ls_s.at[2], ls_r.at[2])
    lm1 = LineSum(L, lambda t: dmix.at[1, dyn(t * 400, 400, 16)], slot_m1, ls_s.at[3], ls_r.at[3])
    lmg = LineSum(L, lambda t: dmerge.at[dyn(t * 400, 400, 16)], slot_mg, ls_s.at[4], ls_r.at[4])
    xa = LineExchange(L, vslot.at[0], ve_s.at[0], ve_r.at[0])
    xb = LineExchange(L, vslot.at[1], ve_s.at[1], ve_r.at[1])
    gw2 = OwnGather(L, lambda: dw2, lambda j: gw2_o.at[j], gs.at[1], gr.at[1], gl.at[1])
    gw1 = OwnGather(L, lambda: lw1.block(p), lambda j: gw1_o.at[j], gs.at[2], gr.at[2], gl.at[2])
    gm0 = OwnGather(L, lambda: lm0.block(p), lambda j: gm0_o.at[j], gs.at[3], gr.at[3], gl.at[3])
    gm1 = OwnGather(L, lambda: lm1.block(p), lambda j: gm1_o.at[j], gs.at[4], gr.at[4], gl.at[4])
    gmg = OwnGather(L, lambda: lmg.block(p), lambda j: gmg_o.at[j], gs.at[5], gr.at[5], gl.at[5])
    gva = OwnGather(L, lambda: va, lambda j: va_o.at[j], gs.at[6], gr.at[6], gl.at[6])
    gvb = OwnGather(L, lambda: vb, lambda j: vb_o.at[j], gs.at[7], gr.at[7], gl.at[7])
    L.barrier((1, 2, 3, 4, 5, 6, 7))

    tangent = cot[...].astype(F32)
    normal2, inverse2 = normalize(hid[...])
    grad2 = sgrad[...]
    hidden_grad = tangent + norm_back(grad2, vectors[5:6], normal2, inverse2)
    igrad_o[...] = hidden_grad
    hlow[:, 0:D] = hidden_grad.astype(BF)
    hlow[:, D:2048] = jnp.zeros((128, 2048 - D), BF)
    va[0:1] = jnp.sum(hidden_grad, axis=0, keepdims=True)
    va[1:2] = jnp.sum(grad2 * normal2, axis=0, keepdims=True)
    va[2:3] = jnp.sum(grad2, axis=0, keepdims=True)
    va[3:4] = jnp.sum(tangent, axis=0, keepdims=True)
    va[4:8] = jnp.zeros((4, D), F32)
    va[4:5, 0:832] = dgb[...]

    def columns(mask):
        to = me ^ mask
        return L.copy(hlow.at[:, dyn(to * 256, 256, 256)], hc.at[me], h_s.at[mask], h_r.at[me], L.peer(mask))

    def columns_in(mask):
        return L.copy(hc.at[me], hc.at[me ^ mask], h_s.at[mask], h_r.at[me ^ mask], L.peer(mask))

    loads[0].wait()
    agrad[...] = dot_t(hlow[:, 0:D], mfull[...]).astype(BF)
    for j in range(8):
        asend[j, 0] = agrad[:, 192 * j : 192 * j + 128].reshape(2, 64, 128)
        tail = agrad[:, 192 * j + 128 : 192 * j + 192]
        asend[j, 1] = jnp.concatenate([tail, jnp.zeros((128, 64), BF)], axis=1).reshape(2, 64, 128)

    def exchange(mask):
        return L.copy(asend.at[me ^ mask], gatt.at[:, :, me], a_s.at[mask], a_r.at[me], L.peer(mask))

    def arrived(mask):
        return L.copy(asend.at[me], gatt.at[:, :, me ^ mask], a_s.at[mask], a_r.at[me ^ mask], L.peer(mask))

    for mask in range(1, 8):
        exchange(mask).start()
    gatt[:, :, me] = asend[me]
    loads[1].wait()
    lw1.start()
    for mask in range(1, 8):
        columns(mask).start()
    loads[2].wait()
    loads[3].wait()
    outs = GroupSum(L, stage, twin, far, rs_s, rs_t, rs_f)
    outs.run(lambda owner: dot(act[dyn(owner * 128, 128, 128)], w2b[...]))
    gw2.start()
    hc[me] = hlow[:, dyn(me * 256, 256, 256)]
    dkv[...] = jnp.zeros(dkv.shape, F32)
    for mask in range(1, 8):
        arrived(mask).wait_recv()

    scale = jnp.asarray(0.125, BF)

    def head_back(pair, head, mask, q, g, o, stat, pieces, allowed):
        delta = jnp.sum(g.astype(F32) * o.astype(F32), axis=1, keepdims=True)
        dq = 0.0
        for start, size, kind in pieces:
            keys = qkv[2 + pair, start : start + size]
            s = dot_t(q, keys)
            if kind:
                s = jnp.where(allowed(kind, start, s.shape), s, -1e30)
            prob = jnp.exp(s - stat)
            ds = (prob * (dot_t(g, qkv[4 + pair, start : start + size]) - delta)).astype(BF)
            dq = dq + dot(ds, keys)
            dkv[pair, 0, start : start + size] += t_dot(ds, q)
            dkv[pair, 1, start : start + size] += t_dot(prob.astype(BF), g)
        return jnp.where(mask, dq, 0.0) * 0.125

    def private_back(pair, half):
        mask = half_mask(half)
        head = 2 * pair + half
        total = 0.0
        for b in range(4):
            at = slice(b * 256, b * 256 + 256)
            blk = (pair, b // 2, pl.ds((b % 2) * 4, 4))
            q = jnp.where(mask, qkv[pair, at], 0) * scale
            g = jnp.where(mask, gatt[blk].reshape(256, 128), 0)
            o = att[blk].reshape(256, 128)
            dq = head_back(
                pair, head, mask, q, g, o, lse[at, head : head + 1], BLOCK_KEYS[b],
                lambda kind, start, shape: triangle(kind, shape),
            )
            total = total + jnp.sum(dq, axis=0, keepdims=True)
            if half == 0:
                mgr[pair, at, 0:128] = dq.astype(BF)
            else:
                mgr[pair, at, 0:128] = mgr[pair, at, 0:128] + dq.astype(BF)
        return total

    def mixer_part(pair):
        mgr[pair, :, 128:256] = dkv[pair, 0].astype(BF)
        mgr[pair, :, 256:384] = dkv[pair, 1].astype(BF)
        va[6:7, pair * 128 : pair * 128 + 128] = jnp.sum(dkv[pair, 1], axis=0, keepdims=True)
        for start in range(0, D, 256):
            size = min(256, D - start)
            x = first_all[:, :, :, start : start + size].reshape(1024, size)
            dmix[pair, start : start + size] = t_dot(x, mgr[pair]).astype(BF)

    qb0 = private_back(0, 0)
    lw1.pump(0)
    qb0 = qb0 + private_back(0, 1)
    va[5:6, 0:128] = qb0
    out_o[...] = (outs.total() + hid[...] + vectors[7:8]).astype(BF)
    outs.finish()
    for mask in (1,) + HOPS:
        pl.semaphore_signal(free, inc=1, device_id=L.peer(mask), device_id_type=MESH_ID)
    loads[4].wait()
    mixer_part(0)
    lm0.start()
    gw2.forward()
    lw1.pump(1)
    qb1 = private_back(1, 0)
    mask1 = half_mask(1)
    own_early, own_late = dyn(me * 64, 64, 64), dyn(512 + me * 64, 64, 64)
    qs = jnp.concatenate([qkv[1, own_early], qkv[1, own_late]], axis=0)
    qs = jnp.where(mask1, qs, 0) * scale
    blank = jnp.zeros((128, 64), BF)
    g_s = jnp.concatenate([blank, agrad[:, 1536:1600]], axis=1)
    o_s = jnp.concatenate([blank, attown[:, 1536:1600]], axis=1)

    def own_allowed(kind, start, shape):
        r = lax.broadcasted_iota(jnp.int32, shape, 0)
        c = lax.broadcasted_iota(jnp.int32, shape, 1) + start
        rp = jnp.where(r < 64, me * 64 + r, 1023 - (me * 64 + r - 64))
        cp = jnp.where(c < 512, c, 1023 - (c - 512))
        return cp <= rp

    dqs = head_back(1, 3, mask1, qs, g_s, o_s, lse[0:128, 3:4], ((0, 512, 1), (512, 512, 1)), own_allowed)
    va[5:6, 128:256] = qb1 + jnp.sum(dqs, axis=0, keepdims=True)
    dqs_low = dqs.astype(BF)
    mgr[1, own_early, 0:128] = mgr[1, own_early, 0:128] + dqs_low[:64]
    mgr[1, own_late, 0:128] = mgr[1, own_late, 0:128] + dqs_low[64:]
    mixer_part(1)
    lm1.start()
    xa.start(va)
    loads[5].wait()
    pl.semaphore_wait(free, 4)
    sums = GroupSum(L, stage, twin, far, rs_s, rs_t, rs_f)

    def first_block(owner):
        early, late = dyn(owner * 64, 64, 64), dyn(512 + owner * 64, 64, 64)
        x0 = jnp.concatenate([mgr[0, early], mgr[0, late]], axis=0)
        x1 = jnp.concatenate([mgr[1, early], mgr[1, late]], axis=0)
        return dot_t(x0, mw[0]) + dot_t(x1, mw[1])

    sums.run(first_block)
    lw1.total()
    gw1.start()
    loads[6].wait()
    for mask in range(1, 8):
        columns_in(mask).wait_recv()
    h2 = hc[...].reshape(1024, 256)
    for start in range(0, D, 256):
        size = min(256, D - start)
        x = att_all[:, :, start : start + size].reshape(1024, size)
        dmerge[start : start + size] = t_dot(x, h2).astype(BF)
    lmg.start()
    first_grad = sums.total()
    rows = tok[...].astype(F32)
    normal1, inverse1 = normalize(rows)
    igrad_o[...] += norm_back(first_grad, vectors[0:1], normal1, inverse1)
    vb[0:1] = jnp.sum(first_grad * normal1, axis=0, keepdims=True)
    vb[1:2] = jnp.sum(first_grad, axis=0, keepdims=True)
    vb[2:8] = jnp.zeros((6, D), F32)
    xb.start(vb)
    total_a = xa.total(va)
    xa.finish(va)
    va[...] = total_a
    gva.start()
    lm0.pump(0)
    lm0.pump(1)
    lm1.pump(0)
    total_b = xb.total(vb)
    xb.finish(vb)
    vb[...] = total_b
    gvb.start()
    lm0.total()
    gm0.start()
    gva.forward()
    lm1.pump(1)
    lmg.pump(0)
    gw1.forward()
    gvb.forward()
    lm1.total()
    gm1.start()
    lmg.pump(1)
    gm0.forward()
    lmg.total()
    gmg.start()
    gm1.forward()
    gmg.forward()
    for g in (gw2, gva, gw1, gvb, gm0, gm1, gmg):
        g.wait()
    for g in (gw2, gw1, gm0, gm1, gmg, gva, gvb):
        g.finish()
    for s in (lw1, lm0, lm1, lmg):
        s.finish()
    for mask in range(1, 8):
        exchange(mask).wait_send()
        columns(mask).wait_send()
    sums.finish()


def run_backward(planes, *operands):
    any_ = pl.BlockSpec(memory_space=pl.ANY)
    vm = pl.BlockSpec(memory_space=pltpu.VMEM)
    S = jax.ShapeDtypeStruct
    V = pltpu.VMEM
    dma = pltpu.SemaphoreType.DMA
    return pl.pallas_call(
        functools.partial(backward_kernel, planes),
        out_shape=(
            S((128, D), F32), S((128, D), BF), S((8, 8, D), F32), S((8, 8, D), F32), S((8, 400, 832), BF), S((8, 208, D), BF),
            S((8, 400, 384), BF), S((8, 400, 384), BF), S((8, 400, 256), BF),
        ),
        in_specs=[vm] * 11 + [any_] * 7,
        out_specs=(vm,) * 2 + (any_,) * 7,
        scratch_shapes=[
            V((D, D), BF), V((2, D, 384), BF), V((2, 8, 64, D), BF), V((D, 832), BF), V((1024, 832), BF), V((832, D), BF),
            V((128, 2048), BF), V((128, D), BF), V((8, 2, 2, 64, 128), BF), V((2, 2, 8, 64, 128), BF),
            V((8, 128, D), BF), V((8, 128, 256), BF), V((2, 2, 1024, 128), F32), V((2, 1024, 384), BF),
            V((2, D, 384), BF), V((D, 256), BF),
            V((6, 400, 832), BF), V((6, 400, 384), BF), V((6, 400, 384), BF), V((6, 400, 256), BF),
            V((8, 128, D), BF), V((4, 128, D), BF), V((3, 128, D), BF), V((8, D), F32), V((8, D), F32), V((2, 3, 8, D), F32),
            dma((7,)), dma((5, 4)), dma((5, 6)), dma((2, 3)), dma((2, 3)), dma((8, 7)), dma((8, 8)), dma((8,)),
            dma((8,)), dma((8,)), dma((8,)), dma((8,)), dma((8,)), dma((4,)), dma((3,)), pltpu.SemaphoreType.REGULAR,
        ],
        compiler_params=pltpu.CompilerParams(collective_id=1, has_side_effects=True, vmem_limit_bytes=63 << 20),
        cost_estimate=pl.CostEstimate(flops=15_000_000_000, bytes_accessed=60_000_000, transcendentals=4_000_000),
    )(*operands)


def assemble_kernel(gw1, gm0, gm1, gmg, expand_o, mixer_o, merge_o):
    for j in range(8):
        for q in range(4):
            expand_o[:, 1600 * q + 200 * j : 1600 * q + 200 * j + 200] = gw1[j, :, 208 * q : 208 * q + 200].astype(F32)
        for n in range(3):
            at = D * n + 192 * j
            mixer_o[:, at : at + 128] = gm0[j, :, 128 * n : 128 * n + 128].astype(F32)
            mixer_o[:, at + 128 : at + 192] = gm1[j, :, 128 * n : 128 * n + 64].astype(F32)
    for n in range(3):
        total = gm1[0, :, 128 * n : 128 * n + 128].astype(F32)
        for j in range(1, 8):
            total += gm1[j, :, 128 * n : 128 * n + 128].astype(F32)
        mixer_o[:, D * n + 1536 : D * n + 1600] = total[:, 64:]
    for j in range(6):
        merge_o[:, 256 * j : 256 * j + 256] = gmg[j].astype(F32)
    merge_o[:, 1536:1600] = gmg[6, :, :64].astype(F32)


def assemble(gw1, gm0, gm1, gmg):
    rows = 80

    def part(width):
        return pl.BlockSpec((8, rows, width), lambda n: (0, n, 0))

    def whole(width):
        return pl.BlockSpec((rows, width), lambda n: (n, 0))

    S = jax.ShapeDtypeStruct
    return pl.pallas_call(
        assemble_kernel,
        grid=(400 // rows,),
        in_specs=[part(832), part(384), part(384), part(256)],
        out_specs=(whole(6400), whole(4800), whole(D)),
        out_shape=(S((400, 6400), F32), S((400, 4800), F32), S((400, D), F32)),
        compiler_params=pltpu.CompilerParams(vmem_limit_bytes=40 << 20),
    )(gw1, gm0, gm1, gmg)


def widen_kernel(x, o):
    o[...] = x[0, :200].astype(F32)


def widen(gw2):
    return pl.pallas_call(
        widen_kernel,
        grid=(8,),
        in_specs=[pl.BlockSpec((1, 208, D), lambda n: (n, 0, 0))],
        out_specs=pl.BlockSpec((200, D), lambda n: (n, 0)),
        out_shape=jax.ShapeDtypeStruct((1600, D), F32),
        compiler_params=pltpu.CompilerParams(vmem_limit_bytes=40 << 20),
    )(gw2)


def local_plain(
    tokens,
    first_gain,
    first_shift,
    mixer_weight,
    query_bias,
    value_bias,
    merge_weight,
    merge_bias,
    second_gain,
    second_shift,
    expand_weight,
    expand_bias,
    shrink_weight,
    shrink_bias,
    cotangent,
):
    planes = lax.axis_size("fsdp")
    ring = lax.axis_size("ctx")
    me = lax.axis_index("ctx")
    blocks = tokens.shape[2]
    local_rows = 2 * blocks
    half = blocks * ring
    length = 2 * half
    private = H // ring
    shared = H - private * ring
    pc, sc = private * HD, shared * HD
    hc = pc + sc
    shared_at = private * ring * HD
    share = D // planes
    ff_plane = expand_bias.shape[0]
    ff_part = ff_plane // ring
    cols = D // ring

    vectors = jnp.stack(
        [first_gain, first_shift, query_bias, value_bias, merge_bias, second_gain, second_shift, shrink_bias]
    )
    vectors = lax.all_gather(vectors, "fsdp", axis=1, tiled=True).astype(F32)
    gain1, shift1, qbias, vbias, mbias, gain2, shift2, sbias = [vectors[n] for n in range(8)]

    def head_columns(weight, base):
        mine = lax.dynamic_slice_in_dim(weight, base + me * pc, pc, weight.ndim - 1)
        every = weight[..., base + shared_at : base + D]
        return [mine, every]

    mixer_part = jnp.concatenate(
        head_columns(mixer_weight, 0) + head_columns(mixer_weight, D) + head_columns(mixer_weight, 2 * D), axis=1
    )
    mixer_mine = lax.all_gather(mixer_part, "fsdp", axis=0, tiled=True)

    merge_part = lax.dynamic_slice_in_dim(merge_weight, me * cols, cols, 1)
    merge_cols = lax.all_gather(merge_part, "fsdp", axis=0, tiled=True)
    merge_full = lax.all_gather(merge_cols, "ctx", axis=1, tiled=True)

    expand_part = expand_weight.reshape(share, planes, ring, ff_part)
    expand_part = lax.dynamic_index_in_dim(expand_part, me, 2, keepdims=False)
    expand_part = lax.all_to_all(expand_part, "fsdp", 1, 0, tiled=False).reshape(D, ff_part)
    expand_mine = lax.all_gather(expand_part, "ctx", axis=1, tiled=True)

    rows = tokens.reshape(local_rows, D).astype(F32)
    normal1, inverse1 = normalize(rows)
    first = (normal1 * gain1 + shift1).astype(BF)
    first_all = lax.all_gather(first.reshape(2, blocks, D), "ctx", axis=1, tiled=True).reshape(length, D)
    tangent_low = cotangent.reshape(local_rows, D)
    tangent = tangent_low.astype(F32)
    tangent_all = lax.all_gather(tangent_low, "fsdp", axis=0, tiled=True)

    mixed = dot(first_all, mixer_mine)
    qb = jnp.concatenate(head_columns(qbias, 0), axis=0)
    vb = jnp.concatenate(head_columns(vbias, 0), axis=0)
    query = (mixed[:, :hc] + qb).astype(BF)
    key = mixed[:, hc : 2 * hc].astype(BF)
    value = (mixed[:, 2 * hc :] + vb).astype(BF)
    half_index = jnp.arange(half, dtype=jnp.int32)
    place = jnp.concatenate([half_index, length - 1 - half_index])
    early = me * blocks + jnp.arange(blocks, dtype=jnp.int32)
    own_place = jnp.concatenate([early, length - 1 - early])
    allowed = place[None, :] <= place[:, None]
    own_allowed = place[None, :] <= own_place[:, None]

    def own_rows(values):
        parts = values.reshape(2, half, values.shape[1])
        return lax.dynamic_slice_in_dim(parts, me * blocks, blocks, 1).reshape(local_rows, values.shape[1])

    qp, kp, vp = heads_first(query[:, :pc]), heads_first(key[:, :pc]), heads_first(value[:, :pc])
    qs, ks, vs = heads_first(own_rows(query[:, pc:])), heads_first(key[:, pc:]), heads_first(value[:, pc:])
    out_p, top_p, total_p = attend(qp, kp, vp, allowed)
    out_s, top_s, total_s = attend(qs, ks, vs, own_allowed)
    att_heads = heads_last(out_p).astype(BF)
    att_pieces = lax.all_to_all(att_heads.reshape(2, ring, blocks, pc), "ctx", 1, 2, tiled=False)
    attended = jnp.concatenate(
        [att_pieces.reshape(local_rows, ring * pc), heads_last(out_s).astype(BF)], axis=1
    )
    hidden = rows + dot(attended, merge_full) + mbias
    normal2, inverse2 = normalize(hidden)
    second = (normal2 * gain2 + shift2).astype(BF)
    second_all = lax.all_gather(second, "fsdp", axis=0, tiled=True)
    attended_all = lax.all_gather(attended, "ctx", axis=0, tiled=True)

    pre = dot(second_all, expand_mine) + expand_bias.astype(F32)
    act, gate_pull = jax.vjp(lambda u: jax.nn.gelu(u, approximate=True), pre)
    act_low = act.astype(BF)
    act_grad = dot_t(tangent_all, shrink_weight)
    (pre_grad,) = gate_pull(act_grad)
    pre_low = pre_grad.astype(BF)
    second_part = dot_t(pre_low, expand_mine).astype(BF)
    second_grad = lax.psum_scatter(second_part, "fsdp", scatter_dimension=0, tiled=True).astype(F32)
    out_part = dot(act_low, shrink_weight).astype(BF)
    out_sum = lax.psum_scatter(out_part, "fsdp", scatter_dimension=0, tiled=True).astype(F32)
    output = (hidden + out_sum + sbias).astype(BF).reshape(1, 2, blocks, D)
    expand_bias_grad = jnp.sum(pre_grad, axis=0)
    shrink_grad = t_dot(act_low, tangent_all).astype(BF)
    shrink_mine = lax.psum_scatter(shrink_grad, "ctx", scatter_dimension=0, tiled=True)
    shrink_owned = lax.all_gather(shrink_mine, "ctx", axis=0, tiled=True).astype(F32)
    expand_grad = t_dot(second_all, pre_low).astype(BF)
    expand_cols = lax.psum_scatter(expand_grad, "ctx", scatter_dimension=1, tiled=True)
    expand_rows = lax.all_to_all(expand_cols.reshape(planes, share, ff_part), "fsdp", 0, 1, tiled=False)
    expand_owned = (
        lax.all_gather(expand_rows, "ctx", axis=2, tiled=False).reshape(share, planes * ff_plane).astype(F32)
    )

    hidden_grad = tangent + norm_back(second_grad, gain2, normal2, inverse2)
    hidden_low = hidden_grad.astype(BF)
    att_grad = dot_t(hidden_low, merge_full).astype(BF)
    grad_pieces = lax.all_to_all(att_grad[:, :shared_at].reshape(2, blocks, ring, pc), "ctx", 2, 1, tiled=False)
    grad_p = heads_first(grad_pieces.reshape(length, pc))
    grad_s = heads_first(att_grad[:, shared_at:])
    dqp, dkp, dvp = attend_back(qp, kp, vp, allowed, top_p, total_p, grad_p)
    dqs, dks, dvs = attend_back(qs, ks, vs, own_allowed, top_s, total_s, grad_s)
    dqs_all = jnp.zeros((2, half, sc), F32)
    dqs_all = lax.dynamic_update_slice_in_dim(dqs_all, heads_last(dqs).reshape(2, blocks, sc), me * blocks, 1)
    mixed_grad = jnp.concatenate(
        [heads_last(dqp), dqs_all.reshape(length, sc)]
        + [heads_last(dkp), heads_last(dks), heads_last(dvp), heads_last(dvs)],
        axis=1,
    )
    bias_sums = jnp.sum(mixed_grad, axis=0)
    mixed_low = mixed_grad.astype(BF)
    first_part = dot_t(mixed_low, mixer_mine).astype(BF)
    first_grad = lax.psum_scatter(
        first_part.reshape(2, half, D), "ctx", scatter_dimension=1, tiled=True
    ).reshape(local_rows, D).astype(F32)
    input_grad = hidden_grad + norm_back(first_grad, gain1, normal1, inverse1)
    mixer_part_grad = t_dot(first_all, mixed_low).astype(BF)
    mixer_rows = lax.psum_scatter(mixer_part_grad, "fsdp", scatter_dimension=0, tiled=True)
    mixer_all = lax.all_gather(mixer_rows, "ctx", axis=0, tiled=False).astype(F32)

    def place_columns(values):
        mine = values[:, :, :pc].transpose(1, 0, 2).reshape(share, ring * pc)
        return [mine, jnp.sum(values[:, :, pc:], axis=0)]

    mixer_owned = jnp.concatenate(
        place_columns(mixer_all[:, :, :hc])
        + place_columns(mixer_all[:, :, hc : 2 * hc])
        + place_columns(mixer_all[:, :, 2 * hc :]),
        axis=1,
    )
    hidden_cols = lax.all_to_all(hidden_low.reshape(local_rows, ring, cols), "ctx", 1, 0, tiled=False)
    merge_grad = t_dot(attended_all, hidden_cols.reshape(length, cols)).astype(BF)
    merge_rows = lax.psum_scatter(merge_grad, "fsdp", scatter_dimension=0, tiled=True)
    merge_owned = lax.all_gather(merge_rows, "ctx", axis=1, tiled=True).astype(F32)

    def spread_bias(values):
        full = jnp.zeros((D,), F32)
        full = lax.dynamic_update_slice_in_dim(full, values[:pc], me * pc, 0)
        return full.at[shared_at:].set(values[pc:])

    sums = jnp.stack(
        [
            jnp.sum(first_grad * normal1, axis=0),
            jnp.sum(first_grad, axis=0),
            spread_bias(bias_sums[:hc]),
            spread_bias(bias_sums[2 * hc :]),
            jnp.sum(hidden_grad, axis=0),
            jnp.sum(second_grad * normal2, axis=0),
            jnp.sum(second_grad, axis=0),
            jnp.sum(tangent, axis=0),
        ]
    )
    sums = lax.psum(sums, ("fsdp", "ctx"))
    mine = lax.dynamic_slice_in_dim(sums, lax.axis_index("fsdp") * share, share, 1)
    expand_bias_owned = lax.psum(expand_bias_grad, "ctx")

    return (
        output,
        input_grad.reshape(1, 2, blocks, D),
        mine[0],
        mine[1],
        mixer_owned,
        mine[2],
        mine[3],
        merge_owned,
        mine[4],
        mine[5],
        mine[6],
        expand_owned,
        expand_bias_owned,
        shrink_owned,
        mine[7],
    )


def head_columns(weight, base):
    private, shared_at = 192, 1536
    mine = lax.dynamic_slice_in_dim(weight, base + lax.axis_index("ctx") * private, private, weight.ndim - 1)
    return jnp.concatenate([mine, weight[..., base + shared_at : base + D]], axis=-1)


def local_kernel(
    tokens,
    first_gain,
    first_shift,
    mixer_weight,
    query_bias,
    value_bias,
    merge_weight,
    merge_bias,
    second_gain,
    second_shift,
    expand_weight,
    expand_bias,
    shrink_weight,
    shrink_bias,
    cotangent,
):
    planes = lax.axis_size("fsdp")
    ring = lax.axis_size("ctx")
    me = lax.axis_index("ctx")
    plane = lax.axis_index("fsdp")
    blocks, half, length, local_rows = 64, 512, 1024, 128
    share = D // planes

    parts = [head_columns(mixer_weight, base) for base in (0, D, 2 * D)]
    m0 = jnp.concatenate([part[:, :128] for part in parts], axis=1)
    m1 = jnp.concatenate([part[:, 128:] for part in parts], axis=1)
    mg = jnp.concatenate([lax.dynamic_slice_in_dim(merge_weight, me * 48, 48, 0), merge_weight[384:]], axis=0)
    pieces = [lax.dynamic_slice_in_dim(expand_weight, 1600 * q + 200 * me, 200, 1) for q in range(4)]
    w1 = jnp.concatenate([jnp.pad(piece, ((0, 0), (0, 8))) for piece in pieces], axis=1)
    w2 = jnp.pad(lax.dynamic_slice_in_dim(shrink_weight, 200 * me, 200, 0), ((0, 8), (0, 0)))

    def spread(vector):
        return lax.dynamic_update_slice_in_dim(jnp.zeros((D,), BF), vector, plane * share, 0)

    def fill(vector):
        return jnp.pad(vector, (0, D - vector.shape[0]))

    bias1 = lax.dynamic_slice_in_dim(expand_bias, 200 * me, 200, 0)
    bias1 = lax.dynamic_update_slice_in_dim(jnp.zeros((D,), BF), bias1, plane * 208, 0)
    vpart = jnp.stack(
        [
            spread(first_gain),
            spread(first_shift),
            fill(head_columns(spread(query_bias), 0)),
            fill(head_columns(spread(value_bias), 0)),
            spread(merge_bias),
            spread(second_gain),
            spread(second_shift),
            spread(shrink_bias),
            bias1,
        ]
        + [jnp.zeros((D,), BF)] * 7
    )

    tok2, cot2 = tokens.reshape(local_rows, D), cotangent.reshape(local_rows, D)
    sgrad, hidden, dw1, dw2, dgb, qkv, attown, heads, vectors, lse, first_all, mws, mfull, act, w2_all, atts = run_forward(
        planes, tok2, cot2, vpart, m0, m1, mg, w1, w2
    )
    input_grad, out_own, va, vb, gw1, gw2, gm0, gm1, gmg = run_backward(
        planes, tok2, cot2, sgrad, hidden, vectors, attown, dgb, lse, qkv, heads, dw2,
        mfull.reshape(D, D), mws, first_all, dw1, act, w2_all, atts
    )
    shrink_owned = widen(gw2)
    expand_owned, mixer_owned, merge_owned = assemble(gw1, gm0, gm1, gmg)

    sums = jnp.sum(va, axis=0)
    lasts = jnp.sum(vb, axis=0)

    def head_vector(n):
        return jnp.concatenate([va[:, n, :192].reshape(1536), sums[n, 192:256]])

    def own(vector):
        return lax.dynamic_slice_in_dim(vector, plane * share, share, 0)

    bias1_all = va[:, 4, :832].reshape(8, 4, 208)[:, :, :200]
    expand_bias_owned = lax.dynamic_index_in_dim(bias1_all, plane, 1, keepdims=False).reshape(1600)

    return (
        out_own.reshape(1, 2, blocks, D),
        input_grad.reshape(1, 2, blocks, D),
        own(lasts[0]),
        own(lasts[1]),
        mixer_owned,
        own(head_vector(5)),
        own(head_vector(6)),
        merge_owned,
        own(sums[0]),
        own(sums[1]),
        own(sums[2]),
        expand_owned,
        expand_bias_owned,
        shrink_owned,
        own(sums[3]),
    )


def aligned(planes, ring, shape):
    return planes == 4 and ring == 8 and shape == (4, 2, 512, D)


def local(tokens, *others):
    planes, ring = lax.axis_size("fsdp"), lax.axis_size("ctx")
    whole = (tokens.shape[0] * planes, 2, tokens.shape[2] * ring, tokens.shape[3])
    if aligned(planes, ring, whole):
        return local_kernel(tokens, *others)
    return local_plain(tokens, *others)


def solution(mesh):
    token_spec = P("fsdp", None, "ctx", None)
    row = P("fsdp")
    matrix = P("fsdp", None)
    in_specs = (
        token_spec,
        row,
        row,
        matrix,
        row,
        row,
        matrix,
        row,
        row,
        row,
        matrix,
        row,
        matrix,
        row,
        token_spec,
    )
    out_specs = (
        token_spec,
        token_spec,
        row,
        row,
        matrix,
        row,
        row,
        matrix,
        row,
        row,
        row,
        matrix,
        row,
        matrix,
        row,
    )
    return jax.shard_map(local, mesh=mesh, in_specs=in_specs, out_specs=out_specs, check_vma=False)
```

```python
import functools

import jax
import jax.numpy as jnp
from jax import lax
from jax.experimental import pallas as pl
from jax.experimental.pallas import tpu as pltpu
from jax.sharding import PartitionSpec as P

D = 1600
H = 25
HD = 64

EPSILON = 1e-05
SCORE_SCALE = 0.125
BF = jnp.bfloat16
F32 = jnp.float32


def normalize(values):
    center = values - jnp.mean(values, axis=-1, keepdims=True)
    spread = jnp.mean(center * center, axis=-1, keepdims=True)
    inverse = lax.rsqrt(spread + EPSILON)
    return center * inverse, inverse


def norm_back(grad, gain, normal, inverse):
    scaled = grad * gain
    mean = jnp.mean(scaled, axis=-1, keepdims=True)
    along = jnp.mean(scaled * normal, axis=-1, keepdims=True)
    return inverse * (scaled - mean - normal * along)


def dot(a, b):
    return jnp.dot(a, b, preferred_element_type=F32)


def dot_t(a, b):
    return lax.dot_general(a, b, (((1,), (1,)), ((), ())), preferred_element_type=F32)


def t_dot(a, b):
    return lax.dot_general(a, b, (((0,), (0,)), ((), ())), preferred_element_type=F32)


def attend(query, key, value, allowed):
    scores = jnp.einsum("hqd,hkd->hqk", query, key, preferred_element_type=F32) * SCORE_SCALE
    scores = jnp.where(allowed[None], scores, -1e30)
    top = jnp.max(scores, axis=-1, keepdims=True)
    expo = jnp.exp(scores - top)
    total = jnp.sum(expo, axis=-1, keepdims=True)
    probs = (expo / total).astype(BF)
    return jnp.einsum("hqk,hkd->hqd", probs, value, preferred_element_type=F32), top, total


def attend_back(query, key, value, allowed, top, total, grad):
    scores = jnp.einsum("hqd,hkd->hqk", query, key, preferred_element_type=F32) * SCORE_SCALE
    scores = jnp.where(allowed[None], scores, -1e30)
    probs = jnp.exp(scores - top) / total
    probs_low = probs.astype(BF)
    prob_grad = jnp.einsum("hqd,hkd->hqk", grad, value, preferred_element_type=F32)
    offset = jnp.sum(prob_grad * probs, axis=-1, keepdims=True)
    score_grad = (probs * (prob_grad - offset)).astype(BF)
    dq = jnp.einsum("hqk,hkd->hqd", score_grad, key, preferred_element_type=F32) * SCORE_SCALE
    dk = jnp.einsum("hqk,hqd->hkd", score_grad, query, preferred_element_type=F32) * SCORE_SCALE
    dv = jnp.einsum("hqk,hqd->hkd", probs_low, grad, preferred_element_type=F32)
    return dq, dk, dv


def heads_first(values):
    rows, columns = values.shape
    return values.reshape(rows, columns // HD, HD).transpose(1, 0, 2)


def heads_last(values):
    heads, rows, _ = values.shape
    return values.transpose(1, 0, 2).reshape(rows, heads * HD)


MESH_ID = pl.DeviceIdType.MESH


def dyn(start, size, step):
    return pl.ds(pl.multiple_of(start, step), size)


class Links:

    def __init__(self, planes):
        self.planes = planes
        self.p = lax.axis_index("fsdp")
        self.me = lax.axis_index("ctx")

    def plane(self, step):
        return (self.p + step, self.me)

    def peer(self, mask):
        return (self.p, self.me ^ mask)

    def copy(self, src, dst, send, recv, device):
        return pltpu.make_async_remote_copy(
            src_ref=src, dst_ref=dst, send_sem=send, recv_sem=recv, device_id=device, device_id_type=MESH_ID
        )

    def barrier(self, masks):
        bar = pltpu.get_barrier_semaphore()
        for mask in masks:
            pl.semaphore_signal(bar, inc=1, device_id=self.peer(mask), device_id_type=MESH_ID)
        for d in range(1, self.planes):
            to = (lax.rem(self.p + d, self.planes), self.me)
            pl.semaphore_signal(bar, inc=1, device_id=to, device_id_type=MESH_ID)
        pl.semaphore_wait(bar, len(masks) + self.planes - 1)


class LineGather:

    def __init__(self, links, src, slot, sems, local_sem):
        self.links, self.src, self.slot, self.sems, self.local_sem = links, src, slot, sems, local_sem

    def send(self, src, block, step):
        way = 1 if step > 0 else 2
        return self.links.copy(
            src, self.slot(block), self.sems.at[way, block], self.sems.at[0, block], self.links.plane(step)
        )

    def arrival(self, block):
        return self.links.copy(
            self.slot(block), self.slot(block), self.sems.at[1, block], self.sems.at[0, block], self.links.plane(0)
        )

    def start(self):
        p, last = self.links.p, self.links.planes - 1

        @pl.when(p < last)
        def _():
            self.send(self.src, p, 1).start()

        @pl.when(p > 0)
        def _():
            self.send(self.src, p, -1).start()

        pltpu.make_async_copy(self.src, self.slot(p), self.local_sem).start()

    def pump(self, d):
        p, last = self.links.p, self.links.planes - 1

        @pl.when(p >= d)
        def _():
            self.arrival(p - d).wait_recv()

            @pl.when(p < last)
            def _():
                self.send(self.slot(p - d), p - d, 1).start()

        @pl.when(p + d <= last)
        def _():
            self.arrival(p + d).wait_recv()

            @pl.when(p > 0)
            def _():
                self.send(self.slot(p + d), p + d, -1).start()

        if d == 1:
            pltpu.make_async_copy(self.src, self.slot(p), self.local_sem).wait()

    def finish(self):
        p, last = self.links.p, self.links.planes - 1
        for d in range(self.links.planes):

            @pl.when((p >= d) & (p < last))
            def _():
                self.send(self.slot(p - d), p - d, 1).wait_send()

            @pl.when((p + d <= last) & (p > 0))
            def _():
                self.send(self.slot(p + d), p + d, -1).wait_send()


class LineExchange:

    def __init__(self, links, slots, send, recv):
        self.links, self.slots, self.send_sem, self.recv_sem = links, slots, send, recv

    def copy(self, src, d):
        planes = self.links.planes
        to = lax.rem(self.links.p + d, planes)
        return self.links.copy(src, self.slots.at[d - 1], self.send_sem.at[d - 1], self.recv_sem.at[d - 1], (to, self.links.me))

    def start(self, src):
        for d in range(1, self.links.planes):
            self.copy(src, d).start()

    def total(self, src):
        acc = src[...].astype(F32)
        for d in range(1, self.links.planes):
            self.copy(src, d).wait_recv()
            acc = acc + self.slots[d - 1].astype(F32)
        return acc

    def finish(self, src):
        for d in range(1, self.links.planes):
            self.copy(src, d).wait_send()


class SmallGather:

    def __init__(self, links, src, slot, send, recv, local_sem):
        self.links, self.src, self.slot, self.send_sem, self.recv_sem, self.local_sem = links, src, slot, send, recv, local_sem

    def copy(self, owner, mask, n):
        src = self.src if n < 4 else self.slot(owner)
        return self.links.copy(src, self.slot(owner), self.send_sem.at[n], self.recv_sem.at[owner, 0], self.links.peer(mask))

    def start(self):
        for n, mask in enumerate((2, 4, 6, 1)):
            self.copy(self.links.me, mask, n).start()
        pltpu.make_async_copy(self.src, self.slot(self.links.me), self.local_sem).start()

    def forward(self):
        for n, mask in enumerate((2, 4, 6)):
            owner = self.links.me ^ mask
            self.copy(owner, mask, 4 + n).wait_recv()
            self.copy(owner, 1, 4 + n).start()

    def wait(self):
        for mask in (1, 3, 5, 7):
            self.copy(self.links.me ^ mask, 1, 4).wait_recv()

    def finish(self):
        for n in range(7):
            self.copy(self.links.me, 1, n).wait_send()
        pltpu.make_async_copy(self.src, self.slot(self.links.me), self.local_sem).wait()


class GroupGather:

    def __init__(self, links, part, send, recv, src=None, local_sem=None):
        self.links, self.part, self.send_sem, self.recv_sem = links, part, send, recv
        self.src, self.local_sem = src, local_sem

    def copy(self, owner, h, mask, n, src=None):
        return self.links.copy(
            self.part(owner, h) if src is None else src,
            self.part(owner, h),
            self.send_sem.at[n],
            self.recv_sem.at[owner, h],
            self.links.peer(mask),
        )

    def own(self, n):
        h, mask = ((1, 2), (0, 4), (0, 2), (1, 4), (0, 1), (1, 1))[n]
        return self.copy(self.links.me, h, mask, n, None if self.src is None else self.src(h))

    def stay(self, h):
        return pltpu.make_async_copy(self.src(h), self.part(self.links.me, h), self.local_sem.at[h])

    def start(self):
        for n in range(6):
            self.own(n).start()
        if self.src is not None:
            for h in range(2):
                self.stay(h).start()

    def pass_on(self, mask, h, n):
        owner = self.links.me ^ mask
        self.copy(owner, h, 1, n).wait_recv()
        if n < 8:
            self.copy(owner, h, 6 - mask, n).start()
        self.copy(owner, h, 1, n + 2).start()

    def forward(self):
        self.pass_on(2, 1, 6)
        self.pass_on(4, 0, 7)
        self.pass_on(2, 0, 8)
        self.pass_on(4, 1, 9)

    def forward_last(self):
        self.pass_on(6, 0, 10)
        self.pass_on(6, 1, 11)

    def wait(self):
        self.forward_last()
        for mask in (1, 3, 5, 7):
            for h in range(2):
                self.copy(self.links.me ^ mask, h, 1, 6).wait_recv()
        if self.src is not None:
            for h in range(2):
                self.stay(h).wait()

    def finish(self):
        me = self.links.me
        for n in range(6):
            self.own(n).wait_send()
        self.copy(me ^ 2, 1, 1, 6).wait_send()
        self.copy(me ^ 4, 0, 1, 7).wait_send()
        for mask, h, n in ((2, 1, 8), (4, 0, 9), (2, 0, 10), (4, 1, 11), (6, 0, 12), (6, 1, 13)):
            self.copy(me ^ mask, h, 1, n).wait_send()


def row_parts(ref, cut):
    rows = ref.shape[-2]
    return lambda j, h: ref.at[j, 0:cut] if h == 0 else ref.at[j, cut:rows]


def own_parts(ref, cut):
    rows = ref.shape[-2]
    return lambda h: ref.at[0:cut] if h == 0 else ref.at[cut:rows]


class GroupSum:

    def __init__(self, links, stage, from_twin, from_far, send, twin_recv, far_recv):
        self.links, self.stage, self.from_twin, self.from_far = links, stage, from_twin, from_far
        self.send, self.twin_recv, self.far_recv = send, twin_recv, far_recv
        self.rows = stage.shape[1] // 2

    def to_twin(self, chip):
        return self.links.copy(
            self.stage.at[4 + chip], self.from_twin.at[chip], self.send.at[4 + chip], self.twin_recv.at[chip], self.links.peer(1)
        )

    def to_far(self, chip, h, mask):
        at = pl.ds(h * self.rows, self.rows)
        n = 2 * (chip - 1) + h
        return self.links.copy(
            self.stage.at[chip, at], self.from_far.at[chip - 1, at], self.send.at[8 + n], self.far_recv.at[n], self.links.peer(mask)
        )

    def run(self, block):
        me = self.links.me
        masks = (0, 2, 4, 6)
        for chip in (3, 1, 2, 0):
            self.stage[4 + chip] = block(me ^ masks[chip] ^ 1).astype(BF)
            self.to_twin(chip).start()
        for chip in (3, 1, 2):
            part = block(me ^ masks[chip])
            self.to_twin(chip).wait_recv()
            self.stage[chip] = (part + self.from_twin[chip].astype(F32)).astype(BF)
            if chip == 3:
                self.to_far(3, 0, 2).start()
                self.to_far(3, 1, 4).start()
            elif chip == 1:
                self.to_far(1, 0, 2).start()
            else:
                self.to_far(2, 1, 4).start()
        self.stage[0] = block(me).astype(BF)

    def relay(self):
        half = self.rows
        for chip, h, mask in ((2, 0, 4), (1, 1, 2)):
            at = slice(h * half, h * half + half)
            self.to_far(3, h, mask).wait_recv()
            self.stage[chip, at] = (self.stage[chip, at].astype(F32) + self.from_far[2, at].astype(F32)).astype(BF)
            self.to_far(chip, h, mask).start()

    def total(self):
        self.to_twin(0).wait_recv()
        acc = self.stage[0].astype(F32) + self.from_twin[0].astype(F32)
        for chip, mask in ((1, 2), (2, 4)):
            for h in range(2):
                self.to_far(chip, h, mask).wait_recv()
            acc += self.from_far[chip - 1].astype(F32)
        return acc

    def finish(self):
        for chip in range(4):
            self.to_twin(chip).wait_send()
        for chip, h, mask in ((3, 0, 2), (3, 1, 4), (1, 0, 2), (1, 1, 2), (2, 0, 4), (2, 1, 4)):
            self.to_far(chip, h, mask).wait_send()


def gelu_parts(u):
    inner = 0.7978845608 * (u + 0.044715 * (u * u * u))
    t = jnp.tanh(inner)
    value = 0.5 * u * (1.0 + t)
    slope = 0.5 * (1.0 + t) + 0.5 * u * (1.0 - t * t) * (0.7978845608 * (1.0 + 3 * 0.044715 * (u * u)))
    return value, slope


BLOCK_KEYS = (
    ((0, 256, 1),),
    ((0, 256, 0), (256, 256, 1)),
    ((0, 512, 0), (512, 256, 2), (768, 256, 0)),
    ((0, 512, 0), (768, 256, 2)),
)


def triangle(kind, shape):
    r = lax.broadcasted_iota(jnp.int32, shape, 0)
    c = lax.broadcasted_iota(jnp.int32, shape, 1)
    return c <= r if kind == 1 else c >= r


def half_mask(half):
    lane = lax.broadcasted_iota(jnp.int32, (1, 128), 1)
    return (lane // 64) == half


def softmax_pieces(q, keys, values, pieces, allowed):
    scores = []
    for start, size, kind in pieces:
        s = dot_t(q, keys[start : start + size])
        if kind:
            s = jnp.where(allowed(kind, start, s.shape), s, -1e30)
        scores.append(s)
    top = jnp.max(scores[0], axis=1, keepdims=True)
    for s in scores[1:]:
        top = jnp.maximum(top, jnp.max(s, axis=1, keepdims=True))
    total, out = 0.0, 0.0
    for s, (start, size, _) in zip(scores, pieces):
        e = jnp.exp(s - top)
        total = total + jnp.sum(e, axis=1, keepdims=True)
        out = out + dot(e.astype(BF), values[start : start + size])
    return out * (1.0 / total), top + jnp.log(total)


def attend_kernel(planes, tok, cot, vpart, m0, m1, mg, w1,
                  hidden_o, qkv_o, att_o, heads_o, vec_o, lse_o,
                  first_o, mw_o, mfull_o, w1_o, sec_o, g_o,
                  vec, mw0, mw1, mgs, mfull, first_all, second, arecv,
                  zs, zl, v_s, v_r, gs, gr, gl, gl2, a_s, a_r, os):
    L = Links(planes)
    qkv, attown, hid, lse, att = qkv_o, att_o, hidden_o, lse_o, heads_o
    p, me = L.p, L.me
    share = 400
    xv = LineExchange(L, vec, v_s, v_r)
    zm0 = LineGather(L, m0, lambda b: mw0.at[dyn(b * share, share, 16)], zs.at[1], zl.at[1])
    zm1 = LineGather(L, m1, lambda b: mw1.at[dyn(b * share, share, 16)], zs.at[2], zl.at[2])
    zmg = LineGather(L, mg, lambda b: mgs.at[b], zs.at[3], zl.at[3])
    zw1 = LineGather(L, w1, lambda b: w1_o.at[dyn(b * share, share, 16)], zs.at[4], zl.at[4])
    gfirst = GroupGather(L, lambda j, h: first_all.at[h, j], gs.at[0], gr.at[0])
    gsec = GroupGather(L, row_parts(sec_o, 64), gs.at[1], gr.at[1], own_parts(second, 64), gl)
    gg = GroupGather(L, row_parts(g_o, 64), gs.at[3], gr.at[3], own_parts(cot, 64), gl2)
    gmerge = GroupGather(L, lambda j, h: mfull.at[2 * h : 2 * h + 2, dyn(j * 48, 48, 16)], gs.at[2], gr.at[2])

    L.barrier((1, 2, 3, 4, 5, 6, 7))
    xv.start(vpart)
    zm0.start()
    rows = tok[...].astype(F32)
    normal, _ = normalize(rows)
    vectors = xv.total(vpart)
    first = (normal * vectors[0:1] + vectors[1:2]).astype(BF)
    first_all[:, me] = first.reshape(2, 64, D)
    gfirst.start()
    zm0.pump(1)
    zm0.pump(2)
    zmg.start()
    gfirst.forward()
    zm0.pump(3)
    zmg.pump(1)
    gfirst.wait()
    zmg.pump(2)
    zm1.start()

    def mix(weights, pair):
        bias_q = vectors[2:3, pair * 128 : pair * 128 + 128]
        bias_v = vectors[3:4, pair * 128 : pair * 128 + 128]

        def body(b, _):
            x = first_all[b // 2, pl.ds((b % 2) * 4, 4)].reshape(256, D)
            mixed = dot(x, weights[...])
            at = dyn(b * 256, 256, 256)
            qkv[pair, at] = (mixed[:, :128] + bias_q).astype(BF)
            qkv[2 + pair, at] = mixed[:, 128:256].astype(BF)
            qkv[4 + pair, at] = (mixed[:, 256:] + bias_v).astype(BF)
            return 0

        lax.fori_loop(0, 4, body, 0)

    lane = lax.broadcasted_iota(jnp.int32, (1, 128), 1)

    def note_lse(head, at, value):
        lse[at] = jnp.where(lane == head, value, lse[at] if head else 0.0)

    def attend_private(pair, half):
        mask = half_mask(half)
        for b in range(4):
            q = jnp.where(mask, qkv[pair, b * 256 : b * 256 + 256], 0) * jnp.asarray(0.125, BF)
            out, l = softmax_pieces(
                q, qkv.at[2 + pair], qkv.at[4 + pair], BLOCK_KEYS[b], lambda kind, start, shape: triangle(kind, shape)
            )
            out = jnp.where(mask, out, 0.0).astype(BF).reshape(4, 64, 128)
            at = pl.ds((b % 2) * 4, 4)
            if half == 0:
                att[pair, b // 2, at] = out
            else:
                att[pair, b // 2, at] = att[pair, b // 2, at] + out
            note_lse(2 * pair + half, slice(b * 256, b * 256 + 256), l)

    def own_allowed(kind, start, shape):
        r = lax.broadcasted_iota(jnp.int32, shape, 0)
        c = lax.broadcasted_iota(jnp.int32, shape, 1)
        rp = jnp.where(r < 64, me * 64 + r, 1023 - (me * 64 + r - 64))
        cp = jnp.where(c < 512, c, 1023 - (c - 512))
        return cp <= rp

    mix(mw0, 0)
    zmg.pump(3)
    for b in range(4):
        mfull[b, dyn(me * 48, 48, 16)] = mgs[b, 0:48]
        mfull[b, 384:400] = mgs[b, 48:64]
    gmerge.start()
    attend_private(0, 0)
    zm1.pump(1)
    attend_private(0, 1)
    zm1.pump(2)
    zw1.start()
    gmerge.forward()
    gg.start()
    zm1.pump(3)
    mix(mw1, 1)
    outs = [
        pltpu.make_async_copy(first_all, first_o, os.at[0]),
        pltpu.make_async_copy(mw0, mw_o.at[0], os.at[1]),
        pltpu.make_async_copy(mw1, mw_o.at[1], os.at[2]),
        pltpu.make_async_copy(mfull, mfull_o, os.at[3]),
    ]
    for c in outs[:3]:
        c.start()
    attend_private(1, 0)
    qs = jnp.concatenate([qkv[1, dyn(me * 64, 64, 64)], qkv[1, dyn(512 + me * 64, 64, 64)]], axis=0)
    mask1 = half_mask(1)
    qs = jnp.where(mask1, qs, 0) * jnp.asarray(0.125, BF)
    out_s, l_s = softmax_pieces(qs, qkv.at[3], qkv.at[5], ((0, 1024, 1),), own_allowed)
    note_lse(3, slice(0, 128), l_s)
    shared_low = jnp.where(mask1, out_s, 0.0).astype(BF)

    def exchange(mask):
        return L.copy(att.at[:, :, me ^ mask], arecv.at[me], a_s.at[mask], a_r.at[me], L.peer(mask))

    def arrived(mask):
        return L.copy(att.at[:, :, me], arecv.at[me ^ mask], a_s.at[mask], a_r.at[me ^ mask], L.peer(mask))

    for mask in range(1, 8):
        exchange(mask).start()
    arecv[me] = att[:, :, me]
    gg.forward()
    for mask in range(1, 8):
        arrived(mask).wait_recv()
    for j in range(8):
        attown[:, 192 * j : 192 * j + 128] = arecv[j, 0].reshape(128, 128)
        attown[:, 192 * j + 128 : 192 * j + 192] = arecv[j, 1].reshape(128, 128)[:, :64]
    attown[:, 1536:1600] = shared_low[:, 64:128]
    gmerge.wait()
    hidden = rows + vectors[4:5]
    hid[...] = hidden
    for b in range(4):
        hid[...] += dot(attown[:, b * 400 : b * 400 + 400], mfull[b])
    normal2, _ = normalize(hid[...])
    second[...] = (normal2 * vectors[5:6] + vectors[6:7]).astype(BF)
    gsec.start()
    outs[3].start()
    vec_o[...] = vectors
    zw1.pump(1)
    gg.wait()
    gsec.forward()
    zw1.pump(2)
    gsec.wait()
    zw1.pump(3)
    for c in outs:
        c.wait()
    xv.finish(vpart)
    for z in (zm0, zm1, zmg, zw1):
        z.finish()
    for g in (gfirst, gg, gsec, gmerge):
        g.finish()
    for mask in range(1, 8):
        exchange(mask).wait_send()


def run_attend(planes, tok, cot, vpart, m0, m1, mg, w1):
    any_ = pl.BlockSpec(memory_space=pl.ANY)
    vm = pl.BlockSpec(memory_space=pltpu.VMEM)
    S = jax.ShapeDtypeStruct
    V = pltpu.VMEM
    dma = pltpu.SemaphoreType.DMA
    return pl.pallas_call(
        functools.partial(attend_kernel, planes),
        out_shape=(
            S((128, D), F32), S((6, 1024, 128), BF), S((128, D), BF), S((2, 2, 8, 64, 128), BF), S((16, D), F32), S((1024, 128), F32),
            S((2, 8, 64, D), BF), S((2, D, 384), BF), S((4, 400, D), BF), S((D, 832), BF),
            S((8, 128, D), BF), S((8, 128, D), BF),
        ),
        in_specs=[vm] * 3 + [any_] * 4,
        out_specs=(vm,) * 6 + (any_,) * 6,
        scratch_shapes=[
            V((3, 16, D), BF), V((D, 384), BF), V((D, 384), BF), V((4, 64, D), BF), V((4, 400, D), BF),
            V((2, 8, 64, D), BF), V((128, D), BF), V((8, 2, 2, 64, 128), BF),
            dma((5, 3, 4)), dma((5,)), dma((3,)), dma((3,)), dma((4, 14)), dma((4, 8, 2)), dma((2,)), dma((2,)),
            dma((8,)), dma((8,)), dma((4,)),
        ],
        compiler_params=pltpu.CompilerParams(collective_id=0, has_side_effects=True, vmem_limit_bytes=60 << 20),
        cost_estimate=pl.CostEstimate(flops=6_000_000_000, bytes_accessed=60_000_000, transcendentals=4_000_000),
    )(tok, cot, vpart, m0, m1, mg, w1)


class LineSum:

    def __init__(self, links, block, slots, send, recv, near=None, near_sem=None):
        self.links, self.block, self.slots, self.send_sem, self.recv_sem = links, block, slots, send, recv
        self.near, self.near_sem = near, near_sem
        self.last = links.planes - 1

    def send(self, t, step):
        slot = t - 1 if step > 0 else self.last + t
        return self.links.copy(
            self.block(t), self.slots.at[slot], self.send_sem.at[t], self.recv_sem.at[slot], self.links.plane(step)
        )

    def arrival(self, slot):
        return self.links.copy(
            self.slots.at[slot], self.slots.at[slot], self.send_sem.at[0], self.recv_sem.at[slot], self.links.plane(0)
        )

    def start(self):
        @pl.when(self.links.p == 0)
        def _():
            for t in range(self.last, 0, -1):
                self.send(t, 1).start()

        @pl.when(self.links.p == self.last)
        def _():
            for t in range(self.last):
                self.send(t, -1).start()

    def add(self, t, slot):
        self.arrival(slot).wait_recv()
        ref = self.block(t)
        came = self.slots.at[slot]
        if self.near is not None:
            copy = pltpu.make_async_copy(came, self.near, self.near_sem)
            copy.start()
            copy.wait()
            came = self.near
        ref[...] = (ref[...].astype(F32) + came[...].astype(F32)).astype(BF)

    def pump(self, u):
        p, last = self.links.p, self.last
        for t in range(1, last + 1):
            at = u - last + t
            if 0 < at < t:

                @pl.when(p == at)
                def _():
                    self.add(t, t - 1)
                    self.send(t, 1).start()

                @pl.when(p == last - at)
                def _():
                    self.add(last - t, 2 * last - t)
                    self.send(last - t, -1).start()

    def total(self):
        p, last = self.links.p, self.last

        @pl.when(p > 0)
        def _():
            self.add(p, p - 1)

        @pl.when(p < last)
        def _():
            self.add(p, last + p)

    def finish(self):
        p = self.links.p
        for t in range(self.last + 1):

            @pl.when(p < t)
            def _():
                self.send(t, 1).wait_send()

            @pl.when(p > t)
            def _():
                self.send(t, -1).wait_send()


def backward_kernel(planes, tok, cot, hid, vectors, attown, lse, qkv, att,
                    w2, w1_h, sec_h, g_h, mfull_h, mw_h, first_h,
                    igrad_o, out_o, va_o, vb_o, gw1_o, gw2_o, gm0_o, gm1_o, gmg_o, atts_o, slot_mg,
                    mfull, mw, sec_all, g_all, w1b, w2b, act, slope, dw1, dw2, hlow, agrad, asend, gatt, hc, dkv, mgr, dmerge,
                    slot_w1, slot_w2, slot_m0, slot_m1, near_mg, stage, twin, far, va, vb, vslot,
                    zs, zl, ld, ls_s, ls_r, ve_s, ve_r, gs, gr, gl, a_s, a_r, h_s, h_r, rs_s, rs_t, rs_f, free):
    L = Links(planes)
    p, me = L.p, L.me
    loads = [
        pltpu.make_async_copy(w1_h, w1b, ld.at[0]),
        pltpu.make_async_copy(sec_h, sec_all, ld.at[1]),
        pltpu.make_async_copy(g_h, g_all, ld.at[7]),
        pltpu.make_async_copy(mfull_h, mfull, ld.at[2]),
        pltpu.make_async_copy(mw_h, mw, ld.at[3]),
    ]
    att_all, first_all = g_all, sec_all
    late_att = pltpu.make_async_copy(atts_o, att_all, ld.at[5])
    late_first = pltpu.make_async_copy(first_h, first_all, ld.at[6])
    for c in loads:
        c.start()
    zw2 = LineGather(L, w2, lambda b: w2b.at[dyn(b * 208, 208, 16)], zs, zl)
    lw2 = LineSum(L, lambda t: dw2.at[dyn(t * 208, 208, 16)], slot_w2, ls_s.at[0], ls_r.at[0])
    lw1 = LineSum(L, lambda t: dw1.at[dyn(t * 400, 400, 16)], slot_w1, ls_s.at[1], ls_r.at[1])
    lm0 = LineSum(L, lambda t: w1b.at[dyn(t * 400, 400, 16), 0:384], slot_m0, ls_s.at[2], ls_r.at[2])
    lm1 = LineSum(L, lambda t: w1b.at[dyn(t * 400, 400, 16), 384:768], slot_m1, ls_s.at[3], ls_r.at[3])
    lmg = LineSum(L, lambda t: dmerge.at[dyn(t * 400, 400, 16)], slot_mg, ls_s.at[4], ls_r.at[4], near_mg, ld.at[4])
    xa = LineExchange(L, vslot.at[0], ve_s.at[0], ve_r.at[0])
    xb = LineExchange(L, vslot.at[1], ve_s.at[1], ve_r.at[1])
    gatt_all = GroupGather(L, row_parts(atts_o, 64), gs.at[1], gr.at[1], own_parts(attown, 64), gl.at[1])
    gw2 = GroupGather(L, row_parts(gw2_o, 112), gs.at[2], gr.at[2], lambda h: dw2.at[dyn(p * 208 + 112 * h, (112, 96)[h], 16)], gl.at[2])

    def share_gather(n, out, line):
        def src(h):
            base, columns = line.home
            return base.at[dyn(p * 400 + 208 * h, (208, 192)[h], 16), columns[0] : columns[1]]

        return GroupGather(L, row_parts(out, 208), gs.at[n], gr.at[n], src, gl.at[n])

    lw1.home, lm0.home, lm1.home, lmg.home = (dw1, (0, 832)), (w1b, (0, 384)), (w1b, (384, 768)), (dmerge, (0, 256))
    gw1 = share_gather(3, gw1_o, lw1)
    gm0 = share_gather(4, gm0_o, lm0)
    gm1 = share_gather(5, gm1_o, lm1)
    gmg = share_gather(6, gmg_o, lmg)
    gva = SmallGather(L, va, lambda j: va_o.at[j], gs.at[7], gr.at[7], gl.at[7, 0])
    gvb = SmallGather(L, vb, lambda j: vb_o.at[j], gs.at[8], gr.at[8], gl.at[8, 0])
    L.barrier((1, 2, 3, 4, 5, 6, 7))
    zw2.start()
    gatt_all.start()

    loads[0].wait()
    loads[1].wait()

    def expand(b, _):
        at = dyn(b * 256, 256, 256)
        pre = dot(sec_all[pl.ds(2 * b, 2)].reshape(256, D), w1b[...]) + vectors[8:9, :832]
        value, s = gelu_parts(pre)
        act[at] = value.astype(BF)
        slope[at] = s.astype(BF)
        return 0

    lax.fori_loop(0, 4, expand, 0)
    loads[2].wait()
    g2 = g_all[...].reshape(1024, D)
    for start, size in ((0, 256), (256, 256), (512, 256), (768, 64)):
        dw2[start : start + size] = t_dot(act[:, start : start + size], g2).astype(BF)
    lw2.start()
    zw2.pump(1)
    gatt_all.forward()
    lw2.pump(1)
    zw2.pump(2)
    gatt_all.wait()
    zw2.pump(3)

    def contract(b, acc):
        at = dyn(b * 256, 256, 256)
        grad = dot_t(g_all[pl.ds(2 * b, 2)].reshape(256, D), w2b[...]) * slope[at].astype(F32)
        slope[at] = grad.astype(BF)
        return acc + jnp.sum(grad, axis=0, keepdims=True)

    dgb = lax.fori_loop(0, 4, contract, jnp.zeros((1, 832), F32))
    late_att.start()
    rounds = [GroupSum(L, stage, twin, far, rs_s.at[n], rs_t.at[n], rs_f.at[n]) for n in range(3)]

    def release(n):
        for mask in (1, 2, 4):
            pl.semaphore_signal(free.at[n], inc=1, device_id=L.peer(mask), device_id_type=MESH_ID)

    for start in range(0, D, 256):
        size = min(256, D - start)
        x = sec_all[:, :, start : start + size].reshape(1024, size)
        dw1[start : start + size] = t_dot(x, slope[...]).astype(BF)
    late_first.start()
    lw2.pump(2)
    lw1.start()
    back = rounds[0]
    back.run(lambda owner: dot_t(slope[dyn(owner * 128, 128, 128)], w1b[...]))
    back.relay()
    grad2 = back.total()
    back.finish()
    release(0)

    tangent = cot[...].astype(F32)
    normal2, inverse2 = normalize(hid[...])
    hidden_grad = tangent + norm_back(grad2, vectors[5:6], normal2, inverse2)
    igrad_o[...] = hidden_grad
    hlow[:, 0:D] = hidden_grad.astype(BF)
    hlow[:, D:2048] = jnp.zeros((128, 2048 - D), BF)
    va[0:1] = jnp.sum(hidden_grad, axis=0, keepdims=True)
    va[1:2] = jnp.sum(grad2 * normal2, axis=0, keepdims=True)
    va[2:3] = jnp.sum(grad2, axis=0, keepdims=True)
    va[3:4] = jnp.sum(tangent, axis=0, keepdims=True)
    va[4:8] = jnp.zeros((4, D), F32)
    va[4:5, 0:832] = dgb

    def columns(mask):
        to = me ^ mask
        return L.copy(hlow.at[:, dyn(to * 256, 256, 256)], hc.at[me], h_s.at[mask], h_r.at[me], L.peer(mask))

    def columns_in(mask):
        return L.copy(hc.at[me], hc.at[me ^ mask], h_s.at[mask], h_r.at[me ^ mask], L.peer(mask))

    loads[3].wait()
    agrad[...] = dot_t(hlow[:, 0:D], mfull[...]).astype(BF)
    for j in range(8):
        asend[j, 0] = agrad[:, 192 * j : 192 * j + 128].reshape(2, 64, 128)
        tail = agrad[:, 192 * j + 128 : 192 * j + 192]
        asend[j, 1] = jnp.concatenate([tail, jnp.zeros((128, 64), BF)], axis=1).reshape(2, 64, 128)

    def exchange(mask):
        return L.copy(asend.at[me ^ mask], gatt.at[:, :, me], a_s.at[mask], a_r.at[me], L.peer(mask))

    def arrived(mask):
        return L.copy(asend.at[me], gatt.at[:, :, me ^ mask], a_s.at[mask], a_r.at[me ^ mask], L.peer(mask))

    for mask in range(1, 8):
        exchange(mask).start()
    gatt[:, :, me] = asend[me]
    for mask in range(1, 8):
        columns(mask).start()
    lw2.total()
    pl.semaphore_wait(free.at[0], 3)
    outs = rounds[1]
    outs.run(lambda owner: dot(act[dyn(owner * 128, 128, 128)], w2b[...]))
    hc[me] = hlow[:, dyn(me * 256, 256, 256)]
    dkv[...] = jnp.zeros(dkv.shape, F32)
    lw1.pump(1)
    for mask in range(1, 8):
        arrived(mask).wait_recv()

    scale = jnp.asarray(0.125, BF)

    def head_back(pair, head, mask, q, g, o, stat, pieces, allowed):
        delta = jnp.sum(g.astype(F32) * o.astype(F32), axis=1, keepdims=True)
        dq = 0.0
        for start, size, kind in pieces:
            keys = qkv[2 + pair, start : start + size]
            s = dot_t(q, keys)
            if kind:
                s = jnp.where(allowed(kind, start, s.shape), s, -1e30)
            prob = jnp.exp(s - stat)
            ds = (prob * (dot_t(g, qkv[4 + pair, start : start + size]) - delta)).astype(BF)
            dq = dq + dot(ds, keys)
            dkv[0, start : start + size] += t_dot(ds, q)
            dkv[1, start : start + size] += t_dot(prob.astype(BF), g)
        return jnp.where(mask, dq, 0.0) * 0.125

    def private_back(pair, half):
        mask = half_mask(half)
        head = 2 * pair + half
        total = 0.0
        for b in range(4):
            at = slice(b * 256, b * 256 + 256)
            blk = (pair, b // 2, pl.ds((b % 2) * 4, 4))
            q = jnp.where(mask, qkv[pair, at], 0) * scale
            g = jnp.where(mask, gatt[blk].reshape(256, 128), 0)
            o = att[blk].reshape(256, 128)
            dq = head_back(
                pair, head, mask, q, g, o, lse[at, head : head + 1], BLOCK_KEYS[b],
                lambda kind, start, shape: triangle(kind, shape),
            )
            total = total + jnp.sum(dq, axis=0, keepdims=True)
            if half == 0:
                mgr[pair, at, 0:128] = dq.astype(BF)
            else:
                mgr[pair, at, 0:128] = mgr[pair, at, 0:128] + dq.astype(BF)
        return total

    def mixer_part(pair):
        mgr[pair, :, 128:256] = dkv[0].astype(BF)
        mgr[pair, :, 256:384] = dkv[1].astype(BF)
        va[6:7, pair * 128 : pair * 128 + 128] = jnp.sum(dkv[1], axis=0, keepdims=True)
        for start in range(0, D, 256):
            size = min(256, D - start)
            x = first_all[:, :, start : start + size].reshape(1024, size)
            w1b[start : start + size, 384 * pair : 384 * pair + 384] = t_dot(x, mgr[pair]).astype(BF)

    qb0 = private_back(0, 0)
    outs.relay()
    gw2.start()
    qb0 = qb0 + private_back(0, 1)
    va[5:6, 0:128] = qb0
    late_first.wait()
    mixer_part(0)
    dkv[...] = jnp.zeros(dkv.shape, F32)
    lm0.start()
    lw1.pump(2)
    qb1 = private_back(1, 0)
    mask1 = half_mask(1)
    own_early, own_late = dyn(me * 64, 64, 64), dyn(512 + me * 64, 64, 64)
    qs = jnp.concatenate([qkv[1, own_early], qkv[1, own_late]], axis=0)
    qs = jnp.where(mask1, qs, 0) * scale
    blank = jnp.zeros((128, 64), BF)
    g_s = jnp.concatenate([blank, agrad[:, 1536:1600]], axis=1)
    o_s = jnp.concatenate([blank, attown[:, 1536:1600]], axis=1)

    def own_allowed(kind, start, shape):
        r = lax.broadcasted_iota(jnp.int32, shape, 0)
        c = lax.broadcasted_iota(jnp.int32, shape, 1) + start
        rp = jnp.where(r < 64, me * 64 + r, 1023 - (me * 64 + r - 64))
        cp = jnp.where(c < 512, c, 1023 - (c - 512))
        return cp <= rp

    dqs = head_back(1, 3, mask1, qs, g_s, o_s, lse[0:128, 3:4], ((0, 512, 1), (512, 512, 1)), own_allowed)
    va[5:6, 128:256] = qb1 + jnp.sum(dqs, axis=0, keepdims=True)
    dqs_low = dqs.astype(BF)
    mgr[1, own_early, 0:128] = mgr[1, own_early, 0:128] + dqs_low[:64]
    mgr[1, own_late, 0:128] = mgr[1, own_late, 0:128] + dqs_low[64:]
    mixer_part(1)
    lm1.start()
    xa.start(va)
    out_o[...] = (outs.total() + hid[...] + vectors[7:8]).astype(BF)
    outs.finish()
    release(1)
    loads[4].wait()
    pl.semaphore_wait(free.at[1], 3)
    sums = rounds[2]

    def first_block(owner):
        early, late = dyn(owner * 64, 64, 64), dyn(512 + owner * 64, 64, 64)
        x0 = jnp.concatenate([mgr[0, early], mgr[0, late]], axis=0)
        x1 = jnp.concatenate([mgr[1, early], mgr[1, late]], axis=0)
        return dot_t(x0, mw[0]) + dot_t(x1, mw[1])

    sums.run(first_block)
    gw2.forward()
    sums.relay()
    lw1.total()
    gw1.start()
    lm0.pump(1)
    late_att.wait()
    for mask in range(1, 8):
        columns_in(mask).wait_recv()
    h2 = hc[...].reshape(1024, 256)
    for start in range(0, D, 256):
        size = min(256, D - start)
        x = att_all[:, :, start : start + size].reshape(1024, size)
        dmerge[start : start + size] = t_dot(x, h2).astype(BF)
    lmg.start()
    lm0.pump(2)
    first_grad = sums.total()
    rows = tok[...].astype(F32)
    normal1, inverse1 = normalize(rows)
    igrad_o[...] += norm_back(first_grad, vectors[0:1], normal1, inverse1)
    vb[0:1] = jnp.sum(first_grad * normal1, axis=0, keepdims=True)
    vb[1:2] = jnp.sum(first_grad, axis=0, keepdims=True)
    vb[2:8] = jnp.zeros((6, D), F32)
    xb.start(vb)
    total_a = xa.total(va)
    xa.finish(va)
    va[...] = total_a
    gva.start()
    lm0.total()
    gm0.start()
    lm1.pump(1)
    gw1.forward()
    gva.forward()
    lm1.pump(2)
    total_b = xb.total(vb)
    xb.finish(vb)
    vb[...] = total_b
    gvb.start()
    gm0.forward()
    lmg.pump(1)
    lm1.total()
    gm1.start()
    lmg.pump(2)
    gvb.forward()
    lmg.total()
    gmg.start()
    gm1.forward()
    gmg.forward()
    for g in (gw2, gva, gw1, gvb, gm0, gm1, gmg):
        g.wait()
    for g in (gatt_all, gw2, gw1, gm0, gm1, gmg, gva, gvb):
        g.finish()
    zw2.finish()
    for s in (lw2, lw1, lm0, lm1, lmg):
        s.finish()
    for mask in range(1, 8):
        exchange(mask).wait_send()
        columns(mask).wait_send()
    sums.finish()


def run_backward(planes, *operands):
    any_ = pl.BlockSpec(memory_space=pl.ANY)
    vm = pl.BlockSpec(memory_space=pltpu.VMEM)
    S = jax.ShapeDtypeStruct
    V = pltpu.VMEM
    dma = pltpu.SemaphoreType.DMA
    return pl.pallas_call(
        functools.partial(backward_kernel, planes),
        out_shape=(
            S((128, D), F32), S((128, D), BF), S((8, 8, D), F32), S((8, 8, D), F32), S((8, 400, 832), BF), S((8, 208, D), BF),
            S((8, 400, 384), BF), S((8, 400, 384), BF), S((8, 400, 256), BF), S((8, 128, D), BF),
            S((6, 400, 256), BF),
        ),
        in_specs=[vm] * 8 + [any_] * 7,
        out_specs=(vm,) * 2 + (any_,) * 9,
        scratch_shapes=[
            V((D, D), BF), V((2, D, 384), BF), V((8, 128, D), BF), V((8, 128, D), BF), V((D, 832), BF), V((832, D), BF),
            V((1024, 832), BF), V((1024, 832), BF), V((D, 832), BF), V((832, D), BF),
            V((128, 2048), BF), V((128, D), BF), V((8, 2, 2, 64, 128), BF), V((2, 2, 8, 64, 128), BF),
            V((8, 128, 256), BF), V((2, 1024, 128), F32), V((2, 1024, 384), BF), V((D, 256), BF),
            V((6, 400, 832), BF), V((6, 208, D), BF), V((6, 400, 384), BF), V((6, 400, 384), BF), V((400, 256), BF),
            V((8, 128, D), BF), V((4, 128, D), BF), V((3, 128, D), BF), V((8, D), F32), V((8, D), F32), V((2, 3, 8, D), F32),
            dma((3, 4)), dma(()), dma((8,)), dma((5, 4)), dma((5, 6)), dma((2, 3)), dma((2, 3)), dma((9, 14)), dma((9, 8, 2)), dma((9, 2)),
            dma((8,)), dma((8,)), dma((8,)), dma((8,)), dma((3, 14)), dma((3, 4)), dma((3, 6)), pltpu.SemaphoreType.REGULAR((2,)),
        ],
        compiler_params=pltpu.CompilerParams(collective_id=1, has_side_effects=True, vmem_limit_bytes=(64 << 20) - 65536),
        cost_estimate=pl.CostEstimate(flops=25_000_000_000, bytes_accessed=60_000_000, transcendentals=4_000_000),
    )(*operands)


def assemble_kernel(gw1, gm0, gm1, gmg, expand_o, mixer_o, merge_o):
    for j in range(8):
        for q in range(4):
            expand_o[:, 1600 * q + 200 * j : 1600 * q + 200 * j + 200] = gw1[j, :, 208 * q : 208 * q + 200].astype(F32)
        for n in range(3):
            at = D * n + 192 * j
            mixer_o[:, at : at + 128] = gm0[j, :, 128 * n : 128 * n + 128].astype(F32)
            mixer_o[:, at + 128 : at + 192] = gm1[j, :, 128 * n : 128 * n + 64].astype(F32)
    for n in range(3):
        total = gm1[0, :, 128 * n : 128 * n + 128].astype(F32)
        for j in range(1, 8):
            total += gm1[j, :, 128 * n : 128 * n + 128].astype(F32)
        mixer_o[:, D * n + 1536 : D * n + 1600] = total[:, 64:]
    for j in range(6):
        merge_o[:, 256 * j : 256 * j + 256] = gmg[j].astype(F32)
    merge_o[:, 1536:1600] = gmg[6, :, :64].astype(F32)


def assemble(gw1, gm0, gm1, gmg):
    rows = 80

    def part(width):
        return pl.BlockSpec((8, rows, width), lambda n: (0, n, 0))

    def whole(width):
        return pl.BlockSpec((rows, width), lambda n: (n, 0))

    S = jax.ShapeDtypeStruct
    return pl.pallas_call(
        assemble_kernel,
        grid=(400 // rows,),
        in_specs=[part(832), part(384), part(384), part(256)],
        out_specs=(whole(6400), whole(4800), whole(D)),
        out_shape=(S((400, 6400), F32), S((400, 4800), F32), S((400, D), F32)),
        compiler_params=pltpu.CompilerParams(vmem_limit_bytes=40 << 20),
    )(gw1, gm0, gm1, gmg)


def widen_kernel(x, o):
    o[...] = x[0, :200].astype(F32)


def widen(gw2):
    return pl.pallas_call(
        widen_kernel,
        grid=(8,),
        in_specs=[pl.BlockSpec((1, 208, D), lambda n: (n, 0, 0))],
        out_specs=pl.BlockSpec((200, D), lambda n: (n, 0)),
        out_shape=jax.ShapeDtypeStruct((1600, D), F32),
        compiler_params=pltpu.CompilerParams(vmem_limit_bytes=40 << 20),
    )(gw2)


def local_plain(
    tokens,
    first_gain,
    first_shift,
    mixer_weight,
    query_bias,
    value_bias,
    merge_weight,
    merge_bias,
    second_gain,
    second_shift,
    expand_weight,
    expand_bias,
    shrink_weight,
    shrink_bias,
    cotangent,
):
    planes = lax.axis_size("fsdp")
    ring = lax.axis_size("ctx")
    me = lax.axis_index("ctx")
    blocks = tokens.shape[2]
    local_rows = 2 * blocks
    half = blocks * ring
    length = 2 * half
    private = H // ring
    shared = H - private * ring
    pc, sc = private * HD, shared * HD
    hc = pc + sc
    shared_at = private * ring * HD
    share = D // planes
    ff_plane = expand_bias.shape[0]
    ff_part = ff_plane // ring
    cols = D // ring

    vectors = jnp.stack(
        [first_gain, first_shift, query_bias, value_bias, merge_bias, second_gain, second_shift, shrink_bias]
    )
    vectors = lax.all_gather(vectors, "fsdp", axis=1, tiled=True).astype(F32)
    gain1, shift1, qbias, vbias, mbias, gain2, shift2, sbias = [vectors[n] for n in range(8)]

    def head_columns(weight, base):
        mine = lax.dynamic_slice_in_dim(weight, base + me * pc, pc, weight.ndim - 1)
        every = weight[..., base + shared_at : base + D]
        return [mine, every]

    mixer_part = jnp.concatenate(
        head_columns(mixer_weight, 0) + head_columns(mixer_weight, D) + head_columns(mixer_weight, 2 * D), axis=1
    )
    mixer_mine = lax.all_gather(mixer_part, "fsdp", axis=0, tiled=True)

    merge_part = lax.dynamic_slice_in_dim(merge_weight, me * cols, cols, 1)
    merge_cols = lax.all_gather(merge_part, "fsdp", axis=0, tiled=True)
    merge_full = lax.all_gather(merge_cols, "ctx", axis=1, tiled=True)

    expand_part = expand_weight.reshape(share, planes, ring, ff_part)
    expand_part = lax.dynamic_index_in_dim(expand_part, me, 2, keepdims=False)
    expand_part = lax.all_to_all(expand_part, "fsdp", 1, 0, tiled=False).reshape(D, ff_part)
    expand_mine = lax.all_gather(expand_part, "ctx", axis=1, tiled=True)

    rows = tokens.reshape(local_rows, D).astype(F32)
    normal1, inverse1 = normalize(rows)
    first = (normal1 * gain1 + shift1).astype(BF)
    first_all = lax.all_gather(first.reshape(2, blocks, D), "ctx", axis=1, tiled=True).reshape(length, D)
    tangent_low = cotangent.reshape(local_rows, D)
    tangent = tangent_low.astype(F32)
    tangent_all = lax.all_gather(tangent_low, "fsdp", axis=0, tiled=True)

    mixed = dot(first_all, mixer_mine)
    qb = jnp.concatenate(head_columns(qbias, 0), axis=0)
    vb = jnp.concatenate(head_columns(vbias, 0), axis=0)
    query = (mixed[:, :hc] + qb).astype(BF)
    key = mixed[:, hc : 2 * hc].astype(BF)
    value = (mixed[:, 2 * hc :] + vb).astype(BF)
    half_index = jnp.arange(half, dtype=jnp.int32)
    place = jnp.concatenate([half_index, length - 1 - half_index])
    early = me * blocks + jnp.arange(blocks, dtype=jnp.int32)
    own_place = jnp.concatenate([early, length - 1 - early])
    allowed = place[None, :] <= place[:, None]
    own_allowed = place[None, :] <= own_place[:, None]

    def own_rows(values):
        parts = values.reshape(2, half, values.shape[1])
        return lax.dynamic_slice_in_dim(parts, me * blocks, blocks, 1).reshape(local_rows, values.shape[1])

    qp, kp, vp = heads_first(query[:, :pc]), heads_first(key[:, :pc]), heads_first(value[:, :pc])
    qs, ks, vs = heads_first(own_rows(query[:, pc:])), heads_first(key[:, pc:]), heads_first(value[:, pc:])
    out_p, top_p, total_p = attend(qp, kp, vp, allowed)
    out_s, top_s, total_s = attend(qs, ks, vs, own_allowed)
    att_heads = heads_last(out_p).astype(BF)
    att_pieces = lax.all_to_all(att_heads.reshape(2, ring, blocks, pc), "ctx", 1, 2, tiled=False)
    attended = jnp.concatenate(
        [att_pieces.reshape(local_rows, ring * pc), heads_last(out_s).astype(BF)], axis=1
    )
    hidden = rows + dot(attended, merge_full) + mbias
    normal2, inverse2 = normalize(hidden)
    second = (normal2 * gain2 + shift2).astype(BF)
    second_all = lax.all_gather(second, "fsdp", axis=0, tiled=True)
    attended_all = lax.all_gather(attended, "ctx", axis=0, tiled=True)

    pre = dot(second_all, expand_mine) + expand_bias.astype(F32)
    act, gate_pull = jax.vjp(lambda u: jax.nn.gelu(u, approximate=True), pre)
    act_low = act.astype(BF)
    act_grad = dot_t(tangent_all, shrink_weight)
    (pre_grad,) = gate_pull(act_grad)
    pre_low = pre_grad.astype(BF)
    second_part = dot_t(pre_low, expand_mine).astype(BF)
    second_grad = lax.psum_scatter(second_part, "fsdp", scatter_dimension=0, tiled=True).astype(F32)
    out_part = dot(act_low, shrink_weight).astype(BF)
    out_sum = lax.psum_scatter(out_part, "fsdp", scatter_dimension=0, tiled=True).astype(F32)
    output = (hidden + out_sum + sbias).astype(BF).reshape(1, 2, blocks, D)
    expand_bias_grad = jnp.sum(pre_grad, axis=0)
    shrink_grad = t_dot(act_low, tangent_all).astype(BF)
    shrink_mine = lax.psum_scatter(shrink_grad, "ctx", scatter_dimension=0, tiled=True)
    shrink_owned = lax.all_gather(shrink_mine, "ctx", axis=0, tiled=True).astype(F32)
    expand_grad = t_dot(second_all, pre_low).astype(BF)
    expand_cols = lax.psum_scatter(expand_grad, "ctx", scatter_dimension=1, tiled=True)
    expand_rows = lax.all_to_all(expand_cols.reshape(planes, share, ff_part), "fsdp", 0, 1, tiled=False)
    expand_owned = (
        lax.all_gather(expand_rows, "ctx", axis=2, tiled=False).reshape(share, planes * ff_plane).astype(F32)
    )

    hidden_grad = tangent + norm_back(second_grad, gain2, normal2, inverse2)
    hidden_low = hidden_grad.astype(BF)
    att_grad = dot_t(hidden_low, merge_full).astype(BF)
    grad_pieces = lax.all_to_all(att_grad[:, :shared_at].reshape(2, blocks, ring, pc), "ctx", 2, 1, tiled=False)
    grad_p = heads_first(grad_pieces.reshape(length, pc))
    grad_s = heads_first(att_grad[:, shared_at:])
    dqp, dkp, dvp = attend_back(qp, kp, vp, allowed, top_p, total_p, grad_p)
    dqs, dks, dvs = attend_back(qs, ks, vs, own_allowed, top_s, total_s, grad_s)
    dqs_all = jnp.zeros((2, half, sc), F32)
    dqs_all = lax.dynamic_update_slice_in_dim(dqs_all, heads_last(dqs).reshape(2, blocks, sc), me * blocks, 1)
    mixed_grad = jnp.concatenate(
        [heads_last(dqp), dqs_all.reshape(length, sc)]
        + [heads_last(dkp), heads_last(dks), heads_last(dvp), heads_last(dvs)],
        axis=1,
    )
    bias_sums = jnp.sum(mixed_grad, axis=0)
    mixed_low = mixed_grad.astype(BF)
    first_part = dot_t(mixed_low, mixer_mine).astype(BF)
    first_grad = lax.psum_scatter(
        first_part.reshape(2, half, D), "ctx", scatter_dimension=1, tiled=True
    ).reshape(local_rows, D).astype(F32)
    input_grad = hidden_grad + norm_back(first_grad, gain1, normal1, inverse1)
    mixer_part_grad = t_dot(first_all, mixed_low).astype(BF)
    mixer_rows = lax.psum_scatter(mixer_part_grad, "fsdp", scatter_dimension=0, tiled=True)
    mixer_all = lax.all_gather(mixer_rows, "ctx", axis=0, tiled=False).astype(F32)

    def place_columns(values):
        mine = values[:, :, :pc].transpose(1, 0, 2).reshape(share, ring * pc)
        return [mine, jnp.sum(values[:, :, pc:], axis=0)]

    mixer_owned = jnp.concatenate(
        place_columns(mixer_all[:, :, :hc])
        + place_columns(mixer_all[:, :, hc : 2 * hc])
        + place_columns(mixer_all[:, :, 2 * hc :]),
        axis=1,
    )
    hidden_cols = lax.all_to_all(hidden_low.reshape(local_rows, ring, cols), "ctx", 1, 0, tiled=False)
    merge_grad = t_dot(attended_all, hidden_cols.reshape(length, cols)).astype(BF)
    merge_rows = lax.psum_scatter(merge_grad, "fsdp", scatter_dimension=0, tiled=True)
    merge_owned = lax.all_gather(merge_rows, "ctx", axis=1, tiled=True).astype(F32)

    def spread_bias(values):
        full = jnp.zeros((D,), F32)
        full = lax.dynamic_update_slice_in_dim(full, values[:pc], me * pc, 0)
        return full.at[shared_at:].set(values[pc:])

    sums = jnp.stack(
        [
            jnp.sum(first_grad * normal1, axis=0),
            jnp.sum(first_grad, axis=0),
            spread_bias(bias_sums[:hc]),
            spread_bias(bias_sums[2 * hc :]),
            jnp.sum(hidden_grad, axis=0),
            jnp.sum(second_grad * normal2, axis=0),
            jnp.sum(second_grad, axis=0),
            jnp.sum(tangent, axis=0),
        ]
    )
    sums = lax.psum(sums, ("fsdp", "ctx"))
    mine = lax.dynamic_slice_in_dim(sums, lax.axis_index("fsdp") * share, share, 1)
    expand_bias_owned = lax.psum(expand_bias_grad, "ctx")

    return (
        output,
        input_grad.reshape(1, 2, blocks, D),
        mine[0],
        mine[1],
        mixer_owned,
        mine[2],
        mine[3],
        merge_owned,
        mine[4],
        mine[5],
        mine[6],
        expand_owned,
        expand_bias_owned,
        shrink_owned,
        mine[7],
    )


def head_columns(weight, base):
    private, shared_at = 192, 1536
    mine = lax.dynamic_slice_in_dim(weight, base + lax.axis_index("ctx") * private, private, weight.ndim - 1)
    return jnp.concatenate([mine, weight[..., base + shared_at : base + D]], axis=-1)


def local_kernel(
    tokens,
    first_gain,
    first_shift,
    mixer_weight,
    query_bias,
    value_bias,
    merge_weight,
    merge_bias,
    second_gain,
    second_shift,
    expand_weight,
    expand_bias,
    shrink_weight,
    shrink_bias,
    cotangent,
):
    planes = lax.axis_size("fsdp")
    ring = lax.axis_size("ctx")
    me = lax.axis_index("ctx")
    plane = lax.axis_index("fsdp")
    blocks, half, length, local_rows = 64, 512, 1024, 128
    share = D // planes

    parts = [head_columns(mixer_weight, base) for base in (0, D, 2 * D)]
    m0 = jnp.concatenate([part[:, :128] for part in parts], axis=1)
    m1 = jnp.concatenate([part[:, 128:] for part in parts], axis=1)
    mg = jnp.concatenate([lax.dynamic_slice_in_dim(merge_weight, me * 48, 48, 0), merge_weight[384:]], axis=0)
    pieces = [lax.dynamic_slice_in_dim(expand_weight, 1600 * q + 200 * me, 200, 1) for q in range(4)]
    w1 = jnp.concatenate([jnp.pad(piece, ((0, 0), (0, 8))) for piece in pieces], axis=1)
    w2 = jnp.pad(lax.dynamic_slice_in_dim(shrink_weight, 200 * me, 200, 0), ((0, 8), (0, 0)))

    def spread(vector):
        return lax.dynamic_update_slice_in_dim(jnp.zeros((D,), BF), vector, plane * share, 0)

    def fill(vector):
        return jnp.pad(vector, (0, D - vector.shape[0]))

    bias1 = lax.dynamic_slice_in_dim(expand_bias, 200 * me, 200, 0)
    bias1 = lax.dynamic_update_slice_in_dim(jnp.zeros((D,), BF), bias1, plane * 208, 0)
    vpart = jnp.stack(
        [
            spread(first_gain),
            spread(first_shift),
            fill(head_columns(spread(query_bias), 0)),
            fill(head_columns(spread(value_bias), 0)),
            spread(merge_bias),
            spread(second_gain),
            spread(second_shift),
            spread(shrink_bias),
            bias1,
        ]
        + [jnp.zeros((D,), BF)] * 7
    )

    tok2, cot2 = tokens.reshape(local_rows, D), cotangent.reshape(local_rows, D)
    hidden, qkv, attown, heads, vectors, lse, first_all, mws, mfull, w1_all, sec_all, g_all = run_attend(
        planes, tok2, cot2, vpart, m0, m1, mg, w1
    )
    input_grad, out_own, va, vb, gw1, gw2, gm0, gm1, gmg, _, _ = run_backward(
        planes, tok2, cot2, hidden, vectors, attown, lse, qkv, heads,
        w2, w1_all, sec_all, g_all, mfull.reshape(D, D), mws, first_all.reshape(8, 128, D)
    )
    shrink_owned = widen(gw2)
    expand_owned, mixer_owned, merge_owned = assemble(gw1, gm0, gm1, gmg)

    sums = jnp.sum(va, axis=0)
    lasts = jnp.sum(vb, axis=0)

    def head_vector(n):
        return jnp.concatenate([va[:, n, :192].reshape(1536), sums[n, 192:256]])

    def own(vector):
        return lax.dynamic_slice_in_dim(vector, plane * share, share, 0)

    bias1_all = va[:, 4, :832].reshape(8, 4, 208)[:, :, :200]
    expand_bias_owned = lax.dynamic_index_in_dim(bias1_all, plane, 1, keepdims=False).reshape(1600)

    return (
        out_own.reshape(1, 2, blocks, D),
        input_grad.reshape(1, 2, blocks, D),
        own(lasts[0]),
        own(lasts[1]),
        mixer_owned,
        own(head_vector(5)),
        own(head_vector(6)),
        merge_owned,
        own(sums[0]),
        own(sums[1]),
        own(sums[2]),
        expand_owned,
        expand_bias_owned,
        shrink_owned,
        own(sums[3]),
    )


def aligned(planes, ring, shape):
    return planes == 4 and ring == 8 and shape == (4, 2, 512, D)


def local(tokens, *others):
    planes, ring = lax.axis_size("fsdp"), lax.axis_size("ctx")
    whole = (tokens.shape[0] * planes, 2, tokens.shape[2] * ring, tokens.shape[3])
    if aligned(planes, ring, whole):
        return local_kernel(tokens, *others)
    return local_plain(tokens, *others)


def solution(mesh):
    token_spec = P("fsdp", None, "ctx", None)
    row = P("fsdp")
    matrix = P("fsdp", None)
    in_specs = (
        token_spec,
        row,
        row,
        matrix,
        row,
        row,
        matrix,
        row,
        row,
        row,
        matrix,
        row,
        matrix,
        row,
        token_spec,
    )
    out_specs = (
        token_spec,
        token_spec,
        row,
        row,
        matrix,
        row,
        row,
        matrix,
        row,
        row,
        row,
        matrix,
        row,
        matrix,
        row,
    )
    return jax.shard_map(local, mesh=mesh, in_specs=in_specs, out_specs=out_specs, check_vma=False)
```

```python
import functools

import jax
import jax.numpy as jnp
from jax import lax
from jax.experimental import pallas as pl
from jax.experimental.pallas import tpu as pltpu
from jax.sharding import PartitionSpec as P

D = 1600
H = 25
HD = 64

EPSILON = 1e-05
SCORE_SCALE = 0.125
BF = jnp.bfloat16
F32 = jnp.float32


def normalize(values):
    center = values - jnp.mean(values, axis=-1, keepdims=True)
    spread = jnp.mean(center * center, axis=-1, keepdims=True)
    inverse = lax.rsqrt(spread + EPSILON)
    return center * inverse, inverse


def norm_back(grad, gain, normal, inverse):
    scaled = grad * gain
    mean = jnp.mean(scaled, axis=-1, keepdims=True)
    along = jnp.mean(scaled * normal, axis=-1, keepdims=True)
    return inverse * (scaled - mean - normal * along)


def dot(a, b):
    return jnp.dot(a, b, preferred_element_type=F32)


def dot_t(a, b):
    return lax.dot_general(a, b, (((1,), (1,)), ((), ())), preferred_element_type=F32)


def t_dot(a, b):
    return lax.dot_general(a, b, (((0,), (0,)), ((), ())), preferred_element_type=F32)


def attend(query, key, value, allowed):
    scores = jnp.einsum("hqd,hkd->hqk", query, key, preferred_element_type=F32) * SCORE_SCALE
    scores = jnp.where(allowed[None], scores, -1e30)
    top = jnp.max(scores, axis=-1, keepdims=True)
    expo = jnp.exp(scores - top)
    total = jnp.sum(expo, axis=-1, keepdims=True)
    probs = (expo / total).astype(BF)
    return jnp.einsum("hqk,hkd->hqd", probs, value, preferred_element_type=F32), top, total


def attend_back(query, key, value, allowed, top, total, grad):
    scores = jnp.einsum("hqd,hkd->hqk", query, key, preferred_element_type=F32) * SCORE_SCALE
    scores = jnp.where(allowed[None], scores, -1e30)
    probs = jnp.exp(scores - top) / total
    probs_low = probs.astype(BF)
    prob_grad = jnp.einsum("hqd,hkd->hqk", grad, value, preferred_element_type=F32)
    offset = jnp.sum(prob_grad * probs, axis=-1, keepdims=True)
    score_grad = (probs * (prob_grad - offset)).astype(BF)
    dq = jnp.einsum("hqk,hkd->hqd", score_grad, key, preferred_element_type=F32) * SCORE_SCALE
    dk = jnp.einsum("hqk,hqd->hkd", score_grad, query, preferred_element_type=F32) * SCORE_SCALE
    dv = jnp.einsum("hqk,hqd->hkd", probs_low, grad, preferred_element_type=F32)
    return dq, dk, dv


def heads_first(values):
    rows, columns = values.shape
    return values.reshape(rows, columns // HD, HD).transpose(1, 0, 2)


def heads_last(values):
    heads, rows, _ = values.shape
    return values.transpose(1, 0, 2).reshape(rows, heads * HD)


MESH_ID = pl.DeviceIdType.MESH


def dyn(start, size, step):
    return pl.ds(pl.multiple_of(start, step), size)


class Links:

    def __init__(self, planes):
        self.planes = planes
        self.p = lax.axis_index("fsdp")
        self.me = lax.axis_index("ctx")

    def plane(self, step):
        return (self.p + step, self.me)

    def peer(self, mask):
        return (self.p, self.me ^ mask)

    def copy(self, src, dst, send, recv, device):
        return pltpu.make_async_remote_copy(
            src_ref=src, dst_ref=dst, send_sem=send, recv_sem=recv, device_id=device, device_id_type=MESH_ID
        )

    def barrier(self, masks):
        bar = pltpu.get_barrier_semaphore()
        for mask in masks:
            pl.semaphore_signal(bar, inc=1, device_id=self.peer(mask), device_id_type=MESH_ID)
        for d in range(1, self.planes):
            to = (lax.rem(self.p + d, self.planes), self.me)
            pl.semaphore_signal(bar, inc=1, device_id=to, device_id_type=MESH_ID)
        pl.semaphore_wait(bar, len(masks) + self.planes - 1)


class LineGather:

    def __init__(self, links, src, slot, sems, local_sem):
        self.links, self.slot, self.sems, self.local_sem = links, slot, sems, local_sem
        self.stays = src is None
        self.src = slot(links.p) if src is None else src

    def send(self, src, block, step):
        way = 1 if step > 0 else 2
        return self.links.copy(
            src, self.slot(block), self.sems.at[way, block], self.sems.at[0, block], self.links.plane(step)
        )

    def arrival(self, block):
        return self.links.copy(
            self.slot(block), self.slot(block), self.sems.at[1, block], self.sems.at[0, block], self.links.plane(0)
        )

    def start(self):
        p, last = self.links.p, self.links.planes - 1

        @pl.when(p < last)
        def _():
            self.send(self.src, p, 1).start()

        @pl.when(p > 0)
        def _():
            self.send(self.src, p, -1).start()

        if not self.stays:
            pltpu.make_async_copy(self.src, self.slot(p), self.local_sem).start()

    def pump(self, d):
        p, last = self.links.p, self.links.planes - 1

        @pl.when(p >= d)
        def _():
            self.arrival(p - d).wait_recv()

            @pl.when(p < last)
            def _():
                self.send(self.slot(p - d), p - d, 1).start()

        @pl.when(p + d <= last)
        def _():
            self.arrival(p + d).wait_recv()

            @pl.when(p > 0)
            def _():
                self.send(self.slot(p + d), p + d, -1).start()

        if d == 1 and not self.stays:
            pltpu.make_async_copy(self.src, self.slot(p), self.local_sem).wait()

    def finish(self):
        p, last = self.links.p, self.links.planes - 1
        for d in range(self.links.planes):

            @pl.when((p >= d) & (p < last))
            def _():
                self.send(self.slot(p - d), p - d, 1).wait_send()

            @pl.when((p + d <= last) & (p > 0))
            def _():
                self.send(self.slot(p + d), p + d, -1).wait_send()


class LineExchange:

    def __init__(self, links, slots, send, recv):
        self.links, self.slots, self.send_sem, self.recv_sem = links, slots, send, recv

    def copy(self, src, d):
        planes = self.links.planes
        to = lax.rem(self.links.p + d, planes)
        return self.links.copy(src, self.slots.at[d - 1], self.send_sem.at[d - 1], self.recv_sem.at[d - 1], (to, self.links.me))

    def start(self, src):
        for d in range(1, self.links.planes):
            self.copy(src, d).start()

    def total(self, src):
        acc = src[...].astype(F32)
        for d in range(1, self.links.planes):
            self.copy(src, d).wait_recv()
            acc = acc + self.slots[d - 1].astype(F32)
        return acc

    def finish(self, src):
        for d in range(1, self.links.planes):
            self.copy(src, d).wait_send()


class SmallGather:

    def __init__(self, links, src, slot, send, recv, local_sem):
        self.links, self.src, self.slot, self.send_sem, self.recv_sem, self.local_sem = links, src, slot, send, recv, local_sem

    def copy(self, owner, mask, n):
        src = self.src if n < 4 else self.slot(owner)
        return self.links.copy(src, self.slot(owner), self.send_sem.at[n], self.recv_sem.at[owner, 0], self.links.peer(mask))

    def start(self):
        for n, mask in enumerate((2, 4, 6, 1)):
            self.copy(self.links.me, mask, n).start()
        pltpu.make_async_copy(self.src, self.slot(self.links.me), self.local_sem).start()

    def forward(self):
        for n, mask in enumerate((2, 4, 6)):
            owner = self.links.me ^ mask
            self.copy(owner, mask, 4 + n).wait_recv()
            self.copy(owner, 1, 4 + n).start()

    def wait(self):
        for mask in (1, 3, 5, 7):
            self.copy(self.links.me ^ mask, 1, 4).wait_recv()

    def finish(self):
        for n in range(7):
            self.copy(self.links.me, 1, n).wait_send()
        pltpu.make_async_copy(self.src, self.slot(self.links.me), self.local_sem).wait()


class GroupGather:

    def __init__(self, links, part, send, recv, src=None, local_sem=None):
        self.links, self.part, self.send_sem, self.recv_sem = links, part, send, recv
        self.src, self.local_sem = src, local_sem

    def copy(self, owner, h, mask, n, src=None):
        return self.links.copy(
            self.part(owner, h) if src is None else src,
            self.part(owner, h),
            self.send_sem.at[n],
            self.recv_sem.at[owner, h],
            self.links.peer(mask),
        )

    def own(self, n):
        h, mask = ((1, 2), (0, 4), (0, 2), (1, 4), (0, 1), (1, 1))[n]
        return self.copy(self.links.me, h, mask, n, None if self.src is None else self.src(h))

    def stay(self, h):
        return pltpu.make_async_copy(self.src(h), self.part(self.links.me, h), self.local_sem.at[h])

    def start(self):
        for n in range(6):
            self.own(n).start()
        if self.src is not None:
            for h in range(2):
                self.stay(h).start()

    def pass_on(self, mask, h, n):
        owner = self.links.me ^ mask
        self.copy(owner, h, 1, n).wait_recv()
        if n < 8:
            self.copy(owner, h, 6 - mask, n).start()
        self.copy(owner, h, 1, n + 2).start()

    def forward(self):
        self.pass_on(2, 1, 6)
        self.pass_on(4, 0, 7)
        self.pass_on(2, 0, 8)
        self.pass_on(4, 1, 9)

    def forward_last(self):
        self.pass_on(6, 0, 10)
        self.pass_on(6, 1, 11)

    def wait(self):
        self.forward_last()
        for mask in (1, 3, 5, 7):
            for h in range(2):
                self.copy(self.links.me ^ mask, h, 1, 6).wait_recv()
        if self.src is not None:
            for h in range(2):
                self.stay(h).wait()

    def finish(self):
        me = self.links.me
        for n in range(6):
            self.own(n).wait_send()
        self.copy(me ^ 2, 1, 1, 6).wait_send()
        self.copy(me ^ 4, 0, 1, 7).wait_send()
        for mask, h, n in ((2, 1, 8), (4, 0, 9), (2, 0, 10), (4, 1, 11), (6, 0, 12), (6, 1, 13)):
            self.copy(me ^ mask, h, 1, n).wait_send()


def row_parts(ref, cut):
    rows = ref.shape[-2]
    return lambda j, h: ref.at[j, 0:cut] if h == 0 else ref.at[j, cut:rows]


def own_parts(ref, cut):
    rows = ref.shape[-2]
    return lambda h: ref.at[0:cut] if h == 0 else ref.at[cut:rows]


class GroupSum:

    def __init__(self, links, stage, from_twin, from_far, send, twin_recv, far_recv):
        self.links, self.stage, self.from_twin, self.from_far = links, stage, from_twin, from_far
        self.send, self.twin_recv, self.far_recv = send, twin_recv, far_recv
        self.rows = stage.shape[1] // 2

    def to_twin(self, chip):
        return self.links.copy(
            self.stage.at[4 + chip], self.from_twin.at[chip], self.send.at[4 + chip], self.twin_recv.at[chip], self.links.peer(1)
        )

    def to_far(self, chip, h, mask):
        at = pl.ds(h * self.rows, self.rows)
        n = 2 * (chip - 1) + h
        return self.links.copy(
            self.stage.at[chip, at], self.from_far.at[chip - 1, at], self.send.at[8 + n], self.far_recv.at[n], self.links.peer(mask)
        )

    def run(self, block):
        me = self.links.me
        masks = (0, 2, 4, 6)
        for chip in (3, 1, 2, 0):
            self.stage[4 + chip] = block(me ^ masks[chip] ^ 1).astype(BF)
            self.to_twin(chip).start()
        for chip in (3, 1, 2):
            part = block(me ^ masks[chip])
            self.to_twin(chip).wait_recv()
            self.stage[chip] = (part + self.from_twin[chip].astype(F32)).astype(BF)
            if chip == 3:
                self.to_far(3, 0, 2).start()
                self.to_far(3, 1, 4).start()
            elif chip == 1:
                self.to_far(1, 0, 2).start()
            else:
                self.to_far(2, 1, 4).start()
        self.stage[0] = block(me).astype(BF)

    def relay(self):
        half = self.rows
        for chip, h, mask in ((2, 0, 4), (1, 1, 2)):
            at = slice(h * half, h * half + half)
            self.to_far(3, h, mask).wait_recv()
            self.stage[chip, at] = (self.stage[chip, at].astype(F32) + self.from_far[2, at].astype(F32)).astype(BF)
            self.to_far(chip, h, mask).start()

    def total(self):
        self.to_twin(0).wait_recv()
        acc = self.stage[0].astype(F32) + self.from_twin[0].astype(F32)
        for chip, mask in ((1, 2), (2, 4)):
            for h in range(2):
                self.to_far(chip, h, mask).wait_recv()
            acc += self.from_far[chip - 1].astype(F32)
        return acc

    def finish(self):
        for chip in range(4):
            self.to_twin(chip).wait_send()
        for chip, h, mask in ((3, 0, 2), (3, 1, 4), (1, 0, 2), (1, 1, 2), (2, 0, 4), (2, 1, 4)):
            self.to_far(chip, h, mask).wait_send()


def gelu_parts(u):
    inner = 0.7978845608 * (u + 0.044715 * (u * u * u))
    t = jnp.tanh(inner)
    value = 0.5 * u * (1.0 + t)
    slope = 0.5 * (1.0 + t) + 0.5 * u * (1.0 - t * t) * (0.7978845608 * (1.0 + 3 * 0.044715 * (u * u)))
    return value, slope


BLOCK_KEYS = (
    ((0, 256, 1),),
    ((0, 256, 0), (256, 256, 1)),
    ((0, 512, 0), (512, 256, 2), (768, 256, 0)),
    ((0, 512, 0), (768, 256, 2)),
)


def triangle(kind, shape):
    r = lax.broadcasted_iota(jnp.int32, shape, 0)
    c = lax.broadcasted_iota(jnp.int32, shape, 1)
    return c <= r if kind == 1 else c >= r


def half_mask(half):
    lane = lax.broadcasted_iota(jnp.int32, (1, 128), 1)
    return (lane // 64) == half


def softmax_pieces(q, keys, values, pieces, allowed):
    scores = []
    for start, size, kind in pieces:
        s = dot_t(q, keys[start : start + size])
        if kind:
            s = jnp.where(allowed(kind, start, s.shape), s, -1e30)
        scores.append(s)
    top = jnp.max(scores[0], axis=1, keepdims=True)
    for s in scores[1:]:
        top = jnp.maximum(top, jnp.max(s, axis=1, keepdims=True))
    total, out = 0.0, 0.0
    for s, (start, size, _) in zip(scores, pieces):
        e = jnp.exp(s - top)
        total = total + jnp.sum(e, axis=1, keepdims=True)
        out = out + dot(e.astype(BF), values[start : start + size])
    return out * (1.0 / total), top + jnp.log(total)


def shift_left(values, lanes):
    return pltpu.roll(values, lax.rem(values.shape[1] - lanes, values.shape[1]), 1)


def small_vectors(parts, p, me):
    wide = 1664
    values = [part[...].astype(F32).reshape(1, part.shape[0]) for part in parts]
    rows = jnp.concatenate([jnp.concatenate(values[:8], axis=0), jnp.zeros((8, wide - 400), F32)], axis=1)
    rows = pltpu.roll(rows, 400 * p, 1)
    mine = shift_left(rows, 192 * me)
    heads = jnp.concatenate([mine[:, :192], rows[:, 1536:1600], jnp.zeros((8, wide - 256), F32)], axis=1)
    n = lax.broadcasted_iota(jnp.int32, (8, 1), 0)
    rows = jnp.where((n == 2) | (n == 3), heads, rows)
    bias = jnp.concatenate([values[8], jnp.zeros((1, wide - 1600), F32)], axis=1)
    bias = shift_left(jnp.broadcast_to(bias, (8, wide)), 200 * me)
    lane = lax.broadcasted_iota(jnp.int32, (1, wide), 1)
    bias = pltpu.roll(jnp.where(lane < 200, bias, 0.0), 208 * p + 8 * lax.rem(me, 2), 1)
    bias = jnp.where(n == 0, bias, 0.0)
    return jnp.concatenate([rows, bias], axis=0).astype(BF)


def attend_kernel(planes, tok, cot, v0, v1, v2, v3, v4, v5, v6, v7, v8, mixer, merge, expand,
                  hidden_o, qkv_o, att_o, heads_o, vec_o, lse_o,
                  first_o, mw_o, mfull_o, w1_o, sec_o, g_o,
                  vpart, raw1, own1, vec, mw0, mw1, mgs, mfull, first_all, second, arecv,
                  zs, zl, v_s, v_r, gs, gr, gl, gl2, a_s, a_r, os):
    L = Links(planes)
    qkv, attown, hid, lse, att = qkv_o, att_o, hidden_o, lse_o, heads_o
    p, me = L.p, L.me
    share = 400
    xv = LineExchange(L, vec, v_s, v_r)
    zm0 = LineGather(L, None, lambda b: mw0.at[dyn(b * share, share, 16)], zs.at[0], zl.at[0])
    zm1 = LineGather(L, None, lambda b: mw1.at[dyn(b * share, share, 16)], zs.at[1], zl.at[0])
    zmg = LineGather(L, None, lambda b: mgs.at[b], zs.at[2], zl.at[0])
    zw1 = LineGather(L, own1, lambda b: w1_o.at[dyn(b * share, share, 16)], zs.at[3], zl.at[0])
    gfirst = GroupGather(L, lambda j, h: first_all.at[h, j], gs.at[0], gr.at[0])
    gsec = GroupGather(L, row_parts(sec_o, 64), gs.at[1], gr.at[1], own_parts(second, 64), gl)
    gg = GroupGather(L, row_parts(g_o, 64), gs.at[3], gr.at[3], own_parts(cot, 64), gl2)
    gmerge = GroupGather(L, lambda j, h: mfull.at[2 * h : 2 * h + 2, dyn(j * 48, 48, 16)], gs.at[2], gr.at[2])

    takes = [
        pltpu.make_async_copy(merge.at[dyn(me * 48, 48, 16)], mgs.at[p, 0:48], zl.at[1]),
        pltpu.make_async_copy(merge.at[384:400], mgs.at[p, 48:64], zl.at[2]),
        pltpu.make_async_copy(expand, raw1, zl.at[3]),
    ]
    for c in takes:
        c.start()
    vpart[...] = small_vectors((v0, v1, v2, v3, v4, v5, v6, v7, v8), p, me)
    at_own = dyn(p * share, share, 16)

    def head_columns(n):
        odd = lax.rem(n + me, 2)
        x = mixer[:, dyn(D * n + 192 * me - 64 * odd, 256, 128)]
        return jnp.where(odd == 1, jnp.concatenate([x[:, 64:], x[:, :64]], axis=1), x)

    for n in range(3):
        mine = head_columns(n)
        mw0[at_own, 128 * n : 128 * n + 128] = mine[:, :128]
        every = mixer[:, D * n + 1536 : D * n + 1600]
        mw1[at_own, 128 * n : 128 * n + 128] = jnp.concatenate([mine[:, 128:192], every], axis=1)
    L.barrier((1, 2, 3, 4, 5, 6, 7))
    xv.start(vpart)
    zm0.start()
    rows = tok[...].astype(F32)
    normal, _ = normalize(rows)
    vectors = xv.total(vpart)[:, :D]
    first = (normal * vectors[0:1] + vectors[1:2]).astype(BF)
    first_all[:, me] = first.reshape(2, 64, D)
    gfirst.start()
    takes[2].wait()
    odd_me = lax.rem(me, 2)
    lane = lax.broadcasted_iota(jnp.int32, (1, 384), 1)
    for q in range(4):
        start = 1600 * q + 200 * me
        base = jnp.minimum(start // 128 * 128, 6400 - 384)
        x = shift_left(raw1[:, dyn(base, 384, 128)].astype(F32), lax.rem(start - base - 8 * odd_me + 384, 384))
        x = jnp.where((lane >= 8 * odd_me) & (lane < 8 * odd_me + 200), x, 0.0)
        own1[:, 208 * q : 208 * q + 208] = x[:, :208].astype(BF)
    zm0.pump(1)
    zm0.pump(2)
    takes[0].wait()
    takes[1].wait()
    zmg.start()
    gfirst.forward()
    zm0.pump(3)
    zmg.pump(1)
    gfirst.wait()
    zmg.pump(2)
    zm1.start()

    def mix(weights, pair):
        bias_q = vectors[2:3, pair * 128 : pair * 128 + 128]
        bias_v = vectors[3:4, pair * 128 : pair * 128 + 128]

        def body(b, _):
            x = first_all[b // 2, pl.ds((b % 2) * 4, 4)].reshape(256, D)
            mixed = dot(x, weights[...])
            at = dyn(b * 256, 256, 256)
            qkv[pair, at] = (mixed[:, :128] + bias_q).astype(BF)
            qkv[2 + pair, at] = mixed[:, 128:256].astype(BF)
            qkv[4 + pair, at] = (mixed[:, 256:] + bias_v).astype(BF)
            return 0

        lax.fori_loop(0, 4, body, 0)

    lane128 = lax.broadcasted_iota(jnp.int32, (1, 128), 1)

    def note_lse(head, at, value):
        lse[at] = jnp.where(lane128 == head, value, lse[at] if head else 0.0)

    def attend_private(pair, half):
        mask = half_mask(half)
        for b in range(4):
            q = jnp.where(mask, qkv[pair, b * 256 : b * 256 + 256], 0) * jnp.asarray(0.125, BF)
            out, l = softmax_pieces(
                q, qkv.at[2 + pair], qkv.at[4 + pair], BLOCK_KEYS[b], lambda kind, start, shape: triangle(kind, shape)
            )
            out = jnp.where(mask, out, 0.0).astype(BF).reshape(4, 64, 128)
            at = pl.ds((b % 2) * 4, 4)
            if half == 0:
                att[pair, b // 2, at] = out
            else:
                att[pair, b // 2, at] = att[pair, b // 2, at] + out
            note_lse(2 * pair + half, slice(b * 256, b * 256 + 256), l)

    def own_allowed(kind, start, shape):
        r = lax.broadcasted_iota(jnp.int32, shape, 0)
        c = lax.broadcasted_iota(jnp.int32, shape, 1)
        rp = jnp.where(r < 64, me * 64 + r, 1023 - (me * 64 + r - 64))
        cp = jnp.where(c < 512, c, 1023 - (c - 512))
        return cp <= rp

    mix(mw0, 0)
    zmg.pump(3)
    for b in range(4):
        mfull[b, dyn(me * 48, 48, 16)] = mgs[b, 0:48]
        mfull[b, 384:400] = mgs[b, 48:64]
    gmerge.start()
    attend_private(0, 0)
    zm1.pump(1)
    attend_private(0, 1)
    zm1.pump(2)
    zw1.start()
    gmerge.forward()
    gg.start()
    zm1.pump(3)
    mix(mw1, 1)
    outs = [
        pltpu.make_async_copy(first_all, first_o, os.at[0]),
        pltpu.make_async_copy(mw0, mw_o.at[0], os.at[1]),
        pltpu.make_async_copy(mw1, mw_o.at[1], os.at[2]),
        pltpu.make_async_copy(mfull, mfull_o, os.at[3]),
    ]
    for c in outs[:3]:
        c.start()
    attend_private(1, 0)
    qs = jnp.concatenate([qkv[1, dyn(me * 64, 64, 64)], qkv[1, dyn(512 + me * 64, 64, 64)]], axis=0)
    mask1 = half_mask(1)
    qs = jnp.where(mask1, qs, 0) * jnp.asarray(0.125, BF)
    out_s, l_s = softmax_pieces(qs, qkv.at[3], qkv.at[5], ((0, 1024, 1),), own_allowed)
    note_lse(3, slice(0, 128), l_s)
    shared_low = jnp.where(mask1, out_s, 0.0).astype(BF)

    def exchange(mask):
        return L.copy(att.at[:, :, me ^ mask], arecv.at[me], a_s.at[mask], a_r.at[me], L.peer(mask))

    def arrived(mask):
        return L.copy(att.at[:, :, me], arecv.at[me ^ mask], a_s.at[mask], a_r.at[me ^ mask], L.peer(mask))

    for mask in range(1, 8):
        exchange(mask).start()
    arecv[me] = att[:, :, me]
    gg.forward()
    for mask in range(1, 8):
        arrived(mask).wait_recv()
    for j in range(8):
        attown[:, 192 * j : 192 * j + 128] = arecv[j, 0].reshape(128, 128)
        attown[:, 192 * j + 128 : 192 * j + 192] = arecv[j, 1].reshape(128, 128)[:, :64]
    attown[:, 1536:1600] = shared_low[:, 64:128]
    gmerge.wait()
    hidden = rows + vectors[4:5]
    hid[...] = hidden
    for b in range(4):
        hid[...] += dot(attown[:, b * 400 : b * 400 + 400], mfull[b])
    normal2, _ = normalize(hid[...])
    second[...] = (normal2 * vectors[5:6] + vectors[6:7]).astype(BF)
    gsec.start()
    outs[3].start()
    vec_o[...] = vectors
    zw1.pump(1)
    gg.wait()
    gsec.forward()
    zw1.pump(2)
    gsec.wait()
    zw1.pump(3)
    for c in outs:
        c.wait()
    xv.finish(vpart)
    for z in (zm0, zm1, zmg, zw1):
        z.finish()
    for g in (gfirst, gg, gsec, gmerge):
        g.finish()
    for mask in range(1, 8):
        exchange(mask).wait_send()


def run_attend(planes, tok, cot, vectors, mixer, merge, expand):
    any_ = pl.BlockSpec(memory_space=pl.ANY)
    vm = pl.BlockSpec(memory_space=pltpu.VMEM)
    S = jax.ShapeDtypeStruct
    V = pltpu.VMEM
    dma = pltpu.SemaphoreType.DMA
    return pl.pallas_call(
        functools.partial(attend_kernel, planes),
        out_shape=(
            S((128, D), F32), S((6, 1024, 128), BF), S((128, D), BF), S((2, 2, 8, 64, 128), BF), S((16, D), F32), S((1024, 128), F32),
            S((2, 8, 64, D), BF), S((2, D, 384), BF), S((4, 400, D), BF), S((D, 832), BF),
            S((8, 128, D), BF), S((8, 128, D), BF),
        ),
        in_specs=[vm] * 12 + [any_] * 2,
        out_specs=(vm,) * 6 + (any_,) * 6,
        scratch_shapes=[
            V((16, 1664), BF), V((400, 6400), BF), V((400, 832), BF), V((3, 16, 1664), BF), V((D, 384), BF), V((D, 384), BF), V((4, 64, D), BF), V((4, 400, D), BF),
            V((2, 8, 64, D), BF), V((128, D), BF), V((8, 2, 2, 64, 128), BF),
            dma((5, 3, 4)), dma((5,)), dma((3,)), dma((3,)), dma((4, 14)), dma((4, 8, 2)), dma((2,)), dma((2,)),
            dma((8,)), dma((8,)), dma((4,)),
        ],
        compiler_params=pltpu.CompilerParams(collective_id=0, has_side_effects=True, vmem_limit_bytes=60 << 20),
        cost_estimate=pl.CostEstimate(flops=6_000_000_000, bytes_accessed=60_000_000, transcendentals=4_000_000),
    )(tok, cot, *vectors, mixer, merge, expand)


class LineSum:

    def __init__(self, links, block, slots, send, recv, near=None, near_sem=None):
        self.links, self.block, self.slots, self.send_sem, self.recv_sem = links, block, slots, send, recv
        self.near, self.near_sem = near, near_sem
        self.last = links.planes - 1

    def send(self, t, step):
        slot = t - 1 if step > 0 else self.last + t
        return self.links.copy(
            self.block(t), self.slots.at[slot], self.send_sem.at[t], self.recv_sem.at[slot], self.links.plane(step)
        )

    def arrival(self, slot):
        return self.links.copy(
            self.slots.at[slot], self.slots.at[slot], self.send_sem.at[0], self.recv_sem.at[slot], self.links.plane(0)
        )

    def start(self):
        @pl.when(self.links.p == 0)
        def _():
            for t in range(self.last, 0, -1):
                self.send(t, 1).start()

        @pl.when(self.links.p == self.last)
        def _():
            for t in range(self.last):
                self.send(t, -1).start()

    def add(self, t, slot):
        self.arrival(slot).wait_recv()
        ref = self.block(t)
        came = self.slots.at[slot]
        if self.near is not None:
            copy = pltpu.make_async_copy(came, self.near, self.near_sem)
            copy.start()
            copy.wait()
            came = self.near
        ref[...] = (ref[...].astype(F32) + came[...].astype(F32)).astype(BF)

    def pump(self, u):
        p, last = self.links.p, self.last
        for t in range(1, last + 1):
            at = u - last + t
            if 0 < at < t:

                @pl.when(p == at)
                def _():
                    self.add(t, t - 1)
                    self.send(t, 1).start()

                @pl.when(p == last - at)
                def _():
                    self.add(last - t, 2 * last - t)
                    self.send(last - t, -1).start()

    def total(self):
        p, last = self.links.p, self.last

        @pl.when(p > 0)
        def _():
            self.add(p, p - 1)

        @pl.when(p < last)
        def _():
            self.add(p, last + p)

    def finish(self):
        p = self.links.p
        for t in range(self.last + 1):

            @pl.when(p < t)
            def _():
                self.send(t, 1).wait_send()

            @pl.when(p > t)
            def _():
                self.send(t, -1).wait_send()


def backward_kernel(planes, tok, cot, hid, vectors, attown, lse, qkv, att,
                    shrink, w1_h, sec_h, g_h, mfull_h, mw_h, first_h,
                    igrad_o, out_o, va_o, vb_o, gw1_o, gw2_o, gm0_o, gm1_o, gmg_o, atts_o, slot_mg,
                    mfull, mw, sec_all, g_all, w1b, w2b, act, slope, dw1, dw2, hlow, agrad, asend, gatt, hc, dkv, mgr, dmerge,
                    slot_w1, slot_w2, slot_m0, slot_m1, near_mg, stage, twin, far, va, vb, vslot,
                    zs, zl, ld, ls_s, ls_r, ve_s, ve_r, gs, gr, gl, a_s, a_r, h_s, h_r, rs_s, rs_t, rs_f, free):
    L = Links(planes)
    p, me = L.p, L.me
    loads = [
        pltpu.make_async_copy(w1_h, w1b, ld.at[0]),
        pltpu.make_async_copy(sec_h, sec_all, ld.at[1]),
        pltpu.make_async_copy(g_h, g_all, ld.at[7]),
        pltpu.make_async_copy(mfull_h, mfull, ld.at[2]),
        pltpu.make_async_copy(mw_h, mw, ld.at[3]),
    ]
    att_all, first_all = g_all, sec_all
    late_att = pltpu.make_async_copy(atts_o, att_all, ld.at[5])
    late_first = pltpu.make_async_copy(first_h, first_all, ld.at[6])
    for c in loads:
        c.start()
    shrink_rows = shrink.at[dyn(200 * me - 8 * lax.rem(me, 2), 208, 16)]
    zw2 = LineGather(L, shrink_rows, lambda b: w2b.at[dyn(b * 208, 208, 16)], zs, zl)
    lw2 = LineSum(L, lambda t: dw2.at[dyn(t * 208, 208, 16)], slot_w2, ls_s.at[0], ls_r.at[0])
    lw1 = LineSum(L, lambda t: dw1.at[dyn(t * 400, 400, 16)], slot_w1, ls_s.at[1], ls_r.at[1])
    lm0 = LineSum(L, lambda t: w1b.at[dyn(t * 400, 400, 16), 0:384], slot_m0, ls_s.at[2], ls_r.at[2])
    lm1 = LineSum(L, lambda t: w1b.at[dyn(t * 400, 400, 16), 384:768], slot_m1, ls_s.at[3], ls_r.at[3])
    lmg = LineSum(L, lambda t: dmerge.at[dyn(t * 400, 400, 16)], slot_mg, ls_s.at[4], ls_r.at[4], near_mg, ld.at[4])
    xa = LineExchange(L, vslot.at[0], ve_s.at[0], ve_r.at[0])
    xb = LineExchange(L, vslot.at[1], ve_s.at[1], ve_r.at[1])
    gatt_all = GroupGather(L, row_parts(atts_o, 64), gs.at[1], gr.at[1], own_parts(attown, 64), gl.at[1])
    gw2 = GroupGather(L, row_parts(gw2_o, 112), gs.at[2], gr.at[2], lambda h: dw2.at[dyn(p * 208 + 112 * h, (112, 96)[h], 16)], gl.at[2])

    def share_gather(n, out, line):
        def src(h):
            base, columns = line.home
            return base.at[dyn(p * 400 + 208 * h, (208, 192)[h], 16), columns[0] : columns[1]]

        return GroupGather(L, row_parts(out, 208), gs.at[n], gr.at[n], src, gl.at[n])

    lw1.home, lm0.home, lm1.home, lmg.home = (dw1, (0, 832)), (w1b, (0, 384)), (w1b, (384, 768)), (dmerge, (0, 256))
    gw1 = share_gather(3, gw1_o, lw1)
    gm0 = share_gather(4, gm0_o, lm0)
    gm1 = share_gather(5, gm1_o, lm1)
    gmg = share_gather(6, gmg_o, lmg)
    gva = SmallGather(L, va, lambda j: va_o.at[j], gs.at[7], gr.at[7], gl.at[7, 0])
    gvb = SmallGather(L, vb, lambda j: vb_o.at[j], gs.at[8], gr.at[8], gl.at[8, 0])
    L.barrier((1, 2, 3, 4, 5, 6, 7))
    zw2.start()
    gatt_all.start()

    loads[0].wait()
    loads[1].wait()

    def expand(b, _):
        at = dyn(b * 256, 256, 256)
        pre = dot(sec_all[pl.ds(2 * b, 2)].reshape(256, D), w1b[...]) + vectors[8:9, :832]
        value, s = gelu_parts(pre)
        act[at] = value.astype(BF)
        slope[at] = s.astype(BF)
        return 0

    lax.fori_loop(0, 4, expand, 0)
    loads[2].wait()
    g2 = g_all[...].reshape(1024, D)
    for start, size in ((0, 256), (256, 256), (512, 256), (768, 64)):
        dw2[start : start + size] = t_dot(act[:, start : start + size], g2).astype(BF)
    lw2.start()
    zw2.pump(1)
    gatt_all.forward()
    lw2.pump(1)
    zw2.pump(2)
    gatt_all.wait()
    zw2.pump(3)

    def contract(b, acc):
        at = dyn(b * 256, 256, 256)
        grad = dot_t(g_all[pl.ds(2 * b, 2)].reshape(256, D), w2b[...]) * slope[at].astype(F32)
        slope[at] = grad.astype(BF)
        return acc + jnp.sum(grad, axis=0, keepdims=True)

    dgb = lax.fori_loop(0, 4, contract, jnp.zeros((1, 832), F32))
    late_att.start()
    rounds = [GroupSum(L, stage, twin, far, rs_s.at[n], rs_t.at[n], rs_f.at[n]) for n in range(3)]

    def release(n):
        for mask in (1, 2, 4):
            pl.semaphore_signal(free.at[n], inc=1, device_id=L.peer(mask), device_id_type=MESH_ID)

    for start in range(0, D, 256):
        size = min(256, D - start)
        x = sec_all[:, :, start : start + size].reshape(1024, size)
        dw1[start : start + size] = t_dot(x, slope[...]).astype(BF)
    late_first.start()
    lw2.pump(2)
    lw1.start()
    back = rounds[0]
    back.run(lambda owner: dot_t(slope[dyn(owner * 128, 128, 128)], w1b[...]))
    back.relay()
    lw2.total()
    grad2 = back.total()
    back.finish()
    release(0)

    tangent = cot[...].astype(F32)
    normal2, inverse2 = normalize(hid[...])
    hidden_grad = tangent + norm_back(grad2, vectors[5:6], normal2, inverse2)
    igrad_o[...] = hidden_grad
    hlow[:, 0:D] = hidden_grad.astype(BF)
    hlow[:, D:2048] = jnp.zeros((128, 2048 - D), BF)
    va[0:1] = jnp.sum(hidden_grad, axis=0, keepdims=True)
    va[1:2] = jnp.sum(grad2 * normal2, axis=0, keepdims=True)
    va[2:3] = jnp.sum(grad2, axis=0, keepdims=True)
    va[3:4] = jnp.sum(tangent, axis=0, keepdims=True)
    va[4:8] = jnp.zeros((4, D), F32)
    va[4:5, 0:832] = dgb

    def columns(mask):
        to = me ^ mask
        return L.copy(hlow.at[:, dyn(to * 256, 256, 256)], hc.at[me], h_s.at[mask], h_r.at[me], L.peer(mask))

    def columns_in(mask):
        return L.copy(hc.at[me], hc.at[me ^ mask], h_s.at[mask], h_r.at[me ^ mask], L.peer(mask))

    loads[3].wait()
    agrad[...] = dot_t(hlow[:, 0:D], mfull[...]).astype(BF)
    for j in range(8):
        asend[j, 0] = agrad[:, 192 * j : 192 * j + 128].reshape(2, 64, 128)
        tail = agrad[:, 192 * j + 128 : 192 * j + 192]
        asend[j, 1] = jnp.concatenate([tail, jnp.zeros((128, 64), BF)], axis=1).reshape(2, 64, 128)

    def exchange(mask):
        return L.copy(asend.at[me ^ mask], gatt.at[:, :, me], a_s.at[mask], a_r.at[me], L.peer(mask))

    def arrived(mask):
        return L.copy(asend.at[me], gatt.at[:, :, me ^ mask], a_s.at[mask], a_r.at[me ^ mask], L.peer(mask))

    for mask in range(1, 8):
        exchange(mask).start()
    gatt[:, :, me] = asend[me]
    for mask in range(1, 8):
        columns(mask).start()
    pl.semaphore_wait(free.at[0], 3)
    outs = rounds[1]
    outs.run(lambda owner: dot(act[dyn(owner * 128, 128, 128)], w2b[...]))
    hc[me] = hlow[:, dyn(me * 256, 256, 256)]
    dkv[...] = jnp.zeros(dkv.shape, F32)
    lw1.pump(1)
    for mask in range(1, 8):
        arrived(mask).wait_recv()

    scale = jnp.asarray(0.125, BF)

    def head_back(pair, head, mask, q, g, o, stat, pieces, allowed):
        delta = jnp.sum(g.astype(F32) * o.astype(F32), axis=1, keepdims=True)
        dq = 0.0
        for start, size, kind in pieces:
            keys = qkv[2 + pair, start : start + size]
            s = dot_t(q, keys)
            if kind:
                s = jnp.where(allowed(kind, start, s.shape), s, -1e30)
            prob = jnp.exp(s - stat)
            ds = (prob * (dot_t(g, qkv[4 + pair, start : start + size]) - delta)).astype(BF)
            dq = dq + dot(ds, keys)
            dkv[0, start : start + size] += t_dot(ds, q)
            dkv[1, start : start + size] += t_dot(prob.astype(BF), g)
        return jnp.where(mask, dq, 0.0) * 0.125

    def private_back(pair, half):
        mask = half_mask(half)
        head = 2 * pair + half
        total = 0.0
        for b in range(4):
            at = slice(b * 256, b * 256 + 256)
            blk = (pair, b // 2, pl.ds((b % 2) * 4, 4))
            q = jnp.where(mask, qkv[pair, at], 0) * scale
            g = jnp.where(mask, gatt[blk].reshape(256, 128), 0)
            o = att[blk].reshape(256, 128)
            dq = head_back(
                pair, head, mask, q, g, o, lse[at, head : head + 1], BLOCK_KEYS[b],
                lambda kind, start, shape: triangle(kind, shape),
            )
            total = total + jnp.sum(dq, axis=0, keepdims=True)
            if half == 0:
                mgr[pair, at, 0:128] = dq.astype(BF)
            else:
                mgr[pair, at, 0:128] = mgr[pair, at, 0:128] + dq.astype(BF)
        return total

    def mixer_part(pair):
        mgr[pair, :, 128:256] = dkv[0].astype(BF)
        mgr[pair, :, 256:384] = dkv[1].astype(BF)
        va[6:7, pair * 128 : pair * 128 + 128] = jnp.sum(dkv[1], axis=0, keepdims=True)
        for start in range(0, D, 256):
            size = min(256, D - start)
            x = first_all[:, :, start : start + size].reshape(1024, size)
            w1b[start : start + size, 384 * pair : 384 * pair + 384] = t_dot(x, mgr[pair]).astype(BF)

    qb0 = private_back(0, 0)
    qb0 = qb0 + private_back(0, 1)
    va[5:6, 0:128] = qb0
    late_first.wait()
    mixer_part(0)
    dkv[...] = jnp.zeros(dkv.shape, F32)
    lm0.start()
    lw1.pump(2)
    outs.relay()
    gw2.start()
    qb1 = private_back(1, 0)
    mask1 = half_mask(1)
    own_early, own_late = dyn(me * 64, 64, 64), dyn(512 + me * 64, 64, 64)
    qs = jnp.concatenate([qkv[1, own_early], qkv[1, own_late]], axis=0)
    qs = jnp.where(mask1, qs, 0) * scale
    blank = jnp.zeros((128, 64), BF)
    g_s = jnp.concatenate([blank, agrad[:, 1536:1600]], axis=1)
    o_s = jnp.concatenate([blank, attown[:, 1536:1600]], axis=1)

    def own_allowed(kind, start, shape):
        r = lax.broadcasted_iota(jnp.int32, shape, 0)
        c = lax.broadcasted_iota(jnp.int32, shape, 1) + start
        rp = jnp.where(r < 64, me * 64 + r, 1023 - (me * 64 + r - 64))
        cp = jnp.where(c < 512, c, 1023 - (c - 512))
        return cp <= rp

    dqs = head_back(1, 3, mask1, qs, g_s, o_s, lse[0:128, 3:4], ((0, 512, 1), (512, 512, 1)), own_allowed)
    va[5:6, 128:256] = qb1 + jnp.sum(dqs, axis=0, keepdims=True)
    dqs_low = dqs.astype(BF)
    mgr[1, own_early, 0:128] = mgr[1, own_early, 0:128] + dqs_low[:64]
    mgr[1, own_late, 0:128] = mgr[1, own_late, 0:128] + dqs_low[64:]
    mixer_part(1)
    lm1.start()
    xa.start(va)
    out_o[...] = (outs.total() + hid[...] + vectors[7:8]).astype(BF)
    outs.finish()
    release(1)
    loads[4].wait()
    pl.semaphore_wait(free.at[1], 3)
    sums = rounds[2]

    def first_block(owner):
        early, late = dyn(owner * 64, 64, 64), dyn(512 + owner * 64, 64, 64)
        x0 = jnp.concatenate([mgr[0, early], mgr[0, late]], axis=0)
        x1 = jnp.concatenate([mgr[1, early], mgr[1, late]], axis=0)
        return dot_t(x0, mw[0]) + dot_t(x1, mw[1])

    sums.run(first_block)
    gw2.forward()
    sums.relay()
    lw1.total()
    gw1.start()
    lm0.pump(1)
    late_att.wait()
    for mask in range(1, 8):
        columns_in(mask).wait_recv()
    h2 = hc[...].reshape(1024, 256)
    for start in range(0, D, 256):
        size = min(256, D - start)
        x = att_all[:, :, start : start + size].reshape(1024, size)
        dmerge[start : start + size] = t_dot(x, h2).astype(BF)
    lmg.start()
    lm0.pump(2)
    first_grad = sums.total()
    rows = tok[...].astype(F32)
    normal1, inverse1 = normalize(rows)
    igrad_o[...] += norm_back(first_grad, vectors[0:1], normal1, inverse1)
    vb[0:1] = jnp.sum(first_grad * normal1, axis=0, keepdims=True)
    vb[1:2] = jnp.sum(first_grad, axis=0, keepdims=True)
    vb[2:8] = jnp.zeros((6, D), F32)
    xb.start(vb)
    lm0.total()
    gm0.start()
    lm1.pump(1)
    gw1.forward()
    lm1.pump(2)
    gm0.forward()
    lm1.total()
    gm1.start()
    lmg.pump(1)
    total_a = xa.total(va)
    xa.finish(va)
    va[...] = total_a
    gva.start()
    lmg.pump(2)
    total_b = xb.total(vb)
    xb.finish(vb)
    vb[...] = total_b
    gvb.start()
    lmg.total()
    gmg.start()
    gm1.forward()
    gva.forward()
    gvb.forward()
    gmg.forward()
    for g in (gw2, gva, gw1, gvb, gm0, gm1, gmg):
        g.wait()
    for g in (gatt_all, gw2, gw1, gm0, gm1, gmg, gva, gvb):
        g.finish()
    zw2.finish()
    for s in (lw2, lw1, lm0, lm1, lmg):
        s.finish()
    for mask in range(1, 8):
        exchange(mask).wait_send()
        columns(mask).wait_send()
    sums.finish()


def run_backward(planes, *operands):
    any_ = pl.BlockSpec(memory_space=pl.ANY)
    vm = pl.BlockSpec(memory_space=pltpu.VMEM)
    S = jax.ShapeDtypeStruct
    V = pltpu.VMEM
    dma = pltpu.SemaphoreType.DMA
    return pl.pallas_call(
        functools.partial(backward_kernel, planes),
        out_shape=(
            S((128, D), F32), S((128, D), BF), S((8, 8, D), F32), S((8, 8, D), F32), S((8, 400, 832), BF), S((8, 208, D), BF),
            S((8, 400, 384), BF), S((8, 400, 384), BF), S((8, 400, 256), BF), S((8, 128, D), BF),
            S((6, 400, 256), BF),
        ),
        in_specs=[vm] * 8 + [any_] * 7,
        out_specs=(vm,) * 2 + (any_,) * 9,
        scratch_shapes=[
            V((D, D), BF), V((2, D, 384), BF), V((8, 128, D), BF), V((8, 128, D), BF), V((D, 832), BF), V((832, D), BF),
            V((1024, 832), BF), V((1024, 832), BF), V((D, 832), BF), V((832, D), BF),
            V((128, 2048), BF), V((128, D), BF), V((8, 2, 2, 64, 128), BF), V((2, 2, 8, 64, 128), BF),
            V((8, 128, 256), BF), V((2, 1024, 128), F32), V((2, 1024, 384), BF), V((D, 256), BF),
            V((6, 400, 832), BF), V((6, 208, D), BF), V((6, 400, 384), BF), V((6, 400, 384), BF), V((400, 256), BF),
            V((8, 128, D), BF), V((4, 128, D), BF), V((3, 128, D), BF), V((8, D), F32), V((8, D), F32), V((2, 3, 8, D), F32),
            dma((3, 4)), dma(()), dma((8,)), dma((5, 4)), dma((5, 6)), dma((2, 3)), dma((2, 3)), dma((9, 14)), dma((9, 8, 2)), dma((9, 2)),
            dma((8,)), dma((8,)), dma((8,)), dma((8,)), dma((3, 14)), dma((3, 4)), dma((3, 6)), pltpu.SemaphoreType.REGULAR((2,)),
        ],
        compiler_params=pltpu.CompilerParams(collective_id=1, has_side_effects=True, vmem_limit_bytes=(64 << 20) - 65536),
        cost_estimate=pl.CostEstimate(flops=25_000_000_000, bytes_accessed=60_000_000, transcendentals=4_000_000),
    )(*operands)


def assemble_kernel(gw1, gm0, gm1, gmg, va, vb, input_grad, output, expand_o, mixer_o, merge_o, input_o, output_o, *vectors_o):
    for j in range(8):
        odd = 8 * (j % 2)
        for q in range(4):
            at = 1600 * q + 200 * j
            expand_o[:, at : at + 200] = gw1[j, :, 208 * q + odd : 208 * q + odd + 200].astype(F32)
        for n in range(3):
            at = D * n + 192 * j
            mixer_o[:, at : at + 128] = gm0[j, :, 128 * n : 128 * n + 128].astype(F32)
            mixer_o[:, at + 128 : at + 192] = gm1[j, :, 128 * n : 128 * n + 64].astype(F32)
    for n in range(3):
        total = gm1[0, :, 128 * n : 128 * n + 128].astype(F32)
        for j in range(1, 8):
            total += gm1[j, :, 128 * n : 128 * n + 128].astype(F32)
        mixer_o[:, D * n + 1536 : D * n + 1600] = total[:, 64:]
    for j in range(6):
        merge_o[:, 256 * j : 256 * j + 256] = gmg[j].astype(F32)
    merge_o[:, 1536:1600] = gmg[6, :, :64].astype(F32)

    @pl.when(pl.program_id(0) == 0)
    def _():
        input_o[...] = input_grad[...]
        output_o[...] = output[...]
        p = lax.axis_index("fsdp")
        early, late = va[0], vb[0]
        for j in range(1, 8):
            early += va[j]
            late += vb[j]

        def per_head(n):
            return jnp.concatenate([va[j, n : n + 1, :192] for j in range(8)] + [early[n : n + 1, 192:256]], axis=1)

        rows = jnp.concatenate(
            [late[0:2], per_head(5), per_head(6), early[0:4]], axis=0
        )
        rows = jnp.concatenate([rows, jnp.zeros((8, 64), F32)], axis=1)
        rows = shift_left(rows, 400 * p)
        bias = jnp.concatenate([va[j, 4:5, :] for j in range(8)], axis=0)
        bias = shift_left(jnp.concatenate([bias, jnp.zeros((8, 64), F32)], axis=1), 208 * p)
        bias = jnp.concatenate([bias[j : j + 1, 8 * (j % 2) : 8 * (j % 2) + 200] for j in range(8)], axis=1)
        for n in range(8):
            vectors_o[n][...] = rows[n, :400]
        vectors_o[8][...] = bias[0]


def assemble(gw1, gm0, gm1, gmg, va, vb, input_grad, output):
    rows = 80

    def part(width):
        return pl.BlockSpec((8, rows, width), lambda n: (0, n, 0))

    def whole(width):
        return pl.BlockSpec((rows, width), lambda n: (n, 0))

    own = pl.BlockSpec((128, D), lambda n: (0, 0))
    small = pl.BlockSpec((8, 8, D), lambda n: (0, 0, 0))

    def vector(width):
        return pl.BlockSpec((width,), lambda n: (0,))

    S = jax.ShapeDtypeStruct
    return pl.pallas_call(
        assemble_kernel,
        grid=(400 // rows,),
        in_specs=[part(832), part(384), part(384), part(256), small, small, own, own],
        out_specs=(whole(6400), whole(4800), whole(D), own, own) + (vector(400),) * 8 + (vector(1600),),
        out_shape=(S((400, 6400), F32), S((400, 4800), F32), S((400, D), F32), S((128, D), F32), S((128, D), BF)) + (S((400,), F32),) * 8 + (S((1600,), F32),),
        compiler_params=pltpu.CompilerParams(vmem_limit_bytes=63 << 20),
    )(gw1, gm0, gm1, gmg, va, vb, input_grad, output)


def widen_kernel(x, o):
    odd = lax.rem(pl.program_id(0), 2)

    @pl.when(odd == 0)
    def _():
        o[...] = x[0, :200].astype(F32)

    @pl.when(odd == 1)
    def _():
        o[...] = x[0, 8:208].astype(F32)


def widen(gw2):
    return pl.pallas_call(
        widen_kernel,
        grid=(8,),
        in_specs=[pl.BlockSpec((1, 208, D), lambda n: (n, 0, 0))],
        out_specs=pl.BlockSpec((200, D), lambda n: (n, 0)),
        out_shape=jax.ShapeDtypeStruct((1600, D), F32),
        compiler_params=pltpu.CompilerParams(vmem_limit_bytes=63 << 20),
    )(gw2)


def local_plain(
    tokens,
    first_gain,
    first_shift,
    mixer_weight,
    query_bias,
    value_bias,
    merge_weight,
    merge_bias,
    second_gain,
    second_shift,
    expand_weight,
    expand_bias,
    shrink_weight,
    shrink_bias,
    cotangent,
):
    planes = lax.axis_size("fsdp")
    ring = lax.axis_size("ctx")
    me = lax.axis_index("ctx")
    blocks = tokens.shape[2]
    local_rows = 2 * blocks
    half = blocks * ring
    length = 2 * half
    private = H // ring
    shared = H - private * ring
    pc, sc = private * HD, shared * HD
    hc = pc + sc
    shared_at = private * ring * HD
    share = D // planes
    ff_plane = expand_bias.shape[0]
    ff_part = ff_plane // ring
    cols = D // ring

    vectors = jnp.stack(
        [first_gain, first_shift, query_bias, value_bias, merge_bias, second_gain, second_shift, shrink_bias]
    )
    vectors = lax.all_gather(vectors, "fsdp", axis=1, tiled=True).astype(F32)
    gain1, shift1, qbias, vbias, mbias, gain2, shift2, sbias = [vectors[n] for n in range(8)]

    def head_columns(weight, base):
        mine = lax.dynamic_slice_in_dim(weight, base + me * pc, pc, weight.ndim - 1)
        every = weight[..., base + shared_at : base + D]
        return [mine, every]

    mixer_part = jnp.concatenate(
        head_columns(mixer_weight, 0) + head_columns(mixer_weight, D) + head_columns(mixer_weight, 2 * D), axis=1
    )
    mixer_mine = lax.all_gather(mixer_part, "fsdp", axis=0, tiled=True)

    merge_part = lax.dynamic_slice_in_dim(merge_weight, me * cols, cols, 1)
    merge_cols = lax.all_gather(merge_part, "fsdp", axis=0, tiled=True)
    merge_full = lax.all_gather(merge_cols, "ctx", axis=1, tiled=True)

    expand_part = expand_weight.reshape(share, planes, ring, ff_part)
    expand_part = lax.dynamic_index_in_dim(expand_part, me, 2, keepdims=False)
    expand_part = lax.all_to_all(expand_part, "fsdp", 1, 0, tiled=False).reshape(D, ff_part)
    expand_mine = lax.all_gather(expand_part, "ctx", axis=1, tiled=True)

    rows = tokens.reshape(local_rows, D).astype(F32)
    normal1, inverse1 = normalize(rows)
    first = (normal1 * gain1 + shift1).astype(BF)
    first_all = lax.all_gather(first.reshape(2, blocks, D), "ctx", axis=1, tiled=True).reshape(length, D)
    tangent_low = cotangent.reshape(local_rows, D)
    tangent = tangent_low.astype(F32)
    tangent_all = lax.all_gather(tangent_low, "fsdp", axis=0, tiled=True)

    mixed = dot(first_all, mixer_mine)
    qb = jnp.concatenate(head_columns(qbias, 0), axis=0)
    vb = jnp.concatenate(head_columns(vbias, 0), axis=0)
    query = (mixed[:, :hc] + qb).astype(BF)
    key = mixed[:, hc : 2 * hc].astype(BF)
    value = (mixed[:, 2 * hc :] + vb).astype(BF)
    half_index = jnp.arange(half, dtype=jnp.int32)
    place = jnp.concatenate([half_index, length - 1 - half_index])
    early = me * blocks + jnp.arange(blocks, dtype=jnp.int32)
    own_place = jnp.concatenate([early, length - 1 - early])
    allowed = place[None, :] <= place[:, None]
    own_allowed = place[None, :] <= own_place[:, None]

    def own_rows(values):
        parts = values.reshape(2, half, values.shape[1])
        return lax.dynamic_slice_in_dim(parts, me * blocks, blocks, 1).reshape(local_rows, values.shape[1])

    qp, kp, vp = heads_first(query[:, :pc]), heads_first(key[:, :pc]), heads_first(value[:, :pc])
    qs, ks, vs = heads_first(own_rows(query[:, pc:])), heads_first(key[:, pc:]), heads_first(value[:, pc:])
    out_p, top_p, total_p = attend(qp, kp, vp, allowed)
    out_s, top_s, total_s = attend(qs, ks, vs, own_allowed)
    att_heads = heads_last(out_p).astype(BF)
    att_pieces = lax.all_to_all(att_heads.reshape(2, ring, blocks, pc), "ctx", 1, 2, tiled=False)
    attended = jnp.concatenate(
        [att_pieces.reshape(local_rows, ring * pc), heads_last(out_s).astype(BF)], axis=1
    )
    hidden = rows + dot(attended, merge_full) + mbias
    normal2, inverse2 = normalize(hidden)
    second = (normal2 * gain2 + shift2).astype(BF)
    second_all = lax.all_gather(second, "fsdp", axis=0, tiled=True)
    attended_all = lax.all_gather(attended, "ctx", axis=0, tiled=True)

    pre = dot(second_all, expand_mine) + expand_bias.astype(F32)
    act, gate_pull = jax.vjp(lambda u: jax.nn.gelu(u, approximate=True), pre)
    act_low = act.astype(BF)
    act_grad = dot_t(tangent_all, shrink_weight)
    (pre_grad,) = gate_pull(act_grad)
    pre_low = pre_grad.astype(BF)
    second_part = dot_t(pre_low, expand_mine).astype(BF)
    second_grad = lax.psum_scatter(second_part, "fsdp", scatter_dimension=0, tiled=True).astype(F32)
    out_part = dot(act_low, shrink_weight).astype(BF)
    out_sum = lax.psum_scatter(out_part, "fsdp", scatter_dimension=0, tiled=True).astype(F32)
    output = (hidden + out_sum + sbias).astype(BF).reshape(1, 2, blocks, D)
    expand_bias_grad = jnp.sum(pre_grad, axis=0)
    shrink_grad = t_dot(act_low, tangent_all).astype(BF)
    shrink_mine = lax.psum_scatter(shrink_grad, "ctx", scatter_dimension=0, tiled=True)
    shrink_owned = lax.all_gather(shrink_mine, "ctx", axis=0, tiled=True).astype(F32)
    expand_grad = t_dot(second_all, pre_low).astype(BF)
    expand_cols = lax.psum_scatter(expand_grad, "ctx", scatter_dimension=1, tiled=True)
    expand_rows = lax.all_to_all(expand_cols.reshape(planes, share, ff_part), "fsdp", 0, 1, tiled=False)
    expand_owned = (
        lax.all_gather(expand_rows, "ctx", axis=2, tiled=False).reshape(share, planes * ff_plane).astype(F32)
    )

    hidden_grad = tangent + norm_back(second_grad, gain2, normal2, inverse2)
    hidden_low = hidden_grad.astype(BF)
    att_grad = dot_t(hidden_low, merge_full).astype(BF)
    grad_pieces = lax.all_to_all(att_grad[:, :shared_at].reshape(2, blocks, ring, pc), "ctx", 2, 1, tiled=False)
    grad_p = heads_first(grad_pieces.reshape(length, pc))
    grad_s = heads_first(att_grad[:, shared_at:])
    dqp, dkp, dvp = attend_back(qp, kp, vp, allowed, top_p, total_p, grad_p)
    dqs, dks, dvs = attend_back(qs, ks, vs, own_allowed, top_s, total_s, grad_s)
    dqs_all = jnp.zeros((2, half, sc), F32)
    dqs_all = lax.dynamic_update_slice_in_dim(dqs_all, heads_last(dqs).reshape(2, blocks, sc), me * blocks, 1)
    mixed_grad = jnp.concatenate(
        [heads_last(dqp), dqs_all.reshape(length, sc)]
        + [heads_last(dkp), heads_last(dks), heads_last(dvp), heads_last(dvs)],
        axis=1,
    )
    bias_sums = jnp.sum(mixed_grad, axis=0)
    mixed_low = mixed_grad.astype(BF)
    first_part = dot_t(mixed_low, mixer_mine).astype(BF)
    first_grad = lax.psum_scatter(
        first_part.reshape(2, half, D), "ctx", scatter_dimension=1, tiled=True
    ).reshape(local_rows, D).astype(F32)
    input_grad = hidden_grad + norm_back(first_grad, gain1, normal1, inverse1)
    mixer_part_grad = t_dot(first_all, mixed_low).astype(BF)
    mixer_rows = lax.psum_scatter(mixer_part_grad, "fsdp", scatter_dimension=0, tiled=True)
    mixer_all = lax.all_gather(mixer_rows, "ctx", axis=0, tiled=False).astype(F32)

    def place_columns(values):
        mine = values[:, :, :pc].transpose(1, 0, 2).reshape(share, ring * pc)
        return [mine, jnp.sum(values[:, :, pc:], axis=0)]

    mixer_owned = jnp.concatenate(
        place_columns(mixer_all[:, :, :hc])
        + place_columns(mixer_all[:, :, hc : 2 * hc])
        + place_columns(mixer_all[:, :, 2 * hc :]),
        axis=1,
    )
    hidden_cols = lax.all_to_all(hidden_low.reshape(local_rows, ring, cols), "ctx", 1, 0, tiled=False)
    merge_grad = t_dot(attended_all, hidden_cols.reshape(length, cols)).astype(BF)
    merge_rows = lax.psum_scatter(merge_grad, "fsdp", scatter_dimension=0, tiled=True)
    merge_owned = lax.all_gather(merge_rows, "ctx", axis=1, tiled=True).astype(F32)

    def spread_bias(values):
        full = jnp.zeros((D,), F32)
        full = lax.dynamic_update_slice_in_dim(full, values[:pc], me * pc, 0)
        return full.at[shared_at:].set(values[pc:])

    sums = jnp.stack(
        [
            jnp.sum(first_grad * normal1, axis=0),
            jnp.sum(first_grad, axis=0),
            spread_bias(bias_sums[:hc]),
            spread_bias(bias_sums[2 * hc :]),
            jnp.sum(hidden_grad, axis=0),
            jnp.sum(second_grad * normal2, axis=0),
            jnp.sum(second_grad, axis=0),
            jnp.sum(tangent, axis=0),
        ]
    )
    sums = lax.psum(sums, ("fsdp", "ctx"))
    mine = lax.dynamic_slice_in_dim(sums, lax.axis_index("fsdp") * share, share, 1)
    expand_bias_owned = lax.psum(expand_bias_grad, "ctx")

    return (
        output,
        input_grad.reshape(1, 2, blocks, D),
        mine[0],
        mine[1],
        mixer_owned,
        mine[2],
        mine[3],
        merge_owned,
        mine[4],
        mine[5],
        mine[6],
        expand_owned,
        expand_bias_owned,
        shrink_owned,
        mine[7],
    )


def local_kernel(
    tokens,
    first_gain,
    first_shift,
    mixer_weight,
    query_bias,
    value_bias,
    merge_weight,
    merge_bias,
    second_gain,
    second_shift,
    expand_weight,
    expand_bias,
    shrink_weight,
    shrink_bias,
    cotangent,
):
    planes = lax.axis_size("fsdp")
    blocks, local_rows = tokens.shape[2], 2 * tokens.shape[2]
    vectors = (
        first_gain, first_shift, query_bias, value_bias, merge_bias, second_gain, second_shift, shrink_bias, expand_bias
    )

    tok2, cot2 = tokens.reshape(local_rows, D), cotangent.reshape(local_rows, D)
    hidden, qkv, attown, heads, whole, lse, first_all, mws, mfull, w1_all, sec_all, g_all = run_attend(
        planes, tok2, cot2, vectors, mixer_weight, merge_weight, expand_weight
    )
    input_part, out_part, va, vb, gw1, gw2, gm0, gm1, gmg, _, _ = run_backward(
        planes, tok2, cot2, hidden, whole, attown, lse, qkv, heads,
        shrink_weight, w1_all, sec_all, g_all, mfull.reshape(D, D), mws, first_all.reshape(8, 128, D)
    )
    shrink_owned = widen(gw2)
    expand_owned, mixer_owned, merge_owned, input_grad, out_own, *small = assemble(
        gw1, gm0, gm1, gmg, va, vb, input_part, out_part
    )
    gain1, shift1, qbias, vbias, mbias, gain2, shift2, sbias, bias1 = small

    return (
        out_own.reshape(1, 2, blocks, D),
        input_grad.reshape(1, 2, blocks, D),
        gain1,
        shift1,
        mixer_owned,
        qbias,
        vbias,
        merge_owned,
        mbias,
        gain2,
        shift2,
        expand_owned,
        bias1,
        shrink_owned,
        sbias,
    )


def aligned(planes, ring, shape):
    return planes == 4 and ring == 8 and shape == (4, 2, 512, D)


def local(tokens, *others):
    planes, ring = lax.axis_size("fsdp"), lax.axis_size("ctx")
    whole = (tokens.shape[0] * planes, 2, tokens.shape[2] * ring, tokens.shape[3])
    if aligned(planes, ring, whole):
        return local_kernel(tokens, *others)
    return local_plain(tokens, *others)


def solution(mesh):
    token_spec = P("fsdp", None, "ctx", None)
    row = P("fsdp")
    matrix = P("fsdp", None)
    in_specs = (
        token_spec,
        row,
        row,
        matrix,
        row,
        row,
        matrix,
        row,
        row,
        row,
        matrix,
        row,
        matrix,
        row,
        token_spec,
    )
    out_specs = (
        token_spec,
        token_spec,
        row,
        row,
        matrix,
        row,
        row,
        matrix,
        row,
        row,
        row,
        matrix,
        row,
        matrix,
        row,
    )
    return jax.shard_map(local, mesh=mesh, in_specs=in_specs, out_specs=out_specs, check_vma=False)
```

```python
import functools

import jax
import jax.numpy as jnp
from jax import lax
from jax.experimental import pallas as pl
from jax.experimental.pallas import tpu as pltpu
from jax.sharding import PartitionSpec as P

D = 1600
H = 25
HD = 64

EPSILON = 1e-05
SCORE_SCALE = 0.125
BF = jnp.bfloat16
F32 = jnp.float32


def normalize(values):
    center = values - jnp.mean(values, axis=-1, keepdims=True)
    spread = jnp.mean(center * center, axis=-1, keepdims=True)
    inverse = lax.rsqrt(spread + EPSILON)
    return center * inverse, inverse


def norm_back(grad, gain, normal, inverse):
    scaled = grad * gain
    mean = jnp.mean(scaled, axis=-1, keepdims=True)
    along = jnp.mean(scaled * normal, axis=-1, keepdims=True)
    return inverse * (scaled - mean - normal * along)


def dot(a, b):
    return jnp.dot(a, b, preferred_element_type=F32)


def dot_t(a, b):
    return lax.dot_general(a, b, (((1,), (1,)), ((), ())), preferred_element_type=F32)


def t_dot(a, b):
    return lax.dot_general(a, b, (((0,), (0,)), ((), ())), preferred_element_type=F32)


def attend(query, key, value, allowed):
    scores = jnp.einsum("hqd,hkd->hqk", query, key, preferred_element_type=F32) * SCORE_SCALE
    scores = jnp.where(allowed[None], scores, -1e30)
    top = jnp.max(scores, axis=-1, keepdims=True)
    expo = jnp.exp(scores - top)
    total = jnp.sum(expo, axis=-1, keepdims=True)
    probs = (expo / total).astype(BF)
    return jnp.einsum("hqk,hkd->hqd", probs, value, preferred_element_type=F32), top, total


def attend_back(query, key, value, allowed, top, total, grad):
    scores = jnp.einsum("hqd,hkd->hqk", query, key, preferred_element_type=F32) * SCORE_SCALE
    scores = jnp.where(allowed[None], scores, -1e30)
    probs = jnp.exp(scores - top) / total
    probs_low = probs.astype(BF)
    prob_grad = jnp.einsum("hqd,hkd->hqk", grad, value, preferred_element_type=F32)
    offset = jnp.sum(prob_grad * probs, axis=-1, keepdims=True)
    score_grad = (probs * (prob_grad - offset)).astype(BF)
    dq = jnp.einsum("hqk,hkd->hqd", score_grad, key, preferred_element_type=F32) * SCORE_SCALE
    dk = jnp.einsum("hqk,hqd->hkd", score_grad, query, preferred_element_type=F32) * SCORE_SCALE
    dv = jnp.einsum("hqk,hqd->hkd", probs_low, grad, preferred_element_type=F32)
    return dq, dk, dv


def heads_first(values):
    rows, columns = values.shape
    return values.reshape(rows, columns // HD, HD).transpose(1, 0, 2)


def heads_last(values):
    heads, rows, _ = values.shape
    return values.transpose(1, 0, 2).reshape(rows, heads * HD)


MESH_ID = pl.DeviceIdType.MESH


def dyn(start, size, step):
    return pl.ds(pl.multiple_of(start, step), size)


class Links:

    def __init__(self, planes):
        self.planes = planes
        self.p = lax.axis_index("fsdp")
        self.me = lax.axis_index("ctx")

    def plane(self, step):
        return (self.p + step, self.me)

    def peer(self, mask):
        return (self.p, self.me ^ mask)

    def copy(self, src, dst, send, recv, device):
        return pltpu.make_async_remote_copy(
            src_ref=src, dst_ref=dst, send_sem=send, recv_sem=recv, device_id=device, device_id_type=MESH_ID
        )

    def barrier(self, masks):
        bar = pltpu.get_barrier_semaphore()
        for mask in masks:
            pl.semaphore_signal(bar, inc=1, device_id=self.peer(mask), device_id_type=MESH_ID)
        for d in range(1, self.planes):
            to = (lax.rem(self.p + d, self.planes), self.me)
            pl.semaphore_signal(bar, inc=1, device_id=to, device_id_type=MESH_ID)
        pl.semaphore_wait(bar, len(masks) + self.planes - 1)


class LineGather:

    def __init__(self, links, src, slot, sems, local_sem):
        self.links, self.slot, self.sems, self.local_sem = links, slot, sems, local_sem
        self.stays = src is None
        self.src = slot(links.p) if src is None else src

    def send(self, src, block, step):
        way = 1 if step > 0 else 2
        return self.links.copy(
            src, self.slot(block), self.sems.at[way, block], self.sems.at[0, block], self.links.plane(step)
        )

    def arrival(self, block):
        return self.links.copy(
            self.slot(block), self.slot(block), self.sems.at[1, block], self.sems.at[0, block], self.links.plane(0)
        )

    def start(self):
        p, last = self.links.p, self.links.planes - 1

        @pl.when(p < last)
        def _():
            self.send(self.src, p, 1).start()

        @pl.when(p > 0)
        def _():
            self.send(self.src, p, -1).start()

        if not self.stays:
            pltpu.make_async_copy(self.src, self.slot(p), self.local_sem).start()

    def pump(self, d):
        p, last = self.links.p, self.links.planes - 1

        @pl.when(p >= d)
        def _():
            self.arrival(p - d).wait_recv()

            @pl.when(p < last)
            def _():
                self.send(self.slot(p - d), p - d, 1).start()

        @pl.when(p + d <= last)
        def _():
            self.arrival(p + d).wait_recv()

            @pl.when(p > 0)
            def _():
                self.send(self.slot(p + d), p + d, -1).start()

        if d == 1 and not self.stays:
            pltpu.make_async_copy(self.src, self.slot(p), self.local_sem).wait()

    def finish(self):
        p, last = self.links.p, self.links.planes - 1
        for d in range(self.links.planes):

            @pl.when((p >= d) & (p < last))
            def _():
                self.send(self.slot(p - d), p - d, 1).wait_send()

            @pl.when((p + d <= last) & (p > 0))
            def _():
                self.send(self.slot(p + d), p + d, -1).wait_send()


class EdgeGather:

    def __init__(self, links, own, early, buffer, send, recv, local):
        self.links, self.own, self.early, self.buffer = links, own, early, buffer
        self.send_sem, self.recv_sem, self.local = send, recv, local

    def block(self, ref, t):
        return ref.at[208 * t : 208 * t + 208]

    def copy(self, src, t, n, to):
        return self.links.copy(
            src, self.block(self.buffer, t), self.send_sem.at[n], self.recv_sem.at[t], (to, self.links.me)
        )


    def outward(self):
        for p, t, to in ((0, 0, 1), (3, 3, 2)):

            @pl.when(self.links.p == p)
            def _():
                self.copy(self.own, t, 0, to).start()

    def between(self):
        for p, t, to in ((1, 1, 2), (2, 2, 1)):

            @pl.when(self.links.p == p)
            def _():
                self.copy(self.own, t, 0, to).start()

    def finish_early(self):
        for p, came in ((0, ()), (1, (0, 2)), (2, (3, 1)), (3, ())):

            @pl.when(self.links.p == p)
            def _():
                self.copy(self.own, p, 0, p ^ 1).wait_send()
                for t in came:
                    self.copy(self.own, t, 0, p ^ 1).wait_recv()


    def loads(self, p):
        made = [pltpu.make_async_copy(self.own, self.block(self.buffer, p), self.local.at[0])]
        for n, t in enumerate(((), (0, 2), (3, 1), ())[p]):
            made.append(pltpu.make_async_copy(self.block(self.early, t), self.block(self.buffer, t), self.local.at[1 + n]))
        return made

    def sent(self, p, n):
        end, far, near, middle = ((0, 3, 2, 2), (3, 0, 1, 1))[p - 1]
        t, to = ((p, end), (near, end), (end, middle), (far, end))[n]
        src = (self.own, self.early, self.early, self.buffer)[n]
        return self.copy(src if n == 0 else self.block(src, t), t, n, to)

    def start(self):
        for p in range(4):

            @pl.when(self.links.p == p)
            def _():
                for c in self.loads(p):
                    c.start()
                if p in (1, 2):
                    for n in range(3):
                        self.sent(p, n).start()

    def relay(self):
        for p, far in ((1, 3), (2, 0)):

            @pl.when(self.links.p == p)
            def _():
                self.copy(self.own, far, 3, p).wait_recv()
                self.sent(p, 3).start()

    def wait(self):
        for p in range(4):

            @pl.when(self.links.p == p)
            def _():
                for c in self.loads(p):
                    c.wait()
                if p in (0, 3):
                    for t in range(4):
                        if t != p:
                            self.copy(self.own, t, 0, p).wait_recv()

    def finish(self):
        for p in (1, 2):

            @pl.when(self.links.p == p)
            def _():
                for n in range(4):
                    self.sent(p, n).wait_send()


class LineExchange:

    def __init__(self, links, slots, send, recv):
        self.links, self.slots, self.send_sem, self.recv_sem = links, slots, send, recv

    def copy(self, src, d):
        planes = self.links.planes
        to = lax.rem(self.links.p + d, planes)
        return self.links.copy(src, self.slots.at[d - 1], self.send_sem.at[d - 1], self.recv_sem.at[d - 1], (to, self.links.me))

    def start(self, src):
        for d in range(1, self.links.planes):
            self.copy(src, d).start()

    def total(self, src):
        acc = src[...].astype(F32)
        for d in range(1, self.links.planes):
            self.copy(src, d).wait_recv()
            acc = acc + self.slots[d - 1].astype(F32)
        return acc

    def finish(self, src):
        for d in range(1, self.links.planes):
            self.copy(src, d).wait_send()


class SmallGather:

    def __init__(self, links, src, slot, send, recv, local_sem):
        self.links, self.src, self.slot, self.send_sem, self.recv_sem, self.local_sem = links, src, slot, send, recv, local_sem

    def copy(self, owner, mask, n):
        src = self.src if n < 4 else self.slot(owner)
        return self.links.copy(src, self.slot(owner), self.send_sem.at[n], self.recv_sem.at[owner, 0], self.links.peer(mask))

    def start(self):
        for n, mask in enumerate((2, 4, 6, 1)):
            self.copy(self.links.me, mask, n).start()
        pltpu.make_async_copy(self.src, self.slot(self.links.me), self.local_sem).start()

    def forward(self):
        for n, mask in enumerate((2, 4, 6)):
            owner = self.links.me ^ mask
            self.copy(owner, mask, 4 + n).wait_recv()
            self.copy(owner, 1, 4 + n).start()

    def wait(self):
        for mask in (1, 3, 5, 7):
            self.copy(self.links.me ^ mask, 1, 4).wait_recv()

    def finish(self):
        for n in range(7):
            self.copy(self.links.me, 1, n).wait_send()
        pltpu.make_async_copy(self.src, self.slot(self.links.me), self.local_sem).wait()


class GroupGather:

    def __init__(self, links, part, send, recv, src=None, local_sem=None):
        self.links, self.part, self.send_sem, self.recv_sem = links, part, send, recv
        self.src, self.local_sem = src, local_sem

    def copy(self, owner, h, mask, n, src=None):
        return self.links.copy(
            self.part(owner, h) if src is None else src,
            self.part(owner, h),
            self.send_sem.at[n],
            self.recv_sem.at[owner, h],
            self.links.peer(mask),
        )

    def own(self, n):
        h, mask = ((1, 2), (0, 4), (0, 2), (1, 4), (0, 1), (1, 1))[n]
        return self.copy(self.links.me, h, mask, n, None if self.src is None else self.src(h))

    def stay(self, h):
        return pltpu.make_async_copy(self.src(h), self.part(self.links.me, h), self.local_sem.at[h])

    def start(self):
        for n in range(6):
            self.own(n).start()
        if self.src is not None:
            for h in range(2):
                self.stay(h).start()

    def pass_on(self, mask, h, n):
        owner = self.links.me ^ mask
        self.copy(owner, h, 1, n).wait_recv()
        if n < 8:
            self.copy(owner, h, 6 - mask, n).start()
        self.copy(owner, h, 1, n + 2).start()

    def forward(self):
        self.pass_on(2, 1, 6)
        self.pass_on(4, 0, 7)
        self.pass_on(2, 0, 8)
        self.pass_on(4, 1, 9)

    def forward_last(self):
        self.pass_on(6, 0, 10)
        self.pass_on(6, 1, 11)

    def wait(self):
        self.forward_last()
        for mask in (1, 3, 5, 7):
            for h in range(2):
                self.copy(self.links.me ^ mask, h, 1, 6).wait_recv()
        if self.src is not None:
            for h in range(2):
                self.stay(h).wait()

    def finish(self):
        me = self.links.me
        for n in range(6):
            self.own(n).wait_send()
        self.copy(me ^ 2, 1, 1, 6).wait_send()
        self.copy(me ^ 4, 0, 1, 7).wait_send()
        for mask, h, n in ((2, 1, 8), (4, 0, 9), (2, 0, 10), (4, 1, 11), (6, 0, 12), (6, 1, 13)):
            self.copy(me ^ mask, h, 1, n).wait_send()


def row_parts(ref, cut):
    rows = ref.shape[-2]
    return lambda j, h: ref.at[j, 0:cut] if h == 0 else ref.at[j, cut:rows]


def own_parts(ref, cut):
    rows = ref.shape[-2]
    return lambda h: ref.at[0:cut] if h == 0 else ref.at[cut:rows]


class GroupSum:

    def __init__(self, links, stage, from_twin, from_far, send, twin_recv, far_recv):
        self.links, self.stage, self.from_twin, self.from_far = links, stage, from_twin, from_far
        self.send, self.twin_recv, self.far_recv = send, twin_recv, far_recv
        self.rows = stage.shape[1] // 2

    def to_twin(self, chip):
        return self.links.copy(
            self.stage.at[4 + chip], self.from_twin.at[chip], self.send.at[4 + chip], self.twin_recv.at[chip], self.links.peer(1)
        )

    def to_far(self, chip, h, mask):
        at = pl.ds(h * self.rows, self.rows)
        n = 2 * (chip - 1) + h
        return self.links.copy(
            self.stage.at[chip, at], self.from_far.at[chip - 1, at], self.send.at[8 + n], self.far_recv.at[n], self.links.peer(mask)
        )

    def run(self, block):
        me = self.links.me
        masks = (0, 2, 4, 6)
        for chip in (3, 1, 2, 0):
            self.stage[4 + chip] = block(me ^ masks[chip] ^ 1).astype(BF)
            self.to_twin(chip).start()
        for chip in (3, 1, 2):
            part = block(me ^ masks[chip])
            self.to_twin(chip).wait_recv()
            self.stage[chip] = (part + self.from_twin[chip].astype(F32)).astype(BF)
            if chip == 3:
                self.to_far(3, 0, 2).start()
                self.to_far(3, 1, 4).start()
            elif chip == 1:
                self.to_far(1, 0, 2).start()
            else:
                self.to_far(2, 1, 4).start()
        self.stage[0] = block(me).astype(BF)

    def relay(self):
        half = self.rows
        for chip, h, mask in ((2, 0, 4), (1, 1, 2)):
            at = slice(h * half, h * half + half)
            self.to_far(3, h, mask).wait_recv()
            self.stage[chip, at] = (self.stage[chip, at].astype(F32) + self.from_far[2, at].astype(F32)).astype(BF)
            self.to_far(chip, h, mask).start()

    def total(self):
        self.to_twin(0).wait_recv()
        acc = self.stage[0].astype(F32) + self.from_twin[0].astype(F32)
        for chip, mask in ((1, 2), (2, 4)):
            for h in range(2):
                self.to_far(chip, h, mask).wait_recv()
            acc += self.from_far[chip - 1].astype(F32)
        return acc

    def finish(self):
        for chip in range(4):
            self.to_twin(chip).wait_send()
        for chip, h, mask in ((3, 0, 2), (3, 1, 4), (1, 0, 2), (1, 1, 2), (2, 0, 4), (2, 1, 4)):
            self.to_far(chip, h, mask).wait_send()


def gelu_parts(u):
    inner = 0.7978845608 * (u + 0.044715 * (u * u * u))
    t = jnp.tanh(inner)
    value = 0.5 * u * (1.0 + t)
    slope = 0.5 * (1.0 + t) + 0.5 * u * (1.0 - t * t) * (0.7978845608 * (1.0 + 3 * 0.044715 * (u * u)))
    return value, slope


BLOCK_KEYS = (
    ((0, 256, 1),),
    ((0, 256, 0), (256, 256, 1)),
    ((0, 512, 0), (512, 256, 2), (768, 256, 0)),
    ((0, 512, 0), (768, 256, 2)),
)


def triangle(kind, shape):
    r = lax.broadcasted_iota(jnp.int32, shape, 0)
    c = lax.broadcasted_iota(jnp.int32, shape, 1)
    return c <= r if kind == 1 else c >= r


def half_mask(half):
    lane = lax.broadcasted_iota(jnp.int32, (1, 128), 1)
    return (lane // 64) == half


def softmax_pieces(q, keys, values, pieces, allowed):
    scores = []
    for start, size, kind in pieces:
        s = dot_t(q, keys[start : start + size])
        if kind:
            s = jnp.where(allowed(kind, start, s.shape), s, -1e30)
        scores.append(s)
    top = jnp.max(scores[0], axis=1, keepdims=True)
    for s in scores[1:]:
        top = jnp.maximum(top, jnp.max(s, axis=1, keepdims=True))
    total, out = 0.0, 0.0
    for s, (start, size, _) in zip(scores, pieces):
        e = jnp.exp(s - top)
        total = total + jnp.sum(e, axis=1, keepdims=True)
        out = out + dot(e.astype(BF), values[start : start + size])
    return out * (1.0 / total), top + jnp.log(total)


def shift_left(values, lanes):
    return pltpu.roll(values, lax.rem(values.shape[1] - lanes, values.shape[1]), 1)


def small_vectors(parts, p, me):
    wide = 1664
    values = [part[...].astype(F32).reshape(1, part.shape[0]) for part in parts]
    rows = jnp.concatenate([jnp.concatenate(values[:8], axis=0), jnp.zeros((8, wide - 400), F32)], axis=1)
    rows = pltpu.roll(rows, 400 * p, 1)
    mine = shift_left(rows, 192 * me)
    heads = jnp.concatenate([mine[:, :192], rows[:, 1536:1600], jnp.zeros((8, wide - 256), F32)], axis=1)
    n = lax.broadcasted_iota(jnp.int32, (8, 1), 0)
    rows = jnp.where((n == 2) | (n == 3), heads, rows)
    bias = jnp.concatenate([values[8], jnp.zeros((1, wide - 1600), F32)], axis=1)
    bias = shift_left(jnp.broadcast_to(bias, (8, wide)), 200 * me)
    lane = lax.broadcasted_iota(jnp.int32, (1, wide), 1)
    bias = pltpu.roll(jnp.where(lane < 200, bias, 0.0), 208 * p + 8 * lax.rem(me, 2), 1)
    bias = jnp.where(n == 0, bias, 0.0)
    return jnp.concatenate([rows, bias], axis=0).astype(BF)


def attend_kernel(planes, tok, cot, v0, v1, v2, v3, v4, v5, v6, v7, v8, mixer, merge, expand, shrink,
                  hidden_o, qkv_o, att_o, heads_o, vec_o, lse_o,
                  first_o, mw_o, mfull_o, w1_o, sec_o, g_o, w2_o,
                  vpart, raw1, own1, vec, mw0, mw1, mgs, mfull, first_all, second, arecv,
                  zs, zl, w2_s, w2_r, v_s, v_r, gs, gr, gl, gl2, a_s, a_r, os):
    L = Links(planes)
    qkv, attown, hid, lse, att = qkv_o, att_o, hidden_o, lse_o, heads_o
    p, me = L.p, L.me
    share = 400
    xv = LineExchange(L, vec, v_s, v_r)
    zm0 = LineGather(L, None, lambda b: mw0.at[dyn(b * share, share, 16)], zs.at[0], zl.at[0])
    zm1 = LineGather(L, None, lambda b: mw1.at[dyn(b * share, share, 16)], zs.at[1], zl.at[0])
    zmg = LineGather(L, None, lambda b: mgs.at[b], zs.at[2], zl.at[0])
    zw1 = LineGather(L, own1, lambda b: w1_o.at[dyn(b * share, share, 16)], zs.at[3], zl.at[0])
    early = EdgeGather(L, shrink.at[dyn(200 * me - 8 * lax.rem(me, 2), 208, 16)], None, w2_o, w2_s, w2_r, None)
    gfirst = GroupGather(L, lambda j, h: first_all.at[h, j], gs.at[0], gr.at[0])
    gsec = GroupGather(L, row_parts(sec_o, 64), gs.at[1], gr.at[1], own_parts(second, 64), gl)
    gg = GroupGather(L, row_parts(g_o, 64), gs.at[3], gr.at[3], own_parts(cot, 64), gl2)
    gmerge = GroupGather(L, lambda j, h: mfull.at[2 * h : 2 * h + 2, dyn(j * 48, 48, 16)], gs.at[2], gr.at[2])

    takes = [
        pltpu.make_async_copy(merge.at[dyn(me * 48, 48, 16)], mgs.at[p, 0:48], zl.at[1]),
        pltpu.make_async_copy(merge.at[384:400], mgs.at[p, 48:64], zl.at[2]),
        pltpu.make_async_copy(expand, raw1, zl.at[3]),
    ]
    for c in takes:
        c.start()
    vpart[...] = small_vectors((v0, v1, v2, v3, v4, v5, v6, v7, v8), p, me)
    at_own = dyn(p * share, share, 16)

    def head_columns(n):
        odd = lax.rem(n + me, 2)
        x = mixer[:, dyn(D * n + 192 * me - 64 * odd, 256, 128)]
        return jnp.where(odd == 1, jnp.concatenate([x[:, 64:], x[:, :64]], axis=1), x)

    for n in range(3):
        mine = head_columns(n)
        mw0[at_own, 128 * n : 128 * n + 128] = mine[:, :128]
        every = mixer[:, D * n + 1536 : D * n + 1600]
        mw1[at_own, 128 * n : 128 * n + 128] = jnp.concatenate([mine[:, 128:192], every], axis=1)
    L.barrier((1, 2, 3, 4, 5, 6, 7))
    xv.start(vpart)
    zm0.start()
    rows = tok[...].astype(F32)
    normal, _ = normalize(rows)
    vectors = xv.total(vpart)[:, :D]
    first = (normal * vectors[0:1] + vectors[1:2]).astype(BF)
    first_all[:, me] = first.reshape(2, 64, D)
    gfirst.start()
    takes[2].wait()
    odd_me = lax.rem(me, 2)
    lane = lax.broadcasted_iota(jnp.int32, (1, 384), 1)
    for q in range(4):
        start = 1600 * q + 200 * me
        base = jnp.minimum(start // 128 * 128, 6400 - 384)
        x = shift_left(raw1[:, dyn(base, 384, 128)].astype(F32), lax.rem(start - base - 8 * odd_me + 384, 384))
        x = jnp.where((lane >= 8 * odd_me) & (lane < 8 * odd_me + 200), x, 0.0)
        own1[:, 208 * q : 208 * q + 208] = x[:, :208].astype(BF)
    zm0.pump(1)
    zm0.pump(2)
    takes[0].wait()
    takes[1].wait()
    zmg.start()
    gfirst.forward()
    zm0.pump(3)
    zmg.pump(1)
    gfirst.wait()
    zmg.pump(2)
    zm1.start()

    def mix(weights, pair):
        bias_q = vectors[2:3, pair * 128 : pair * 128 + 128]
        bias_v = vectors[3:4, pair * 128 : pair * 128 + 128]

        def body(b, _):
            x = first_all[b // 2, pl.ds((b % 2) * 4, 4)].reshape(256, D)
            mixed = dot(x, weights[...])
            at = dyn(b * 256, 256, 256)
            qkv[pair, at] = (mixed[:, :128] + bias_q).astype(BF)
            qkv[2 + pair, at] = mixed[:, 128:256].astype(BF)
            qkv[4 + pair, at] = (mixed[:, 256:] + bias_v).astype(BF)
            return 0

        lax.fori_loop(0, 4, body, 0)

    lane128 = lax.broadcasted_iota(jnp.int32, (1, 128), 1)

    def note_lse(head, at, value):
        lse[at] = jnp.where(lane128 == head, value, lse[at] if head else 0.0)

    def attend_private(pair, half):
        mask = half_mask(half)
        for b in range(4):
            q = jnp.where(mask, qkv[pair, b * 256 : b * 256 + 256], 0) * jnp.asarray(0.125, BF)
            out, l = softmax_pieces(
                q, qkv.at[2 + pair], qkv.at[4 + pair], BLOCK_KEYS[b], lambda kind, start, shape: triangle(kind, shape)
            )
            out = jnp.where(mask, out, 0.0).astype(BF).reshape(4, 64, 128)
            at = pl.ds((b % 2) * 4, 4)
            if half == 0:
                att[pair, b // 2, at] = out
            else:
                att[pair, b // 2, at] = att[pair, b // 2, at] + out
            note_lse(2 * pair + half, slice(b * 256, b * 256 + 256), l)

    def own_allowed(kind, start, shape):
        r = lax.broadcasted_iota(jnp.int32, shape, 0)
        c = lax.broadcasted_iota(jnp.int32, shape, 1)
        rp = jnp.where(r < 64, me * 64 + r, 1023 - (me * 64 + r - 64))
        cp = jnp.where(c < 512, c, 1023 - (c - 512))
        return cp <= rp

    mix(mw0, 0)
    zmg.pump(3)
    for b in range(4):
        mfull[b, dyn(me * 48, 48, 16)] = mgs[b, 0:48]
        mfull[b, 384:400] = mgs[b, 48:64]
    gmerge.start()
    attend_private(0, 0)
    zm1.pump(1)
    attend_private(0, 1)
    zm1.pump(2)
    zw1.start()
    gmerge.forward()
    gg.start()
    zm1.pump(3)
    mix(mw1, 1)
    outs = [
        pltpu.make_async_copy(first_all, first_o, os.at[0]),
        pltpu.make_async_copy(mw0, mw_o.at[0], os.at[1]),
        pltpu.make_async_copy(mw1, mw_o.at[1], os.at[2]),
        pltpu.make_async_copy(mfull, mfull_o, os.at[3]),
    ]
    for c in outs[:3]:
        c.start()
    attend_private(1, 0)
    qs = jnp.concatenate([qkv[1, dyn(me * 64, 64, 64)], qkv[1, dyn(512 + me * 64, 64, 64)]], axis=0)
    mask1 = half_mask(1)
    qs = jnp.where(mask1, qs, 0) * jnp.asarray(0.125, BF)
    out_s, l_s = softmax_pieces(qs, qkv.at[3], qkv.at[5], ((0, 1024, 1),), own_allowed)
    note_lse(3, slice(0, 128), l_s)
    shared_low = jnp.where(mask1, out_s, 0.0).astype(BF)

    def exchange(mask):
        return L.copy(att.at[:, :, me ^ mask], arecv.at[me], a_s.at[mask], a_r.at[me], L.peer(mask))

    def arrived(mask):
        return L.copy(att.at[:, :, me], arecv.at[me ^ mask], a_s.at[mask], a_r.at[me ^ mask], L.peer(mask))

    for mask in range(1, 8):
        exchange(mask).start()
    arecv[me] = att[:, :, me]
    gg.forward()
    for mask in range(1, 8):
        arrived(mask).wait_recv()
    for j in range(8):
        attown[:, 192 * j : 192 * j + 128] = arecv[j, 0].reshape(128, 128)
        attown[:, 192 * j + 128 : 192 * j + 192] = arecv[j, 1].reshape(128, 128)[:, :64]
    attown[:, 1536:1600] = shared_low[:, 64:128]
    gmerge.wait()
    hidden = rows + vectors[4:5]
    hid[...] = hidden
    for b in range(4):
        hid[...] += dot(attown[:, b * 400 : b * 400 + 400], mfull[b])
    normal2, _ = normalize(hid[...])
    second[...] = (normal2 * vectors[5:6] + vectors[6:7]).astype(BF)
    gsec.start()
    outs[3].start()
    vec_o[...] = vectors
    zw1.pump(1)
    early.outward()
    gg.wait()
    gsec.forward()
    zw1.pump(2)
    early.between()
    gsec.wait()
    zw1.pump(3)
    for c in outs:
        c.wait()
    xv.finish(vpart)
    early.finish_early()
    for z in (zm0, zm1, zmg, zw1):
        z.finish()
    for g in (gfirst, gg, gsec, gmerge):
        g.finish()
    for mask in range(1, 8):
        exchange(mask).wait_send()


def run_attend(planes, tok, cot, vectors, mixer, merge, expand, shrink):
    any_ = pl.BlockSpec(memory_space=pl.ANY)
    vm = pl.BlockSpec(memory_space=pltpu.VMEM)
    S = jax.ShapeDtypeStruct
    V = pltpu.VMEM
    dma = pltpu.SemaphoreType.DMA
    return pl.pallas_call(
        functools.partial(attend_kernel, planes),
        out_shape=(
            S((128, D), F32), S((6, 1024, 128), BF), S((128, D), BF), S((2, 2, 8, 64, 128), BF), S((16, D), F32), S((1024, 128), F32),
            S((2, 8, 64, D), BF), S((2, D, 384), BF), S((4, 400, D), BF), S((D, 832), BF),
            S((8, 128, D), BF), S((8, 128, D), BF), S((832, D), BF),
        ),
        in_specs=[vm] * 12 + [any_] * 3,
        out_specs=(vm,) * 6 + (any_,) * 7,
        scratch_shapes=[
            V((16, 1664), BF), V((400, 6400), BF), V((400, 832), BF), V((3, 16, 1664), BF), V((D, 384), BF), V((D, 384), BF), V((4, 64, D), BF), V((4, 400, D), BF),
            V((2, 8, 64, D), BF), V((128, D), BF), V((8, 2, 2, 64, 128), BF),
            dma((5, 3, 4)), dma((5,)), dma((1,)), dma((4,)), dma((3,)), dma((3,)), dma((4, 14)), dma((4, 8, 2)), dma((2,)), dma((2,)),
            dma((8,)), dma((8,)), dma((4,)),
        ],
        compiler_params=pltpu.CompilerParams(collective_id=0, has_side_effects=True, vmem_limit_bytes=60 << 20),
        cost_estimate=pl.CostEstimate(flops=6_000_000_000, bytes_accessed=60_000_000, transcendentals=4_000_000),
    )(tok, cot, *vectors, mixer, merge, expand, shrink)


class LineSum:

    def __init__(self, links, block, slots, send, recv, near=None, near_sem=None):
        self.links, self.block, self.send_sem, self.recv_sem = links, block, send, recv
        self.slots = slots if callable(slots) else lambda s: slots.at[s]
        self.near, self.near_sem = near, near_sem
        self.last = links.planes - 1

    def send(self, t, step):
        slot = t - 1 if step > 0 else self.left_slot(t)
        return self.links.copy(
            self.block(t), self.slots(slot), self.send_sem.at[t], self.recv_sem.at[slot], self.links.plane(step)
        )

    def left_slot(self, t):
        return (self.last + t) % (self.last + 2)

    def arrival(self, slot):
        return self.links.copy(
            self.slots(slot), self.slots(slot), self.send_sem.at[0], self.recv_sem.at[slot], self.links.plane(0)
        )

    def start(self):
        @pl.when(self.links.p == 0)
        def _():
            for t in range(self.last, 0, -1):
                self.send(t, 1).start()

        @pl.when(self.links.p == self.last)
        def _():
            for t in range(self.last):
                self.send(t, -1).start()

    def add(self, t, slot):
        self.arrival(slot).wait_recv()
        ref = self.block(t)
        came = self.slots(slot)
        if self.near is not None:
            copy = pltpu.make_async_copy(came, self.near, self.near_sem)
            copy.start()
            copy.wait()
            came = self.near
        ref[...] = (ref[...].astype(F32) + came[...].astype(F32)).astype(BF)

    def pump(self, u):
        p, last = self.links.p, self.last
        for t in range(1, last + 1):
            at = u - last + t
            if 0 < at < t:

                @pl.when(p == at)
                def _():
                    self.add(t, t - 1)
                    self.send(t, 1).start()

                @pl.when(p == last - at)
                def _():
                    self.add(last - t, self.left_slot(last - t))
                    self.send(last - t, -1).start()

    def total(self):
        p, last = self.links.p, self.last
        for t in range(last + 1):

            @pl.when(p == t)
            def _():
                if t > 0:
                    self.add(t, t - 1)
                if t < last:
                    self.add(t, self.left_slot(t))

    def finish(self):
        p = self.links.p
        for t in range(self.last + 1):

            @pl.when(p < t)
            def _():
                self.send(t, 1).wait_send()

            @pl.when(p > t)
            def _():
                self.send(t, -1).wait_send()


def backward_kernel(planes, tok, cot, hid, vectors, attown, lse, qkv, att,
                    shrink, w2_h, w1_h, sec_h, g_h, mfull_h, mw_h, first_h,
                    igrad_o, out_o, va_o, vb_o, gw1_o, gw2_o, gm0_o, gm1_o, gmg_o, atts_o, slot_mg,
                    mfull, mw, sec_all, g_all, w1b, w2b, act, slope, dw1, dw2, hlow, agrad, asend, gatt, hc, dkv, mgr, dmerge,
                    slot_w1, slot_w2, slot_m0, slot_m1, near_mg, stage, twin, far, va, vb, vslot,
                    zs, zr, zl, ld, ls_s, ls_r, ve_s, ve_r, gs, gr, gl, a_s, a_r, h_s, h_r, rs_s, rs_t, rs_f, free):
    L = Links(planes)
    p, me = L.p, L.me
    loads = [
        pltpu.make_async_copy(w1_h, w1b, ld.at[0]),
        pltpu.make_async_copy(sec_h, sec_all, ld.at[1]),
        pltpu.make_async_copy(g_h, g_all, ld.at[7]),
        pltpu.make_async_copy(mfull_h, mfull, ld.at[2]),
        pltpu.make_async_copy(mw_h, mw, ld.at[3]),
    ]
    att_all, first_all = g_all, sec_all
    late_att = pltpu.make_async_copy(atts_o, att_all, ld.at[5])
    late_first = pltpu.make_async_copy(first_h, first_all, ld.at[6])
    for c in loads:
        c.start()
    zw2 = EdgeGather(L, shrink.at[dyn(200 * me - 8 * lax.rem(me, 2), 208, 16)], w2_h, w2b, zs, zr, zl)
    cut2 = 768

    def shrink_line(n, first, last):
        return LineSum(
            L, lambda t: dw2.at[dyn(t * 208, 208, 16), first:last], lambda s: slot_w2.at[s, :, first:last], ls_s.at[n], ls_r.at[n]
        )

    lw2a, lw2b = shrink_line(0, 0, cut2), shrink_line(5, cut2, D)
    lw1 = LineSum(L, lambda t: dw1.at[dyn(t * 400, 400, 16)], slot_w1, ls_s.at[1], ls_r.at[1])
    lm0 = LineSum(L, lambda t: w1b.at[dyn(t * 400, 400, 16), 0:384], slot_m0, ls_s.at[2], ls_r.at[2])
    lm1 = LineSum(L, lambda t: w1b.at[dyn(t * 400, 400, 16), 384:768], slot_m1, ls_s.at[3], ls_r.at[3])
    lmg = LineSum(L, lambda t: dmerge.at[dyn(t * 400, 400, 16)], slot_mg, ls_s.at[4], ls_r.at[4], near_mg, ld.at[4])
    xa = LineExchange(L, vslot.at[0], ve_s.at[0], ve_r.at[0])
    xb = LineExchange(L, vslot.at[1], ve_s.at[1], ve_r.at[1])
    gatt_all = GroupGather(L, row_parts(atts_o, 64), gs.at[1], gr.at[1], own_parts(attown, 64), gl.at[1])

    def shrink_gather(n, first, last):
        sizes = (112, 96)

        def part(j, h):
            return gw2_o.at[j, 112 * h : 112 * h + sizes[h], first:last]

        def src(h):
            return dw2.at[dyn(p * 208 + 112 * h, sizes[h], 16), first:last]

        return GroupGather(L, part, gs.at[n], gr.at[n], src, gl.at[n])

    gw2a, gw2b = shrink_gather(0, 0, cut2), shrink_gather(2, cut2, D)
    def share_gather(n, out, line):
        def src(h):
            base, columns = line.home
            return base.at[dyn(p * 400 + 208 * h, (208, 192)[h], 16), columns[0] : columns[1]]

        return GroupGather(L, row_parts(out, 208), gs.at[n], gr.at[n], src, gl.at[n])

    lw1.home, lm0.home, lm1.home, lmg.home = (dw1, (0, 832)), (w1b, (0, 384)), (w1b, (384, 768)), (dmerge, (0, 256))
    gw1 = share_gather(3, gw1_o, lw1)
    gm0 = share_gather(4, gm0_o, lm0)
    gm1 = share_gather(5, gm1_o, lm1)
    gmg = share_gather(6, gmg_o, lmg)
    gva = SmallGather(L, va, lambda j: va_o.at[j], gs.at[7], gr.at[7], gl.at[7, 0])
    gvb = SmallGather(L, vb, lambda j: vb_o.at[j], gs.at[8], gr.at[8], gl.at[8, 0])
    L.barrier((1, 2, 3, 4, 5, 6, 7))
    zw2.start()
    gatt_all.start()

    loads[0].wait()
    loads[1].wait()

    def expand(b, _):
        at = dyn(b * 256, 256, 256)
        pre = dot(sec_all[pl.ds(2 * b, 2)].reshape(256, D), w1b[...]) + vectors[8:9, :832]
        value, s = gelu_parts(pre)
        act[at] = value.astype(BF)
        slope[at] = s.astype(BF)
        return 0

    lax.fori_loop(0, 4, expand, 0)
    loads[2].wait()
    g2 = g_all[...].reshape(1024, D)
    for part, columns in ((lw2a, slice(0, cut2)), (lw2b, slice(cut2, D))):
        for start, size in ((0, 256), (256, 256), (512, 256), (768, 64)):
            dw2[start : start + size, columns] = t_dot(act[:, start : start + size], g2[:, columns]).astype(BF)
        if part is lw2a:
            lw2a.start()
    zw2.relay()
    gatt_all.forward()
    lw2a.pump(1)
    gatt_all.wait()
    lw2a.pump(2)
    lw2b.start()
    zw2.wait()

    def contract(b, acc):
        at = dyn(b * 256, 256, 256)
        grad = dot_t(g_all[pl.ds(2 * b, 2)].reshape(256, D), w2b[...]) * slope[at].astype(F32)
        slope[at] = grad.astype(BF)
        return acc + jnp.sum(grad, axis=0, keepdims=True)

    dgb = lax.fori_loop(0, 4, contract, jnp.zeros((1, 832), F32))
    late_att.start()
    rounds = [GroupSum(L, stage, twin, far, rs_s.at[n], rs_t.at[n], rs_f.at[n]) for n in range(3)]

    def release(n):
        for mask in (1, 2, 4):
            pl.semaphore_signal(free.at[n], inc=1, device_id=L.peer(mask), device_id_type=MESH_ID)

    back = rounds[0]
    back.run(lambda owner: dot_t(slope[dyn(owner * 128, 128, 128)], w1b[...]))
    lw2b.pump(1)
    for start in range(0, D, 256):
        size = min(256, D - start)
        x = sec_all[:, :, start : start + size].reshape(1024, size)
        dw1[start : start + size] = t_dot(x, slope[...]).astype(BF)
    late_first.start()
    lw1.start()
    back.relay()
    lw2b.pump(2)
    lw2a.total()
    gw2a.start()
    grad2 = back.total()
    back.finish()
    release(0)

    tangent = cot[...].astype(F32)
    normal2, inverse2 = normalize(hid[...])
    hidden_grad = tangent + norm_back(grad2, vectors[5:6], normal2, inverse2)
    igrad_o[...] = hidden_grad
    hlow[:, 0:D] = hidden_grad.astype(BF)
    hlow[:, D:2048] = jnp.zeros((128, 2048 - D), BF)
    va[0:1] = jnp.sum(hidden_grad, axis=0, keepdims=True)
    va[1:2] = jnp.sum(grad2 * normal2, axis=0, keepdims=True)
    va[2:3] = jnp.sum(grad2, axis=0, keepdims=True)
    va[3:4] = jnp.sum(tangent, axis=0, keepdims=True)
    va[4:8] = jnp.zeros((4, D), F32)
    va[4:5, 0:832] = dgb

    def columns(mask):
        to = me ^ mask
        return L.copy(hlow.at[:, dyn(to * 256, 256, 256)], hc.at[me], h_s.at[mask], h_r.at[me], L.peer(mask))

    def columns_in(mask):
        return L.copy(hc.at[me], hc.at[me ^ mask], h_s.at[mask], h_r.at[me ^ mask], L.peer(mask))

    loads[3].wait()
    agrad[...] = dot_t(hlow[:, 0:D], mfull[...]).astype(BF)
    for j in range(8):
        asend[j, 0] = agrad[:, 192 * j : 192 * j + 128].reshape(2, 64, 128)
        tail = agrad[:, 192 * j + 128 : 192 * j + 192]
        asend[j, 1] = jnp.concatenate([tail, jnp.zeros((128, 64), BF)], axis=1).reshape(2, 64, 128)

    def exchange(mask):
        return L.copy(asend.at[me ^ mask], gatt.at[:, :, me], a_s.at[mask], a_r.at[me], L.peer(mask))

    def arrived(mask):
        return L.copy(asend.at[me], gatt.at[:, :, me ^ mask], a_s.at[mask], a_r.at[me ^ mask], L.peer(mask))

    for mask in range(1, 8):
        exchange(mask).start()
    gatt[:, :, me] = asend[me]
    for mask in range(1, 8):
        columns(mask).start()
    pl.semaphore_wait(free.at[0], 3)
    outs = rounds[1]
    outs.run(lambda owner: dot(act[dyn(owner * 128, 128, 128)], w2b[...]))
    hc[me] = hlow[:, dyn(me * 256, 256, 256)]
    dkv[...] = jnp.zeros(dkv.shape, F32)
    for mask in range(1, 8):
        arrived(mask).wait_recv()

    scale = jnp.asarray(0.125, BF)

    def head_back(pair, head, mask, q, g, o, stat, pieces, allowed):
        delta = jnp.sum(g.astype(F32) * o.astype(F32), axis=1, keepdims=True)
        dq = 0.0
        for start, size, kind in pieces:
            keys = qkv[2 + pair, start : start + size]
            s = dot_t(q, keys)
            if kind:
                s = jnp.where(allowed(kind, start, s.shape), s, -1e30)
            prob = jnp.exp(s - stat)
            ds = (prob * (dot_t(g, qkv[4 + pair, start : start + size]) - delta)).astype(BF)
            dq = dq + dot(ds, keys)
            dkv[0, start : start + size] += t_dot(ds, q)
            dkv[1, start : start + size] += t_dot(prob.astype(BF), g)
        return jnp.where(mask, dq, 0.0) * 0.125

    def private_back(pair, half):
        mask = half_mask(half)
        head = 2 * pair + half
        total = 0.0
        for b in range(4):
            at = slice(b * 256, b * 256 + 256)
            blk = (pair, b // 2, pl.ds((b % 2) * 4, 4))
            q = jnp.where(mask, qkv[pair, at], 0) * scale
            g = jnp.where(mask, gatt[blk].reshape(256, 128), 0)
            o = att[blk].reshape(256, 128)
            dq = head_back(
                pair, head, mask, q, g, o, lse[at, head : head + 1], BLOCK_KEYS[b],
                lambda kind, start, shape: triangle(kind, shape),
            )
            total = total + jnp.sum(dq, axis=0, keepdims=True)
            if half == 0:
                mgr[pair, at, 0:128] = dq.astype(BF)
            else:
                mgr[pair, at, 0:128] = mgr[pair, at, 0:128] + dq.astype(BF)
        return total

    def mixer_part(pair):
        mgr[pair, :, 128:256] = dkv[0].astype(BF)
        mgr[pair, :, 256:384] = dkv[1].astype(BF)
        va[6:7, pair * 128 : pair * 128 + 128] = jnp.sum(dkv[1], axis=0, keepdims=True)
        for start in range(0, D, 256):
            size = min(256, D - start)
            x = first_all[:, :, start : start + size].reshape(1024, size)
            w1b[start : start + size, 384 * pair : 384 * pair + 384] = t_dot(x, mgr[pair]).astype(BF)

    qb0 = private_back(0, 0)
    gw2a.forward()
    qb0 = qb0 + private_back(0, 1)
    va[5:6, 0:128] = qb0
    late_first.wait()
    mixer_part(0)
    dkv[...] = jnp.zeros(dkv.shape, F32)
    lm0.start()
    outs.relay()
    lw2b.total()
    gw2b.start()
    qb1 = private_back(1, 0)
    mask1 = half_mask(1)
    own_early, own_late = dyn(me * 64, 64, 64), dyn(512 + me * 64, 64, 64)
    qs = jnp.concatenate([qkv[1, own_early], qkv[1, own_late]], axis=0)
    qs = jnp.where(mask1, qs, 0) * scale
    blank = jnp.zeros((128, 64), BF)
    g_s = jnp.concatenate([blank, agrad[:, 1536:1600]], axis=1)
    o_s = jnp.concatenate([blank, attown[:, 1536:1600]], axis=1)

    def own_allowed(kind, start, shape):
        r = lax.broadcasted_iota(jnp.int32, shape, 0)
        c = lax.broadcasted_iota(jnp.int32, shape, 1) + start
        rp = jnp.where(r < 64, me * 64 + r, 1023 - (me * 64 + r - 64))
        cp = jnp.where(c < 512, c, 1023 - (c - 512))
        return cp <= rp

    dqs = head_back(1, 3, mask1, qs, g_s, o_s, lse[0:128, 3:4], ((0, 512, 1), (512, 512, 1)), own_allowed)
    va[5:6, 128:256] = qb1 + jnp.sum(dqs, axis=0, keepdims=True)
    dqs_low = dqs.astype(BF)
    mgr[1, own_early, 0:128] = mgr[1, own_early, 0:128] + dqs_low[:64]
    mgr[1, own_late, 0:128] = mgr[1, own_late, 0:128] + dqs_low[64:]
    mixer_part(1)
    lm1.start()
    xa.start(va)
    lw1.pump(1)
    out_o[...] = (outs.total() + hid[...] + vectors[7:8]).astype(BF)
    outs.finish()
    release(1)
    loads[4].wait()
    pl.semaphore_wait(free.at[1], 3)
    sums = rounds[2]

    def first_block(owner):
        early, late = dyn(owner * 64, 64, 64), dyn(512 + owner * 64, 64, 64)
        x0 = jnp.concatenate([mgr[0, early], mgr[0, late]], axis=0)
        x1 = jnp.concatenate([mgr[1, early], mgr[1, late]], axis=0)
        return dot_t(x0, mw[0]) + dot_t(x1, mw[1])

    sums.run(first_block)
    gw2b.forward()
    lw1.pump(2)
    sums.relay()
    lw1.total()
    gw1.start()
    lm0.pump(1)
    late_att.wait()
    for mask in range(1, 8):
        columns_in(mask).wait_recv()
    h2 = hc[...].reshape(1024, 256)
    for start in range(0, D, 256):
        size = min(256, D - start)
        x = att_all[:, :, start : start + size].reshape(1024, size)
        dmerge[start : start + size] = t_dot(x, h2).astype(BF)
    lmg.start()
    lm0.pump(2)
    first_grad = sums.total()
    rows = tok[...].astype(F32)
    normal1, inverse1 = normalize(rows)
    igrad_o[...] += norm_back(first_grad, vectors[0:1], normal1, inverse1)
    vb[0:1] = jnp.sum(first_grad * normal1, axis=0, keepdims=True)
    vb[1:2] = jnp.sum(first_grad, axis=0, keepdims=True)
    vb[2:8] = jnp.zeros((6, D), F32)
    xb.start(vb)
    lm0.total()
    gm0.start()
    lm1.pump(1)
    gw1.forward()
    lm1.pump(2)
    gm0.forward()
    lm1.total()
    gm1.start()
    lmg.pump(1)
    total_a = xa.total(va)
    xa.finish(va)
    va[...] = total_a
    gva.start()
    lmg.pump(2)
    total_b = xb.total(vb)
    xb.finish(vb)
    vb[...] = total_b
    gvb.start()
    lmg.total()
    gmg.start()
    gm1.forward()
    gva.forward()
    gvb.forward()
    gmg.forward()
    for g in (gw2a, gw2b, gva, gw1, gvb, gm0, gm1, gmg):
        g.wait()
    for g in (gatt_all, gw2a, gw2b, gw1, gm0, gm1, gmg, gva, gvb):
        g.finish()
    zw2.finish()
    for s in (lw2a, lw2b, lw1, lm0, lm1, lmg):
        s.finish()
    for mask in range(1, 8):
        exchange(mask).wait_send()
        columns(mask).wait_send()
    sums.finish()


def run_backward(planes, *operands):
    any_ = pl.BlockSpec(memory_space=pl.ANY)
    vm = pl.BlockSpec(memory_space=pltpu.VMEM)
    S = jax.ShapeDtypeStruct
    V = pltpu.VMEM
    dma = pltpu.SemaphoreType.DMA
    return pl.pallas_call(
        functools.partial(backward_kernel, planes),
        out_shape=(
            S((128, D), F32), S((128, D), BF), S((8, 8, D), F32), S((8, 8, D), F32), S((8, 400, 832), BF), S((8, 208, D), BF),
            S((8, 400, 384), BF), S((8, 400, 384), BF), S((8, 400, 256), BF), S((8, 128, D), BF),
            S((5, 400, 256), BF),
        ),
        in_specs=[vm] * 8 + [any_] * 8,
        out_specs=(vm,) * 2 + (any_,) * 9,
        scratch_shapes=[
            V((D, D), BF), V((2, D, 384), BF), V((8, 128, D), BF), V((8, 128, D), BF), V((D, 832), BF), V((832, D), BF),
            V((1024, 832), BF), V((1024, 832), BF), V((D, 832), BF), V((832, D), BF),
            V((128, 2048), BF), V((128, D), BF), V((8, 2, 2, 64, 128), BF), V((2, 2, 8, 64, 128), BF),
            V((8, 128, 256), BF), V((2, 1024, 128), F32), V((2, 1024, 384), BF), V((D, 256), BF),
            V((5, 400, 832), BF), V((5, 208, D), BF), V((5, 400, 384), BF), V((5, 400, 384), BF), V((400, 256), BF),
            V((8, 128, D), BF), V((4, 128, D), BF), V((3, 128, D), BF), V((8, D), F32), V((8, D), F32), V((2, 3, 8, D), F32),
            dma((4,)), dma((4,)), dma((3,)), dma((8,)), dma((6, 4)), dma((6, 5)), dma((2, 3)), dma((2, 3)), dma((9, 14)), dma((9, 8, 2)), dma((9, 2)),
            dma((8,)), dma((8,)), dma((8,)), dma((8,)), dma((3, 14)), dma((3, 4)), dma((3, 6)), pltpu.SemaphoreType.REGULAR((2,)),
        ],
        compiler_params=pltpu.CompilerParams(collective_id=1, has_side_effects=True, vmem_limit_bytes=(64 << 20) - 65536),
        cost_estimate=pl.CostEstimate(flops=25_000_000_000, bytes_accessed=60_000_000, transcendentals=4_000_000),
    )(*operands)


def assemble_kernel(gw1, gm0, gm1, gmg, gw2, va, vb, input_grad, output,
                    expand_o, mixer_o, merge_o, shrink_o, input_o, output_o, *vectors_o):
    step = pl.program_id(0)

    @pl.when(step < 5)
    def _():
        assemble_rows(gw1, gm0, gm1, gmg, expand_o, mixer_o, merge_o)

    for odd in range(2):

        @pl.when((step >= 5) & (lax.rem(step, 2) == 1 - odd))
        def _():
            shrink_o[...] = gw2[0, 8 * odd : 8 * odd + 200].astype(F32)

    @pl.when(step == 0)
    def _():
        input_o[...] = input_grad[...]
        output_o[...] = output[...]
        assemble_vectors(va, vb, vectors_o)


def assemble_rows(gw1, gm0, gm1, gmg, expand_o, mixer_o, merge_o):
    for j in range(8):
        odd = 8 * (j % 2)
        for q in range(4):
            at = 1600 * q + 200 * j
            expand_o[:, at : at + 200] = gw1[j, :, 208 * q + odd : 208 * q + odd + 200].astype(F32)
        for n in range(3):
            at = D * n + 192 * j
            mixer_o[:, at : at + 128] = gm0[j, :, 128 * n : 128 * n + 128].astype(F32)
            mixer_o[:, at + 128 : at + 192] = gm1[j, :, 128 * n : 128 * n + 64].astype(F32)
    for n in range(3):
        total = gm1[0, :, 128 * n : 128 * n + 128].astype(F32)
        for j in range(1, 8):
            total += gm1[j, :, 128 * n : 128 * n + 128].astype(F32)
        mixer_o[:, D * n + 1536 : D * n + 1600] = total[:, 64:]
    for j in range(6):
        merge_o[:, 256 * j : 256 * j + 256] = gmg[j].astype(F32)
    merge_o[:, 1536:1600] = gmg[6, :, :64].astype(F32)


def assemble_vectors(va, vb, vectors_o):
    p = lax.axis_index("fsdp")
    early, late = va[0], vb[0]
    for j in range(1, 8):
        early += va[j]
        late += vb[j]

    def per_head(n):
        return jnp.concatenate([va[j, n : n + 1, :192] for j in range(8)] + [early[n : n + 1, 192:256]], axis=1)

    rows = jnp.concatenate(
        [late[0:2], per_head(5), per_head(6), early[0:4]], axis=0
    )
    rows = jnp.concatenate([rows, jnp.zeros((8, 64), F32)], axis=1)
    rows = shift_left(rows, 400 * p)
    bias = jnp.concatenate([va[j, 4:5, :] for j in range(8)], axis=0)
    bias = shift_left(jnp.concatenate([bias, jnp.zeros((8, 64), F32)], axis=1), 208 * p)
    bias = jnp.concatenate([bias[j : j + 1, 8 * (j % 2) : 8 * (j % 2) + 200] for j in range(8)], axis=1)
    for n in range(8):
        vectors_o[n][...] = rows[n, :400]
    vectors_o[8][...] = bias[0]


def assemble(gw1, gm0, gm1, gmg, gw2, va, vb, input_grad, output):
    rows, first = 80, 5

    def part(width):
        return pl.BlockSpec((8, rows, width), lambda n: (0, jnp.minimum(n, first - 1), 0))

    def whole(width):
        return pl.BlockSpec((rows, width), lambda n: (jnp.minimum(n, first - 1), 0))

    own = pl.BlockSpec((128, D), lambda n: (0, 0))
    small = pl.BlockSpec((8, 8, D), lambda n: (0, 0, 0))

    def vector(width):
        return pl.BlockSpec((width,), lambda n: (0,))

    S = jax.ShapeDtypeStruct
    return pl.pallas_call(
        assemble_kernel,
        grid=(first + 8,),
        in_specs=[part(832), part(384), part(384), part(256), pl.BlockSpec((1, 208, D), lambda n: (jnp.maximum(n - first, 0), 0, 0)), small, small, own, own],
        out_specs=(whole(6400), whole(4800), whole(D), pl.BlockSpec((200, D), lambda n: (jnp.maximum(n - first, 0), 0)), own, own) + (vector(400),) * 8 + (vector(1600),),
        out_shape=(S((400, 6400), F32), S((400, 4800), F32), S((400, D), F32), S((1600, D), F32), S((128, D), F32), S((128, D), BF)) + (S((400,), F32),) * 8 + (S((1600,), F32),),
        compiler_params=pltpu.CompilerParams(vmem_limit_bytes=63 << 20),
    )(gw1, gm0, gm1, gmg, gw2, va, vb, input_grad, output)


def local_plain(
    tokens,
    first_gain,
    first_shift,
    mixer_weight,
    query_bias,
    value_bias,
    merge_weight,
    merge_bias,
    second_gain,
    second_shift,
    expand_weight,
    expand_bias,
    shrink_weight,
    shrink_bias,
    cotangent,
):
    planes = lax.axis_size("fsdp")
    ring = lax.axis_size("ctx")
    me = lax.axis_index("ctx")
    blocks = tokens.shape[2]
    local_rows = 2 * blocks
    half = blocks * ring
    length = 2 * half
    private = H // ring
    shared = H - private * ring
    pc, sc = private * HD, shared * HD
    hc = pc + sc
    shared_at = private * ring * HD
    share = D // planes
    ff_plane = expand_bias.shape[0]
    ff_part = ff_plane // ring
    cols = D // ring

    vectors = jnp.stack(
        [first_gain, first_shift, query_bias, value_bias, merge_bias, second_gain, second_shift, shrink_bias]
    )
    vectors = lax.all_gather(vectors, "fsdp", axis=1, tiled=True).astype(F32)
    gain1, shift1, qbias, vbias, mbias, gain2, shift2, sbias = [vectors[n] for n in range(8)]

    def head_columns(weight, base):
        mine = lax.dynamic_slice_in_dim(weight, base + me * pc, pc, weight.ndim - 1)
        every = weight[..., base + shared_at : base + D]
        return [mine, every]

    mixer_part = jnp.concatenate(
        head_columns(mixer_weight, 0) + head_columns(mixer_weight, D) + head_columns(mixer_weight, 2 * D), axis=1
    )
    mixer_mine = lax.all_gather(mixer_part, "fsdp", axis=0, tiled=True)

    merge_part = lax.dynamic_slice_in_dim(merge_weight, me * cols, cols, 1)
    merge_cols = lax.all_gather(merge_part, "fsdp", axis=0, tiled=True)
    merge_full = lax.all_gather(merge_cols, "ctx", axis=1, tiled=True)

    expand_part = expand_weight.reshape(share, planes, ring, ff_part)
    expand_part = lax.dynamic_index_in_dim(expand_part, me, 2, keepdims=False)
    expand_part = lax.all_to_all(expand_part, "fsdp", 1, 0, tiled=False).reshape(D, ff_part)
    expand_mine = lax.all_gather(expand_part, "ctx", axis=1, tiled=True)

    rows = tokens.reshape(local_rows, D).astype(F32)
    normal1, inverse1 = normalize(rows)
    first = (normal1 * gain1 + shift1).astype(BF)
    first_all = lax.all_gather(first.reshape(2, blocks, D), "ctx", axis=1, tiled=True).reshape(length, D)
    tangent_low = cotangent.reshape(local_rows, D)
    tangent = tangent_low.astype(F32)
    tangent_all = lax.all_gather(tangent_low, "fsdp", axis=0, tiled=True)

    mixed = dot(first_all, mixer_mine)
    qb = jnp.concatenate(head_columns(qbias, 0), axis=0)
    vb = jnp.concatenate(head_columns(vbias, 0), axis=0)
    query = (mixed[:, :hc] + qb).astype(BF)
    key = mixed[:, hc : 2 * hc].astype(BF)
    value = (mixed[:, 2 * hc :] + vb).astype(BF)
    half_index = jnp.arange(half, dtype=jnp.int32)
    place = jnp.concatenate([half_index, length - 1 - half_index])
    early = me * blocks + jnp.arange(blocks, dtype=jnp.int32)
    own_place = jnp.concatenate([early, length - 1 - early])
    allowed = place[None, :] <= place[:, None]
    own_allowed = place[None, :] <= own_place[:, None]

    def own_rows(values):
        parts = values.reshape(2, half, values.shape[1])
        return lax.dynamic_slice_in_dim(parts, me * blocks, blocks, 1).reshape(local_rows, values.shape[1])

    qp, kp, vp = heads_first(query[:, :pc]), heads_first(key[:, :pc]), heads_first(value[:, :pc])
    qs, ks, vs = heads_first(own_rows(query[:, pc:])), heads_first(key[:, pc:]), heads_first(value[:, pc:])
    out_p, top_p, total_p = attend(qp, kp, vp, allowed)
    out_s, top_s, total_s = attend(qs, ks, vs, own_allowed)
    att_heads = heads_last(out_p).astype(BF)
    att_pieces = lax.all_to_all(att_heads.reshape(2, ring, blocks, pc), "ctx", 1, 2, tiled=False)
    attended = jnp.concatenate(
        [att_pieces.reshape(local_rows, ring * pc), heads_last(out_s).astype(BF)], axis=1
    )
    hidden = rows + dot(attended, merge_full) + mbias
    normal2, inverse2 = normalize(hidden)
    second = (normal2 * gain2 + shift2).astype(BF)
    second_all = lax.all_gather(second, "fsdp", axis=0, tiled=True)
    attended_all = lax.all_gather(attended, "ctx", axis=0, tiled=True)

    pre = dot(second_all, expand_mine) + expand_bias.astype(F32)
    act, gate_pull = jax.vjp(lambda u: jax.nn.gelu(u, approximate=True), pre)
    act_low = act.astype(BF)
    act_grad = dot_t(tangent_all, shrink_weight)
    (pre_grad,) = gate_pull(act_grad)
    pre_low = pre_grad.astype(BF)
    second_part = dot_t(pre_low, expand_mine).astype(BF)
    second_grad = lax.psum_scatter(second_part, "fsdp", scatter_dimension=0, tiled=True).astype(F32)
    out_part = dot(act_low, shrink_weight).astype(BF)
    out_sum = lax.psum_scatter(out_part, "fsdp", scatter_dimension=0, tiled=True).astype(F32)
    output = (hidden + out_sum + sbias).astype(BF).reshape(1, 2, blocks, D)
    expand_bias_grad = jnp.sum(pre_grad, axis=0)
    shrink_grad = t_dot(act_low, tangent_all).astype(BF)
    shrink_mine = lax.psum_scatter(shrink_grad, "ctx", scatter_dimension=0, tiled=True)
    shrink_owned = lax.all_gather(shrink_mine, "ctx", axis=0, tiled=True).astype(F32)
    expand_grad = t_dot(second_all, pre_low).astype(BF)
    expand_cols = lax.psum_scatter(expand_grad, "ctx", scatter_dimension=1, tiled=True)
    expand_rows = lax.all_to_all(expand_cols.reshape(planes, share, ff_part), "fsdp", 0, 1, tiled=False)
    expand_owned = (
        lax.all_gather(expand_rows, "ctx", axis=2, tiled=False).reshape(share, planes * ff_plane).astype(F32)
    )

    hidden_grad = tangent + norm_back(second_grad, gain2, normal2, inverse2)
    hidden_low = hidden_grad.astype(BF)
    att_grad = dot_t(hidden_low, merge_full).astype(BF)
    grad_pieces = lax.all_to_all(att_grad[:, :shared_at].reshape(2, blocks, ring, pc), "ctx", 2, 1, tiled=False)
    grad_p = heads_first(grad_pieces.reshape(length, pc))
    grad_s = heads_first(att_grad[:, shared_at:])
    dqp, dkp, dvp = attend_back(qp, kp, vp, allowed, top_p, total_p, grad_p)
    dqs, dks, dvs = attend_back(qs, ks, vs, own_allowed, top_s, total_s, grad_s)
    dqs_all = jnp.zeros((2, half, sc), F32)
    dqs_all = lax.dynamic_update_slice_in_dim(dqs_all, heads_last(dqs).reshape(2, blocks, sc), me * blocks, 1)
    mixed_grad = jnp.concatenate(
        [heads_last(dqp), dqs_all.reshape(length, sc)]
        + [heads_last(dkp), heads_last(dks), heads_last(dvp), heads_last(dvs)],
        axis=1,
    )
    bias_sums = jnp.sum(mixed_grad, axis=0)
    mixed_low = mixed_grad.astype(BF)
    first_part = dot_t(mixed_low, mixer_mine).astype(BF)
    first_grad = lax.psum_scatter(
        first_part.reshape(2, half, D), "ctx", scatter_dimension=1, tiled=True
    ).reshape(local_rows, D).astype(F32)
    input_grad = hidden_grad + norm_back(first_grad, gain1, normal1, inverse1)
    mixer_part_grad = t_dot(first_all, mixed_low).astype(BF)
    mixer_rows = lax.psum_scatter(mixer_part_grad, "fsdp", scatter_dimension=0, tiled=True)
    mixer_all = lax.all_gather(mixer_rows, "ctx", axis=0, tiled=False).astype(F32)

    def place_columns(values):
        mine = values[:, :, :pc].transpose(1, 0, 2).reshape(share, ring * pc)
        return [mine, jnp.sum(values[:, :, pc:], axis=0)]

    mixer_owned = jnp.concatenate(
        place_columns(mixer_all[:, :, :hc])
        + place_columns(mixer_all[:, :, hc : 2 * hc])
        + place_columns(mixer_all[:, :, 2 * hc :]),
        axis=1,
    )
    hidden_cols = lax.all_to_all(hidden_low.reshape(local_rows, ring, cols), "ctx", 1, 0, tiled=False)
    merge_grad = t_dot(attended_all, hidden_cols.reshape(length, cols)).astype(BF)
    merge_rows = lax.psum_scatter(merge_grad, "fsdp", scatter_dimension=0, tiled=True)
    merge_owned = lax.all_gather(merge_rows, "ctx", axis=1, tiled=True).astype(F32)

    def spread_bias(values):
        full = jnp.zeros((D,), F32)
        full = lax.dynamic_update_slice_in_dim(full, values[:pc], me * pc, 0)
        return full.at[shared_at:].set(values[pc:])

    sums = jnp.stack(
        [
            jnp.sum(first_grad * normal1, axis=0),
            jnp.sum(first_grad, axis=0),
            spread_bias(bias_sums[:hc]),
            spread_bias(bias_sums[2 * hc :]),
            jnp.sum(hidden_grad, axis=0),
            jnp.sum(second_grad * normal2, axis=0),
            jnp.sum(second_grad, axis=0),
            jnp.sum(tangent, axis=0),
        ]
    )
    sums = lax.psum(sums, ("fsdp", "ctx"))
    mine = lax.dynamic_slice_in_dim(sums, lax.axis_index("fsdp") * share, share, 1)
    expand_bias_owned = lax.psum(expand_bias_grad, "ctx")

    return (
        output,
        input_grad.reshape(1, 2, blocks, D),
        mine[0],
        mine[1],
        mixer_owned,
        mine[2],
        mine[3],
        merge_owned,
        mine[4],
        mine[5],
        mine[6],
        expand_owned,
        expand_bias_owned,
        shrink_owned,
        mine[7],
    )


def local_kernel(
    tokens,
    first_gain,
    first_shift,
    mixer_weight,
    query_bias,
    value_bias,
    merge_weight,
    merge_bias,
    second_gain,
    second_shift,
    expand_weight,
    expand_bias,
    shrink_weight,
    shrink_bias,
    cotangent,
):
    planes = lax.axis_size("fsdp")
    blocks, local_rows = tokens.shape[2], 2 * tokens.shape[2]
    vectors = (
        first_gain, first_shift, query_bias, value_bias, merge_bias, second_gain, second_shift, shrink_bias, expand_bias
    )

    tok2, cot2 = tokens.reshape(local_rows, D), cotangent.reshape(local_rows, D)
    hidden, qkv, attown, heads, whole, lse, first_all, mws, mfull, w1_all, sec_all, g_all, w2_early = run_attend(
        planes, tok2, cot2, vectors, mixer_weight, merge_weight, expand_weight, shrink_weight
    )
    input_part, out_part, va, vb, gw1, gw2, gm0, gm1, gmg, _, _ = run_backward(
        planes, tok2, cot2, hidden, whole, attown, lse, qkv, heads,
        shrink_weight, w2_early, w1_all, sec_all, g_all, mfull.reshape(D, D), mws, first_all.reshape(8, 128, D)
    )
    expand_owned, mixer_owned, merge_owned, shrink_owned, input_grad, out_own, *small = assemble(
        gw1, gm0, gm1, gmg, gw2, va, vb, input_part, out_part
    )
    gain1, shift1, qbias, vbias, mbias, gain2, shift2, sbias, bias1 = small

    return (
        out_own.reshape(1, 2, blocks, D),
        input_grad.reshape(1, 2, blocks, D),
        gain1,
        shift1,
        mixer_owned,
        qbias,
        vbias,
        merge_owned,
        mbias,
        gain2,
        shift2,
        expand_owned,
        bias1,
        shrink_owned,
        sbias,
    )


def aligned(planes, ring, shape):
    return planes == 4 and ring == 8 and shape == (4, 2, 512, D)


def local(tokens, *others):
    planes, ring = lax.axis_size("fsdp"), lax.axis_size("ctx")
    whole = (tokens.shape[0] * planes, 2, tokens.shape[2] * ring, tokens.shape[3])
    if aligned(planes, ring, whole):
        return local_kernel(tokens, *others)
    return local_plain(tokens, *others)


def solution(mesh):
    token_spec = P("fsdp", None, "ctx", None)
    row = P("fsdp")
    matrix = P("fsdp", None)
    in_specs = (
        token_spec,
        row,
        row,
        matrix,
        row,
        row,
        matrix,
        row,
        row,
        row,
        matrix,
        row,
        matrix,
        row,
        token_spec,
    )
    out_specs = (
        token_spec,
        token_spec,
        row,
        row,
        matrix,
        row,
        row,
        matrix,
        row,
        row,
        row,
        matrix,
        row,
        matrix,
        row,
    )
    return jax.shard_map(local, mesh=mesh, in_specs=in_specs, out_specs=out_specs, check_vma=False)
```

```python
import functools

import jax
import jax.numpy as jnp
from jax import lax
from jax.experimental import pallas as pl
from jax.experimental.pallas import tpu as pltpu
from jax.sharding import PartitionSpec as P

D = 1600
H = 25
HD = 64

EPSILON = 1e-05
SCORE_SCALE = 0.125
BF = jnp.bfloat16
F32 = jnp.float32


def normalize(values):
    center = values - jnp.mean(values, axis=-1, keepdims=True)
    spread = jnp.mean(center * center, axis=-1, keepdims=True)
    inverse = lax.rsqrt(spread + EPSILON)
    return center * inverse, inverse


def norm_back(grad, gain, normal, inverse):
    scaled = grad * gain
    mean = jnp.mean(scaled, axis=-1, keepdims=True)
    along = jnp.mean(scaled * normal, axis=-1, keepdims=True)
    return inverse * (scaled - mean - normal * along)


def dot(a, b):
    return jnp.dot(a, b, preferred_element_type=F32)


def dot_t(a, b):
    return lax.dot_general(a, b, (((1,), (1,)), ((), ())), preferred_element_type=F32)


def t_dot(a, b):
    return lax.dot_general(a, b, (((0,), (0,)), ((), ())), preferred_element_type=F32)


def attend(query, key, value, allowed):
    scores = jnp.einsum("hqd,hkd->hqk", query, key, preferred_element_type=F32) * SCORE_SCALE
    scores = jnp.where(allowed[None], scores, -1e30)
    top = jnp.max(scores, axis=-1, keepdims=True)
    expo = jnp.exp(scores - top)
    total = jnp.sum(expo, axis=-1, keepdims=True)
    probs = (expo / total).astype(BF)
    return jnp.einsum("hqk,hkd->hqd", probs, value, preferred_element_type=F32), top, total


def attend_back(query, key, value, allowed, top, total, grad):
    scores = jnp.einsum("hqd,hkd->hqk", query, key, preferred_element_type=F32) * SCORE_SCALE
    scores = jnp.where(allowed[None], scores, -1e30)
    probs = jnp.exp(scores - top) / total
    probs_low = probs.astype(BF)
    prob_grad = jnp.einsum("hqd,hkd->hqk", grad, value, preferred_element_type=F32)
    offset = jnp.sum(prob_grad * probs, axis=-1, keepdims=True)
    score_grad = (probs * (prob_grad - offset)).astype(BF)
    dq = jnp.einsum("hqk,hkd->hqd", score_grad, key, preferred_element_type=F32) * SCORE_SCALE
    dk = jnp.einsum("hqk,hqd->hkd", score_grad, query, preferred_element_type=F32) * SCORE_SCALE
    dv = jnp.einsum("hqk,hqd->hkd", probs_low, grad, preferred_element_type=F32)
    return dq, dk, dv


def heads_first(values):
    rows, columns = values.shape
    return values.reshape(rows, columns // HD, HD).transpose(1, 0, 2)


def heads_last(values):
    heads, rows, _ = values.shape
    return values.transpose(1, 0, 2).reshape(rows, heads * HD)


MESH_ID = pl.DeviceIdType.MESH


def dyn(start, size, step):
    return pl.ds(pl.multiple_of(start, step), size)


class Links:

    def __init__(self, planes):
        self.planes = planes
        self.p = lax.axis_index("fsdp")
        self.me = lax.axis_index("ctx")

    def plane(self, step):
        return (self.p + step, self.me)

    def peer(self, mask):
        return (self.p, self.me ^ mask)

    def copy(self, src, dst, send, recv, device):
        return pltpu.make_async_remote_copy(
            src_ref=src, dst_ref=dst, send_sem=send, recv_sem=recv, device_id=device, device_id_type=MESH_ID
        )

    def arrive(self, masks):
        bar = pltpu.get_barrier_semaphore()
        for mask in masks:
            pl.semaphore_signal(bar, inc=1, device_id=self.peer(mask), device_id_type=MESH_ID)
        for d in range(1, self.planes):
            to = (lax.rem(self.p + d, self.planes), self.me)
            pl.semaphore_signal(bar, inc=1, device_id=to, device_id_type=MESH_ID)

    def barrier(self, masks):
        pl.semaphore_wait(pltpu.get_barrier_semaphore(), len(masks) + self.planes - 1)


class LineGather:

    def __init__(self, links, src, slot, sems, local_sem):
        self.links, self.slot, self.sems, self.local_sem = links, slot, sems, local_sem
        self.stays = src is None
        self.src = slot(links.p) if src is None else src

    def send(self, src, block, step):
        way = 1 if step > 0 else 2
        return self.links.copy(
            src, self.slot(block), self.sems.at[way, block], self.sems.at[0, block], self.links.plane(step)
        )

    def arrival(self, block):
        return self.links.copy(
            self.slot(block), self.slot(block), self.sems.at[1, block], self.sems.at[0, block], self.links.plane(0)
        )

    def start(self):
        p, last = self.links.p, self.links.planes - 1

        @pl.when(p < last)
        def _():
            self.send(self.src, p, 1).start()

        @pl.when(p > 0)
        def _():
            self.send(self.src, p, -1).start()

        if not self.stays:
            pltpu.make_async_copy(self.src, self.slot(p), self.local_sem).start()

    def pump(self, d):
        p, last = self.links.p, self.links.planes - 1

        @pl.when(p >= d)
        def _():
            self.arrival(p - d).wait_recv()

            @pl.when(p < last)
            def _():
                self.send(self.slot(p - d), p - d, 1).start()

        @pl.when(p + d <= last)
        def _():
            self.arrival(p + d).wait_recv()

            @pl.when(p > 0)
            def _():
                self.send(self.slot(p + d), p + d, -1).start()

        if d == 1 and not self.stays:
            pltpu.make_async_copy(self.src, self.slot(p), self.local_sem).wait()

    def finish(self):
        p, last = self.links.p, self.links.planes - 1
        for d in range(self.links.planes):

            @pl.when((p >= d) & (p < last))
            def _():
                self.send(self.slot(p - d), p - d, 1).wait_send()

            @pl.when((p + d <= last) & (p > 0))
            def _():
                self.send(self.slot(p + d), p + d, -1).wait_send()


class EdgeGather:

    def __init__(self, links, own, early, buffer, send, recv, local):
        self.links, self.own, self.early, self.buffer = links, own, early, buffer
        self.send_sem, self.recv_sem, self.local = send, recv, local

    def block(self, ref, t):
        return ref.at[208 * t : 208 * t + 208]

    def copy(self, src, t, n, to):
        return self.links.copy(
            src, self.block(self.buffer, t), self.send_sem.at[n], self.recv_sem.at[t], (to, self.links.me)
        )


    def outward(self):
        for p, t, to in ((0, 0, 1), (3, 3, 2)):

            @pl.when(self.links.p == p)
            def _():
                self.copy(self.own, t, 0, to).start()

    def between(self):
        for p, t, to in ((1, 1, 2), (2, 2, 1)):

            @pl.when(self.links.p == p)
            def _():
                self.copy(self.own, t, 0, to).start()

    def finish_early(self):
        for p, came in ((0, ()), (1, (0, 2)), (2, (3, 1)), (3, ())):

            @pl.when(self.links.p == p)
            def _():
                self.copy(self.own, p, 0, p ^ 1).wait_send()
                for t in came:
                    self.copy(self.own, t, 0, p ^ 1).wait_recv()


    def loads(self, p):
        made = [pltpu.make_async_copy(self.own, self.block(self.buffer, p), self.local.at[0])]
        for n, t in enumerate(((), (0, 2), (3, 1), ())[p]):
            made.append(pltpu.make_async_copy(self.block(self.early, t), self.block(self.buffer, t), self.local.at[1 + n]))
        return made

    def sent(self, p, n):
        end, far, near, middle = ((0, 3, 2, 2), (3, 0, 1, 1))[p - 1]
        t, to = ((p, end), (near, end), (end, middle), (far, end))[n]
        src = (self.own, self.early, self.early, self.buffer)[n]
        return self.copy(src if n == 0 else self.block(src, t), t, n, to)

    def start(self):
        for p in range(4):

            @pl.when(self.links.p == p)
            def _():
                for c in self.loads(p):
                    c.start()
                if p in (1, 2):
                    for n in range(3):
                        self.sent(p, n).start()

    def relay(self):
        for p, far in ((1, 3), (2, 0)):

            @pl.when(self.links.p == p)
            def _():
                self.copy(self.own, far, 3, p).wait_recv()
                self.sent(p, 3).start()

    def wait(self):
        for p in range(4):

            @pl.when(self.links.p == p)
            def _():
                for c in self.loads(p):
                    c.wait()
                if p in (0, 3):
                    for t in range(4):
                        if t != p:
                            self.copy(self.own, t, 0, p).wait_recv()

    def finish(self):
        for p in (1, 2):

            @pl.when(self.links.p == p)
            def _():
                for n in range(4):
                    self.sent(p, n).wait_send()


class LineExchange:

    def __init__(self, links, slots, send, recv):
        self.links, self.slots, self.send_sem, self.recv_sem = links, slots, send, recv

    def copy(self, src, d):
        planes = self.links.planes
        to = lax.rem(self.links.p + d, planes)
        return self.links.copy(src, self.slots.at[d - 1], self.send_sem.at[d - 1], self.recv_sem.at[d - 1], (to, self.links.me))

    def start(self, src):
        for d in range(1, self.links.planes):
            self.copy(src, d).start()

    def total(self, src):
        acc = src[...].astype(F32)
        for d in range(1, self.links.planes):
            self.copy(src, d).wait_recv()
            acc = acc + self.slots[d - 1].astype(F32)
        return acc

    def finish(self, src):
        for d in range(1, self.links.planes):
            self.copy(src, d).wait_send()


class SmallGather:

    def __init__(self, links, src, slot, send, recv, local_sem):
        self.links, self.src, self.slot, self.send_sem, self.recv_sem, self.local_sem = links, src, slot, send, recv, local_sem

    def copy(self, owner, mask, n):
        src = self.src if n < 4 else self.slot(owner)
        return self.links.copy(src, self.slot(owner), self.send_sem.at[n], self.recv_sem.at[owner, 0], self.links.peer(mask))

    def start(self):
        for n, mask in enumerate((2, 4, 6, 1)):
            self.copy(self.links.me, mask, n).start()
        pltpu.make_async_copy(self.src, self.slot(self.links.me), self.local_sem).start()

    def forward(self):
        for n, mask in enumerate((2, 4, 6)):
            owner = self.links.me ^ mask
            self.copy(owner, mask, 4 + n).wait_recv()
            self.copy(owner, 1, 4 + n).start()

    def wait(self):
        for mask in (1, 3, 5, 7):
            self.copy(self.links.me ^ mask, 1, 4).wait_recv()

    def finish(self):
        for n in range(7):
            self.copy(self.links.me, 1, n).wait_send()
        pltpu.make_async_copy(self.src, self.slot(self.links.me), self.local_sem).wait()


class GroupGather:

    def __init__(self, links, part, send, recv, src=None, local_sem=None):
        self.links, self.part, self.send_sem, self.recv_sem = links, part, send, recv
        self.src, self.local_sem = src, local_sem

    def copy(self, owner, h, mask, n, src=None):
        return self.links.copy(
            self.part(owner, h) if src is None else src,
            self.part(owner, h),
            self.send_sem.at[n],
            self.recv_sem.at[owner, h],
            self.links.peer(mask),
        )

    def own(self, n):
        h, mask = ((1, 2), (0, 4), (0, 2), (1, 4), (0, 1), (1, 1))[n]
        return self.copy(self.links.me, h, mask, n, None if self.src is None else self.src(h))

    def stay(self, h):
        return pltpu.make_async_copy(self.src(h), self.part(self.links.me, h), self.local_sem.at[h])

    def start(self):
        for n in range(6):
            self.own(n).start()
        if self.src is not None:
            for h in range(2):
                self.stay(h).start()

    def pass_on(self, mask, h, n):
        owner = self.links.me ^ mask
        self.copy(owner, h, 1, n).wait_recv()
        if n < 8:
            self.copy(owner, h, 6 - mask, n).start()
        self.copy(owner, h, 1, n + 2).start()

    def forward(self):
        self.pass_on(2, 1, 6)
        self.pass_on(4, 0, 7)
        self.pass_on(2, 0, 8)
        self.pass_on(4, 1, 9)

    def forward_last(self):
        self.pass_on(6, 0, 10)
        self.pass_on(6, 1, 11)

    def wait(self):
        self.forward_last()
        for mask in (1, 3, 5, 7):
            for h in range(2):
                self.copy(self.links.me ^ mask, h, 1, 6).wait_recv()
        if self.src is not None:
            for h in range(2):
                self.stay(h).wait()

    def finish(self):
        me = self.links.me
        for n in range(6):
            self.own(n).wait_send()
        self.copy(me ^ 2, 1, 1, 6).wait_send()
        self.copy(me ^ 4, 0, 1, 7).wait_send()
        for mask, h, n in ((2, 1, 8), (4, 0, 9), (2, 0, 10), (4, 1, 11), (6, 0, 12), (6, 1, 13)):
            self.copy(me ^ mask, h, 1, n).wait_send()


def row_parts(ref, cut):
    rows = ref.shape[-2]
    return lambda j, h: ref.at[j, 0:cut] if h == 0 else ref.at[j, cut:rows]


def own_parts(ref, cut):
    rows = ref.shape[-2]
    return lambda h: ref.at[0:cut] if h == 0 else ref.at[cut:rows]


class GroupSum:

    def __init__(self, links, stage, from_twin, from_far, send, twin_recv, far_recv):
        self.links, self.stage, self.from_twin, self.from_far = links, stage, from_twin, from_far
        self.send, self.twin_recv, self.far_recv = send, twin_recv, far_recv
        self.rows = stage.shape[1] // 2

    def to_twin(self, chip):
        return self.links.copy(
            self.stage.at[4 + chip], self.from_twin.at[chip], self.send.at[4 + chip], self.twin_recv.at[chip], self.links.peer(1)
        )

    def to_far(self, chip, h, mask):
        at = pl.ds(h * self.rows, self.rows)
        n = 2 * (chip - 1) + h
        return self.links.copy(
            self.stage.at[chip, at], self.from_far.at[chip - 1, at], self.send.at[8 + n], self.far_recv.at[n], self.links.peer(mask)
        )

    def run(self, block):
        me = self.links.me
        masks = (0, 2, 4, 6)
        for chip in (3, 1, 2, 0):
            self.stage[4 + chip] = block(me ^ masks[chip] ^ 1).astype(BF)
            self.to_twin(chip).start()
        for chip in (3, 1, 2):
            part = block(me ^ masks[chip])
            self.to_twin(chip).wait_recv()
            self.stage[chip] = (part + self.from_twin[chip].astype(F32)).astype(BF)
            if chip == 3:
                self.to_far(3, 0, 2).start()
                self.to_far(3, 1, 4).start()
            elif chip == 1:
                self.to_far(1, 0, 2).start()
            else:
                self.to_far(2, 1, 4).start()
        self.stage[0] = block(me).astype(BF)

    def relay(self):
        half = self.rows
        for chip, h, mask in ((2, 0, 4), (1, 1, 2)):
            at = slice(h * half, h * half + half)
            self.to_far(3, h, mask).wait_recv()
            self.stage[chip, at] = (self.stage[chip, at].astype(F32) + self.from_far[2, at].astype(F32)).astype(BF)
            self.to_far(chip, h, mask).start()

    def total(self):
        self.to_twin(0).wait_recv()
        acc = self.stage[0].astype(F32) + self.from_twin[0].astype(F32)
        for chip, mask in ((1, 2), (2, 4)):
            for h in range(2):
                self.to_far(chip, h, mask).wait_recv()
            acc += self.from_far[chip - 1].astype(F32)
        return acc

    def finish(self):
        for chip in range(4):
            self.to_twin(chip).wait_send()
        for chip, h, mask in ((3, 0, 2), (3, 1, 4), (1, 0, 2), (1, 1, 2), (2, 0, 4), (2, 1, 4)):
            self.to_far(chip, h, mask).wait_send()


def gelu_parts(u):
    inner = 0.7978845608 * (u + 0.044715 * (u * u * u))
    t = jnp.tanh(inner)
    value = 0.5 * u * (1.0 + t)
    slope = 0.5 * (1.0 + t) + 0.5 * u * (1.0 - t * t) * (0.7978845608 * (1.0 + 3 * 0.044715 * (u * u)))
    return value, slope


BLOCK_KEYS = (
    ((0, 256, 1),),
    ((0, 256, 0), (256, 256, 1)),
    ((0, 512, 0), (512, 256, 2), (768, 256, 0)),
    ((0, 512, 0), (768, 256, 2)),
)


def triangle(kind, shape):
    r = lax.broadcasted_iota(jnp.int32, shape, 0)
    c = lax.broadcasted_iota(jnp.int32, shape, 1)
    return c <= r if kind == 1 else c >= r


def half_mask(half):
    lane = lax.broadcasted_iota(jnp.int32, (1, 128), 1)
    return (lane // 64) == half


def softmax_pieces(q, keys, values, pieces, allowed):
    scores = []
    for start, size, kind in pieces:
        s = dot_t(q, keys[start : start + size])
        if kind:
            s = jnp.where(allowed(kind, start, s.shape), s, -1e30)
        scores.append(s)
    top = jnp.max(scores[0], axis=1, keepdims=True)
    for s in scores[1:]:
        top = jnp.maximum(top, jnp.max(s, axis=1, keepdims=True))
    total, out = 0.0, 0.0
    for s, (start, size, _) in zip(scores, pieces):
        e = jnp.exp(s - top)
        total = total + jnp.sum(e, axis=1, keepdims=True)
        out = out + dot(e.astype(BF), values[start : start + size])
    return out * (1.0 / total), top + jnp.log(total)


def shift_left(values, lanes):
    return pltpu.roll(values, lax.rem(values.shape[1] - lanes, values.shape[1]), 1)


def small_vectors(parts, p, me):
    wide = 1664
    values = [part[...].astype(F32).reshape(1, part.shape[0]) for part in parts]
    rows = jnp.concatenate([jnp.concatenate(values[:8], axis=0), jnp.zeros((8, wide - 400), F32)], axis=1)
    rows = pltpu.roll(rows, 400 * p, 1)
    mine = shift_left(rows, 192 * me)
    heads = jnp.concatenate([mine[:, :192], rows[:, 1536:1600], jnp.zeros((8, wide - 256), F32)], axis=1)
    n = lax.broadcasted_iota(jnp.int32, (8, 1), 0)
    rows = jnp.where((n == 2) | (n == 3), heads, rows)
    bias = jnp.concatenate([values[8], jnp.zeros((1, wide - 1600), F32)], axis=1)
    bias = shift_left(jnp.broadcast_to(bias, (8, wide)), 200 * me)
    lane = lax.broadcasted_iota(jnp.int32, (1, wide), 1)
    bias = pltpu.roll(jnp.where(lane < 200, bias, 0.0), 208 * p + 8 * lax.rem(me, 2), 1)
    bias = jnp.where(n == 0, bias, 0.0)
    return jnp.concatenate([rows, bias], axis=0).astype(BF)


def attend_kernel(planes, tok, cot, v0, v1, v2, v3, v4, v5, v6, v7, v8, mixer, merge, expand, shrink,
                  hidden_o, qkv_o, att_o, heads_o, vec_o, lse_o,
                  first_o, mw_o, mfull_o, w1_o, sec_o, g_o, w2_o,
                  vpart, raw1, own1, vec, mw0, mw1, mgs, mfull, first_all, second, arecv,
                  zs, zl, w2_s, w2_r, v_s, v_r, gs, gr, gl, gl2, a_s, a_r, os):
    L = Links(planes)
    L.arrive(range(1, 8))
    qkv, attown, hid, lse, att = qkv_o, att_o, hidden_o, lse_o, heads_o
    p, me = L.p, L.me
    share = 400
    xv = LineExchange(L, vec, v_s, v_r)
    zm0 = LineGather(L, None, lambda b: mw0.at[dyn(b * share, share, 16)], zs.at[0], zl.at[0])
    zm1 = LineGather(L, None, lambda b: mw1.at[dyn(b * share, share, 16)], zs.at[1], zl.at[0])
    zmg = LineGather(L, None, lambda b: mgs.at[b], zs.at[2], zl.at[0])
    zw1 = LineGather(L, own1, lambda b: w1_o.at[dyn(b * share, share, 16)], zs.at[3], zl.at[0])
    early = EdgeGather(L, shrink.at[dyn(200 * me - 8 * lax.rem(me, 2), 208, 16)], None, w2_o, w2_s, w2_r, None)
    gfirst = GroupGather(L, lambda j, h: first_all.at[h, j], gs.at[0], gr.at[0])
    gsec = GroupGather(L, row_parts(sec_o, 64), gs.at[1], gr.at[1], own_parts(second, 64), gl)
    gg = GroupGather(L, row_parts(g_o, 64), gs.at[3], gr.at[3], own_parts(cot, 64), gl2)
    gmerge = GroupGather(L, lambda j, h: mfull.at[2 * h : 2 * h + 2, dyn(j * 48, 48, 16)], gs.at[2], gr.at[2])

    takes = [
        pltpu.make_async_copy(merge.at[dyn(me * 48, 48, 16)], mgs.at[p, 0:48], zl.at[1]),
        pltpu.make_async_copy(merge.at[384:400], mgs.at[p, 48:64], zl.at[2]),
        pltpu.make_async_copy(expand, raw1, zl.at[3]),
    ]
    for c in takes:
        c.start()
    vpart[...] = small_vectors((v0, v1, v2, v3, v4, v5, v6, v7, v8), p, me)
    at_own = dyn(p * share, share, 16)

    def head_columns(n):
        odd = lax.rem(n + me, 2)
        x = mixer[:, dyn(D * n + 192 * me - 64 * odd, 256, 128)]
        return jnp.where(odd == 1, jnp.concatenate([x[:, 64:], x[:, :64]], axis=1), x)

    for n in range(3):
        mine = head_columns(n)
        mw0[at_own, 128 * n : 128 * n + 128] = mine[:, :128]
        every = mixer[:, D * n + 1536 : D * n + 1600]
        mw1[at_own, 128 * n : 128 * n + 128] = jnp.concatenate([mine[:, 128:192], every], axis=1)
    L.barrier(range(1, 8))
    xv.start(vpart)
    zm0.start()
    rows = tok[...].astype(F32)
    normal, _ = normalize(rows)
    vectors = xv.total(vpart)[:, :D]
    first = (normal * vectors[0:1] + vectors[1:2]).astype(BF)
    first_all[:, me] = first.reshape(2, 64, D)
    gfirst.start()
    takes[2].wait()
    odd_me = lax.rem(me, 2)
    lane = lax.broadcasted_iota(jnp.int32, (1, 384), 1)
    for q in range(4):
        start = 1600 * q + 200 * me
        base = jnp.minimum(start // 128 * 128, 6400 - 384)
        x = shift_left(raw1[:, dyn(base, 384, 128)].astype(F32), lax.rem(start - base - 8 * odd_me + 384, 384))
        x = jnp.where((lane >= 8 * odd_me) & (lane < 8 * odd_me + 200), x, 0.0)
        own1[:, 208 * q : 208 * q + 208] = x[:, :208].astype(BF)
    zm0.pump(1)
    zm0.pump(2)
    takes[0].wait()
    takes[1].wait()
    zmg.start()
    gfirst.forward()
    zm0.pump(3)
    zmg.pump(1)
    gfirst.wait()
    zmg.pump(2)
    zm1.start()

    def mix(weights, pair):
        bias_q = vectors[2:3, pair * 128 : pair * 128 + 128]
        bias_v = vectors[3:4, pair * 128 : pair * 128 + 128]

        def body(b, _):
            x = first_all[b // 2, pl.ds((b % 2) * 4, 4)].reshape(256, D)
            mixed = dot(x, weights[...])
            at = dyn(b * 256, 256, 256)
            qkv[pair, at] = (mixed[:, :128] + bias_q).astype(BF)
            qkv[2 + pair, at] = mixed[:, 128:256].astype(BF)
            qkv[4 + pair, at] = (mixed[:, 256:] + bias_v).astype(BF)
            return 0

        lax.fori_loop(0, 4, body, 0)

    lane128 = lax.broadcasted_iota(jnp.int32, (1, 128), 1)

    def note_lse(head, at, value):
        lse[at] = jnp.where(lane128 == head, value, lse[at] if head else 0.0)

    def attend_private(pair, half):
        mask = half_mask(half)
        for b in range(4):
            q = jnp.where(mask, qkv[pair, b * 256 : b * 256 + 256], 0) * jnp.asarray(0.125, BF)
            out, l = softmax_pieces(
                q, qkv.at[2 + pair], qkv.at[4 + pair], BLOCK_KEYS[b], lambda kind, start, shape: triangle(kind, shape)
            )
            out = jnp.where(mask, out, 0.0).astype(BF).reshape(4, 64, 128)
            at = pl.ds((b % 2) * 4, 4)
            if half == 0:
                att[pair, b // 2, at] = out
            else:
                att[pair, b // 2, at] = att[pair, b // 2, at] + out
            note_lse(2 * pair + half, slice(b * 256, b * 256 + 256), l)

    def own_allowed(kind, start, shape):
        r = lax.broadcasted_iota(jnp.int32, shape, 0)
        c = lax.broadcasted_iota(jnp.int32, shape, 1)
        rp = jnp.where(r < 64, me * 64 + r, 1023 - (me * 64 + r - 64))
        cp = jnp.where(c < 512, c, 1023 - (c - 512))
        return cp <= rp

    mix(mw0, 0)
    zmg.pump(3)
    for b in range(4):
        mfull[b, dyn(me * 48, 48, 16)] = mgs[b, 0:48]
        mfull[b, 384:400] = mgs[b, 48:64]
    gmerge.start()
    attend_private(0, 0)
    zm1.pump(1)
    attend_private(0, 1)
    zm1.pump(2)
    zw1.start()
    gmerge.forward()
    gg.start()
    zm1.pump(3)
    mix(mw1, 1)
    outs = [
        pltpu.make_async_copy(first_all, first_o, os.at[0]),
        pltpu.make_async_copy(mw0, mw_o.at[0], os.at[1]),
        pltpu.make_async_copy(mw1, mw_o.at[1], os.at[2]),
        pltpu.make_async_copy(mfull, mfull_o, os.at[3]),
    ]
    for c in outs[:3]:
        c.start()
    attend_private(1, 0)
    qs = jnp.concatenate([qkv[1, dyn(me * 64, 64, 64)], qkv[1, dyn(512 + me * 64, 64, 64)]], axis=0)
    mask1 = half_mask(1)
    qs = jnp.where(mask1, qs, 0) * jnp.asarray(0.125, BF)
    out_s, l_s = softmax_pieces(qs, qkv.at[3], qkv.at[5], ((0, 1024, 1),), own_allowed)
    note_lse(3, slice(0, 128), l_s)
    shared_low = jnp.where(mask1, out_s, 0.0).astype(BF)

    def exchange(mask):
        return L.copy(att.at[:, :, me ^ mask], arecv.at[me], a_s.at[mask], a_r.at[me], L.peer(mask))

    def arrived(mask):
        return L.copy(att.at[:, :, me], arecv.at[me ^ mask], a_s.at[mask], a_r.at[me ^ mask], L.peer(mask))

    for mask in range(1, 8):
        exchange(mask).start()
    arecv[me] = att[:, :, me]
    gg.forward()
    for mask in range(1, 8):
        arrived(mask).wait_recv()
    for j in range(8):
        attown[:, 192 * j : 192 * j + 128] = arecv[j, 0].reshape(128, 128)
        attown[:, 192 * j + 128 : 192 * j + 192] = arecv[j, 1].reshape(128, 128)[:, :64]
    attown[:, 1536:1600] = shared_low[:, 64:128]
    gmerge.wait()
    hidden = rows + vectors[4:5]
    hid[...] = hidden
    for b in range(4):
        hid[...] += dot(attown[:, b * 400 : b * 400 + 400], mfull[b])
    normal2, _ = normalize(hid[...])
    second[...] = (normal2 * vectors[5:6] + vectors[6:7]).astype(BF)
    gsec.start()
    outs[3].start()
    vec_o[...] = vectors
    zw1.pump(1)
    early.outward()
    gg.wait()
    gsec.forward()
    zw1.pump(2)
    early.between()
    gsec.wait()
    zw1.pump(3)
    for c in outs:
        c.wait()
    xv.finish(vpart)
    early.finish_early()
    for z in (zm0, zm1, zmg, zw1):
        z.finish()
    for g in (gfirst, gg, gsec, gmerge):
        g.finish()
    for mask in range(1, 8):
        exchange(mask).wait_send()


def run_attend(planes, tok, cot, vectors, mixer, merge, expand, shrink):
    any_ = pl.BlockSpec(memory_space=pl.ANY)
    vm = pl.BlockSpec(memory_space=pltpu.VMEM)
    S = jax.ShapeDtypeStruct
    V = pltpu.VMEM
    dma = pltpu.SemaphoreType.DMA
    return pl.pallas_call(
        functools.partial(attend_kernel, planes),
        out_shape=(
            S((128, D), F32), S((6, 1024, 128), BF), S((128, D), BF), S((2, 2, 8, 64, 128), BF), S((16, D), F32), S((1024, 128), F32),
            S((2, 8, 64, D), BF), S((2, D, 384), BF), S((4, 400, D), BF), S((D, 832), BF),
            S((8, 128, D), BF), S((8, 128, D), BF), S((832, D), BF),
        ),
        in_specs=[vm] * 12 + [any_] * 3,
        out_specs=(vm,) * 6 + (any_,) * 7,
        scratch_shapes=[
            V((16, 1664), BF), V((400, 6400), BF), V((400, 832), BF), V((3, 16, 1664), BF), V((D, 384), BF), V((D, 384), BF), V((4, 64, D), BF), V((4, 400, D), BF),
            V((2, 8, 64, D), BF), V((128, D), BF), V((8, 2, 2, 64, 128), BF),
            dma((5, 3, 4)), dma((5,)), dma((1,)), dma((4,)), dma((3,)), dma((3,)), dma((4, 14)), dma((4, 8, 2)), dma((2,)), dma((2,)),
            dma((8,)), dma((8,)), dma((4,)),
        ],
        compiler_params=pltpu.CompilerParams(collective_id=0, has_side_effects=True, vmem_limit_bytes=60 << 20),
        cost_estimate=pl.CostEstimate(flops=6_000_000_000, bytes_accessed=60_000_000, transcendentals=4_000_000),
    )(tok, cot, *vectors, mixer, merge, expand, shrink)


class LineSum:

    def __init__(self, links, block, slots, send, recv, near=None, near_sem=None):
        self.links, self.block, self.send_sem, self.recv_sem = links, block, send, recv
        self.slots = slots if callable(slots) else lambda s: slots.at[s]
        self.near, self.near_sem = near, near_sem
        self.last = links.planes - 1

    def send(self, t, step):
        slot = t - 1 if step > 0 else self.left_slot(t)
        return self.links.copy(
            self.block(t), self.slots(slot), self.send_sem.at[t], self.recv_sem.at[slot], self.links.plane(step)
        )

    def left_slot(self, t):
        return (self.last + t) % (self.last + 2)

    def arrival(self, slot):
        return self.links.copy(
            self.slots(slot), self.slots(slot), self.send_sem.at[0], self.recv_sem.at[slot], self.links.plane(0)
        )

    def start(self):
        @pl.when(self.links.p == 0)
        def _():
            for t in range(self.last, 0, -1):
                self.send(t, 1).start()

        @pl.when(self.links.p == self.last)
        def _():
            for t in range(self.last):
                self.send(t, -1).start()

    def add(self, t, slot):
        self.arrival(slot).wait_recv()
        ref = self.block(t)
        came = self.slots(slot)
        if self.near is not None:
            copy = pltpu.make_async_copy(came, self.near, self.near_sem)
            copy.start()
            copy.wait()
            came = self.near
        ref[...] = (ref[...].astype(F32) + came[...].astype(F32)).astype(BF)

    def pump(self, u):
        p, last = self.links.p, self.last
        for t in range(1, last + 1):
            at = u - last + t
            if 0 < at < t:

                @pl.when(p == at)
                def _():
                    self.add(t, t - 1)
                    self.send(t, 1).start()

                @pl.when(p == last - at)
                def _():
                    self.add(last - t, self.left_slot(last - t))
                    self.send(last - t, -1).start()

    def total(self):
        p, last = self.links.p, self.last
        for t in range(last + 1):

            @pl.when(p == t)
            def _():
                if t > 0:
                    self.add(t, t - 1)
                if t < last:
                    self.add(t, self.left_slot(t))

    def finish(self):
        p = self.links.p
        for t in range(self.last + 1):

            @pl.when(p < t)
            def _():
                self.send(t, 1).wait_send()

            @pl.when(p > t)
            def _():
                self.send(t, -1).wait_send()


def backward_kernel(planes, vectors, attown, tok_h, cot_h, hid_h, lse_h, qkv_h, att_h,
                    shrink, w2_h, w1_h, sec_h, g_h, mfull_h, mw_h, first_h,
                    igrad_o, out_o, va_o, vb_o, gw1_o, gw2_o, gm0_o, gm1_o, gmg_o, atts_o, slot_mg,
                    tok, cot, hid, lse, qkv, att, mfull, mw, sec_all, g_all, w1b, w2b, act, slope, dw1, dw2, hlow, agrad, asend, gatt, hc, dkv, mgr, dmerge,
                    slot_w1, slot_w2, slot_m0, slot_m1, near_mg, stage, twin, far, va, vb, vslot,
                    zs, zr, zl, ld, ls_s, ls_r, ve_s, ve_r, gs, gr, gl, a_s, a_r, h_s, h_r, rs_s, rs_t, rs_f, free, sm):
    L = Links(planes)
    L.arrive(range(1, 8))
    p, me = L.p, L.me
    loads = [
        pltpu.make_async_copy(w1_h, w1b, ld.at[0]),
        pltpu.make_async_copy(sec_h, sec_all, ld.at[1]),
        pltpu.make_async_copy(g_h, g_all, ld.at[7]),
        pltpu.make_async_copy(mfull_h, mfull, ld.at[2]),
        pltpu.make_async_copy(mw_h, mw, ld.at[3]),
    ]
    small = [
        pltpu.make_async_copy(src, dst, sm.at[n])
        for n, (src, dst) in enumerate(
            ((tok_h, tok), (cot_h, cot), (hid_h, hid), (lse_h, lse), (qkv_h, qkv), (att_h, att))
        )
    ]
    att_all, first_all = g_all, sec_all
    late_att = pltpu.make_async_copy(atts_o, att_all, ld.at[5])
    late_first = pltpu.make_async_copy(first_h, first_all, ld.at[6])
    for c in loads + small:
        c.start()
    zw2 = EdgeGather(L, shrink.at[dyn(200 * me - 8 * lax.rem(me, 2), 208, 16)], w2_h, w2b, zs, zr, zl)
    cut2 = 768

    def shrink_line(n, first, last):
        return LineSum(
            L, lambda t: dw2.at[dyn(t * 208, 208, 16), first:last], lambda s: slot_w2.at[s, :, first:last], ls_s.at[n], ls_r.at[n]
        )

    lw2a, lw2b = shrink_line(0, 0, cut2), shrink_line(5, cut2, D)
    lw1 = LineSum(L, lambda t: dw1.at[dyn(t * 400, 400, 16)], slot_w1, ls_s.at[1], ls_r.at[1])
    lm0 = LineSum(L, lambda t: w1b.at[dyn(t * 400, 400, 16), 0:384], slot_m0, ls_s.at[2], ls_r.at[2])
    lm1 = LineSum(L, lambda t: w1b.at[dyn(t * 400, 400, 16), 384:768], slot_m1, ls_s.at[3], ls_r.at[3])
    lmg = LineSum(L, lambda t: dmerge.at[dyn(t * 400, 400, 16)], slot_mg, ls_s.at[4], ls_r.at[4], near_mg, ld.at[4])
    xa = LineExchange(L, vslot.at[0], ve_s.at[0], ve_r.at[0])
    xb = LineExchange(L, vslot.at[1], ve_s.at[1], ve_r.at[1])
    gatt_all = GroupGather(L, row_parts(atts_o, 64), gs.at[1], gr.at[1], own_parts(attown, 64), gl.at[1])

    def shrink_gather(n, first, last):
        sizes = (112, 96)

        def part(j, h):
            return gw2_o.at[j, 112 * h : 112 * h + sizes[h], first:last]

        def src(h):
            return dw2.at[dyn(p * 208 + 112 * h, sizes[h], 16), first:last]

        return GroupGather(L, part, gs.at[n], gr.at[n], src, gl.at[n])

    gw2a, gw2b = shrink_gather(0, 0, cut2), shrink_gather(2, cut2, D)
    def share_gather(n, out, line):
        def src(h):
            base, columns = line.home
            return base.at[dyn(p * 400 + 208 * h, (208, 192)[h], 16), columns[0] : columns[1]]

        return GroupGather(L, row_parts(out, 208), gs.at[n], gr.at[n], src, gl.at[n])

    lw1.home, lm0.home, lm1.home, lmg.home = (dw1, (0, 832)), (w1b, (0, 384)), (w1b, (384, 768)), (dmerge, (0, 256))
    gw1 = share_gather(3, gw1_o, lw1)
    gm0 = share_gather(4, gm0_o, lm0)
    gm1 = share_gather(5, gm1_o, lm1)
    gmg = share_gather(6, gmg_o, lmg)
    gva = SmallGather(L, va, lambda j: va_o.at[j], gs.at[7], gr.at[7], gl.at[7, 0])
    gvb = SmallGather(L, vb, lambda j: vb_o.at[j], gs.at[8], gr.at[8], gl.at[8, 0])
    L.barrier(range(1, 8))
    zw2.start()
    gatt_all.start()

    loads[0].wait()
    loads[1].wait()

    def expand(b, _):
        at = dyn(b * 256, 256, 256)
        pre = dot(sec_all[pl.ds(2 * b, 2)].reshape(256, D), w1b[...]) + vectors[8:9, :832]
        value, s = gelu_parts(pre)
        act[at] = value.astype(BF)
        slope[at] = s.astype(BF)
        return 0

    lax.fori_loop(0, 4, expand, 0)
    loads[2].wait()
    g2 = g_all[...].reshape(1024, D)
    for part, columns in ((lw2a, slice(0, cut2)), (lw2b, slice(cut2, D))):
        for start, size in ((0, 256), (256, 256), (512, 256), (768, 64)):
            dw2[start : start + size, columns] = t_dot(act[:, start : start + size], g2[:, columns]).astype(BF)
        if part is lw2a:
            lw2a.start()
    zw2.relay()
    gatt_all.forward()
    lw2a.pump(1)
    gatt_all.wait()
    lw2a.pump(2)
    lw2b.start()
    zw2.wait()

    def contract(b, acc):
        at = dyn(b * 256, 256, 256)
        grad = dot_t(g_all[pl.ds(2 * b, 2)].reshape(256, D), w2b[...]) * slope[at].astype(F32)
        slope[at] = grad.astype(BF)
        return acc + jnp.sum(grad, axis=0, keepdims=True)

    dgb = lax.fori_loop(0, 4, contract, jnp.zeros((1, 832), F32))
    late_att.start()
    rounds = [GroupSum(L, stage, twin, far, rs_s.at[n], rs_t.at[n], rs_f.at[n]) for n in range(3)]

    def release(n):
        for mask in (1, 2, 4):
            pl.semaphore_signal(free.at[n], inc=1, device_id=L.peer(mask), device_id_type=MESH_ID)

    back = rounds[0]
    back.run(lambda owner: dot_t(slope[dyn(owner * 128, 128, 128)], w1b[...]))
    lw2b.pump(1)
    for start in range(0, D, 256):
        size = min(256, D - start)
        x = sec_all[:, :, start : start + size].reshape(1024, size)
        dw1[start : start + size] = t_dot(x, slope[...]).astype(BF)
    late_first.start()
    lw1.start()
    back.relay()
    lw2b.pump(2)
    lw2a.total()
    gw2a.start()
    grad2 = back.total()
    back.finish()
    release(0)

    for c in small:
        c.wait()
    tangent = cot[...].astype(F32)
    normal2, inverse2 = normalize(hid[...])
    hidden_grad = tangent + norm_back(grad2, vectors[5:6], normal2, inverse2)
    igrad_o[...] = hidden_grad
    hlow[:, 0:D] = hidden_grad.astype(BF)
    hlow[:, D:2048] = jnp.zeros((128, 2048 - D), BF)
    va[0:1] = jnp.sum(hidden_grad, axis=0, keepdims=True)
    va[1:2] = jnp.sum(grad2 * normal2, axis=0, keepdims=True)
    va[2:3] = jnp.sum(grad2, axis=0, keepdims=True)
    va[3:4] = jnp.sum(tangent, axis=0, keepdims=True)
    va[4:8] = jnp.zeros((4, D), F32)
    va[4:5, 0:832] = dgb

    def columns(mask):
        to = me ^ mask
        return L.copy(hlow.at[:, dyn(to * 256, 256, 256)], hc.at[me], h_s.at[mask], h_r.at[me], L.peer(mask))

    def columns_in(mask):
        return L.copy(hc.at[me], hc.at[me ^ mask], h_s.at[mask], h_r.at[me ^ mask], L.peer(mask))

    loads[3].wait()
    agrad[...] = dot_t(hlow[:, 0:D], mfull[...]).astype(BF)
    for j in range(8):
        asend[j, 0] = agrad[:, 192 * j : 192 * j + 128].reshape(2, 64, 128)
        tail = agrad[:, 192 * j + 128 : 192 * j + 192]
        asend[j, 1] = jnp.concatenate([tail, jnp.zeros((128, 64), BF)], axis=1).reshape(2, 64, 128)

    def exchange(mask):
        return L.copy(asend.at[me ^ mask], gatt.at[:, :, me], a_s.at[mask], a_r.at[me], L.peer(mask))

    def arrived(mask):
        return L.copy(asend.at[me], gatt.at[:, :, me ^ mask], a_s.at[mask], a_r.at[me ^ mask], L.peer(mask))

    for mask in range(1, 8):
        exchange(mask).start()
    gatt[:, :, me] = asend[me]
    for mask in range(1, 8):
        columns(mask).start()
    pl.semaphore_wait(free.at[0], 3)
    outs = rounds[1]
    outs.run(lambda owner: dot(act[dyn(owner * 128, 128, 128)], w2b[...]))
    hc[me] = hlow[:, dyn(me * 256, 256, 256)]
    dkv[...] = jnp.zeros(dkv.shape, F32)
    for mask in range(1, 8):
        arrived(mask).wait_recv()

    scale = jnp.asarray(0.125, BF)

    def head_back(pair, head, mask, q, g, o, stat, pieces, allowed):
        delta = jnp.sum(g.astype(F32) * o.astype(F32), axis=1, keepdims=True)
        dq = 0.0
        for start, size, kind in pieces:
            keys = qkv[2 + pair, start : start + size]
            s = dot_t(q, keys)
            if kind:
                s = jnp.where(allowed(kind, start, s.shape), s, -1e30)
            prob = jnp.exp(s - stat)
            ds = (prob * (dot_t(g, qkv[4 + pair, start : start + size]) - delta)).astype(BF)
            dq = dq + dot(ds, keys)
            dkv[0, start : start + size] += t_dot(ds, q)
            dkv[1, start : start + size] += t_dot(prob.astype(BF), g)
        return jnp.where(mask, dq, 0.0) * 0.125

    def private_back(pair, half):
        mask = half_mask(half)
        head = 2 * pair + half
        total = 0.0
        for b in range(4):
            at = slice(b * 256, b * 256 + 256)
            blk = (pair, b // 2, pl.ds((b % 2) * 4, 4))
            q = jnp.where(mask, qkv[pair, at], 0) * scale
            g = jnp.where(mask, gatt[blk].reshape(256, 128), 0)
            o = att[blk].reshape(256, 128)
            dq = head_back(
                pair, head, mask, q, g, o, lse[at, head : head + 1], BLOCK_KEYS[b],
                lambda kind, start, shape: triangle(kind, shape),
            )
            total = total + jnp.sum(dq, axis=0, keepdims=True)
            if half == 0:
                mgr[pair, at, 0:128] = dq.astype(BF)
            else:
                mgr[pair, at, 0:128] = mgr[pair, at, 0:128] + dq.astype(BF)
        return total

    def mixer_part(pair):
        mgr[pair, :, 128:256] = dkv[0].astype(BF)
        mgr[pair, :, 256:384] = dkv[1].astype(BF)
        va[6:7, pair * 128 : pair * 128 + 128] = jnp.sum(dkv[1], axis=0, keepdims=True)
        for start in range(0, D, 256):
            size = min(256, D - start)
            x = first_all[:, :, start : start + size].reshape(1024, size)
            w1b[start : start + size, 384 * pair : 384 * pair + 384] = t_dot(x, mgr[pair]).astype(BF)

    qb0 = private_back(0, 0)
    gw2a.forward()
    qb0 = qb0 + private_back(0, 1)
    va[5:6, 0:128] = qb0
    late_first.wait()
    mixer_part(0)
    dkv[...] = jnp.zeros(dkv.shape, F32)
    lm0.start()
    outs.relay()
    lw2b.total()
    gw2b.start()
    qb1 = private_back(1, 0)
    mask1 = half_mask(1)
    own_early, own_late = dyn(me * 64, 64, 64), dyn(512 + me * 64, 64, 64)
    qs = jnp.concatenate([qkv[1, own_early], qkv[1, own_late]], axis=0)
    qs = jnp.where(mask1, qs, 0) * scale
    blank = jnp.zeros((128, 64), BF)
    g_s = jnp.concatenate([blank, agrad[:, 1536:1600]], axis=1)
    o_s = jnp.concatenate([blank, attown[:, 1536:1600]], axis=1)

    def own_allowed(kind, start, shape):
        r = lax.broadcasted_iota(jnp.int32, shape, 0)
        c = lax.broadcasted_iota(jnp.int32, shape, 1) + start
        rp = jnp.where(r < 64, me * 64 + r, 1023 - (me * 64 + r - 64))
        cp = jnp.where(c < 512, c, 1023 - (c - 512))
        return cp <= rp

    dqs = head_back(1, 3, mask1, qs, g_s, o_s, lse[0:128, 3:4], ((0, 512, 1), (512, 512, 1)), own_allowed)
    va[5:6, 128:256] = qb1 + jnp.sum(dqs, axis=0, keepdims=True)
    dqs_low = dqs.astype(BF)
    mgr[1, own_early, 0:128] = mgr[1, own_early, 0:128] + dqs_low[:64]
    mgr[1, own_late, 0:128] = mgr[1, own_late, 0:128] + dqs_low[64:]
    mixer_part(1)
    lm1.start()
    xa.start(va)
    lw1.pump(1)
    out_o[...] = (outs.total() + hid[...] + vectors[7:8]).astype(BF)
    outs.finish()
    release(1)
    loads[4].wait()
    pl.semaphore_wait(free.at[1], 3)
    sums = rounds[2]

    def first_block(owner):
        early, late = dyn(owner * 64, 64, 64), dyn(512 + owner * 64, 64, 64)
        x0 = jnp.concatenate([mgr[0, early], mgr[0, late]], axis=0)
        x1 = jnp.concatenate([mgr[1, early], mgr[1, late]], axis=0)
        return dot_t(x0, mw[0]) + dot_t(x1, mw[1])

    sums.run(first_block)
    gw2b.forward()
    lw1.pump(2)
    sums.relay()
    lw1.total()
    gw1.start()
    lm0.pump(1)
    late_att.wait()
    for mask in range(1, 8):
        columns_in(mask).wait_recv()
    h2 = hc[...].reshape(1024, 256)
    for start in range(0, D, 256):
        size = min(256, D - start)
        x = att_all[:, :, start : start + size].reshape(1024, size)
        dmerge[start : start + size] = t_dot(x, h2).astype(BF)
    lmg.start()
    lm0.pump(2)
    first_grad = sums.total()
    rows = tok[...].astype(F32)
    normal1, inverse1 = normalize(rows)
    igrad_o[...] += norm_back(first_grad, vectors[0:1], normal1, inverse1)
    vb[0:1] = jnp.sum(first_grad * normal1, axis=0, keepdims=True)
    vb[1:2] = jnp.sum(first_grad, axis=0, keepdims=True)
    vb[2:8] = jnp.zeros((6, D), F32)
    xb.start(vb)
    lm0.total()
    gm0.start()
    lm1.pump(1)
    gw1.forward()
    lm1.pump(2)
    gm0.forward()
    lm1.total()
    gm1.start()
    lmg.pump(1)
    total_a = xa.total(va)
    xa.finish(va)
    va[...] = total_a
    gva.start()
    lmg.pump(2)
    total_b = xb.total(vb)
    xb.finish(vb)
    vb[...] = total_b
    gvb.start()
    lmg.total()
    gmg.start()
    gm1.forward()
    gva.forward()
    gvb.forward()
    gmg.forward()
    for g in (gw2a, gw2b, gva, gw1, gvb, gm0, gm1, gmg):
        g.wait()
    for g in (gatt_all, gw2a, gw2b, gw1, gm0, gm1, gmg, gva, gvb):
        g.finish()
    zw2.finish()
    for s in (lw2a, lw2b, lw1, lm0, lm1, lmg):
        s.finish()
    for mask in range(1, 8):
        exchange(mask).wait_send()
        columns(mask).wait_send()
    sums.finish()


def run_backward(planes, *operands):
    any_ = pl.BlockSpec(memory_space=pl.ANY)
    vm = pl.BlockSpec(memory_space=pltpu.VMEM)
    S = jax.ShapeDtypeStruct
    V = pltpu.VMEM
    dma = pltpu.SemaphoreType.DMA
    return pl.pallas_call(
        functools.partial(backward_kernel, planes),
        out_shape=(
            S((128, D), F32), S((128, D), BF), S((8, 8, D), F32), S((8, 8, D), F32), S((8, 400, 832), BF), S((8, 208, D), BF),
            S((8, 400, 384), BF), S((8, 400, 384), BF), S((8, 400, 256), BF), S((8, 128, D), BF),
            S((5, 400, 256), BF),
        ),
        in_specs=[vm] * 2 + [any_] * 14,
        out_specs=(vm,) * 2 + (any_,) * 9,
        scratch_shapes=[
            V((128, D), BF), V((128, D), BF), V((128, D), F32), V((1024, 128), F32), V((6, 1024, 128), BF), V((2, 2, 8, 64, 128), BF),
            V((D, D), BF), V((2, D, 384), BF), V((8, 128, D), BF), V((8, 128, D), BF), V((D, 832), BF), V((832, D), BF),
            V((1024, 832), BF), V((1024, 832), BF), V((D, 832), BF), V((832, D), BF),
            V((128, 2048), BF), V((128, D), BF), V((8, 2, 2, 64, 128), BF), V((2, 2, 8, 64, 128), BF),
            V((8, 128, 256), BF), V((2, 1024, 128), F32), V((2, 1024, 384), BF), V((D, 256), BF),
            V((5, 400, 832), BF), V((5, 208, D), BF), V((5, 400, 384), BF), V((5, 400, 384), BF), V((400, 256), BF),
            V((8, 128, D), BF), V((4, 128, D), BF), V((3, 128, D), BF), V((8, D), F32), V((8, D), F32), V((2, 3, 8, D), F32),
            dma((4,)), dma((4,)), dma((3,)), dma((8,)), dma((6, 4)), dma((6, 5)), dma((2, 3)), dma((2, 3)), dma((9, 14)), dma((9, 8, 2)), dma((9, 2)),
            dma((8,)), dma((8,)), dma((8,)), dma((8,)), dma((3, 14)), dma((3, 4)), dma((3, 6)), pltpu.SemaphoreType.REGULAR((2,)), dma((6,)),
        ],
        compiler_params=pltpu.CompilerParams(collective_id=1, has_side_effects=True, vmem_limit_bytes=(64 << 20) - 65536),
        cost_estimate=pl.CostEstimate(flops=25_000_000_000, bytes_accessed=60_000_000, transcendentals=4_000_000),
    )(*operands)


def assemble_kernel(gw1, gm0, gm1, gmg, gw2, va, vb, input_grad, output,
                    expand_o, mixer_o, merge_o, shrink_o, input_o, output_o, *vectors_o):
    step = pl.program_id(0)

    @pl.when(step < 5)
    def _():
        assemble_rows(gw1, gm0, gm1, gmg, expand_o, mixer_o, merge_o)

    @pl.when(step >= 5)
    def _():
        for odd in range(2):
            shrink_o[200 * odd : 200 * odd + 200] = gw2[odd, 8 * odd : 8 * odd + 200].astype(F32)

    @pl.when(step == 0)
    def _():
        input_o[...] = input_grad[...]
        output_o[...] = output[...]
        assemble_vectors(va, vb, vectors_o)


def assemble_rows(gw1, gm0, gm1, gmg, expand_o, mixer_o, merge_o):
    for j in range(8):
        odd = 8 * (j % 2)
        for q in range(4):
            at = 1600 * q + 200 * j
            expand_o[:, at : at + 200] = gw1[j, :, 208 * q + odd : 208 * q + odd + 200].astype(F32)
        for n in range(3):
            at = D * n + 192 * j
            mixer_o[:, at : at + 128] = gm0[j, :, 128 * n : 128 * n + 128].astype(F32)
            mixer_o[:, at + 128 : at + 192] = gm1[j, :, 128 * n : 128 * n + 64].astype(F32)
    for n in range(3):
        total = gm1[0, :, 128 * n : 128 * n + 128].astype(F32)
        for j in range(1, 8):
            total += gm1[j, :, 128 * n : 128 * n + 128].astype(F32)
        mixer_o[:, D * n + 1536 : D * n + 1600] = total[:, 64:]
    for j in range(6):
        merge_o[:, 256 * j : 256 * j + 256] = gmg[j].astype(F32)
    merge_o[:, 1536:1600] = gmg[6, :, :64].astype(F32)


def assemble_vectors(va, vb, vectors_o):
    p = lax.axis_index("fsdp")
    early, late = va[0], vb[0]
    for j in range(1, 8):
        early += va[j]
        late += vb[j]

    def per_head(n):
        return jnp.concatenate([va[j, n : n + 1, :192] for j in range(8)] + [early[n : n + 1, 192:256]], axis=1)

    rows = jnp.concatenate(
        [late[0:2], per_head(5), per_head(6), early[0:4]], axis=0
    )
    rows = jnp.concatenate([rows, jnp.zeros((8, 64), F32)], axis=1)
    rows = shift_left(rows, 400 * p)
    bias = jnp.concatenate([va[j, 4:5, :] for j in range(8)], axis=0)
    bias = shift_left(jnp.concatenate([bias, jnp.zeros((8, 64), F32)], axis=1), 208 * p)
    bias = jnp.concatenate([bias[j : j + 1, 8 * (j % 2) : 8 * (j % 2) + 200] for j in range(8)], axis=1)
    for n in range(8):
        vectors_o[n][...] = rows[n, :400]
    vectors_o[8][...] = bias[0]


def assemble(gw1, gm0, gm1, gmg, gw2, va, vb, input_grad, output):
    rows, first = 80, 5

    def part(width):
        return pl.BlockSpec((8, rows, width), lambda n: (0, jnp.minimum(n, first - 1), 0))

    def whole(width):
        return pl.BlockSpec((rows, width), lambda n: (jnp.minimum(n, first - 1), 0))

    own = pl.BlockSpec((128, D), lambda n: (0, 0))
    small = pl.BlockSpec((8, 8, D), lambda n: (0, 0, 0))

    def vector(width):
        return pl.BlockSpec((width,), lambda n: (0,))

    S = jax.ShapeDtypeStruct
    return pl.pallas_call(
        assemble_kernel,
        grid=(first + 4,),
        in_specs=[part(832), part(384), part(384), part(256), pl.BlockSpec((2, 208, D), lambda n: (jnp.maximum(n - first, 0), 0, 0)), small, small, own, own],
        out_specs=(whole(6400), whole(4800), whole(D), pl.BlockSpec((400, D), lambda n: (jnp.maximum(n - first, 0), 0)), own, own) + (vector(400),) * 8 + (vector(1600),),
        out_shape=(S((400, 6400), F32), S((400, 4800), F32), S((400, D), F32), S((1600, D), F32), S((128, D), F32), S((128, D), BF)) + (S((400,), F32),) * 8 + (S((1600,), F32),),
        compiler_params=pltpu.CompilerParams(vmem_limit_bytes=63 << 20),
    )(gw1, gm0, gm1, gmg, gw2, va, vb, input_grad, output)


def local_plain(
    tokens,
    first_gain,
    first_shift,
    mixer_weight,
    query_bias,
    value_bias,
    merge_weight,
    merge_bias,
    second_gain,
    second_shift,
    expand_weight,
    expand_bias,
    shrink_weight,
    shrink_bias,
    cotangent,
):
    planes = lax.axis_size("fsdp")
    ring = lax.axis_size("ctx")
    me = lax.axis_index("ctx")
    blocks = tokens.shape[2]
    local_rows = 2 * blocks
    half = blocks * ring
    length = 2 * half
    private = H // ring
    shared = H - private * ring
    pc, sc = private * HD, shared * HD
    hc = pc + sc
    shared_at = private * ring * HD
    share = D // planes
    ff_plane = expand_bias.shape[0]
    ff_part = ff_plane // ring
    cols = D // ring

    vectors = jnp.stack(
        [first_gain, first_shift, query_bias, value_bias, merge_bias, second_gain, second_shift, shrink_bias]
    )
    vectors = lax.all_gather(vectors, "fsdp", axis=1, tiled=True).astype(F32)
    gain1, shift1, qbias, vbias, mbias, gain2, shift2, sbias = [vectors[n] for n in range(8)]

    def head_columns(weight, base):
        mine = lax.dynamic_slice_in_dim(weight, base + me * pc, pc, weight.ndim - 1)
        every = weight[..., base + shared_at : base + D]
        return [mine, every]

    mixer_part = jnp.concatenate(
        head_columns(mixer_weight, 0) + head_columns(mixer_weight, D) + head_columns(mixer_weight, 2 * D), axis=1
    )
    mixer_mine = lax.all_gather(mixer_part, "fsdp", axis=0, tiled=True)

    merge_part = lax.dynamic_slice_in_dim(merge_weight, me * cols, cols, 1)
    merge_cols = lax.all_gather(merge_part, "fsdp", axis=0, tiled=True)
    merge_full = lax.all_gather(merge_cols, "ctx", axis=1, tiled=True)

    expand_part = expand_weight.reshape(share, planes, ring, ff_part)
    expand_part = lax.dynamic_index_in_dim(expand_part, me, 2, keepdims=False)
    expand_part = lax.all_to_all(expand_part, "fsdp", 1, 0, tiled=False).reshape(D, ff_part)
    expand_mine = lax.all_gather(expand_part, "ctx", axis=1, tiled=True)

    rows = tokens.reshape(local_rows, D).astype(F32)
    normal1, inverse1 = normalize(rows)
    first = (normal1 * gain1 + shift1).astype(BF)
    first_all = lax.all_gather(first.reshape(2, blocks, D), "ctx", axis=1, tiled=True).reshape(length, D)
    tangent_low = cotangent.reshape(local_rows, D)
    tangent = tangent_low.astype(F32)
    tangent_all = lax.all_gather(tangent_low, "fsdp", axis=0, tiled=True)

    mixed = dot(first_all, mixer_mine)
    qb = jnp.concatenate(head_columns(qbias, 0), axis=0)
    vb = jnp.concatenate(head_columns(vbias, 0), axis=0)
    query = (mixed[:, :hc] + qb).astype(BF)
    key = mixed[:, hc : 2 * hc].astype(BF)
    value = (mixed[:, 2 * hc :] + vb).astype(BF)
    half_index = jnp.arange(half, dtype=jnp.int32)
    place = jnp.concatenate([half_index, length - 1 - half_index])
    early = me * blocks + jnp.arange(blocks, dtype=jnp.int32)
    own_place = jnp.concatenate([early, length - 1 - early])
    allowed = place[None, :] <= place[:, None]
    own_allowed = place[None, :] <= own_place[:, None]

    def own_rows(values):
        parts = values.reshape(2, half, values.shape[1])
        return lax.dynamic_slice_in_dim(parts, me * blocks, blocks, 1).reshape(local_rows, values.shape[1])

    qp, kp, vp = heads_first(query[:, :pc]), heads_first(key[:, :pc]), heads_first(value[:, :pc])
    qs, ks, vs = heads_first(own_rows(query[:, pc:])), heads_first(key[:, pc:]), heads_first(value[:, pc:])
    out_p, top_p, total_p = attend(qp, kp, vp, allowed)
    out_s, top_s, total_s = attend(qs, ks, vs, own_allowed)
    att_heads = heads_last(out_p).astype(BF)
    att_pieces = lax.all_to_all(att_heads.reshape(2, ring, blocks, pc), "ctx", 1, 2, tiled=False)
    attended = jnp.concatenate(
        [att_pieces.reshape(local_rows, ring * pc), heads_last(out_s).astype(BF)], axis=1
    )
    hidden = rows + dot(attended, merge_full) + mbias
    normal2, inverse2 = normalize(hidden)
    second = (normal2 * gain2 + shift2).astype(BF)
    second_all = lax.all_gather(second, "fsdp", axis=0, tiled=True)
    attended_all = lax.all_gather(attended, "ctx", axis=0, tiled=True)

    pre = dot(second_all, expand_mine) + expand_bias.astype(F32)
    act, gate_pull = jax.vjp(lambda u: jax.nn.gelu(u, approximate=True), pre)
    act_low = act.astype(BF)
    act_grad = dot_t(tangent_all, shrink_weight)
    (pre_grad,) = gate_pull(act_grad)
    pre_low = pre_grad.astype(BF)
    second_part = dot_t(pre_low, expand_mine).astype(BF)
    second_grad = lax.psum_scatter(second_part, "fsdp", scatter_dimension=0, tiled=True).astype(F32)
    out_part = dot(act_low, shrink_weight).astype(BF)
    out_sum = lax.psum_scatter(out_part, "fsdp", scatter_dimension=0, tiled=True).astype(F32)
    output = (hidden + out_sum + sbias).astype(BF).reshape(1, 2, blocks, D)
    expand_bias_grad = jnp.sum(pre_grad, axis=0)
    shrink_grad = t_dot(act_low, tangent_all).astype(BF)
    shrink_mine = lax.psum_scatter(shrink_grad, "ctx", scatter_dimension=0, tiled=True)
    shrink_owned = lax.all_gather(shrink_mine, "ctx", axis=0, tiled=True).astype(F32)
    expand_grad = t_dot(second_all, pre_low).astype(BF)
    expand_cols = lax.psum_scatter(expand_grad, "ctx", scatter_dimension=1, tiled=True)
    expand_rows = lax.all_to_all(expand_cols.reshape(planes, share, ff_part), "fsdp", 0, 1, tiled=False)
    expand_owned = (
        lax.all_gather(expand_rows, "ctx", axis=2, tiled=False).reshape(share, planes * ff_plane).astype(F32)
    )

    hidden_grad = tangent + norm_back(second_grad, gain2, normal2, inverse2)
    hidden_low = hidden_grad.astype(BF)
    att_grad = dot_t(hidden_low, merge_full).astype(BF)
    grad_pieces = lax.all_to_all(att_grad[:, :shared_at].reshape(2, blocks, ring, pc), "ctx", 2, 1, tiled=False)
    grad_p = heads_first(grad_pieces.reshape(length, pc))
    grad_s = heads_first(att_grad[:, shared_at:])
    dqp, dkp, dvp = attend_back(qp, kp, vp, allowed, top_p, total_p, grad_p)
    dqs, dks, dvs = attend_back(qs, ks, vs, own_allowed, top_s, total_s, grad_s)
    dqs_all = jnp.zeros((2, half, sc), F32)
    dqs_all = lax.dynamic_update_slice_in_dim(dqs_all, heads_last(dqs).reshape(2, blocks, sc), me * blocks, 1)
    mixed_grad = jnp.concatenate(
        [heads_last(dqp), dqs_all.reshape(length, sc)]
        + [heads_last(dkp), heads_last(dks), heads_last(dvp), heads_last(dvs)],
        axis=1,
    )
    bias_sums = jnp.sum(mixed_grad, axis=0)
    mixed_low = mixed_grad.astype(BF)
    first_part = dot_t(mixed_low, mixer_mine).astype(BF)
    first_grad = lax.psum_scatter(
        first_part.reshape(2, half, D), "ctx", scatter_dimension=1, tiled=True
    ).reshape(local_rows, D).astype(F32)
    input_grad = hidden_grad + norm_back(first_grad, gain1, normal1, inverse1)
    mixer_part_grad = t_dot(first_all, mixed_low).astype(BF)
    mixer_rows = lax.psum_scatter(mixer_part_grad, "fsdp", scatter_dimension=0, tiled=True)
    mixer_all = lax.all_gather(mixer_rows, "ctx", axis=0, tiled=False).astype(F32)

    def place_columns(values):
        mine = values[:, :, :pc].transpose(1, 0, 2).reshape(share, ring * pc)
        return [mine, jnp.sum(values[:, :, pc:], axis=0)]

    mixer_owned = jnp.concatenate(
        place_columns(mixer_all[:, :, :hc])
        + place_columns(mixer_all[:, :, hc : 2 * hc])
        + place_columns(mixer_all[:, :, 2 * hc :]),
        axis=1,
    )
    hidden_cols = lax.all_to_all(hidden_low.reshape(local_rows, ring, cols), "ctx", 1, 0, tiled=False)
    merge_grad = t_dot(attended_all, hidden_cols.reshape(length, cols)).astype(BF)
    merge_rows = lax.psum_scatter(merge_grad, "fsdp", scatter_dimension=0, tiled=True)
    merge_owned = lax.all_gather(merge_rows, "ctx", axis=1, tiled=True).astype(F32)

    def spread_bias(values):
        full = jnp.zeros((D,), F32)
        full = lax.dynamic_update_slice_in_dim(full, values[:pc], me * pc, 0)
        return full.at[shared_at:].set(values[pc:])

    sums = jnp.stack(
        [
            jnp.sum(first_grad * normal1, axis=0),
            jnp.sum(first_grad, axis=0),
            spread_bias(bias_sums[:hc]),
            spread_bias(bias_sums[2 * hc :]),
            jnp.sum(hidden_grad, axis=0),
            jnp.sum(second_grad * normal2, axis=0),
            jnp.sum(second_grad, axis=0),
            jnp.sum(tangent, axis=0),
        ]
    )
    sums = lax.psum(sums, ("fsdp", "ctx"))
    mine = lax.dynamic_slice_in_dim(sums, lax.axis_index("fsdp") * share, share, 1)
    expand_bias_owned = lax.psum(expand_bias_grad, "ctx")

    return (
        output,
        input_grad.reshape(1, 2, blocks, D),
        mine[0],
        mine[1],
        mixer_owned,
        mine[2],
        mine[3],
        merge_owned,
        mine[4],
        mine[5],
        mine[6],
        expand_owned,
        expand_bias_owned,
        shrink_owned,
        mine[7],
    )


def local_kernel(
    tokens,
    first_gain,
    first_shift,
    mixer_weight,
    query_bias,
    value_bias,
    merge_weight,
    merge_bias,
    second_gain,
    second_shift,
    expand_weight,
    expand_bias,
    shrink_weight,
    shrink_bias,
    cotangent,
):
    planes = lax.axis_size("fsdp")
    blocks, local_rows = tokens.shape[2], 2 * tokens.shape[2]
    vectors = (
        first_gain, first_shift, query_bias, value_bias, merge_bias, second_gain, second_shift, shrink_bias, expand_bias
    )

    tok2, cot2 = tokens.reshape(local_rows, D), cotangent.reshape(local_rows, D)
    hidden, qkv, attown, heads, whole, lse, first_all, mws, mfull, w1_all, sec_all, g_all, w2_early = run_attend(
        planes, tok2, cot2, vectors, mixer_weight, merge_weight, expand_weight, shrink_weight
    )
    input_part, out_part, va, vb, gw1, gw2, gm0, gm1, gmg, _, _ = run_backward(
        planes, whole, attown, tok2, cot2, hidden, lse, qkv, heads,
        shrink_weight, w2_early, w1_all, sec_all, g_all, mfull.reshape(D, D), mws, first_all.reshape(8, 128, D)
    )
    expand_owned, mixer_owned, merge_owned, shrink_owned, input_grad, out_own, *small = assemble(
        gw1, gm0, gm1, gmg, gw2, va, vb, input_part, out_part
    )
    gain1, shift1, qbias, vbias, mbias, gain2, shift2, sbias, bias1 = small

    return (
        out_own.reshape(1, 2, blocks, D),
        input_grad.reshape(1, 2, blocks, D),
        gain1,
        shift1,
        mixer_owned,
        qbias,
        vbias,
        merge_owned,
        mbias,
        gain2,
        shift2,
        expand_owned,
        bias1,
        shrink_owned,
        sbias,
    )


def aligned(planes, ring, shape):
    return planes == 4 and ring == 8 and shape == (4, 2, 512, D)


def local(tokens, *others):
    planes, ring = lax.axis_size("fsdp"), lax.axis_size("ctx")
    whole = (tokens.shape[0] * planes, 2, tokens.shape[2] * ring, tokens.shape[3])
    if aligned(planes, ring, whole):
        return local_kernel(tokens, *others)
    return local_plain(tokens, *others)


def solution(mesh):
    token_spec = P("fsdp", None, "ctx", None)
    row = P("fsdp")
    matrix = P("fsdp", None)
    in_specs = (
        token_spec,
        row,
        row,
        matrix,
        row,
        row,
        matrix,
        row,
        row,
        row,
        matrix,
        row,
        matrix,
        row,
        token_spec,
    )
    out_specs = (
        token_spec,
        token_spec,
        row,
        row,
        matrix,
        row,
        row,
        matrix,
        row,
        row,
        row,
        matrix,
        row,
        matrix,
        row,
    )
    return jax.shard_map(local, mesh=mesh, in_specs=in_specs, out_specs=out_specs, check_vma=False)
```

```python
import functools

import jax
import jax.numpy as jnp
from jax import lax
from jax.experimental import pallas as pl
from jax.experimental.pallas import tpu as pltpu
from jax.sharding import PartitionSpec as P

D = 1600
H = 25
HD = 64

EPSILON = 1e-05
SCORE_SCALE = 0.125
BF = jnp.bfloat16
F32 = jnp.float32


def normalize(values):
    center = values - jnp.mean(values, axis=-1, keepdims=True)
    spread = jnp.mean(center * center, axis=-1, keepdims=True)
    inverse = lax.rsqrt(spread + EPSILON)
    return center * inverse, inverse


def norm_back(grad, gain, normal, inverse):
    scaled = grad * gain
    mean = jnp.mean(scaled, axis=-1, keepdims=True)
    along = jnp.mean(scaled * normal, axis=-1, keepdims=True)
    return inverse * (scaled - mean - normal * along)


def dot(a, b):
    return jnp.dot(a, b, preferred_element_type=F32)


def dot_t(a, b):
    return lax.dot_general(a, b, (((1,), (1,)), ((), ())), preferred_element_type=F32)


def t_dot(a, b):
    return lax.dot_general(a, b, (((0,), (0,)), ((), ())), preferred_element_type=F32)


def attend(query, key, value, allowed):
    scores = jnp.einsum("hqd,hkd->hqk", query, key, preferred_element_type=F32) * SCORE_SCALE
    scores = jnp.where(allowed[None], scores, -1e30)
    top = jnp.max(scores, axis=-1, keepdims=True)
    expo = jnp.exp(scores - top)
    total = jnp.sum(expo, axis=-1, keepdims=True)
    probs = (expo / total).astype(BF)
    return jnp.einsum("hqk,hkd->hqd", probs, value, preferred_element_type=F32), top, total


def attend_back(query, key, value, allowed, top, total, grad):
    scores = jnp.einsum("hqd,hkd->hqk", query, key, preferred_element_type=F32) * SCORE_SCALE
    scores = jnp.where(allowed[None], scores, -1e30)
    probs = jnp.exp(scores - top) / total
    probs_low = probs.astype(BF)
    prob_grad = jnp.einsum("hqd,hkd->hqk", grad, value, preferred_element_type=F32)
    offset = jnp.sum(prob_grad * probs, axis=-1, keepdims=True)
    score_grad = (probs * (prob_grad - offset)).astype(BF)
    dq = jnp.einsum("hqk,hkd->hqd", score_grad, key, preferred_element_type=F32) * SCORE_SCALE
    dk = jnp.einsum("hqk,hqd->hkd", score_grad, query, preferred_element_type=F32) * SCORE_SCALE
    dv = jnp.einsum("hqk,hqd->hkd", probs_low, grad, preferred_element_type=F32)
    return dq, dk, dv


def heads_first(values):
    rows, columns = values.shape
    return values.reshape(rows, columns // HD, HD).transpose(1, 0, 2)


def heads_last(values):
    heads, rows, _ = values.shape
    return values.transpose(1, 0, 2).reshape(rows, heads * HD)


MESH_ID = pl.DeviceIdType.MESH


def dyn(start, size, step):
    return pl.ds(pl.multiple_of(start, step), size)


class Links:

    def __init__(self, planes):
        self.planes = planes
        self.p = lax.axis_index("fsdp")
        self.me = lax.axis_index("ctx")

    def plane(self, step):
        return (self.p + step, self.me)

    def peer(self, mask):
        return (self.p, self.me ^ mask)

    def copy(self, src, dst, send, recv, device):
        return pltpu.make_async_remote_copy(
            src_ref=src, dst_ref=dst, send_sem=send, recv_sem=recv, device_id=device, device_id_type=MESH_ID
        )

    def arrive(self, masks):
        bar = pltpu.get_barrier_semaphore()
        for mask in masks:
            pl.semaphore_signal(bar, inc=1, device_id=self.peer(mask), device_id_type=MESH_ID)
        for d in range(1, self.planes):
            to = (lax.rem(self.p + d, self.planes), self.me)
            pl.semaphore_signal(bar, inc=1, device_id=to, device_id_type=MESH_ID)

    def barrier(self, masks):
        pl.semaphore_wait(pltpu.get_barrier_semaphore(), len(masks) + self.planes - 1)


class LineGather:

    def __init__(self, links, src, slot, sems, local_sem):
        self.links, self.slot, self.sems, self.local_sem = links, slot, sems, local_sem
        self.stays = src is None
        self.src = slot(links.p) if src is None else src

    def send(self, src, block, step):
        way = 1 if step > 0 else 2
        return self.links.copy(
            src, self.slot(block), self.sems.at[way, block], self.sems.at[0, block], self.links.plane(step)
        )

    def arrival(self, block):
        return self.links.copy(
            self.slot(block), self.slot(block), self.sems.at[1, block], self.sems.at[0, block], self.links.plane(0)
        )

    def start(self):
        p, last = self.links.p, self.links.planes - 1

        @pl.when(p < last)
        def _():
            self.send(self.src, p, 1).start()

        @pl.when(p > 0)
        def _():
            self.send(self.src, p, -1).start()

        if not self.stays:
            pltpu.make_async_copy(self.src, self.slot(p), self.local_sem).start()

    def pump(self, d):
        p, last = self.links.p, self.links.planes - 1

        @pl.when(p >= d)
        def _():
            self.arrival(p - d).wait_recv()

            @pl.when(p < last)
            def _():
                self.send(self.slot(p - d), p - d, 1).start()

        @pl.when(p + d <= last)
        def _():
            self.arrival(p + d).wait_recv()

            @pl.when(p > 0)
            def _():
                self.send(self.slot(p + d), p + d, -1).start()

        if d == 1 and not self.stays:
            pltpu.make_async_copy(self.src, self.slot(p), self.local_sem).wait()

    def finish(self):
        p, last = self.links.p, self.links.planes - 1
        for d in range(self.links.planes):

            @pl.when((p >= d) & (p < last))
            def _():
                self.send(self.slot(p - d), p - d, 1).wait_send()

            @pl.when((p + d <= last) & (p > 0))
            def _():
                self.send(self.slot(p + d), p + d, -1).wait_send()


class EdgeGather:

    def __init__(self, links, own, early, buffer, send, recv, local):
        self.links, self.own, self.early, self.buffer = links, own, early, buffer
        self.send_sem, self.recv_sem, self.local = send, recv, local

    def block(self, ref, t):
        return ref.at[208 * t : 208 * t + 208]

    def copy(self, src, t, n, to):
        return self.links.copy(
            src, self.block(self.buffer, t), self.send_sem.at[n], self.recv_sem.at[t], (to, self.links.me)
        )


    def outward(self):
        for p, t, to in ((0, 0, 1), (3, 3, 2)):

            @pl.when(self.links.p == p)
            def _():
                self.copy(self.own, t, 0, to).start()

    def between(self):
        for p, t, to in ((1, 1, 2), (2, 2, 1)):

            @pl.when(self.links.p == p)
            def _():
                self.copy(self.own, t, 0, to).start()

    def finish_early(self):
        for p, came in ((0, ()), (1, (0, 2)), (2, (3, 1)), (3, ())):

            @pl.when(self.links.p == p)
            def _():
                self.copy(self.own, p, 0, p ^ 1).wait_send()
                for t in came:
                    self.copy(self.own, t, 0, p ^ 1).wait_recv()


    def loads(self, p):
        made = [pltpu.make_async_copy(self.own, self.block(self.buffer, p), self.local.at[0])]
        for n, t in enumerate(((), (0, 2), (3, 1), ())[p]):
            made.append(pltpu.make_async_copy(self.block(self.early, t), self.block(self.buffer, t), self.local.at[1 + n]))
        return made

    def sent(self, p, n):
        end, far, near, middle = ((0, 3, 2, 2), (3, 0, 1, 1))[p - 1]
        t, to = ((p, end), (near, end), (end, middle), (far, end))[n]
        src = (self.own, self.early, self.early, self.buffer)[n]
        return self.copy(src if n == 0 else self.block(src, t), t, n, to)

    def start(self):
        for p in range(4):

            @pl.when(self.links.p == p)
            def _():
                for c in self.loads(p):
                    c.start()
                if p in (1, 2):
                    for n in range(3):
                        self.sent(p, n).start()

    def relay(self):
        for p, far in ((1, 3), (2, 0)):

            @pl.when(self.links.p == p)
            def _():
                self.copy(self.own, far, 3, p).wait_recv()
                self.sent(p, 3).start()

    def wait(self):
        for p in range(4):

            @pl.when(self.links.p == p)
            def _():
                for c in self.loads(p):
                    c.wait()
                if p in (0, 3):
                    for t in range(4):
                        if t != p:
                            self.copy(self.own, t, 0, p).wait_recv()

    def finish(self):
        for p in (1, 2):

            @pl.when(self.links.p == p)
            def _():
                for n in range(4):
                    self.sent(p, n).wait_send()


class LineExchange:

    def __init__(self, links, slots, send, recv):
        self.links, self.slots, self.send_sem, self.recv_sem = links, slots, send, recv

    def copy(self, src, d):
        planes = self.links.planes
        to = lax.rem(self.links.p + d, planes)
        return self.links.copy(src, self.slots.at[d - 1], self.send_sem.at[d - 1], self.recv_sem.at[d - 1], (to, self.links.me))

    def start(self, src):
        for d in range(1, self.links.planes):
            self.copy(src, d).start()

    def total(self, src):
        acc = src[...].astype(F32)
        for d in range(1, self.links.planes):
            self.copy(src, d).wait_recv()
            acc = acc + self.slots[d - 1].astype(F32)
        return acc

    def finish(self, src):
        for d in range(1, self.links.planes):
            self.copy(src, d).wait_send()


class SmallGather:

    def __init__(self, links, src, slot, send, recv, local_sem):
        self.links, self.src, self.slot, self.send_sem, self.recv_sem, self.local_sem = links, src, slot, send, recv, local_sem

    def copy(self, owner, mask, n):
        src = self.src if n < 4 else self.slot(owner)
        return self.links.copy(src, self.slot(owner), self.send_sem.at[n], self.recv_sem.at[owner, 0], self.links.peer(mask))

    def start(self):
        for n, mask in enumerate((2, 4, 6, 1)):
            self.copy(self.links.me, mask, n).start()
        pltpu.make_async_copy(self.src, self.slot(self.links.me), self.local_sem).start()

    def forward(self):
        for n, mask in enumerate((2, 4, 6)):
            owner = self.links.me ^ mask
            self.copy(owner, mask, 4 + n).wait_recv()
            self.copy(owner, 1, 4 + n).start()

    def wait(self):
        for mask in (1, 3, 5, 7):
            self.copy(self.links.me ^ mask, 1, 4).wait_recv()

    def finish(self):
        for n in range(7):
            self.copy(self.links.me, 1, n).wait_send()
        pltpu.make_async_copy(self.src, self.slot(self.links.me), self.local_sem).wait()


class GroupGather:

    def __init__(self, links, part, send, recv, src=None, local_sem=None):
        self.links, self.part, self.send_sem, self.recv_sem = links, part, send, recv
        self.src, self.local_sem = src, local_sem

    def copy(self, owner, h, mask, n, src=None):
        return self.links.copy(
            self.part(owner, h) if src is None else src,
            self.part(owner, h),
            self.send_sem.at[n],
            self.recv_sem.at[owner, h],
            self.links.peer(mask),
        )

    def own(self, n):
        h, mask = ((1, 2), (0, 4), (0, 2), (1, 4), (0, 1), (1, 1))[n]
        return self.copy(self.links.me, h, mask, n, None if self.src is None else self.src(h))

    def stay(self, h):
        return pltpu.make_async_copy(self.src(h), self.part(self.links.me, h), self.local_sem.at[h])

    def start(self):
        for n in range(6):
            self.own(n).start()
        if self.src is not None:
            for h in range(2):
                self.stay(h).start()

    def pass_on(self, mask, h, n):
        owner = self.links.me ^ mask
        self.copy(owner, h, 1, n).wait_recv()
        if n < 8:
            self.copy(owner, h, 6 - mask, n).start()
        self.copy(owner, h, 1, n + 2).start()

    def forward(self):
        self.pass_on(2, 1, 6)
        self.pass_on(4, 0, 7)
        self.pass_on(2, 0, 8)
        self.pass_on(4, 1, 9)

    def forward_last(self):
        self.pass_on(6, 0, 10)
        self.pass_on(6, 1, 11)

    def wait(self):
        self.forward_last()
        for mask in (1, 3, 5, 7):
            for h in range(2):
                self.copy(self.links.me ^ mask, h, 1, 6).wait_recv()
        if self.src is not None:
            for h in range(2):
                self.stay(h).wait()

    def finish(self):
        me = self.links.me
        for n in range(6):
            self.own(n).wait_send()
        self.copy(me ^ 2, 1, 1, 6).wait_send()
        self.copy(me ^ 4, 0, 1, 7).wait_send()
        for mask, h, n in ((2, 1, 8), (4, 0, 9), (2, 0, 10), (4, 1, 11), (6, 0, 12), (6, 1, 13)):
            self.copy(me ^ mask, h, 1, n).wait_send()


def row_parts(ref, cut):
    rows = ref.shape[-2]
    return lambda j, h: ref.at[j, 0:cut] if h == 0 else ref.at[j, cut:rows]


def own_parts(ref, cut):
    rows = ref.shape[-2]
    return lambda h: ref.at[0:cut] if h == 0 else ref.at[cut:rows]


class GroupSum:

    def __init__(self, links, stage, from_twin, from_far, send, twin_recv, far_recv):
        self.links, self.stage, self.from_twin, self.from_far = links, stage, from_twin, from_far
        self.send, self.twin_recv, self.far_recv = send, twin_recv, far_recv
        self.rows = stage.shape[1] // 2

    def to_twin(self, chip):
        return self.links.copy(
            self.stage.at[4 + chip], self.from_twin.at[chip], self.send.at[4 + chip], self.twin_recv.at[chip], self.links.peer(1)
        )

    def to_far(self, chip, h, mask):
        at = pl.ds(h * self.rows, self.rows)
        n = 2 * (chip - 1) + h
        return self.links.copy(
            self.stage.at[chip, at], self.from_far.at[chip - 1, at], self.send.at[8 + n], self.far_recv.at[n], self.links.peer(mask)
        )

    def run(self, block):
        me = self.links.me
        masks = (0, 2, 4, 6)
        for chip in (3, 1, 2, 0):
            self.stage[4 + chip] = block(me ^ masks[chip] ^ 1).astype(BF)
            self.to_twin(chip).start()
        for chip in (3, 1, 2):
            part = block(me ^ masks[chip])
            self.to_twin(chip).wait_recv()
            self.stage[chip] = (part + self.from_twin[chip].astype(F32)).astype(BF)
            if chip == 3:
                self.to_far(3, 0, 2).start()
                self.to_far(3, 1, 4).start()
            elif chip == 1:
                self.to_far(1, 0, 2).start()
            else:
                self.to_far(2, 1, 4).start()
        self.stage[0] = block(me).astype(BF)

    def relay(self):
        half = self.rows
        for chip, h, mask in ((2, 0, 4), (1, 1, 2)):
            at = slice(h * half, h * half + half)
            self.to_far(3, h, mask).wait_recv()
            self.stage[chip, at] = (self.stage[chip, at].astype(F32) + self.from_far[2, at].astype(F32)).astype(BF)
            self.to_far(chip, h, mask).start()

    def total(self):
        self.to_twin(0).wait_recv()
        acc = self.stage[0].astype(F32) + self.from_twin[0].astype(F32)
        for chip, mask in ((1, 2), (2, 4)):
            for h in range(2):
                self.to_far(chip, h, mask).wait_recv()
            acc += self.from_far[chip - 1].astype(F32)
        return acc

    def finish(self):
        for chip in range(4):
            self.to_twin(chip).wait_send()
        for chip, h, mask in ((3, 0, 2), (3, 1, 4), (1, 0, 2), (1, 1, 2), (2, 0, 4), (2, 1, 4)):
            self.to_far(chip, h, mask).wait_send()


def gelu_parts(u):
    inner = 0.7978845608 * (u + 0.044715 * (u * u * u))
    t = jnp.tanh(inner)
    value = 0.5 * u * (1.0 + t)
    slope = 0.5 * (1.0 + t) + 0.5 * u * (1.0 - t * t) * (0.7978845608 * (1.0 + 3 * 0.044715 * (u * u)))
    return value, slope


BLOCK_KEYS = (
    ((0, 256, 1),),
    ((0, 256, 0), (256, 256, 1)),
    ((0, 512, 0), (512, 256, 2), (768, 256, 0)),
    ((0, 512, 0), (768, 256, 2)),
)


def triangle(kind, shape):
    r = lax.broadcasted_iota(jnp.int32, shape, 0)
    c = lax.broadcasted_iota(jnp.int32, shape, 1)
    return c <= r if kind == 1 else c >= r


def half_mask(half):
    lane = lax.broadcasted_iota(jnp.int32, (1, 128), 1)
    return (lane // 64) == half


def softmax_pieces(q, keys, values, pieces, allowed):
    scores = []
    for start, size, kind in pieces:
        s = dot_t(q, keys[start : start + size])
        if kind:
            s = jnp.where(allowed(kind, start, s.shape), s, -1e30)
        scores.append(s)
    top = jnp.max(scores[0], axis=1, keepdims=True)
    for s in scores[1:]:
        top = jnp.maximum(top, jnp.max(s, axis=1, keepdims=True))
    total, out = 0.0, 0.0
    for s, (start, size, _) in zip(scores, pieces):
        e = jnp.exp(s - top)
        total = total + jnp.sum(e, axis=1, keepdims=True)
        out = out + dot(e.astype(BF), values[start : start + size])
    return out * (1.0 / total), top + jnp.log(total)


def shift_left(values, lanes):
    return pltpu.roll(values, lax.rem(values.shape[1] - lanes, values.shape[1]), 1)


def small_vectors(parts, p, me):
    wide = 1664
    values = [part[...].astype(F32).reshape(1, part.shape[0]) for part in parts]
    rows = jnp.concatenate([jnp.concatenate(values[:8], axis=0), jnp.zeros((8, wide - 400), F32)], axis=1)
    rows = pltpu.roll(rows, 400 * p, 1)
    mine = shift_left(rows, 192 * me)
    heads = jnp.concatenate([mine[:, :192], rows[:, 1536:1600], jnp.zeros((8, wide - 256), F32)], axis=1)
    n = lax.broadcasted_iota(jnp.int32, (8, 1), 0)
    rows = jnp.where((n == 2) | (n == 3), heads, rows)
    bias = jnp.concatenate([values[8], jnp.zeros((1, wide - 1600), F32)], axis=1)
    bias = shift_left(jnp.broadcast_to(bias, (8, wide)), 200 * me)
    lane = lax.broadcasted_iota(jnp.int32, (1, wide), 1)
    bias = pltpu.roll(jnp.where(lane < 200, bias, 0.0), 208 * p + 8 * lax.rem(me, 2), 1)
    bias = jnp.where(n == 0, bias, 0.0)
    return jnp.concatenate([rows, bias], axis=0).astype(BF)


def attend_kernel(planes, tok, cot, v0, v1, v2, v3, v4, v5, v6, v7, v8, mixer_h, merge, expand, shrink,
                  hidden_o, qkv_o, att_o, heads_o, vec_o, lse_o,
                  first_o, mw_o, mfull_o, w1_o, sec_o, g_o, w2_o,
                  mixer, vpart, raw1, own1, vec, mw0, mw1, mgs, mfull, first_all, second, arecv,
                  zs, zl, w2_s, w2_r, v_s, v_r, gs, gr, gl, gl2, a_s, a_r, os):
    L = Links(planes)
    L.arrive(range(1, 8))
    qkv, attown, hid, lse, att = qkv_o, att_o, hidden_o, lse_o, heads_o
    p, me = L.p, L.me
    share = 400
    xv = LineExchange(L, vec, v_s, v_r)
    zm0 = LineGather(L, None, lambda b: mw0.at[dyn(b * share, share, 16)], zs.at[0], zl.at[0])
    zm1 = LineGather(L, None, lambda b: mw1.at[dyn(b * share, share, 16)], zs.at[1], zl.at[0])
    zmg = LineGather(L, None, lambda b: mgs.at[b], zs.at[2], zl.at[0])
    zw1 = LineGather(L, own1, lambda b: w1_o.at[dyn(b * share, share, 16)], zs.at[3], zl.at[0])
    early = EdgeGather(L, shrink.at[dyn(200 * me - 8 * lax.rem(me, 2), 208, 16)], None, w2_o, w2_s, w2_r, None)
    gfirst = GroupGather(L, lambda j, h: first_all.at[h, j], gs.at[0], gr.at[0])
    gsec = GroupGather(L, row_parts(sec_o, 64), gs.at[1], gr.at[1], own_parts(second, 64), gl)
    gg = GroupGather(L, row_parts(g_o, 64), gs.at[3], gr.at[3], own_parts(cot, 64), gl2)
    gmerge = GroupGather(L, lambda j, h: mfull.at[2 * h : 2 * h + 2, dyn(j * 48, 48, 16)], gs.at[2], gr.at[2])

    takes = [
        pltpu.make_async_copy(merge.at[dyn(me * 48, 48, 16)], mgs.at[p, 0:48], zl.at[1]),
        pltpu.make_async_copy(merge.at[384:400], mgs.at[p, 48:64], zl.at[2]),
        pltpu.make_async_copy(expand, raw1, zl.at[3]),
    ]
    mixer_in = pltpu.make_async_copy(mixer_h, mixer, zl.at[4])
    mixer_in.start()
    for c in takes:
        c.start()
    vpart[...] = small_vectors((v0, v1, v2, v3, v4, v5, v6, v7, v8), p, me)
    at_own = dyn(p * share, share, 16)
    mixer_in.wait()

    def head_columns(n):
        odd = lax.rem(n + me, 2)
        x = mixer[:, dyn(D * n + 192 * me - 64 * odd, 256, 128)]
        return jnp.where(odd == 1, jnp.concatenate([x[:, 64:], x[:, :64]], axis=1), x)

    for n in range(3):
        mine = head_columns(n)
        mw0[at_own, 128 * n : 128 * n + 128] = mine[:, :128]
        every = mixer[:, D * n + 1536 : D * n + 1600]
        mw1[at_own, 128 * n : 128 * n + 128] = jnp.concatenate([mine[:, 128:192], every], axis=1)
    L.barrier(range(1, 8))
    xv.start(vpart)
    zm0.start()
    rows = tok[...].astype(F32)
    normal, _ = normalize(rows)
    vectors = xv.total(vpart)[:, :D]
    first = (normal * vectors[0:1] + vectors[1:2]).astype(BF)
    first_all[:, me] = first.reshape(2, 64, D)
    gfirst.start()
    takes[2].wait()
    odd_me = lax.rem(me, 2)
    lane = lax.broadcasted_iota(jnp.int32, (1, 384), 1)
    for q in range(4):
        start = 1600 * q + 200 * me
        base = jnp.minimum(start // 128 * 128, 6400 - 384)
        x = shift_left(raw1[:, dyn(base, 384, 128)].astype(F32), lax.rem(start - base - 8 * odd_me + 384, 384))
        x = jnp.where((lane >= 8 * odd_me) & (lane < 8 * odd_me + 200), x, 0.0)
        own1[:, 208 * q : 208 * q + 208] = x[:, :208].astype(BF)
    zm0.pump(1)
    zm0.pump(2)
    takes[0].wait()
    takes[1].wait()
    zmg.start()
    gfirst.forward()
    zm0.pump(3)
    zmg.pump(1)
    gfirst.wait()
    zmg.pump(2)
    zm1.start()

    def mix(weights, pair):
        bias_q = vectors[2:3, pair * 128 : pair * 128 + 128]
        bias_v = vectors[3:4, pair * 128 : pair * 128 + 128]

        def body(b, _):
            x = first_all[b // 2, pl.ds((b % 2) * 4, 4)].reshape(256, D)
            mixed = dot(x, weights[...])
            at = dyn(b * 256, 256, 256)
            qkv[pair, at] = (mixed[:, :128] + bias_q).astype(BF)
            qkv[2 + pair, at] = mixed[:, 128:256].astype(BF)
            qkv[4 + pair, at] = (mixed[:, 256:] + bias_v).astype(BF)
            return 0

        lax.fori_loop(0, 4, body, 0)

    lane128 = lax.broadcasted_iota(jnp.int32, (1, 128), 1)

    def note_lse(head, at, value):
        lse[at] = jnp.where(lane128 == head, value, lse[at] if head else 0.0)

    def attend_private(pair, half):
        mask = half_mask(half)
        for b in range(4):
            q = jnp.where(mask, qkv[pair, b * 256 : b * 256 + 256], 0) * jnp.asarray(0.125, BF)
            out, l = softmax_pieces(
                q, qkv.at[2 + pair], qkv.at[4 + pair], BLOCK_KEYS[b], lambda kind, start, shape: triangle(kind, shape)
            )
            out = jnp.where(mask, out, 0.0).astype(BF).reshape(4, 64, 128)
            at = pl.ds((b % 2) * 4, 4)
            if half == 0:
                att[pair, b // 2, at] = out
            else:
                att[pair, b // 2, at] = att[pair, b // 2, at] + out
            note_lse(2 * pair + half, slice(b * 256, b * 256 + 256), l)

    def own_allowed(kind, start, shape):
        r = lax.broadcasted_iota(jnp.int32, shape, 0)
        c = lax.broadcasted_iota(jnp.int32, shape, 1)
        rp = jnp.where(r < 64, me * 64 + r, 1023 - (me * 64 + r - 64))
        cp = jnp.where(c < 512, c, 1023 - (c - 512))
        return cp <= rp

    mix(mw0, 0)
    zmg.pump(3)
    for b in range(4):
        mfull[b, dyn(me * 48, 48, 16)] = mgs[b, 0:48]
        mfull[b, 384:400] = mgs[b, 48:64]
    gmerge.start()
    attend_private(0, 0)
    zm1.pump(1)
    attend_private(0, 1)
    zm1.pump(2)
    zw1.start()
    gmerge.forward()
    gg.start()
    zm1.pump(3)
    mix(mw1, 1)
    outs = [
        pltpu.make_async_copy(first_all, first_o, os.at[0]),
        pltpu.make_async_copy(mw0, mw_o.at[0], os.at[1]),
        pltpu.make_async_copy(mw1, mw_o.at[1], os.at[2]),
        pltpu.make_async_copy(mfull, mfull_o, os.at[3]),
    ]
    for c in outs[:3]:
        c.start()
    attend_private(1, 0)
    qs = jnp.concatenate([qkv[1, dyn(me * 64, 64, 64)], qkv[1, dyn(512 + me * 64, 64, 64)]], axis=0)
    mask1 = half_mask(1)
    qs = jnp.where(mask1, qs, 0) * jnp.asarray(0.125, BF)
    out_s, l_s = softmax_pieces(qs, qkv.at[3], qkv.at[5], ((0, 1024, 1),), own_allowed)
    note_lse(3, slice(0, 128), l_s)
    shared_low = jnp.where(mask1, out_s, 0.0).astype(BF)

    def exchange(mask):
        return L.copy(att.at[:, :, me ^ mask], arecv.at[me], a_s.at[mask], a_r.at[me], L.peer(mask))

    def arrived(mask):
        return L.copy(att.at[:, :, me], arecv.at[me ^ mask], a_s.at[mask], a_r.at[me ^ mask], L.peer(mask))

    for mask in range(1, 8):
        exchange(mask).start()
    arecv[me] = att[:, :, me]
    gg.forward()
    for mask in range(1, 8):
        arrived(mask).wait_recv()
    for j in range(8):
        attown[:, 192 * j : 192 * j + 128] = arecv[j, 0].reshape(128, 128)
        attown[:, 192 * j + 128 : 192 * j + 192] = arecv[j, 1].reshape(128, 128)[:, :64]
    attown[:, 1536:1600] = shared_low[:, 64:128]
    gmerge.wait()
    hidden = rows + vectors[4:5]
    hid[...] = hidden
    for b in range(4):
        hid[...] += dot(attown[:, b * 400 : b * 400 + 400], mfull[b])
    normal2, _ = normalize(hid[...])
    second[...] = (normal2 * vectors[5:6] + vectors[6:7]).astype(BF)
    gsec.start()
    outs[3].start()
    vec_o[...] = vectors
    zw1.pump(1)
    early.outward()
    gg.wait()
    gsec.forward()
    zw1.pump(2)
    early.between()
    gsec.wait()
    zw1.pump(3)
    for c in outs:
        c.wait()
    xv.finish(vpart)
    early.finish_early()
    for z in (zm0, zm1, zmg, zw1):
        z.finish()
    for g in (gfirst, gg, gsec, gmerge):
        g.finish()
    for mask in range(1, 8):
        exchange(mask).wait_send()


def run_attend(planes, tok, cot, vectors, mixer, merge, expand, shrink):
    any_ = pl.BlockSpec(memory_space=pl.ANY)
    vm = pl.BlockSpec(memory_space=pltpu.VMEM)
    S = jax.ShapeDtypeStruct
    V = pltpu.VMEM
    dma = pltpu.SemaphoreType.DMA
    return pl.pallas_call(
        functools.partial(attend_kernel, planes),
        out_shape=(
            S((128, D), F32), S((6, 1024, 128), BF), S((128, D), BF), S((2, 2, 8, 64, 128), BF), S((16, D), F32), S((1024, 128), F32),
            S((2, 8, 64, D), BF), S((2, D, 384), BF), S((4, 400, D), BF), S((D, 832), BF),
            S((8, 128, D), BF), S((8, 128, D), BF), S((832, D), BF),
        ),
        in_specs=[vm] * 11 + [any_] * 4,
        out_specs=(vm,) * 6 + (any_,) * 7,
        scratch_shapes=[
            V((400, 4800), BF), V((16, 1664), BF), V((400, 6400), BF), V((400, 832), BF), V((3, 16, 1664), BF), V((D, 384), BF), V((D, 384), BF), V((4, 64, D), BF), V((4, 400, D), BF),
            V((2, 8, 64, D), BF), V((128, D), BF), V((8, 2, 2, 64, 128), BF),
            dma((5, 3, 4)), dma((5,)), dma((1,)), dma((4,)), dma((3,)), dma((3,)), dma((4, 14)), dma((4, 8, 2)), dma((2,)), dma((2,)),
            dma((8,)), dma((8,)), dma((4,)),
        ],
        compiler_params=pltpu.CompilerParams(collective_id=0, has_side_effects=True, vmem_limit_bytes=60 << 20),
        cost_estimate=pl.CostEstimate(flops=6_000_000_000, bytes_accessed=60_000_000, transcendentals=4_000_000),
    )(tok, cot, *vectors, mixer, merge, expand, shrink)


class LineSum:

    def __init__(self, links, block, slots, send, recv, near=None, near_sem=None):
        self.links, self.block, self.send_sem, self.recv_sem = links, block, send, recv
        self.slots = slots if callable(slots) else lambda s: slots.at[s]
        self.near, self.near_sem = near, near_sem
        self.last = links.planes - 1

    def send(self, t, step):
        slot = t - 1 if step > 0 else self.left_slot(t)
        return self.links.copy(
            self.block(t), self.slots(slot), self.send_sem.at[t], self.recv_sem.at[slot], self.links.plane(step)
        )

    def left_slot(self, t):
        return (self.last + t) % (self.last + 2)

    def arrival(self, slot):
        return self.links.copy(
            self.slots(slot), self.slots(slot), self.send_sem.at[0], self.recv_sem.at[slot], self.links.plane(0)
        )

    def start(self):
        @pl.when(self.links.p == 0)
        def _():
            for t in range(self.last, 0, -1):
                self.send(t, 1).start()

        @pl.when(self.links.p == self.last)
        def _():
            for t in range(self.last):
                self.send(t, -1).start()

    def add(self, t, slot):
        self.arrival(slot).wait_recv()
        ref = self.block(t)
        came = self.slots(slot)
        if self.near is not None:
            copy = pltpu.make_async_copy(came, self.near, self.near_sem)
            copy.start()
            copy.wait()
            came = self.near
        ref[...] = (ref[...].astype(F32) + came[...].astype(F32)).astype(BF)

    def pump(self, u):
        p, last = self.links.p, self.last
        for t in range(1, last + 1):
            at = u - last + t
            if 0 < at < t:

                @pl.when(p == at)
                def _():
                    self.add(t, t - 1)
                    self.send(t, 1).start()

                @pl.when(p == last - at)
                def _():
                    self.add(last - t, self.left_slot(last - t))
                    self.send(last - t, -1).start()

    def total(self):
        p, last = self.links.p, self.last
        for t in range(last + 1):

            @pl.when(p == t)
            def _():
                if t > 0:
                    self.add(t, t - 1)
                if t < last:
                    self.add(t, self.left_slot(t))

    def finish(self):
        p = self.links.p
        for t in range(self.last + 1):

            @pl.when(p < t)
            def _():
                self.send(t, 1).wait_send()

            @pl.when(p > t)
            def _():
                self.send(t, -1).wait_send()


def backward_kernel(planes, vectors, attown, tok_h, cot_h, hid_h, lse_h, qkv_h, att_h,
                    shrink, w2_h, w1_h, sec_h, g_h, mfull_h, mw_h, first_h,
                    igrad_o, out_o, va_o, vb_o, gw1_o, gw2_o, gm0_o, gm1_o, gmg_o, atts_o, slot_mg,
                    tok, cot, hid, lse, qkv, att, mfull, mw, sec_all, g_all, w1b, w2b, act, slope, dw1, dw2, hlow, agrad, asend, gatt, hc, dkv, mgr, dmerge,
                    slot_w1, slot_w2, slot_m0, slot_m1, near_mg, stage, twin, far, va, vb, vslot,
                    zs, zr, zl, ld, ls_s, ls_r, ve_s, ve_r, gs, gr, gl, a_s, a_r, h_s, h_r, rs_s, rs_t, rs_f, free, sm):
    L = Links(planes)
    L.arrive(range(1, 8))
    p, me = L.p, L.me
    loads = [
        pltpu.make_async_copy(w1_h, w1b, ld.at[0]),
        pltpu.make_async_copy(sec_h, sec_all, ld.at[1]),
        pltpu.make_async_copy(g_h, g_all, ld.at[7]),
        pltpu.make_async_copy(mfull_h, mfull, ld.at[2]),
        pltpu.make_async_copy(mw_h, mw, ld.at[3]),
    ]
    small = [
        pltpu.make_async_copy(src, dst, sm.at[n])
        for n, (src, dst) in enumerate(
            ((tok_h, tok), (cot_h, cot), (hid_h, hid), (lse_h, lse), (qkv_h, qkv), (att_h, att))
        )
    ]
    att_all, first_all = g_all, sec_all
    late_att = pltpu.make_async_copy(atts_o, att_all, ld.at[5])
    late_first = pltpu.make_async_copy(first_h, first_all, ld.at[6])
    for c in loads + small:
        c.start()
    zw2 = EdgeGather(L, shrink.at[dyn(200 * me - 8 * lax.rem(me, 2), 208, 16)], w2_h, w2b, zs, zr, zl)
    cut2 = 768

    def shrink_line(n, first, last):
        return LineSum(
            L, lambda t: dw2.at[dyn(t * 208, 208, 16), first:last], lambda s: slot_w2.at[s, :, first:last], ls_s.at[n], ls_r.at[n]
        )

    lw2a, lw2b = shrink_line(0, 0, cut2), shrink_line(5, cut2, D)
    lw1 = LineSum(L, lambda t: dw1.at[dyn(t * 400, 400, 16)], slot_w1, ls_s.at[1], ls_r.at[1])
    lm0 = LineSum(L, lambda t: w1b.at[dyn(t * 400, 400, 16), 0:384], slot_m0, ls_s.at[2], ls_r.at[2])
    lm1 = LineSum(L, lambda t: w1b.at[dyn(t * 400, 400, 16), 384:768], slot_m1, ls_s.at[3], ls_r.at[3])
    lmg = LineSum(L, lambda t: dmerge.at[dyn(t * 400, 400, 16)], slot_mg, ls_s.at[4], ls_r.at[4], near_mg, ld.at[4])
    xa = LineExchange(L, vslot.at[0], ve_s.at[0], ve_r.at[0])
    xb = LineExchange(L, vslot.at[1], ve_s.at[1], ve_r.at[1])
    gatt_all = GroupGather(L, row_parts(atts_o, 64), gs.at[1], gr.at[1], own_parts(attown, 64), gl.at[1])

    def shrink_gather(n, first, last):
        sizes = (112, 96)

        def part(j, h):
            return gw2_o.at[j, 112 * h : 112 * h + sizes[h], first:last]

        def src(h):
            return dw2.at[dyn(p * 208 + 112 * h, sizes[h], 16), first:last]

        return GroupGather(L, part, gs.at[n], gr.at[n], src, gl.at[n])

    gw2a, gw2b = shrink_gather(0, 0, cut2), shrink_gather(2, cut2, D)
    def share_gather(n, out, line):
        def src(h):
            base, columns = line.home
            return base.at[dyn(p * 400 + 208 * h, (208, 192)[h], 16), columns[0] : columns[1]]

        return GroupGather(L, row_parts(out, 208), gs.at[n], gr.at[n], src, gl.at[n])

    lw1.home, lm0.home, lm1.home, lmg.home = (dw1, (0, 832)), (w1b, (0, 384)), (w1b, (384, 768)), (dmerge, (0, 256))
    gw1 = share_gather(3, gw1_o, lw1)
    gm0 = share_gather(4, gm0_o, lm0)
    gm1 = share_gather(5, gm1_o, lm1)
    gmg = share_gather(6, gmg_o, lmg)
    gva = SmallGather(L, va, lambda j: va_o.at[j], gs.at[7], gr.at[7], gl.at[7, 0])
    gvb = SmallGather(L, vb, lambda j: vb_o.at[j], gs.at[8], gr.at[8], gl.at[8, 0])
    L.barrier(range(1, 8))
    zw2.start()
    gatt_all.start()

    loads[0].wait()
    loads[1].wait()

    def expand(b, _):
        at = dyn(b * 256, 256, 256)
        pre = dot(sec_all[pl.ds(2 * b, 2)].reshape(256, D), w1b[...]) + vectors[8:9, :832]
        value, s = gelu_parts(pre)
        act[at] = value.astype(BF)
        slope[at] = s.astype(BF)
        return 0

    lax.fori_loop(0, 4, expand, 0)
    loads[2].wait()
    g2 = g_all[...].reshape(1024, D)
    for part, columns in ((lw2a, slice(0, cut2)), (lw2b, slice(cut2, D))):
        for start, size in ((0, 256), (256, 256), (512, 256), (768, 64)):
            dw2[start : start + size, columns] = t_dot(act[:, start : start + size], g2[:, columns]).astype(BF)
        if part is lw2a:
            lw2a.start()
    zw2.relay()
    gatt_all.forward()
    lw2a.pump(1)
    gatt_all.wait()
    lw2a.pump(2)
    lw2b.start()
    zw2.wait()

    def contract(b, acc):
        at = dyn(b * 256, 256, 256)
        grad = dot_t(g_all[pl.ds(2 * b, 2)].reshape(256, D), w2b[...]) * slope[at].astype(F32)
        slope[at] = grad.astype(BF)
        return acc + jnp.sum(grad, axis=0, keepdims=True)

    dgb = lax.fori_loop(0, 4, contract, jnp.zeros((1, 832), F32))
    late_att.start()
    rounds = [GroupSum(L, stage, twin, far, rs_s.at[n], rs_t.at[n], rs_f.at[n]) for n in range(3)]

    def release(n):
        for mask in (1, 2, 4):
            pl.semaphore_signal(free.at[n], inc=1, device_id=L.peer(mask), device_id_type=MESH_ID)

    back = rounds[0]
    back.run(lambda owner: dot_t(slope[dyn(owner * 128, 128, 128)], w1b[...]))
    lw2b.pump(1)
    for start in range(0, D, 256):
        size = min(256, D - start)
        x = sec_all[:, :, start : start + size].reshape(1024, size)
        dw1[start : start + size] = t_dot(x, slope[...]).astype(BF)
    late_first.start()
    lw1.start()
    back.relay()
    lw2b.pump(2)
    lw2a.total()
    gw2a.start()
    grad2 = back.total()
    back.finish()
    release(0)

    for c in small:
        c.wait()
    tangent = cot[...].astype(F32)
    normal2, inverse2 = normalize(hid[...])
    hidden_grad = tangent + norm_back(grad2, vectors[5:6], normal2, inverse2)
    igrad_o[...] = hidden_grad
    hlow[:, 0:D] = hidden_grad.astype(BF)
    hlow[:, D:2048] = jnp.zeros((128, 2048 - D), BF)
    va[0:1] = jnp.sum(hidden_grad, axis=0, keepdims=True)
    va[1:2] = jnp.sum(grad2 * normal2, axis=0, keepdims=True)
    va[2:3] = jnp.sum(grad2, axis=0, keepdims=True)
    va[3:4] = jnp.sum(tangent, axis=0, keepdims=True)
    va[4:8] = jnp.zeros((4, D), F32)
    va[4:5, 0:832] = dgb

    def columns(mask):
        to = me ^ mask
        return L.copy(hlow.at[:, dyn(to * 256, 256, 256)], hc.at[me], h_s.at[mask], h_r.at[me], L.peer(mask))

    def columns_in(mask):
        return L.copy(hc.at[me], hc.at[me ^ mask], h_s.at[mask], h_r.at[me ^ mask], L.peer(mask))

    loads[3].wait()
    agrad[...] = dot_t(hlow[:, 0:D], mfull[...]).astype(BF)
    for j in range(8):
        asend[j, 0] = agrad[:, 192 * j : 192 * j + 128].reshape(2, 64, 128)
        tail = agrad[:, 192 * j + 128 : 192 * j + 192]
        asend[j, 1] = jnp.concatenate([tail, jnp.zeros((128, 64), BF)], axis=1).reshape(2, 64, 128)

    def exchange(mask):
        return L.copy(asend.at[me ^ mask], gatt.at[:, :, me], a_s.at[mask], a_r.at[me], L.peer(mask))

    def arrived(mask):
        return L.copy(asend.at[me], gatt.at[:, :, me ^ mask], a_s.at[mask], a_r.at[me ^ mask], L.peer(mask))

    for mask in range(1, 8):
        exchange(mask).start()
    gatt[:, :, me] = asend[me]
    for mask in range(1, 8):
        columns(mask).start()
    pl.semaphore_wait(free.at[0], 3)
    outs = rounds[1]
    outs.run(lambda owner: dot(act[dyn(owner * 128, 128, 128)], w2b[...]))
    hc[me] = hlow[:, dyn(me * 256, 256, 256)]
    dkv[...] = jnp.zeros(dkv.shape, F32)
    for mask in range(1, 8):
        arrived(mask).wait_recv()

    scale = jnp.asarray(0.125, BF)

    def head_back(pair, head, mask, q, g, o, stat, pieces, allowed):
        delta = jnp.sum(g.astype(F32) * o.astype(F32), axis=1, keepdims=True)
        dq = 0.0
        for start, size, kind in pieces:
            keys = qkv[2 + pair, start : start + size]
            s = dot_t(q, keys)
            if kind:
                s = jnp.where(allowed(kind, start, s.shape), s, -1e30)
            prob = jnp.exp(s - stat)
            ds = (prob * (dot_t(g, qkv[4 + pair, start : start + size]) - delta)).astype(BF)
            dq = dq + dot(ds, keys)
            dkv[0, start : start + size] += t_dot(ds, q)
            dkv[1, start : start + size] += t_dot(prob.astype(BF), g)
        return jnp.where(mask, dq, 0.0) * 0.125

    def private_back(pair, half):
        mask = half_mask(half)
        head = 2 * pair + half
        total = 0.0
        for b in range(4):
            at = slice(b * 256, b * 256 + 256)
            blk = (pair, b // 2, pl.ds((b % 2) * 4, 4))
            q = jnp.where(mask, qkv[pair, at], 0) * scale
            g = jnp.where(mask, gatt[blk].reshape(256, 128), 0)
            o = att[blk].reshape(256, 128)
            dq = head_back(
                pair, head, mask, q, g, o, lse[at, head : head + 1], BLOCK_KEYS[b],
                lambda kind, start, shape: triangle(kind, shape),
            )
            total = total + jnp.sum(dq, axis=0, keepdims=True)
            if half == 0:
                mgr[pair, at, 0:128] = dq.astype(BF)
            else:
                mgr[pair, at, 0:128] = mgr[pair, at, 0:128] + dq.astype(BF)
        return total

    def mixer_part(pair):
        mgr[pair, :, 128:256] = dkv[0].astype(BF)
        mgr[pair, :, 256:384] = dkv[1].astype(BF)
        va[6:7, pair * 128 : pair * 128 + 128] = jnp.sum(dkv[1], axis=0, keepdims=True)
        for start in range(0, D, 256):
            size = min(256, D - start)
            x = first_all[:, :, start : start + size].reshape(1024, size)
            w1b[start : start + size, 384 * pair : 384 * pair + 384] = t_dot(x, mgr[pair]).astype(BF)

    qb0 = private_back(0, 0)
    gw2a.forward()
    qb0 = qb0 + private_back(0, 1)
    va[5:6, 0:128] = qb0
    late_first.wait()
    mixer_part(0)
    dkv[...] = jnp.zeros(dkv.shape, F32)
    lm0.start()
    outs.relay()
    lw2b.total()
    gw2b.start()
    qb1 = private_back(1, 0)
    mask1 = half_mask(1)
    own_early, own_late = dyn(me * 64, 64, 64), dyn(512 + me * 64, 64, 64)
    qs = jnp.concatenate([qkv[1, own_early], qkv[1, own_late]], axis=0)
    qs = jnp.where(mask1, qs, 0) * scale
    blank = jnp.zeros((128, 64), BF)
    g_s = jnp.concatenate([blank, agrad[:, 1536:1600]], axis=1)
    o_s = jnp.concatenate([blank, attown[:, 1536:1600]], axis=1)

    def own_allowed(kind, start, shape):
        r = lax.broadcasted_iota(jnp.int32, shape, 0)
        c = lax.broadcasted_iota(jnp.int32, shape, 1) + start
        rp = jnp.where(r < 64, me * 64 + r, 1023 - (me * 64 + r - 64))
        cp = jnp.where(c < 512, c, 1023 - (c - 512))
        return cp <= rp

    dqs = head_back(1, 3, mask1, qs, g_s, o_s, lse[0:128, 3:4], ((0, 512, 1), (512, 512, 1)), own_allowed)
    va[5:6, 128:256] = qb1 + jnp.sum(dqs, axis=0, keepdims=True)
    dqs_low = dqs.astype(BF)
    mgr[1, own_early, 0:128] = mgr[1, own_early, 0:128] + dqs_low[:64]
    mgr[1, own_late, 0:128] = mgr[1, own_late, 0:128] + dqs_low[64:]
    mixer_part(1)
    lm1.start()
    xa.start(va)
    lw1.pump(1)
    out_o[...] = (outs.total() + hid[...] + vectors[7:8]).astype(BF)
    outs.finish()
    release(1)
    loads[4].wait()
    pl.semaphore_wait(free.at[1], 3)
    sums = rounds[2]

    def first_block(owner):
        early, late = dyn(owner * 64, 64, 64), dyn(512 + owner * 64, 64, 64)
        x0 = jnp.concatenate([mgr[0, early], mgr[0, late]], axis=0)
        x1 = jnp.concatenate([mgr[1, early], mgr[1, late]], axis=0)
        return dot_t(x0, mw[0]) + dot_t(x1, mw[1])

    sums.run(first_block)
    gw2b.forward()
    lw1.pump(2)
    sums.relay()
    lw1.total()
    gw1.start()
    lm0.pump(1)
    late_att.wait()
    for mask in range(1, 8):
        columns_in(mask).wait_recv()
    h2 = hc[...].reshape(1024, 256)
    for start in range(0, D, 256):
        size = min(256, D - start)
        x = att_all[:, :, start : start + size].reshape(1024, size)
        dmerge[start : start + size] = t_dot(x, h2).astype(BF)
    lmg.start()
    lm0.pump(2)
    first_grad = sums.total()
    rows = tok[...].astype(F32)
    normal1, inverse1 = normalize(rows)
    igrad_o[...] += norm_back(first_grad, vectors[0:1], normal1, inverse1)
    vb[0:1] = jnp.sum(first_grad * normal1, axis=0, keepdims=True)
    vb[1:2] = jnp.sum(first_grad, axis=0, keepdims=True)
    vb[2:8] = jnp.zeros((6, D), F32)
    xb.start(vb)
    lm0.total()
    gm0.start()
    lm1.pump(1)
    gw1.forward()
    lm1.pump(2)
    gm0.forward()
    lm1.total()
    gm1.start()
    lmg.pump(1)
    total_a = xa.total(va)
    xa.finish(va)
    va[...] = total_a
    gva.start()
    lmg.pump(2)
    total_b = xb.total(vb)
    xb.finish(vb)
    vb[...] = total_b
    gvb.start()
    lmg.total()
    gmg.start()
    gm1.forward()
    gva.forward()
    gvb.forward()
    gmg.forward()
    for g in (gw2a, gw2b, gva, gw1, gvb, gm0, gm1, gmg):
        g.wait()
    for g in (gatt_all, gw2a, gw2b, gw1, gm0, gm1, gmg, gva, gvb):
        g.finish()
    zw2.finish()
    for s in (lw2a, lw2b, lw1, lm0, lm1, lmg):
        s.finish()
    for mask in range(1, 8):
        exchange(mask).wait_send()
        columns(mask).wait_send()
    sums.finish()


def run_backward(planes, *operands):
    any_ = pl.BlockSpec(memory_space=pl.ANY)
    vm = pl.BlockSpec(memory_space=pltpu.VMEM)
    S = jax.ShapeDtypeStruct
    V = pltpu.VMEM
    dma = pltpu.SemaphoreType.DMA
    return pl.pallas_call(
        functools.partial(backward_kernel, planes),
        out_shape=(
            S((128, D), F32), S((128, D), BF), S((8, 8, D), F32), S((8, 8, D), F32), S((8, 400, 832), BF), S((8, 208, D), BF),
            S((8, 400, 384), BF), S((8, 400, 384), BF), S((8, 400, 256), BF), S((8, 128, D), BF),
            S((5, 400, 256), BF),
        ),
        in_specs=[vm] * 2 + [any_] * 14,
        out_specs=(vm,) * 2 + (any_,) * 9,
        scratch_shapes=[
            V((128, D), BF), V((128, D), BF), V((128, D), F32), V((1024, 128), F32), V((6, 1024, 128), BF), V((2, 2, 8, 64, 128), BF),
            V((D, D), BF), V((2, D, 384), BF), V((8, 128, D), BF), V((8, 128, D), BF), V((D, 832), BF), V((832, D), BF),
            V((1024, 832), BF), V((1024, 832), BF), V((D, 832), BF), V((832, D), BF),
            V((128, 2048), BF), V((128, D), BF), V((8, 2, 2, 64, 128), BF), V((2, 2, 8, 64, 128), BF),
            V((8, 128, 256), BF), V((2, 1024, 128), F32), V((2, 1024, 384), BF), V((D, 256), BF),
            V((5, 400, 832), BF), V((5, 208, D), BF), V((5, 400, 384), BF), V((5, 400, 384), BF), V((400, 256), BF),
            V((8, 128, D), BF), V((4, 128, D), BF), V((3, 128, D), BF), V((8, D), F32), V((8, D), F32), V((2, 3, 8, D), F32),
            dma((4,)), dma((4,)), dma((3,)), dma((8,)), dma((6, 4)), dma((6, 5)), dma((2, 3)), dma((2, 3)), dma((9, 14)), dma((9, 8, 2)), dma((9, 2)),
            dma((8,)), dma((8,)), dma((8,)), dma((8,)), dma((3, 14)), dma((3, 4)), dma((3, 6)), pltpu.SemaphoreType.REGULAR((2,)), dma((6,)),
        ],
        compiler_params=pltpu.CompilerParams(collective_id=1, has_side_effects=True, vmem_limit_bytes=(64 << 20) - 65536),
        cost_estimate=pl.CostEstimate(flops=25_000_000_000, bytes_accessed=60_000_000, transcendentals=4_000_000),
    )(*operands)


def assemble_kernel(gw1, gm0, gm1, gmg, gw2, va, vb, input_grad, output,
                    expand_o, mixer_o, merge_o, shrink_o, input_o, output_o, *vectors_o):
    step = pl.program_id(0)

    @pl.when(step < 5)
    def _():
        assemble_rows(gw1, gm0, gm1, gmg, expand_o, mixer_o, merge_o)

    @pl.when(step >= 5)
    def _():
        for odd in range(2):
            shrink_o[200 * odd : 200 * odd + 200] = gw2[odd, 8 * odd : 8 * odd + 200].astype(F32)

    @pl.when(step == 0)
    def _():
        input_o[...] = input_grad[...]
        output_o[...] = output[...]
        assemble_vectors(va, vb, vectors_o)


def assemble_rows(gw1, gm0, gm1, gmg, expand_o, mixer_o, merge_o):
    for j in range(8):
        odd = 8 * (j % 2)
        for q in range(4):
            at = 1600 * q + 200 * j
            expand_o[:, at : at + 200] = gw1[j, :, 208 * q + odd : 208 * q + odd + 200].astype(F32)
        for n in range(3):
            at = D * n + 192 * j
            mixer_o[:, at : at + 128] = gm0[j, :, 128 * n : 128 * n + 128].astype(F32)
            mixer_o[:, at + 128 : at + 192] = gm1[j, :, 128 * n : 128 * n + 64].astype(F32)
    for n in range(3):
        total = gm1[0, :, 128 * n : 128 * n + 128].astype(F32)
        for j in range(1, 8):
            total += gm1[j, :, 128 * n : 128 * n + 128].astype(F32)
        mixer_o[:, D * n + 1536 : D * n + 1600] = total[:, 64:]
    for j in range(6):
        merge_o[:, 256 * j : 256 * j + 256] = gmg[j].astype(F32)
    merge_o[:, 1536:1600] = gmg[6, :, :64].astype(F32)


def assemble_vectors(va, vb, vectors_o):
    p = lax.axis_index("fsdp")
    early, late = va[0], vb[0]
    for j in range(1, 8):
        early += va[j]
        late += vb[j]

    def per_head(n):
        return jnp.concatenate([va[j, n : n + 1, :192] for j in range(8)] + [early[n : n + 1, 192:256]], axis=1)

    rows = jnp.concatenate(
        [late[0:2], per_head(5), per_head(6), early[0:4]], axis=0
    )
    rows = jnp.concatenate([rows, jnp.zeros((8, 64), F32)], axis=1)
    rows = shift_left(rows, 400 * p)
    bias = jnp.concatenate([va[j, 4:5, :] for j in range(8)], axis=0)
    bias = shift_left(jnp.concatenate([bias, jnp.zeros((8, 64), F32)], axis=1), 208 * p)
    bias = jnp.concatenate([bias[j : j + 1, 8 * (j % 2) : 8 * (j % 2) + 200] for j in range(8)], axis=1)
    for n in range(8):
        vectors_o[n][...] = rows[n, :400]
    vectors_o[8][...] = bias[0]


def assemble(gw1, gm0, gm1, gmg, gw2, va, vb, input_grad, output):
    rows, first = 80, 5

    def part(width):
        return pl.BlockSpec((8, rows, width), lambda n: (0, jnp.minimum(n, first - 1), 0))

    def whole(width):
        return pl.BlockSpec((rows, width), lambda n: (jnp.minimum(n, first - 1), 0))

    own = pl.BlockSpec((128, D), lambda n: (0, 0))
    small = pl.BlockSpec((8, 8, D), lambda n: (0, 0, 0))

    def vector(width):
        return pl.BlockSpec((width,), lambda n: (0,))

    S = jax.ShapeDtypeStruct
    return pl.pallas_call(
        assemble_kernel,
        grid=(first + 4,),
        in_specs=[part(832), part(384), part(384), part(256), pl.BlockSpec((2, 208, D), lambda n: (jnp.maximum(n - first, 0), 0, 0)), small, small, own, own],
        out_specs=(whole(6400), whole(4800), whole(D), pl.BlockSpec((400, D), lambda n: (jnp.maximum(n - first, 0), 0)), own, own) + (vector(400),) * 8 + (vector(1600),),
        out_shape=(S((400, 6400), F32), S((400, 4800), F32), S((400, D), F32), S((1600, D), F32), S((128, D), F32), S((128, D), BF)) + (S((400,), F32),) * 8 + (S((1600,), F32),),
        compiler_params=pltpu.CompilerParams(vmem_limit_bytes=63 << 20),
    )(gw1, gm0, gm1, gmg, gw2, va, vb, input_grad, output)


def local_plain(
    tokens,
    first_gain,
    first_shift,
    mixer_weight,
    query_bias,
    value_bias,
    merge_weight,
    merge_bias,
    second_gain,
    second_shift,
    expand_weight,
    expand_bias,
    shrink_weight,
    shrink_bias,
    cotangent,
):
    planes = lax.axis_size("fsdp")
    ring = lax.axis_size("ctx")
    me = lax.axis_index("ctx")
    blocks = tokens.shape[2]
    local_rows = 2 * blocks
    half = blocks * ring
    length = 2 * half
    private = H // ring
    shared = H - private * ring
    pc, sc = private * HD, shared * HD
    hc = pc + sc
    shared_at = private * ring * HD
    share = D // planes
    ff_plane = expand_bias.shape[0]
    ff_part = ff_plane // ring
    cols = D // ring

    vectors = jnp.stack(
        [first_gain, first_shift, query_bias, value_bias, merge_bias, second_gain, second_shift, shrink_bias]
    )
    vectors = lax.all_gather(vectors, "fsdp", axis=1, tiled=True).astype(F32)
    gain1, shift1, qbias, vbias, mbias, gain2, shift2, sbias = [vectors[n] for n in range(8)]

    def head_columns(weight, base):
        mine = lax.dynamic_slice_in_dim(weight, base + me * pc, pc, weight.ndim - 1)
        every = weight[..., base + shared_at : base + D]
        return [mine, every]

    mixer_part = jnp.concatenate(
        head_columns(mixer_weight, 0) + head_columns(mixer_weight, D) + head_columns(mixer_weight, 2 * D), axis=1
    )
    mixer_mine = lax.all_gather(mixer_part, "fsdp", axis=0, tiled=True)

    merge_part = lax.dynamic_slice_in_dim(merge_weight, me * cols, cols, 1)
    merge_cols = lax.all_gather(merge_part, "fsdp", axis=0, tiled=True)
    merge_full = lax.all_gather(merge_cols, "ctx", axis=1, tiled=True)

    expand_part = expand_weight.reshape(share, planes, ring, ff_part)
    expand_part = lax.dynamic_index_in_dim(expand_part, me, 2, keepdims=False)
    expand_part = lax.all_to_all(expand_part, "fsdp", 1, 0, tiled=False).reshape(D, ff_part)
    expand_mine = lax.all_gather(expand_part, "ctx", axis=1, tiled=True)

    rows = tokens.reshape(local_rows, D).astype(F32)
    normal1, inverse1 = normalize(rows)
    first = (normal1 * gain1 + shift1).astype(BF)
    first_all = lax.all_gather(first.reshape(2, blocks, D), "ctx", axis=1, tiled=True).reshape(length, D)
    tangent_low = cotangent.reshape(local_rows, D)
    tangent = tangent_low.astype(F32)
    tangent_all = lax.all_gather(tangent_low, "fsdp", axis=0, tiled=True)

    mixed = dot(first_all, mixer_mine)
    qb = jnp.concatenate(head_columns(qbias, 0), axis=0)
    vb = jnp.concatenate(head_columns(vbias, 0), axis=0)
    query = (mixed[:, :hc] + qb).astype(BF)
    key = mixed[:, hc : 2 * hc].astype(BF)
    value = (mixed[:, 2 * hc :] + vb).astype(BF)
    half_index = jnp.arange(half, dtype=jnp.int32)
    place = jnp.concatenate([half_index, length - 1 - half_index])
    early = me * blocks + jnp.arange(blocks, dtype=jnp.int32)
    own_place = jnp.concatenate([early, length - 1 - early])
    allowed = place[None, :] <= place[:, None]
    own_allowed = place[None, :] <= own_place[:, None]

    def own_rows(values):
        parts = values.reshape(2, half, values.shape[1])
        return lax.dynamic_slice_in_dim(parts, me * blocks, blocks, 1).reshape(local_rows, values.shape[1])

    qp, kp, vp = heads_first(query[:, :pc]), heads_first(key[:, :pc]), heads_first(value[:, :pc])
    qs, ks, vs = heads_first(own_rows(query[:, pc:])), heads_first(key[:, pc:]), heads_first(value[:, pc:])
    out_p, top_p, total_p = attend(qp, kp, vp, allowed)
    out_s, top_s, total_s = attend(qs, ks, vs, own_allowed)
    att_heads = heads_last(out_p).astype(BF)
    att_pieces = lax.all_to_all(att_heads.reshape(2, ring, blocks, pc), "ctx", 1, 2, tiled=False)
    attended = jnp.concatenate(
        [att_pieces.reshape(local_rows, ring * pc), heads_last(out_s).astype(BF)], axis=1
    )
    hidden = rows + dot(attended, merge_full) + mbias
    normal2, inverse2 = normalize(hidden)
    second = (normal2 * gain2 + shift2).astype(BF)
    second_all = lax.all_gather(second, "fsdp", axis=0, tiled=True)
    attended_all = lax.all_gather(attended, "ctx", axis=0, tiled=True)

    pre = dot(second_all, expand_mine) + expand_bias.astype(F32)
    act, gate_pull = jax.vjp(lambda u: jax.nn.gelu(u, approximate=True), pre)
    act_low = act.astype(BF)
    act_grad = dot_t(tangent_all, shrink_weight)
    (pre_grad,) = gate_pull(act_grad)
    pre_low = pre_grad.astype(BF)
    second_part = dot_t(pre_low, expand_mine).astype(BF)
    second_grad = lax.psum_scatter(second_part, "fsdp", scatter_dimension=0, tiled=True).astype(F32)
    out_part = dot(act_low, shrink_weight).astype(BF)
    out_sum = lax.psum_scatter(out_part, "fsdp", scatter_dimension=0, tiled=True).astype(F32)
    output = (hidden + out_sum + sbias).astype(BF).reshape(1, 2, blocks, D)
    expand_bias_grad = jnp.sum(pre_grad, axis=0)
    shrink_grad = t_dot(act_low, tangent_all).astype(BF)
    shrink_mine = lax.psum_scatter(shrink_grad, "ctx", scatter_dimension=0, tiled=True)
    shrink_owned = lax.all_gather(shrink_mine, "ctx", axis=0, tiled=True).astype(F32)
    expand_grad = t_dot(second_all, pre_low).astype(BF)
    expand_cols = lax.psum_scatter(expand_grad, "ctx", scatter_dimension=1, tiled=True)
    expand_rows = lax.all_to_all(expand_cols.reshape(planes, share, ff_part), "fsdp", 0, 1, tiled=False)
    expand_owned = (
        lax.all_gather(expand_rows, "ctx", axis=2, tiled=False).reshape(share, planes * ff_plane).astype(F32)
    )

    hidden_grad = tangent + norm_back(second_grad, gain2, normal2, inverse2)
    hidden_low = hidden_grad.astype(BF)
    att_grad = dot_t(hidden_low, merge_full).astype(BF)
    grad_pieces = lax.all_to_all(att_grad[:, :shared_at].reshape(2, blocks, ring, pc), "ctx", 2, 1, tiled=False)
    grad_p = heads_first(grad_pieces.reshape(length, pc))
    grad_s = heads_first(att_grad[:, shared_at:])
    dqp, dkp, dvp = attend_back(qp, kp, vp, allowed, top_p, total_p, grad_p)
    dqs, dks, dvs = attend_back(qs, ks, vs, own_allowed, top_s, total_s, grad_s)
    dqs_all = jnp.zeros((2, half, sc), F32)
    dqs_all = lax.dynamic_update_slice_in_dim(dqs_all, heads_last(dqs).reshape(2, blocks, sc), me * blocks, 1)
    mixed_grad = jnp.concatenate(
        [heads_last(dqp), dqs_all.reshape(length, sc)]
        + [heads_last(dkp), heads_last(dks), heads_last(dvp), heads_last(dvs)],
        axis=1,
    )
    bias_sums = jnp.sum(mixed_grad, axis=0)
    mixed_low = mixed_grad.astype(BF)
    first_part = dot_t(mixed_low, mixer_mine).astype(BF)
    first_grad = lax.psum_scatter(
        first_part.reshape(2, half, D), "ctx", scatter_dimension=1, tiled=True
    ).reshape(local_rows, D).astype(F32)
    input_grad = hidden_grad + norm_back(first_grad, gain1, normal1, inverse1)
    mixer_part_grad = t_dot(first_all, mixed_low).astype(BF)
    mixer_rows = lax.psum_scatter(mixer_part_grad, "fsdp", scatter_dimension=0, tiled=True)
    mixer_all = lax.all_gather(mixer_rows, "ctx", axis=0, tiled=False).astype(F32)

    def place_columns(values):
        mine = values[:, :, :pc].transpose(1, 0, 2).reshape(share, ring * pc)
        return [mine, jnp.sum(values[:, :, pc:], axis=0)]

    mixer_owned = jnp.concatenate(
        place_columns(mixer_all[:, :, :hc])
        + place_columns(mixer_all[:, :, hc : 2 * hc])
        + place_columns(mixer_all[:, :, 2 * hc :]),
        axis=1,
    )
    hidden_cols = lax.all_to_all(hidden_low.reshape(local_rows, ring, cols), "ctx", 1, 0, tiled=False)
    merge_grad = t_dot(attended_all, hidden_cols.reshape(length, cols)).astype(BF)
    merge_rows = lax.psum_scatter(merge_grad, "fsdp", scatter_dimension=0, tiled=True)
    merge_owned = lax.all_gather(merge_rows, "ctx", axis=1, tiled=True).astype(F32)

    def spread_bias(values):
        full = jnp.zeros((D,), F32)
        full = lax.dynamic_update_slice_in_dim(full, values[:pc], me * pc, 0)
        return full.at[shared_at:].set(values[pc:])

    sums = jnp.stack(
        [
            jnp.sum(first_grad * normal1, axis=0),
            jnp.sum(first_grad, axis=0),
            spread_bias(bias_sums[:hc]),
            spread_bias(bias_sums[2 * hc :]),
            jnp.sum(hidden_grad, axis=0),
            jnp.sum(second_grad * normal2, axis=0),
            jnp.sum(second_grad, axis=0),
            jnp.sum(tangent, axis=0),
        ]
    )
    sums = lax.psum(sums, ("fsdp", "ctx"))
    mine = lax.dynamic_slice_in_dim(sums, lax.axis_index("fsdp") * share, share, 1)
    expand_bias_owned = lax.psum(expand_bias_grad, "ctx")

    return (
        output,
        input_grad.reshape(1, 2, blocks, D),
        mine[0],
        mine[1],
        mixer_owned,
        mine[2],
        mine[3],
        merge_owned,
        mine[4],
        mine[5],
        mine[6],
        expand_owned,
        expand_bias_owned,
        shrink_owned,
        mine[7],
    )


def local_kernel(
    tokens,
    first_gain,
    first_shift,
    mixer_weight,
    query_bias,
    value_bias,
    merge_weight,
    merge_bias,
    second_gain,
    second_shift,
    expand_weight,
    expand_bias,
    shrink_weight,
    shrink_bias,
    cotangent,
):
    planes = lax.axis_size("fsdp")
    blocks, local_rows = tokens.shape[2], 2 * tokens.shape[2]
    vectors = (
        first_gain, first_shift, query_bias, value_bias, merge_bias, second_gain, second_shift, shrink_bias, expand_bias
    )

    tok2, cot2 = tokens.reshape(local_rows, D), cotangent.reshape(local_rows, D)
    hidden, qkv, attown, heads, whole, lse, first_all, mws, mfull, w1_all, sec_all, g_all, w2_early = run_attend(
        planes, tok2, cot2, vectors, mixer_weight, merge_weight, expand_weight, shrink_weight
    )
    input_part, out_part, va, vb, gw1, gw2, gm0, gm1, gmg, _, _ = run_backward(
        planes, whole, attown, tok2, cot2, hidden, lse, qkv, heads,
        shrink_weight, w2_early, w1_all, sec_all, g_all, mfull.reshape(D, D), mws, first_all.reshape(8, 128, D)
    )
    expand_owned, mixer_owned, merge_owned, shrink_owned, input_grad, out_own, *small = assemble(
        gw1, gm0, gm1, gmg, gw2, va, vb, input_part, out_part
    )
    gain1, shift1, qbias, vbias, mbias, gain2, shift2, sbias, bias1 = small

    return (
        out_own.reshape(1, 2, blocks, D),
        input_grad.reshape(1, 2, blocks, D),
        gain1,
        shift1,
        mixer_owned,
        qbias,
        vbias,
        merge_owned,
        mbias,
        gain2,
        shift2,
        expand_owned,
        bias1,
        shrink_owned,
        sbias,
    )


def aligned(planes, ring, shape):
    return planes == 4 and ring == 8 and shape == (4, 2, 512, D)


def local(tokens, *others):
    planes, ring = lax.axis_size("fsdp"), lax.axis_size("ctx")
    whole = (tokens.shape[0] * planes, 2, tokens.shape[2] * ring, tokens.shape[3])
    if aligned(planes, ring, whole):
        return local_kernel(tokens, *others)
    return local_plain(tokens, *others)


def solution(mesh):
    token_spec = P("fsdp", None, "ctx", None)
    row = P("fsdp")
    matrix = P("fsdp", None)
    in_specs = (
        token_spec,
        row,
        row,
        matrix,
        row,
        row,
        matrix,
        row,
        row,
        row,
        matrix,
        row,
        matrix,
        row,
        token_spec,
    )
    out_specs = (
        token_spec,
        token_spec,
        row,
        row,
        matrix,
        row,
        row,
        matrix,
        row,
        row,
        row,
        matrix,
        row,
        matrix,
        row,
    )
    return jax.shard_map(local, mesh=mesh, in_specs=in_specs, out_specs=out_specs, check_vma=False)
```
